32 devices in a mesh: gx: 2 (over y), gy: 4 (over x, core), gz: 4 (over z).
Axes of the slice: x: 2, y: 2, z: 4, core: 2. Of those that a mesh axis runs over, the one named last changes fastest.
Arguments:
- volume: bfloat16 [32, 16, 32, 128], P('gz', 'gx', 'gy'), may hold values from -6 to 6
- cotangent: bfloat16 [32, 16, 32, 128], P('gz', 'gx', 'gy'), may hold values from -0.125 to 0.125
- w_conv: bfloat16 [128, 27, 128], replicated, may hold values from -0.109375 to 0.109375
- w_down: bfloat16 [8, 128, 512], replicated, may hold values from -0.25 to 0.25
- w_bottle: bfloat16 [512, 27, 512], P(None, None, 'gz'), may hold values from -0.0546875 to 0.0546875
- w_up: bfloat16 [8, 512, 128], replicated, may hold values from -0.375 to 0.375
Outputs:
- output: bfloat16 [32, 16, 32, 128], P('gz', 'gx', 'gy')
- grad_conv: float32 [128, 27, 128], P(('gx', 'gy'))
- grad_bottle: float32 [512, 27, 512], P(('gx', 'gy'), None, 'gz')
The draws below stay inside these ranges and needn't reach their ends.
All inputs are finite; a program needn't handle non-finite values.
Results may differ from the reference program's by a relative error of at most 0.015.
Values may be sent and summed in bfloat16 or wider, within the bound.
No kernel may reach another device: no remote copies, remote signals or barrier semaphores. Data moves between devices by JAX's collectives and lax.ppermute only.
A program may use at most 64 MiB of HBM per device.

```python
import jax
import jax.numpy as jnp
from jax import lax

C = 128
CB = 512
ZF = 32
XF = 16
YF = 32


def block_levels(key, shape, shards, least, largest):
    level, own = 1.0, jax.random.fold_in(key, 6)
    for dim, shards_of in shards:
        draws = jnp.exp(jax.random.uniform(jax.random.fold_in(own, dim), (shards_of,), jnp.float32, least / len(shards), largest / len(shards)))
        level = level * jnp.repeat(draws, shape[dim] // shards_of).reshape([-1 if axis == dim else 1 for axis in range(len(shape))])
    return level


def scatter_about(own_key, shape, deviation, bound, cuts=(), kind=jnp.bfloat16):
    factor_of = block_levels(own_key, shape, cuts, -0.22, 0.18) if cuts else 1.0
    drawn = jax.random.normal(own_key, shape, jnp.float32) * deviation * factor_of
    return jnp.minimum(jnp.maximum(drawn, -bound), bound).astype(kind)


def setup_inputs(seed: int = 0) -> dict:
    key_of = jax.random.split(jax.random.key(seed), 7)
    volume = scatter_about(key_of[0], (ZF, XF, YF, C), 1.0, 6.0, ((0, 4), (1, 2), (2, 4)))
    cotangent = scatter_about(key_of[1], (ZF, XF, YF, C), ((ZF * XF * YF) ** -0.5), 0.125, ((0, 4), (1, 2), (2, 4)))
    w_conv = scatter_about(key_of[2], (C, 27, C), (27 * C) ** -0.5, 0.109375)
    w_down = scatter_about(key_of[3], (8, C, CB), (4 * C) ** -0.5, 0.25)
    w_bottle = scatter_about(key_of[4], (CB, 27, CB), (27 * CB) ** -0.5, 0.0546875, ((2, 4),))
    w_up = scatter_about(key_of[5], (8, CB, C), (CB // 2) ** -0.5, 0.375)
    return dict(volume=volume, cotangent=cotangent, w_conv=w_conv, w_down=w_down, w_bottle=w_bottle, w_up=w_up)


def silu_slope(values):
    sig = jax.nn.sigmoid(values)
    return sig * (1.0 + values * (1.0 - sig))

def conv_forward(padded, weight, extent):
    size_z, size_x, size_y = extent
    count_cells = size_z * size_x * size_y
    summed = jnp.zeros((count_cells, weight.shape[2]), jnp.float32)
    for tap_index in range(27):
        shift_z, shift_x, shift_y = (tap_index // 9, tap_index // 3 % 3, tap_index % 3)
        window = padded[shift_z:shift_z + size_z, shift_x:shift_x + size_x, shift_y:shift_y + size_y, :]
        window = window.reshape(count_cells, padded.shape[3])
        summed = summed + jnp.dot(window, weight[:, tap_index, :], preferred_element_type=jnp.float32)
    return summed.reshape(size_z, size_x, size_y, weight.shape[2])

def conv_weight_grad(padded, gradient, extent):
    size_z, size_x, size_y = extent
    count_cells = size_z * size_x * size_y
    flat_gradient = gradient.reshape(count_cells, gradient.shape[3])
    pieces = []
    for tap_index in range(27):
        shift_z, shift_x, shift_y = (tap_index // 9, tap_index // 3 % 3, tap_index % 3)
        window = padded[shift_z:shift_z + size_z, shift_x:shift_x + size_x, shift_y:shift_y + size_y, :]
        window = window.reshape(count_cells, padded.shape[3])
        pieces.append(lax.dot_general(window, flat_gradient, (((0,), (0,)), ((), ())), preferred_element_type=jnp.float32))
    return jnp.stack(pieces, axis=1)

def conv_input_grad(padded, weight, extent):
    size_z, size_x, size_y = extent
    count_cells = size_z * size_x * size_y
    summed = jnp.zeros((count_cells, weight.shape[0]), jnp.float32)
    for tap_index in range(27):
        shift_z, shift_x, shift_y = (2 - tap_index // 9, 2 - tap_index // 3 % 3, 2 - tap_index % 3)
        window = padded[shift_z:shift_z + size_z, shift_x:shift_x + size_x, shift_y:shift_y + size_y, :]
        window = window.reshape(count_cells, padded.shape[3])
        summed = summed + lax.dot_general(window, weight[:, tap_index, :], (((1,), (1,)), ((), ())), preferred_element_type=jnp.float32)
    return summed.reshape(size_z, size_x, size_y, weight.shape[0])

def pool_features(fine, kernel):
    size_z, size_x, size_y, channels = fine.shape
    blocks = fine.reshape(size_z // 2, 2, size_x // 2, 2, size_y // 2, 2, channels).astype(jnp.float32)
    kernel_cube = kernel.reshape(2, 2, 2, kernel.shape[1], kernel.shape[2]).astype(jnp.float32)
    return jnp.einsum('zaxbycf,abcfg->zxyg', blocks, kernel_cube)

def pool_adjoint(coarse_in, kernel):
    size_z, size_x, size_y, wide_channels = coarse_in.shape
    kernel_cube = kernel.reshape(2, 2, 2, kernel.shape[1], kernel.shape[2]).astype(jnp.float32)
    result = jnp.einsum('zxyg,abcfg->zaxbycf', coarse_in.astype(jnp.float32), kernel_cube)
    return result.reshape(2 * size_z, 2 * size_x, 2 * size_y, kernel.shape[1])

def lift_features(coarse_in, kernel):
    size_z, size_x, size_y, wide_channels = coarse_in.shape
    kernel_cube = kernel.reshape(2, 2, 2, kernel.shape[1], kernel.shape[2]).astype(jnp.float32)
    result = jnp.einsum('zxyg,abcgf->zaxbycf', coarse_in.astype(jnp.float32), kernel_cube)
    return result.reshape(2 * size_z, 2 * size_x, 2 * size_y, kernel.shape[2])

def lift_adjoint(fine, kernel):
    size_z, size_x, size_y, channels = fine.shape
    blocks = fine.reshape(size_z // 2, 2, size_x // 2, 2, size_y // 2, 2, channels).astype(jnp.float32)
    kernel_cube = kernel.reshape(2, 2, 2, kernel.shape[1], kernel.shape[2]).astype(jnp.float32)
    return jnp.einsum('zaxbycf,abcgf->zxyg', blocks, kernel_cube)

def reference(volume, cotangent, w_conv, w_down, w_bottle, w_up):
    size_z, size_x, size_y, channels = volume.shape
    fine_extent = (size_z, size_x, size_y)
    coarse_extent = (size_z // 2, size_x // 2, size_y // 2)
    padded = jnp.pad(volume, ((1, 1), (1, 1), (1, 1), (0, 0)))
    pre_hidden = conv_forward(padded, w_conv, fine_extent)
    hidden = jax.nn.silu(pre_hidden).astype(jnp.bfloat16)
    coarse = pool_features(hidden, w_down).astype(jnp.bfloat16)
    coarse_pad = jnp.pad(coarse, ((1, 1), (1, 1), (1, 1), (0, 0)))
    pre_bottle = conv_forward(coarse_pad, w_bottle, coarse_extent)
    bottle = jax.nn.silu(pre_bottle).astype(jnp.bfloat16)
    lifted = lift_features(bottle, w_up)
    output = (lifted + hidden.astype(jnp.float32)).astype(jnp.bfloat16)
    back_bottle = lift_adjoint(cotangent, w_up).astype(jnp.bfloat16)
    bottle_grad = (back_bottle.astype(jnp.float32) * silu_slope(pre_bottle)).astype(jnp.bfloat16)
    grad_bottle = conv_weight_grad(coarse_pad, bottle_grad, coarse_extent)
    grad_pad = jnp.pad(bottle_grad, ((1, 1), (1, 1), (1, 1), (0, 0)))
    coarse_grad = conv_input_grad(grad_pad, w_bottle, coarse_extent).astype(jnp.bfloat16)
    hidden_grad = ((pool_adjoint(coarse_grad, w_down) + cotangent.astype(jnp.float32)) * silu_slope(pre_hidden)).astype(jnp.bfloat16)
    grad_conv = conv_weight_grad(padded, hidden_grad, fine_extent)
    return (output, grad_conv, grad_bottle)
```

```python
import numpy as np
import jax
import jax.numpy as jnp
from jax import lax
from jax.experimental import pallas as pl
from jax.experimental.pallas import tpu as pltpu
from jax.sharding import PartitionSpec as P

BF16 = jnp.bfloat16
F32 = jnp.float32
VMEM_LIMIT = 56 * 1024 * 1024


def local_call(kernel, name, out_shapes, scratch=()):
    whole = pl.BlockSpec(memory_space=pltpu.VMEM)

    def call(*operands):
        return pl.pallas_call(
            kernel,
            name=name,
            out_shape=out_shapes,
            in_specs=[whole] * len(operands),
            out_specs=jax.tree.map(lambda _: whole, out_shapes),
            scratch_shapes=list(scratch),
            compiler_params=pltpu.CompilerParams(vmem_limit_bytes=VMEM_LIMIT),
        )(*operands)

    return call


def matmul(left, right):
    return jnp.dot(left, right, preferred_element_type=F32)


def matmul_nt(left, right):
    return lax.dot_general(left, right, (((1,), (1,)), ((), ())), preferred_element_type=F32)


def sub_order(size_x, size_y):
    half_x, half_y = size_x // 2, size_y // 2
    return {
        (2 * kx + b, 2 * ky + c): ((2 * b + c) * half_x + kx) * half_y + ky
        for b in range(2)
        for c in range(2)
        for kx in range(half_x)
        for ky in range(half_y)
    }


def fine_maps(size_x, size_y):
    own = size_x * size_y
    rows = sub_order(size_x, size_y)
    order = np.zeros((own, own), np.float32)
    taps = np.zeros((9, own, 2 * own), np.float32)
    for (x, y), row in rows.items():
        order[row, x * size_y + y] = 1
        for b in range(3):
            for c in range(3):
                sx, sy = x + b - 1, y + c - 1
                if sx < 0:
                    part = 0 if 0 <= sy < size_y else (4 if sy < 0 else 5)
                    source = own + 8 * part + sy % size_y
                elif sx >= size_x:
                    part = 1 if 0 <= sy < size_y else (6 if sy < 0 else 7)
                    source = own + 8 * part + sy % size_y
                elif sy < 0:
                    source = own + 16 + sx
                elif sy >= size_y:
                    source = own + 24 + sx
                else:
                    source = sx * size_y + sy
                taps[3 * b + c, row, source] = 1
    return order, taps


def coarse_maps(count_x, count_y, half_x, half_y):
    wide_x, wide_y = count_x * half_x, count_y * half_y

    def row_of(x, y):
        brick = (x // half_x) * count_y + y // half_y
        return (brick * half_x + x % half_x) * half_y + y % half_y

    shift = np.zeros((9, wide_x * wide_y, wide_x * wide_y), np.float32)
    for x in range(wide_x):
        for y in range(wide_y):
            for b in range(3):
                for c in range(3):
                    sx, sy = x + b - 1, y + c - 1
                    if 0 <= sx < wide_x and 0 <= sy < wide_y:
                        shift[3 * b + c, row_of(x, y), row_of(sx, sy)] = 1
    return shift


def spread(blocks, axes):
    return lax.all_to_all(blocks, axes, 0, 0, tiled=True)


def plane_rows(ref, z):
    _, size_x, size_y, channels = ref.shape
    return ref[z].astype(F32).reshape(size_x * size_y, channels)


def back_kernel(volume, cotangent, w_up, order, send, ordered):
    size_z, size_x, size_y, channels = volume.shape
    own = size_x * size_y
    quarter = own // 4
    count_z = send.shape[0]
    pz = lax.axis_index("gz")
    for z in range(size_z):
        ordered[z] = matmul(order[...], plane_rows(cotangent, z).astype(BF16)).astype(BF16)
    back = None
    for s in range(8):
        a, bc = s // 4, s % 4
        cells = jnp.concatenate(
            [ordered[2 * kz + a, bc * quarter : (bc + 1) * quarter, :] for kz in range(size_z // 2)], axis=0
        )
        term = matmul_nt(cells, w_up[s])
        back = term if back is None else back + term
    back = back.astype(BF16)
    group = back.shape[1] // count_z
    low = plane_rows(volume, 0).astype(BF16)
    high = plane_rows(volume, size_z - 1).astype(BF16)
    for q in range(count_z):
        send[q, :own, :] = jnp.where(q > pz, high, low)
        send[q, own:, :] = back[:, q * group : (q + 1) * group]


def depth_rim(volume, from_z, z):
    size_z, size_x, size_y, _ = volume.shape
    own = size_x * size_y
    count_z = from_z.shape[0]
    pz = lax.axis_index("gz")
    if z < 0:
        rows = from_z[jnp.maximum(pz - 1, 0), :own, :].astype(F32)
        return jnp.where(pz > 0, rows, 0.0)
    if z >= size_z:
        rows = from_z[jnp.minimum(pz + 1, count_z - 1), :own, :].astype(F32)
        return jnp.where(pz < count_z - 1, rows, 0.0)
    return plane_rows(volume, z)


def faces_kernel(count_y, volume, from_z, send, deep):
    size_z, size_x, size_y, channels = volume.shape
    own = size_x * size_y
    planes = size_z + 2
    px, py = lax.axis_index("gx"), lax.axis_index("gy")
    for z in range(planes):
        deep[z * own : (z + 1) * own, :] = depth_rim(volume, from_z, z - 1)

    def x_face(x):
        return jnp.concatenate(
            [deep[z * own + x * size_y : z * own + (x + 1) * size_y, :] for z in range(planes)], axis=0
        ).astype(BF16)

    def y_face(y):
        return deep[pl.ds(y, planes * size_x, stride=size_y), :].astype(BF16)

    x_low, x_high = x_face(0), x_face(size_x - 1)
    y_low, y_high = y_face(0), y_face(size_y - 1)
    for p in range(send.shape[0]):
        qx, qy = p // count_y, p % count_y
        along_y = jnp.where(qy > py, y_high, y_low)
        send[p] = jnp.where(qx > px, x_high, jnp.where(qx < px, x_low, along_y))


def hidden_kernel(
    count_x, count_y, volume, from_z, from_xy, taps, w_conv, w_down, hidden, slope, send, rim, rim32, cells
):
    size_z, size_x, size_y, channels = volume.shape
    own = size_x * size_y
    quarter = own // 4
    planes = size_z + 2
    px, py = lax.axis_index("gx"), lax.axis_index("gy")
    for z in range(planes):
        rim32[z, :own, :] = depth_rim(volume, from_z, z - 1)
    sides = ((-1, 0), (1, 0), (0, -1), (0, 1), (-1, -1), (-1, 1), (1, -1), (1, 1))
    for part, (dx, dy) in enumerate(sides):
        qx, qy = px + dx, py + dy
        inside = (qx >= 0) & (qx < count_x) & (qy >= 0) & (qy < count_y)
        source = jnp.where(inside, qx * count_y + qy, 0)
        block = jnp.where(inside, from_xy[source].astype(F32), 0.0)
        rim32[:, own + 8 * part : own + 8 * (part + 1), :] = block.reshape(planes, 8, channels)
    for z in range(planes):
        rows = rim32[z].astype(BF16)
        rim[z] = rows
        moved = matmul(taps[...], rows).astype(BF16)
        for bc in range(9):
            cells[z, :, bc * channels : (bc + 1) * channels] = moved[bc * own : (bc + 1) * own, :]
    pre = None
    for a in range(3):
        window = cells[a : a + size_z].reshape(size_z * own, 9 * channels)
        weight = w_conv[9 * a : 9 * (a + 1)].reshape(9 * channels, channels)
        term = matmul(window, weight)
        pre = term if pre is None else pre + term
    sig = jax.nn.sigmoid(pre)
    slope[...] = (sig * (1.0 + pre * (1.0 - sig))).reshape(size_z, own, channels)
    hidden[...] = (pre * sig).astype(BF16).reshape(size_z, own, channels)
    parts = []
    for s in range(8):
        a, bc = s // 4, s % 4
        parts.append(
            jnp.concatenate(
                [hidden[2 * kz + a, bc * quarter : (bc + 1) * quarter, :] for kz in range(size_z // 2)], axis=0
            )
        )
    coarse = matmul(jnp.concatenate(parts, axis=1), w_down[...].reshape(8 * channels, w_down.shape[2]))
    count_p = count_x * count_y
    count_z = send.shape[0] // count_p
    half_rows = coarse.shape[0] // 2
    lane = lax.broadcasted_iota(jnp.int32, (half_rows, 128), 1)
    for pair in range(count_p // 2):
        top = coarse[:half_rows, pair * 128 : (pair + 1) * 128]
        low = coarse[half_rows:, pair * 128 : (pair + 1) * 128]
        first = jnp.where(lane < 64, top, pltpu.roll(low, 64, 1)).astype(BF16)
        second = jnp.where(lane < 64, pltpu.roll(top, 64, 1), low).astype(BF16)
        for q in range(count_z):
            send[2 * pair * count_z + q] = first
            send[(2 * pair + 1) * count_z + q] = second


def rim_transpose_kernel(rim, taps_t, turned):
    planes, rows, channels = rim.shape
    for pair in range(planes // 2):
        sides = [rim[2 * pair + i].astype(F32).T for i in range(2)]
        moved = matmul(jnp.concatenate(sides, axis=1).astype(BF16), taps_t[...]).astype(BF16)
        for bc in range(9):
            turned[bc * channels : (bc + 1) * channels, pair * rows : (pair + 1) * rows] = moved[
                :, bc * rows : (bc + 1) * rows
            ]


def packed_plane(ref, count_p, pz, k, count_z, quarter):
    return jnp.concatenate(
        [ref[p * count_z + pz, k * quarter : (k + 1) * quarter, :] for p in range(count_p)], axis=0
    )


def bottle_kernel(count_p, count_z, quarter, coarse, shift, w_slice, send, weight, moved, total):
    rows = count_p * quarter
    channels = w_slice.shape[1]
    outs = w_slice.shape[2]
    weight[...] = jnp.zeros_like(weight)
    for bc in range(9):
        for a in range(3):
            block = w_slice[9 * a + bc]
            for h in range(2):
                slot = 2 * h + 2 - a
                weight[
                    (2 * bc + h) * channels : (2 * bc + h + 1) * channels, slot * outs : (slot + 1) * outs
                ] = block
    total[...] = jnp.zeros_like(total)
    for pz in range(count_z):
        for k in range(2):
            plane = packed_plane(coarse, count_p, pz, k, count_z, quarter)
            shifted = matmul(shift[...], plane).astype(BF16)
            for bc in range(9):
                moved[:, bc * 128 : (bc + 1) * 128] = shifted[bc * rows : (bc + 1) * rows, :]
            spread_out = matmul(moved[...], weight[...])
            first = 4 * pz + k
            for slot in range(5):
                total[first + slot] += spread_out[:, slot * outs : (slot + 1) * outs]
    for z in range(4 * count_z):
        plane = total[z + 1].astype(BF16)
        for p in range(count_p):
            send[p, z * quarter : (z + 1) * quarter, :] = plane[p * quarter : (p + 1) * quarter, :]


def bottle_grad_kernel(own, parts, from_z, bottle, send):
    pre = parts[0].astype(F32)
    for p in range(1, parts.shape[0]):
        pre = pre + parts[p].astype(F32)
    sig = jax.nn.sigmoid(pre)
    bottle[...] = (pre * sig).astype(BF16)
    slope = sig * (1.0 + pre * (1.0 - sig))
    back = jnp.concatenate([from_z[q, own:, :] for q in range(from_z.shape[0])], axis=0)
    grad = (back.astype(F32) * slope).astype(BF16)
    for p in range(send.shape[0]):
        send[p] = grad


def coarse_grad_kernel(count_y, quarter, grads, bottle, shift, w_bottle, send, window):
    count_p, cells, outs = grads.shape
    rows = count_p * quarter
    depth = cells // quarter
    count_z, own_cells, _ = send.shape
    inputs = w_bottle.shape[1]
    p = lax.axis_index("gx") * count_y + lax.axis_index("gy")
    mine = pl.multiple_of(p * quarter, quarter)
    picks = jnp.concatenate([shift[pl.ds((8 - bc) * rows + mine, quarter), :] for bc in range(9)], axis=0)
    window[:quarter, :] = jnp.zeros((quarter, 9 * outs), BF16)
    window[(depth + 1) * quarter :, :] = jnp.zeros((quarter, 9 * outs), BF16)
    for z in range(depth):
        plane = jnp.concatenate([grads[q, z * quarter : (z + 1) * quarter, :] for q in range(count_p)], axis=0)
        moved = matmul(picks, plane).astype(BF16)
        for bc in range(9):
            window[(z + 1) * quarter : (z + 2) * quarter, bc * outs : (bc + 1) * outs] = moved[
                bc * quarter : (bc + 1) * quarter, :
            ]
    total = None
    for a in range(3):
        for bc in range(9):
            term = matmul_nt(
                window[(2 - a) * quarter : (2 - a + depth) * quarter, bc * outs : (bc + 1) * outs],
                w_bottle[9 * a + bc],
            )
            total = term if total is None else total + term
    total = total.astype(BF16)
    for q in range(count_z):
        send[q, :, :inputs] = total[q * own_cells : (q + 1) * own_cells, :]
        send[q, :, inputs:] = bottle[q * own_cells : (q + 1) * own_cells, :]


def grad_bottle_kernel(count_p, count_z, quarter, coarse, grads, shift, out, turned, wide):
    rows = count_p * quarter
    depth = 4 * count_z
    outs = grads.shape[2]
    channels = out.shape[1]
    wide[...] = jnp.zeros_like(wide)
    planes = [
        jnp.concatenate([grads[q, z * quarter : (z + 1) * quarter, :] for q in range(count_p)], axis=0)
        for z in range(depth)
    ]
    for pz in range(count_z):
        for k in range(2):
            j = 2 * pz + k
            plane = packed_plane(coarse, count_p, pz, k, count_z, quarter).astype(F32).T.astype(BF16)
            for bc in range(9):
                turned[bc * 128 : (bc + 1) * 128, j * rows : (j + 1) * rows] = matmul(
                    plane, shift[(8 - bc) * rows : (9 - bc) * rows, :]
                ).astype(BF16)
            for slot in range(5):
                z = 4 * pz + k + slot - 1
                if 0 <= z < depth:
                    wide[j * rows : (j + 1) * rows, slot * outs : (slot + 1) * outs] = planes[z]
    for bc in range(9):
        full = matmul(turned[bc * 128 : (bc + 1) * 128, :], wide[...])
        for a in range(3):
            out[9 * a + bc] = (
                full[:channels, (2 - a) * outs : (3 - a) * outs] + full[channels:, (4 - a) * outs : (5 - a) * outs]
            )


def hidden_grad_kernel(
    from_z, hidden, slope, ordered, w_up, w_down, turned, order_t, output, send, shifted, rows_out
):
    count_z, own_cells, _ = from_z.shape
    size_z, own, channels = hidden.shape
    quarter = own // 4
    inputs = w_down.shape[2]
    grad = from_z[0, :, :inputs].astype(F32)
    for q in range(1, count_z):
        grad = grad + from_z[q, :, :inputs].astype(F32)
    grad = grad.astype(BF16)
    bottle = jnp.concatenate([from_z[q, :, inputs:] for q in range(count_z)], axis=1)
    shifted[...] = jnp.zeros_like(shifted)
    for s in range(8):
        a, bc = s // 4, s % 4
        lifted = matmul(bottle, w_up[s])
        spread_grad = matmul_nt(grad, w_down[s])
        for kz in range(size_z // 2):
            z = 2 * kz + a
            part = slice(bc * quarter, (bc + 1) * quarter)
            line = slice(kz * quarter, (kz + 1) * quarter)
            rows_out[z, part, :] = (lifted[line, :] + hidden[z, part, :].astype(F32)).astype(BF16)
            value = ((spread_grad[line, :] + ordered[z, part, :].astype(F32)) * slope[z, part, :]).astype(BF16)
            for t in range(3):
                start = (z + t) * own + bc * quarter
                shifted[start : start + quarter, t * channels : (t + 1) * channels] = value
    for z in range(size_z):
        plane = matmul(order_t[...], rows_out[z])
        output[z] = plane.reshape(output.shape[1:]).astype(BF16)
    full = matmul(turned[...], shifted[...])
    count_p = send.shape[0]
    group = channels // count_p
    for bc in range(9):
        for a in range(3):
            t = 9 * a + bc
            block = full[bc * channels : (bc + 1) * channels, a * channels : (a + 1) * channels].astype(BF16)
            for p in range(count_p):
                send[p, t * group : (t + 1) * group, :] = block[p * group : (p + 1) * group, :]


def plane_sum_kernel(parts, send):
    count, rows, channels = parts.shape
    total = parts[0].astype(F32)
    for p in range(1, count):
        total = total + parts[p].astype(F32)
    total = total.astype(BF16)
    count_z, share, _ = send.shape
    for q in range(count_z):
        size = min(share, rows - q * share)
        send[q, :size, :] = total[q * share : q * share + size, :]
        if size < share:
            send[q, size:, :] = jnp.zeros((share - size, channels), BF16)


def depth_sum_kernel(parts, send):
    total = parts[0].astype(F32)
    for p in range(1, parts.shape[0]):
        total = total + parts[p].astype(F32)
    total = total.astype(BF16)
    for q in range(send.shape[0]):
        send[q] = total


def grad_conv_kernel(parts, out):
    share = parts.shape[1]
    taps, group, _ = out.shape
    for t in range(taps):
        q, start = t * group // share, t * group % share
        out[t] = parts[q, start : start + group, :].astype(F32)


def shape_of(shape, dtype=BF16):
    return jax.ShapeDtypeStruct(shape, dtype)


def gathered_body(counts, volume, cotangent, w_conv, w_down, w_bottle, w_up):
    count_x, count_y, count_z = counts
    count_p = count_x * count_y
    size_z, size_x, size_y, channels = volume.shape
    wide = w_down.shape[2]
    group = w_bottle.shape[2]
    half_x, half_y = size_x // 2, size_y // 2
    own = size_x * size_y
    quarter = half_x * half_y
    own_cells = size_z // 2 * quarter
    cells = count_z * own_cells
    depth = count_z * size_z // 2
    rows = count_p * quarter
    planes = size_z + 2
    share_c = channels // count_p
    share_w = wide // count_p

    order, taps = fine_maps(size_x, size_y)
    pair_taps = np.zeros((2, 2 * own, 9, 2, own), np.float32)
    for i in range(2):
        pair_taps[i, :, :, i, :] = taps.transpose(2, 0, 1)
    shift = coarse_maps(count_x, count_y, half_x, half_y)
    order_m = jnp.asarray(order, BF16)
    order_t = jnp.asarray(order.T, BF16)
    taps_m = jnp.asarray(taps.reshape(9 * own, 2 * own), BF16)
    taps_t = jnp.asarray(pair_taps.reshape(4 * own, 18 * own), BF16)
    shift_m = jnp.asarray(shift.reshape(9 * rows, rows), BF16)

    w_conv_t = jnp.transpose(w_conv, (1, 0, 2))
    w_bottle_t = jnp.transpose(w_bottle, (1, 0, 2))
    plane_index = lax.axis_index("gx") * count_y + lax.axis_index("gy")
    w_slice = lax.dynamic_slice_in_dim(w_bottle_t, plane_index * share_w, share_w, 1)

    send, ordered = local_call(
        back_kernel,
        "back",
        [shape_of((count_z, own + own_cells, channels)), shape_of((size_z, own, channels))],
    )(volume, cotangent, w_up, order_m)
    from_z = spread(send, "gz")
    send = local_call(
        lambda *refs: faces_kernel(count_y, *refs),
        "faces",
        shape_of((count_p, planes * 8, channels)),
        [pltpu.VMEM((planes * own, channels), F32)],
    )(volume, from_z)
    from_xy = spread(send, ("gx", "gy"))
    hidden, slope, send, rim = local_call(
        lambda *refs: hidden_kernel(count_x, count_y, *refs),
        "hidden",
        [
            shape_of((size_z, own, channels)),
            shape_of((size_z, own, channels), F32),
            shape_of((count_p * count_z, own_cells // 2, 128)),
            shape_of((planes, 2 * own, channels)),
        ],
        [pltpu.VMEM((planes, 2 * own, channels), F32), pltpu.VMEM((planes, own, 9 * channels), BF16)],
    )(volume, from_z, from_xy, taps_m, w_conv_t, w_down)
    coarse = spread(send, ("gx", "gy", "gz"))
    turned = local_call(
        rim_transpose_kernel,
        "rim_transpose",
        shape_of((9 * channels, planes * own)),
    )(rim, taps_t)
    send = local_call(
        lambda *refs: bottle_kernel(count_p, count_z, quarter, *refs),
        "bottle",
        shape_of((count_p, cells, group)),
        [
            pltpu.VMEM((18 * share_w, 5 * group), BF16),
            pltpu.VMEM((rows, 18 * share_w), BF16),
            pltpu.VMEM((depth + 2, rows, group), F32),
        ],
    )(coarse, shift_m, w_slice)
    parts = spread(send, ("gx", "gy"))
    bottle, send = local_call(
        lambda *refs: bottle_grad_kernel(own, *refs),
        "bottle_grad",
        [shape_of((cells, group)), shape_of((count_p, cells, group))],
    )(parts, from_z)
    grads = spread(send, ("gx", "gy"))
    send = local_call(
        lambda *refs: coarse_grad_kernel(count_y, quarter, *refs),
        "coarse_grad",
        shape_of((count_z, own_cells, wide + group)),
        [pltpu.VMEM(((depth + 2) * quarter, 9 * group), BF16)],
    )(grads, bottle, shift_m, w_bottle_t)
    from_z = spread(send, "gz")
    grad_bottle = local_call(
        lambda *refs: grad_bottle_kernel(count_p, count_z, quarter, *refs),
        "grad_bottle",
        shape_of((27, share_w, group), F32),
        [
            pltpu.VMEM((18 * share_w, 2 * count_z * rows), BF16),
            pltpu.VMEM((2 * count_z * rows, 5 * group), BF16),
        ],
    )(coarse, grads, shift_m)
    output, send = local_call(
        hidden_grad_kernel,
        "hidden_grad",
        [shape_of(volume.shape), shape_of((count_p, 27 * share_c, channels))],
        [pltpu.VMEM((planes * own, 3 * channels), BF16), pltpu.VMEM((size_z, own, channels), BF16)],
    )(from_z, hidden, slope, ordered, w_up, w_down, turned, order_t)
    parts = spread(send, ("gx", "gy"))
    share = -(-27 * share_c // (16 * count_z)) * 16
    send = local_call(plane_sum_kernel, "plane_sum", shape_of((count_z, share, channels)))(parts)
    parts = spread(send, "gz")
    send = local_call(depth_sum_kernel, "depth_sum", shape_of((count_z, share, channels)))(parts)
    parts = spread(send, "gz")
    grad_conv = local_call(
        grad_conv_kernel,
        "grad_conv",
        shape_of((27, share_c, channels), F32),
    )(parts)
    return (output, jnp.transpose(grad_conv, (1, 0, 2)), jnp.transpose(grad_bottle, (1, 0, 2)))


def with_halo(cells, sides, width):
    for axis, dim in sides:
        count = lax.axis_size(axis)
        ends = count - 1
        head = lax.slice_in_dim(cells, 0, width, axis=dim)
        tail = lax.slice_in_dim(cells, cells.shape[dim] - width, cells.shape[dim], axis=dim)
        cells = jnp.concatenate(
            [
                lax.ppermute(tail, axis, [(i, (i + 1) % count) for i in range(ends)]),
                cells,
                lax.ppermute(head, axis, [((i + 1) % count, i) for i in range(ends)]),
            ],
            axis=dim,
        )
    return cells


def silu_slope(values):
    sig = jax.nn.sigmoid(values)
    return sig * (1.0 + values * (1.0 - sig))


def conv_forward(padded, weight, extent):
    size_z, size_x, size_y = extent
    count_cells = size_z * size_x * size_y
    summed = jnp.zeros((count_cells, weight.shape[2]), jnp.float32)
    for tap_index in range(27):
        shift_z, shift_x, shift_y = (tap_index // 9, tap_index // 3 % 3, tap_index % 3)
        window = padded[
            shift_z : shift_z + size_z, shift_x : shift_x + size_x, shift_y : shift_y + size_y, :
        ]
        window = window.reshape(count_cells, padded.shape[3])
        summed = summed + jnp.dot(
            window, weight[:, tap_index, :], preferred_element_type=jnp.float32
        )
    return summed.reshape(size_z, size_x, size_y, weight.shape[2])


def conv_weight_grad(padded, gradient, extent):
    size_z, size_x, size_y = extent
    count_cells = size_z * size_x * size_y
    flat_gradient = gradient.reshape(count_cells, gradient.shape[3])
    pieces = []
    for tap_index in range(27):
        shift_z, shift_x, shift_y = (tap_index // 9, tap_index // 3 % 3, tap_index % 3)
        window = padded[
            shift_z : shift_z + size_z, shift_x : shift_x + size_x, shift_y : shift_y + size_y, :
        ]
        window = window.reshape(count_cells, padded.shape[3])
        pieces.append(
            lax.dot_general(
                window, flat_gradient, (((0,), (0,)), ((), ())), preferred_element_type=jnp.float32
            )
        )
    return jnp.stack(pieces, axis=1)


def conv_input_grad(padded, weight, extent):
    size_z, size_x, size_y = extent
    count_cells = size_z * size_x * size_y
    summed = jnp.zeros((count_cells, weight.shape[0]), jnp.float32)
    for tap_index in range(27):
        shift_z, shift_x, shift_y = (2 - tap_index // 9, 2 - tap_index // 3 % 3, 2 - tap_index % 3)
        window = padded[
            shift_z : shift_z + size_z, shift_x : shift_x + size_x, shift_y : shift_y + size_y, :
        ]
        window = window.reshape(count_cells, padded.shape[3])
        summed = summed + lax.dot_general(
            window,
            weight[:, tap_index, :],
            (((1,), (1,)), ((), ())),
            preferred_element_type=jnp.float32,
        )
    return summed.reshape(size_z, size_x, size_y, weight.shape[0])


def pool_features(fine, kernel):
    size_z, size_x, size_y, channels = fine.shape
    blocks = fine.reshape(size_z // 2, 2, size_x // 2, 2, size_y // 2, 2, channels)
    kernel_cube = kernel.reshape(2, 2, 2, kernel.shape[1], kernel.shape[2])
    return jnp.einsum(
        "zaxbycf,abcfg->zxyg", blocks, kernel_cube, preferred_element_type=jnp.float32
    )


def pool_adjoint(coarse_in, kernel):
    size_z, size_x, size_y, wide_channels = coarse_in.shape
    kernel_cube = kernel.reshape(2, 2, 2, kernel.shape[1], kernel.shape[2])
    result = jnp.einsum(
        "zxyg,abcfg->zaxbycf", coarse_in, kernel_cube, preferred_element_type=jnp.float32
    )
    return result.reshape(2 * size_z, 2 * size_x, 2 * size_y, kernel.shape[1])


def lift_features(coarse_in, kernel):
    size_z, size_x, size_y, wide_channels = coarse_in.shape
    kernel_cube = kernel.reshape(2, 2, 2, kernel.shape[1], kernel.shape[2])
    result = jnp.einsum(
        "zxyg,abcgf->zaxbycf", coarse_in, kernel_cube, preferred_element_type=jnp.float32
    )
    return result.reshape(2 * size_z, 2 * size_x, 2 * size_y, kernel.shape[2])


def lift_adjoint(fine, kernel):
    size_z, size_x, size_y, channels = fine.shape
    blocks = fine.reshape(size_z // 2, 2, size_x // 2, 2, size_y // 2, 2, channels)
    kernel_cube = kernel.reshape(2, 2, 2, kernel.shape[1], kernel.shape[2])
    return jnp.einsum(
        "zaxbycf,abcgf->zxyg", blocks, kernel_cube, preferred_element_type=jnp.float32
    )


def column_body(volume, cotangent, w_conv, w_down, w_bottle, w_up):
    size_z, size_x, size_y, channels = volume.shape
    group_channels = w_bottle.shape[2]
    half_x = size_x // 2
    half_y = size_y // 2
    padded = with_halo(volume, (("gx", 1), ("gy", 2), ("gz", 0)), 1)
    pre_hidden = conv_forward(padded, w_conv, (size_z, size_x, size_y))
    hidden = jax.nn.silu(pre_hidden).astype(jnp.bfloat16)
    hidden_slope = silu_slope(pre_hidden)
    coarse = pool_features(hidden, w_down).astype(jnp.bfloat16)
    stacked = lax.all_gather(coarse, "gz", axis=0, tiled=True)
    rimmed = with_halo(stacked, (("gx", 1), ("gy", 2)), 1)
    column_z = rimmed.shape[0]
    coarse_pad = jnp.pad(rimmed, ((1, 1), (0, 0), (0, 0), (0, 0)))
    pre_bottle = conv_forward(coarse_pad, w_bottle, (column_z, half_x, half_y))
    bottle = jax.nn.silu(pre_bottle).astype(jnp.bfloat16)
    bottle_slope = silu_slope(pre_bottle)
    own_start = lax.axis_index("gz") * group_channels
    own_up = lax.dynamic_slice_in_dim(w_up, own_start, group_channels, 1)
    lifted = lax.psum_scatter(
        lift_features(bottle, own_up).astype(jnp.bfloat16), "gz", scatter_dimension=0, tiled=True
    ).astype(jnp.float32)
    output = (lifted + hidden.astype(jnp.float32)).astype(jnp.bfloat16)
    back_bottle = lift_adjoint(cotangent, w_up).astype(jnp.bfloat16)
    split_grad = lax.all_to_all(back_bottle, "gz", split_axis=3, concat_axis=0, tiled=True)
    bottle_grad = (split_grad.astype(jnp.float32) * bottle_slope).astype(jnp.bfloat16)
    grad_bottle = lax.psum_scatter(
        conv_weight_grad(coarse_pad, bottle_grad, (column_z, half_x, half_y)),
        ("gx", "gy"),
        scatter_dimension=0,
        tiled=True,
    )
    grad_rimmed = with_halo(bottle_grad, (("gx", 1), ("gy", 2)), 1)
    grad_pad = jnp.pad(grad_rimmed, ((1, 1), (0, 0), (0, 0), (0, 0)))
    coarse_grad = lax.psum_scatter(
        conv_input_grad(
            grad_pad, w_bottle, (lax.axis_size("gz") * (size_z // 2), half_x, half_y)
        ).astype(jnp.bfloat16),
        "gz",
        scatter_dimension=0,
        tiled=True,
    )
    hidden_grad = (
        (pool_adjoint(coarse_grad, w_down) + cotangent.astype(jnp.float32)) * hidden_slope
    ).astype(jnp.bfloat16)
    full_term = conv_weight_grad(padded, hidden_grad, (size_z, size_x, size_y))
    depth_summed = lax.psum(full_term.astype(jnp.bfloat16), "gz").astype(jnp.float32)
    grad_conv = lax.psum_scatter(depth_summed, ("gx", "gy"), scatter_dimension=0, tiled=True)
    return (output, grad_conv, grad_bottle)


def fits_one_plane(counts, brick, wide):
    count_p = counts[0] * counts[1]
    size_z, size_x, size_y, channels = brick
    return (
        count_p * (size_x // 2) * (size_y // 2) == 128
        and wide // count_p == 64
        and (size_z, size_x, size_y, channels) == (8, 8, 8, 128)
    )


def solution(mesh):
    in_specs = (
        P("gz", "gx", "gy", None),
        P("gz", "gx", "gy", None),
        P(),
        P(),
        P(None, None, "gz"),
        P(),
    )
    out_specs = (
        P("gz", "gx", "gy", None),
        P(("gx", "gy"), None, None),
        P(("gx", "gy"), None, "gz"),
    )
    counts = (mesh.shape["gx"], mesh.shape["gy"], mesh.shape["gz"])

    def body(volume, cotangent, w_conv, w_down, w_bottle, w_up):
        if fits_one_plane(counts, volume.shape, w_down.shape[2]):
            return gathered_body(counts, volume, cotangent, w_conv, w_down, w_bottle, w_up)
        return column_body(volume, cotangent, w_conv, w_down, w_bottle, w_up)

    return jax.shard_map(body, mesh=mesh, in_specs=in_specs, out_specs=out_specs, check_vma=False)
```

```python
import numpy as np
import jax
import jax.numpy as jnp
from jax import lax
from jax.experimental import pallas as pl
from jax.experimental.pallas import tpu as pltpu
from jax.sharding import PartitionSpec as P

BF16 = jnp.bfloat16
F32 = jnp.float32
VMEM_LIMIT = 24 * 1024 * 1024


def local_call(kernel, name, out_shapes, scratch=()):
    whole = pl.BlockSpec(memory_space=pltpu.VMEM)

    def call(*operands):
        return pl.pallas_call(
            kernel,
            name=name,
            out_shape=out_shapes,
            in_specs=[whole] * len(operands),
            out_specs=jax.tree.map(lambda _: whole, out_shapes),
            scratch_shapes=list(scratch),
            compiler_params=pltpu.CompilerParams(vmem_limit_bytes=VMEM_LIMIT),
        )(*operands)

    return call


def matmul(left, right):
    return jnp.dot(left, right, preferred_element_type=F32)


def matmul_nt(left, right):
    return lax.dot_general(left, right, (((1,), (1,)), ((), ())), preferred_element_type=F32)


def sub_order(size_x, size_y):
    half_x, half_y = size_x // 2, size_y // 2
    return {
        (2 * kx + b, 2 * ky + c): ((2 * b + c) * half_x + kx) * half_y + ky
        for b in range(2)
        for c in range(2)
        for kx in range(half_x)
        for ky in range(half_y)
    }


def fine_maps(size_x, size_y):
    own = size_x * size_y
    rows = sub_order(size_x, size_y)
    order = np.zeros((own, own), np.float32)
    taps = np.zeros((9, own, 2 * own), np.float32)
    for (x, y), row in rows.items():
        order[row, x * size_y + y] = 1
        for b in range(3):
            for c in range(3):
                sx, sy = x + b - 1, y + c - 1
                if sx < 0:
                    part = 0 if 0 <= sy < size_y else (4 if sy < 0 else 5)
                    source = own + 8 * part + sy % size_y
                elif sx >= size_x:
                    part = 1 if 0 <= sy < size_y else (6 if sy < 0 else 7)
                    source = own + 8 * part + sy % size_y
                elif sy < 0:
                    source = own + 16 + sx
                elif sy >= size_y:
                    source = own + 24 + sx
                else:
                    source = sx * size_y + sy
                taps[3 * b + c, row, source] = 1
    return order, taps


def coarse_maps(count_x, count_y, half_x, half_y):
    wide_x, wide_y = count_x * half_x, count_y * half_y

    def row_of(x, y):
        brick = (x // half_x) * count_y + y // half_y
        return (brick * half_x + x % half_x) * half_y + y % half_y

    shift = np.zeros((9, wide_x * wide_y, wide_x * wide_y), np.float32)
    for x in range(wide_x):
        for y in range(wide_y):
            for b in range(3):
                for c in range(3):
                    sx, sy = x + b - 1, y + c - 1
                    if 0 <= sx < wide_x and 0 <= sy < wide_y:
                        shift[3 * b + c, row_of(x, y), row_of(sx, sy)] = 1
    return shift


def spread(blocks, axes):
    return lax.all_to_all(blocks, axes, 0, 0, tiled=True)


def swap(block, axes, count, distance):
    return lax.ppermute(block, axes, [(i, i ^ distance) for i in range(count)])


def trade(blocks, axes, count):
    got = {d: swap(blocks[d], axes, count, d) for d in reversed(range(1, count))}
    return [blocks[0]] + [got[d] for d in range(1, count)]


def plane_index(count_y):
    return lax.axis_index("gx") * count_y + lax.axis_index("gy")


def plane_rows(ref, z):
    _, size_x, size_y, channels = ref.shape
    return ref[z].astype(F32).reshape(size_x * size_y, channels)


def hand_out(blocks, outs, me):
    for d, out in enumerate(outs):
        out[...] = blocks[me ^ d]


def take_in(parts, blocks, me):
    for d, part in enumerate(parts):
        blocks[me ^ d] = part[...]


def total_of(parts):
    terms = [part[...].astype(F32) for part in parts]
    while len(terms) > 1:
        terms = [terms[i] + terms[i + 1] for i in range(0, len(terms), 2)]
    return terms[0]


def back_kernel(count_z, cotangent, w_up, order, *refs):
    sends, (ordered, blocks) = refs[:count_z], refs[count_z:]
    size_z, size_x, size_y, channels = cotangent.shape
    own = size_x * size_y
    quarter = own // 4
    for z in range(size_z):
        ordered[z] = matmul(order[...], plane_rows(cotangent, z).astype(BF16)).astype(BF16)
    back = None
    for s in range(8):
        a, bc = s // 4, s % 4
        cells = jnp.concatenate(
            [ordered[2 * kz + a, bc * quarter : (bc + 1) * quarter, :] for kz in range(size_z // 2)], axis=0
        )
        term = matmul_nt(cells, w_up[s])
        back = term if back is None else back + term
    back = back.astype(BF16)
    group = back.shape[1] // count_z
    for q in range(count_z):
        blocks[q] = back[:, q * group : (q + 1) * group]
    hand_out(blocks, sends, lax.axis_index("gz"))


def depth_rim(volume, below, above, z):
    size_z, size_x, size_y, channels = volume.shape
    if z < 0:
        return below[...].astype(F32).reshape(size_x * size_y, channels)
    if z >= size_z:
        return above[...].astype(F32).reshape(size_x * size_y, channels)
    return plane_rows(volume, z)


def faces_kernel(volume, below, above, x_send, y_low_send, y_high_send, deep):
    size_z, size_x, size_y, channels = volume.shape
    own = size_x * size_y
    planes = size_z + 2
    for z in range(planes):
        deep[z * own : (z + 1) * own, :] = depth_rim(volume, below, above, z - 1)

    def x_face(x):
        return jnp.concatenate(
            [deep[z * own + x * size_y : z * own + (x + 1) * size_y, :] for z in range(planes)], axis=0
        ).astype(BF16)

    x_send[...] = jnp.where(lax.axis_index("gx") == 0, x_face(size_x - 1), x_face(0))
    y_low_send[...] = deep[pl.ds(0, planes * size_x, stride=size_y), :].astype(BF16)
    y_high_send[...] = deep[pl.ds(size_y - 1, planes * size_x, stride=size_y), :].astype(BF16)


def hidden_kernel(
    count_p, count_z, volume, below, above, x_rim, y_low, y_high, xy_low, xy_high, taps, w_conv, w_down,
    hidden, slope, send, rim, rim32, cells,
):
    size_z, size_x, size_y, channels = volume.shape
    own = size_x * size_y
    quarter = own // 4
    planes = size_z + 2
    first = lax.axis_index("gx") == 0
    for z in range(planes):
        rim32[z, :own, :] = depth_rim(volume, below, above, z - 1)
    sides = (
        (x_rim, False),
        (x_rim, True),
        (y_low, None),
        (y_high, None),
        (xy_low, False),
        (xy_high, False),
        (xy_low, True),
        (xy_high, True),
    )
    for part, (block, high) in enumerate(sides):
        rows = block[...].astype(F32).reshape(planes, 8, channels)
        if high is not None:
            rows = jnp.where(first == high, rows, 0.0)
        rim32[:, own + 8 * part : own + 8 * (part + 1), :] = rows
    for z in range(planes):
        rows = rim32[z].astype(BF16)
        rim[z] = rows
        moved = matmul(taps[...], rows).astype(BF16)
        for bc in range(9):
            cells[z, :, bc * channels : (bc + 1) * channels] = moved[bc * own : (bc + 1) * own, :]
    pre = None
    for a in range(3):
        window = cells[a : a + size_z].reshape(size_z * own, 9 * channels)
        weight = w_conv[9 * a : 9 * (a + 1)].reshape(9 * channels, channels)
        term = matmul(window, weight)
        pre = term if pre is None else pre + term
    sig = jax.nn.sigmoid(pre)
    slope[...] = (sig * (1.0 + pre * (1.0 - sig))).reshape(size_z, own, channels)
    hidden[...] = (pre * sig).astype(BF16).reshape(size_z, own, channels)
    parts = []
    for s in range(8):
        a, bc = s // 4, s % 4
        parts.append(
            jnp.concatenate(
                [hidden[2 * kz + a, bc * quarter : (bc + 1) * quarter, :] for kz in range(size_z // 2)], axis=0
            )
        )
    coarse = matmul(jnp.concatenate(parts, axis=1), w_down[...].reshape(8 * channels, w_down.shape[2]))
    half_rows = coarse.shape[0] // 2
    lane = lax.broadcasted_iota(jnp.int32, (half_rows, 128), 1)
    for pair in range(count_p // 2):
        top = coarse[:half_rows, pair * 128 : (pair + 1) * 128]
        low = coarse[half_rows:, pair * 128 : (pair + 1) * 128]
        left = jnp.where(lane < 64, top, pltpu.roll(low, 64, 1)).astype(BF16)
        right = jnp.where(lane < 64, pltpu.roll(top, 64, 1), low).astype(BF16)
        for q in range(count_z):
            send[2 * pair * count_z + q] = left
            send[(2 * pair + 1) * count_z + q] = right


def rim_transpose_kernel(rim, taps_t, turned):
    planes, rows, channels = rim.shape
    for pair in range(planes // 2):
        sides = [rim[2 * pair + i].astype(F32).T for i in range(2)]
        moved = matmul(jnp.concatenate(sides, axis=1).astype(BF16), taps_t[...]).astype(BF16)
        for bc in range(9):
            turned[bc * channels : (bc + 1) * channels, pair * rows : (pair + 1) * rows] = moved[
                :, bc * rows : (bc + 1) * rows
            ]


def packed_plane(ref, count_p, pz, k, count_z, quarter):
    return jnp.concatenate(
        [ref[p * count_z + pz, k * quarter : (k + 1) * quarter, :] for p in range(count_p)], axis=0
    )


def bottle_kernel(count_y, count_z, quarter, coarse, shift, w_slice, *refs):
    sends, (weight, moved, total, blocks) = refs[:-4], refs[-4:]
    count_p = len(sends)
    rows = count_p * quarter
    channels = w_slice.shape[1]
    outs = w_slice.shape[2]
    weight[...] = jnp.zeros_like(weight)
    for bc in range(9):
        for a in range(3):
            block = w_slice[9 * a + bc]
            for h in range(2):
                slot = 2 * h + 2 - a
                weight[
                    (2 * bc + h) * channels : (2 * bc + h + 1) * channels, slot * outs : (slot + 1) * outs
                ] = block
    total[...] = jnp.zeros_like(total)
    for pz in range(count_z):
        for k in range(2):
            plane = packed_plane(coarse, count_p, pz, k, count_z, quarter)
            shifted = matmul(shift[...], plane).astype(BF16)
            for bc in range(9):
                moved[:, bc * 128 : (bc + 1) * 128] = shifted[bc * rows : (bc + 1) * rows, :]
            spread_out = matmul(moved[...], weight[...])
            first = 4 * pz + k
            for slot in range(5):
                total[first + slot] += spread_out[:, slot * outs : (slot + 1) * outs]
    for z in range(4 * count_z):
        plane = total[z + 1].astype(BF16)
        for p in range(count_p):
            blocks[p, z * quarter : (z + 1) * quarter, :] = plane[p * quarter : (p + 1) * quarter, :]
    hand_out(blocks, sends, plane_index(count_y))


def bottle_grad_kernel(count_p, *refs):
    parts, backs, (bottle, grad, back) = refs[:count_p], refs[count_p:-3], refs[-3:]
    pre = total_of(parts)
    sig = jax.nn.sigmoid(pre)
    bottle[...] = (pre * sig).astype(BF16)
    slope = sig * (1.0 + pre * (1.0 - sig))
    take_in(backs, back, lax.axis_index("gz"))
    grad[...] = (back[...].reshape(pre.shape).astype(F32) * slope).astype(BF16)


def coarse_grad_kernel(count_y, count_z, quarter, *refs):
    grads, (bottle, shift, w_bottle) = refs[: -count_z - 6], refs[-count_z - 6 : -count_z - 3]
    sends, (window, gathered, blocks) = refs[-count_z - 3 : -3], refs[-3:]
    count_p = len(grads)
    cells, outs = grads[0].shape
    rows = count_p * quarter
    depth = cells // quarter
    own_cells = cells // count_z
    inputs = w_bottle.shape[1]
    p = plane_index(count_y)
    take_in(grads, gathered, p)
    mine = pl.multiple_of(p * quarter, quarter)
    picks = jnp.concatenate([shift[pl.ds((8 - bc) * rows + mine, quarter), :] for bc in range(9)], axis=0)
    window[:quarter, :] = jnp.zeros((quarter, 9 * outs), BF16)
    window[(depth + 1) * quarter :, :] = jnp.zeros((quarter, 9 * outs), BF16)
    for z in range(depth):
        plane = jnp.concatenate([gathered[q, z * quarter : (z + 1) * quarter, :] for q in range(count_p)], axis=0)
        moved = matmul(picks, plane).astype(BF16)
        for bc in range(9):
            window[(z + 1) * quarter : (z + 2) * quarter, bc * outs : (bc + 1) * outs] = moved[
                bc * quarter : (bc + 1) * quarter, :
            ]
    total = None
    for a in range(3):
        for bc in range(9):
            term = matmul_nt(
                window[(2 - a) * quarter : (2 - a + depth) * quarter, bc * outs : (bc + 1) * outs],
                w_bottle[9 * a + bc],
            )
            total = term if total is None else total + term
    total = total.astype(BF16)
    for q in range(count_z):
        blocks[q, :, :inputs] = total[q * own_cells : (q + 1) * own_cells, :]
        blocks[q, :, inputs:] = bottle[q * own_cells : (q + 1) * own_cells, :]
    hand_out(blocks, sends, lax.axis_index("gz"))


def grad_bottle_kernel(count_y, count_z, quarter, coarse, shift, *refs):
    grads, (out, turned, wide, gathered) = refs[:-4], refs[-4:]
    count_p = len(grads)
    rows = count_p * quarter
    depth = 4 * count_z
    outs = gathered.shape[2]
    channels = out.shape[1]
    take_in(grads, gathered, plane_index(count_y))
    wide[...] = jnp.zeros_like(wide)
    planes = [
        jnp.concatenate([gathered[q, z * quarter : (z + 1) * quarter, :] for q in range(count_p)], axis=0)
        for z in range(depth)
    ]
    for pz in range(count_z):
        for k in range(2):
            j = 2 * pz + k
            plane = packed_plane(coarse, count_p, pz, k, count_z, quarter).astype(F32).T.astype(BF16)
            for bc in range(9):
                turned[bc * 128 : (bc + 1) * 128, j * rows : (j + 1) * rows] = matmul(
                    plane, shift[(8 - bc) * rows : (9 - bc) * rows, :]
                ).astype(BF16)
            for slot in range(5):
                z = 4 * pz + k + slot - 1
                if 0 <= z < depth:
                    wide[j * rows : (j + 1) * rows, slot * outs : (slot + 1) * outs] = planes[z]
    for bc in range(9):
        full = matmul(turned[bc * 128 : (bc + 1) * 128, :], wide[...])
        for a in range(3):
            out[9 * a + bc] = (
                full[:channels, (2 - a) * outs : (3 - a) * outs] + full[channels:, (4 - a) * outs : (5 - a) * outs]
            )


def hidden_grad_kernel(count_y, count_z, *refs):
    parts, (hidden, slope, ordered, w_up, w_down, turned, order_t) = refs[:count_z], refs[count_z : count_z + 7]
    output, sends, (shifted, rows_out, bottles, blocks) = refs[count_z + 7], refs[count_z + 8 : -4], refs[-4:]
    count_p = len(sends)
    size_z, own, channels = hidden.shape
    quarter = own // 4
    inputs = w_down.shape[2]
    pz = lax.axis_index("gz")
    grad = parts[0][:, :inputs].astype(F32)
    for part in parts[1:]:
        grad = grad + part[:, :inputs].astype(F32)
    grad = grad.astype(BF16)
    for d, part in enumerate(parts):
        bottles[pz ^ d] = part[:, inputs:]
    bottle = jnp.concatenate([bottles[q] for q in range(count_z)], axis=1)
    shifted[...] = jnp.zeros_like(shifted)
    for s in range(8):
        a, bc = s // 4, s % 4
        lifted = matmul(bottle, w_up[s])
        spread_grad = matmul_nt(grad, w_down[s])
        for kz in range(size_z // 2):
            z = 2 * kz + a
            part = slice(bc * quarter, (bc + 1) * quarter)
            line = slice(kz * quarter, (kz + 1) * quarter)
            rows_out[z, part, :] = (lifted[line, :] + hidden[z, part, :].astype(F32)).astype(BF16)
            value = ((spread_grad[line, :] + ordered[z, part, :].astype(F32)) * slope[z, part, :]).astype(BF16)
            for t in range(3):
                start = (z + t) * own + bc * quarter
                shifted[start : start + quarter, t * channels : (t + 1) * channels] = value
    for z in range(size_z):
        plane = matmul(order_t[...], rows_out[z])
        output[z] = plane.reshape(output.shape[1:]).astype(BF16)
    full = matmul(turned[...], shifted[...])
    group = channels // count_p
    for bc in range(9):
        for a in range(3):
            t = 9 * a + bc
            block = full[bc * channels : (bc + 1) * channels, a * channels : (a + 1) * channels].astype(BF16)
            for p in range(count_p):
                blocks[p, t * group : (t + 1) * group, :] = block[p * group : (p + 1) * group, :]
    hand_out(blocks, sends, plane_index(count_y))


def plane_sum_kernel(*refs):
    refs[-1][...] = total_of(refs[:-1]).astype(BF16)


def grad_conv_kernel(*refs):
    out = refs[-1]
    out[...] = total_of(refs[:-1]).reshape(out.shape)


def shape_of(shape, dtype=BF16):
    return jax.ShapeDtypeStruct(shape, dtype)


def gathered_body(counts, volume, cotangent, w_conv, w_down, w_bottle, w_up):
    count_x, count_y, count_z = counts
    count_p = count_x * count_y
    size_z, size_x, size_y, channels = volume.shape
    wide = w_down.shape[2]
    group = w_bottle.shape[2]
    half_x, half_y = size_x // 2, size_y // 2
    own = size_x * size_y
    quarter = half_x * half_y
    own_cells = size_z // 2 * quarter
    cells = count_z * own_cells
    depth = count_z * size_z // 2
    rows = count_p * quarter
    planes = size_z + 2
    share_c = channels // count_p
    share_w = wide // count_p
    plane_axes = ("gx", "gy")

    order, taps = fine_maps(size_x, size_y)
    pair_taps = np.zeros((2, 2 * own, 9, 2, own), np.float32)
    for i in range(2):
        pair_taps[i, :, :, i, :] = taps.transpose(2, 0, 1)
    shift = coarse_maps(count_x, count_y, half_x, half_y)
    order_m = jnp.asarray(order, BF16)
    order_t = jnp.asarray(order.T, BF16)
    taps_m = jnp.asarray(taps.reshape(9 * own, 2 * own), BF16)
    taps_t = jnp.asarray(pair_taps.reshape(4 * own, 18 * own), BF16)
    shift_m = jnp.asarray(shift.reshape(9 * rows, rows), BF16)

    w_conv_t = jnp.transpose(w_conv, (1, 0, 2))
    w_bottle_t = jnp.transpose(w_bottle, (1, 0, 2))
    w_slice = lax.dynamic_slice_in_dim(w_bottle_t, plane_index(count_y) * share_w, share_w, 1)

    up_z = [(i, i + 1) for i in range(count_z - 1)]
    down_z = [(i + 1, i) for i in range(count_z - 1)]
    below = lax.ppermute(volume[size_z - 1], "gz", up_z)
    above = lax.ppermute(volume[0], "gz", down_z)
    *sends, ordered = local_call(
        lambda *refs: back_kernel(count_z, *refs),
        "back",
        [shape_of((own_cells, group))] * count_z + [shape_of((size_z, own, channels))],
        [pltpu.VMEM((count_z, own_cells, group), BF16)],
    )(cotangent, w_up, order_m)
    x_send, y_low_send, y_high_send = local_call(
        faces_kernel,
        "faces",
        [shape_of((planes * 8, channels))] * 3,
        [pltpu.VMEM((planes * own, channels), F32)],
    )(volume, below, above)
    ups = [(x * count_y + y, x * count_y + y + 1) for x in range(count_x) for y in range(count_y - 1)]
    cross = [((1 - i // count_y) * count_y + i % count_y, j) for i, j in ups]
    xy_low = lax.ppermute(x_send, plane_axes, cross)
    xy_high = lax.ppermute(x_send, plane_axes, [(j, i) for i, j in cross])
    x_rim = lax.ppermute(x_send, "gx", [(0, 1), (1, 0)])
    y_low = lax.ppermute(y_high_send, plane_axes, ups)
    y_high = lax.ppermute(y_low_send, plane_axes, [(j, i) for i, j in ups])
    hidden, slope, send, rim = local_call(
        lambda *refs: hidden_kernel(count_p, count_z, *refs),
        "hidden",
        [
            shape_of((size_z, own, channels)),
            shape_of((size_z, own, channels), F32),
            shape_of((count_p * count_z, own_cells // 2, 128)),
            shape_of((planes, 2 * own, channels)),
        ],
        [pltpu.VMEM((planes, 2 * own, channels), F32), pltpu.VMEM((planes, own, 9 * channels), BF16)],
    )(volume, below, above, x_rim, y_low, y_high, xy_low, xy_high, taps_m, w_conv_t, w_down)
    coarse = spread(send, ("gx", "gy", "gz"))
    *sends, rim = lax.optimization_barrier((*sends, rim))
    backs = trade(sends, "gz", count_z)
    turned = local_call(
        rim_transpose_kernel,
        "rim_transpose",
        shape_of((9 * channels, planes * own)),
    )(rim, taps_t)
    sends = local_call(
        lambda *refs: bottle_kernel(count_y, count_z, quarter, *refs),
        "bottle",
        [shape_of((cells, group))] * count_p,
        [
            pltpu.VMEM((18 * share_w, 5 * group), BF16),
            pltpu.VMEM((rows, 18 * share_w), BF16),
            pltpu.VMEM((depth + 2, rows, group), F32),
            pltpu.VMEM((count_p, cells, group), BF16),
        ],
    )(coarse, shift_m, w_slice)
    parts = trade(sends, plane_axes, count_p)
    bottle, grad = local_call(
        lambda *refs: bottle_grad_kernel(count_p, *refs),
        "bottle_grad",
        [shape_of((cells, group))] * 2,
        [pltpu.VMEM((count_z, own_cells, group), BF16)],
    )(*parts, *backs)
    grads = trade([grad] * count_p, plane_axes, count_p)
    sends = local_call(
        lambda *refs: coarse_grad_kernel(count_y, count_z, quarter, *refs),
        "coarse_grad",
        [shape_of((own_cells, wide + group))] * count_z,
        [
            pltpu.VMEM(((depth + 2) * quarter, 9 * group), BF16),
            pltpu.VMEM((count_p, cells, group), BF16),
            pltpu.VMEM((count_z, own_cells, wide + group), BF16),
        ],
    )(*grads, bottle, shift_m, w_bottle_t)
    parts = trade(sends, "gz", count_z)
    output, *sends = local_call(
        lambda *refs: hidden_grad_kernel(count_y, count_z, *refs),
        "hidden_grad",
        [shape_of(volume.shape)] + [shape_of((27 * share_c, channels))] * count_p,
        [
            pltpu.VMEM((planes * own, 3 * channels), BF16),
            pltpu.VMEM((size_z, own, channels), BF16),
            pltpu.VMEM((count_z, own_cells, group), BF16),
            pltpu.VMEM((count_p, 27 * share_c, channels), BF16),
        ],
    )(*parts, hidden, slope, ordered, w_up, w_down, turned, order_t)
    parts = trade(sends, plane_axes, count_p)
    part = local_call(plane_sum_kernel, "plane_sum", shape_of((27 * share_c, channels)))(*parts)
    parts = trade([part] * count_z, "gz", count_z)
    grad_bottle = local_call(
        lambda *refs: grad_bottle_kernel(count_y, count_z, quarter, *refs),
        "grad_bottle",
        shape_of((27, share_w, group), F32),
        [
            pltpu.VMEM((18 * share_w, 2 * count_z * rows), BF16),
            pltpu.VMEM((2 * count_z * rows, 5 * group), BF16),
            pltpu.VMEM((count_p, cells, group), BF16),
        ],
    )(coarse, shift_m, *grads)
    grad_conv = local_call(
        grad_conv_kernel,
        "grad_conv",
        shape_of((27, share_c, channels), F32),
    )(*parts)
    return (output, jnp.transpose(grad_conv, (1, 0, 2)), jnp.transpose(grad_bottle, (1, 0, 2)))


def with_halo(cells, sides, width):
    for axis, dim in sides:
        count = lax.axis_size(axis)
        ends = count - 1
        head = lax.slice_in_dim(cells, 0, width, axis=dim)
        tail = lax.slice_in_dim(cells, cells.shape[dim] - width, cells.shape[dim], axis=dim)
        cells = jnp.concatenate(
            [
                lax.ppermute(tail, axis, [(i, (i + 1) % count) for i in range(ends)]),
                cells,
                lax.ppermute(head, axis, [((i + 1) % count, i) for i in range(ends)]),
            ],
            axis=dim,
        )
    return cells


def silu_slope(values):
    sig = jax.nn.sigmoid(values)
    return sig * (1.0 + values * (1.0 - sig))


def conv_forward(padded, weight, extent):
    size_z, size_x, size_y = extent
    count_cells = size_z * size_x * size_y
    summed = jnp.zeros((count_cells, weight.shape[2]), jnp.float32)
    for tap_index in range(27):
        shift_z, shift_x, shift_y = (tap_index // 9, tap_index // 3 % 3, tap_index % 3)
        window = padded[
            shift_z : shift_z + size_z, shift_x : shift_x + size_x, shift_y : shift_y + size_y, :
        ]
        window = window.reshape(count_cells, padded.shape[3])
        summed = summed + jnp.dot(
            window, weight[:, tap_index, :], preferred_element_type=jnp.float32
        )
    return summed.reshape(size_z, size_x, size_y, weight.shape[2])


def conv_weight_grad(padded, gradient, extent):
    size_z, size_x, size_y = extent
    count_cells = size_z * size_x * size_y
    flat_gradient = gradient.reshape(count_cells, gradient.shape[3])
    pieces = []
    for tap_index in range(27):
        shift_z, shift_x, shift_y = (tap_index // 9, tap_index // 3 % 3, tap_index % 3)
        window = padded[
            shift_z : shift_z + size_z, shift_x : shift_x + size_x, shift_y : shift_y + size_y, :
        ]
        window = window.reshape(count_cells, padded.shape[3])
        pieces.append(
            lax.dot_general(
                window, flat_gradient, (((0,), (0,)), ((), ())), preferred_element_type=jnp.float32
            )
        )
    return jnp.stack(pieces, axis=1)


def conv_input_grad(padded, weight, extent):
    size_z, size_x, size_y = extent
    count_cells = size_z * size_x * size_y
    summed = jnp.zeros((count_cells, weight.shape[0]), jnp.float32)
    for tap_index in range(27):
        shift_z, shift_x, shift_y = (2 - tap_index // 9, 2 - tap_index // 3 % 3, 2 - tap_index % 3)
        window = padded[
            shift_z : shift_z + size_z, shift_x : shift_x + size_x, shift_y : shift_y + size_y, :
        ]
        window = window.reshape(count_cells, padded.shape[3])
        summed = summed + lax.dot_general(
            window,
            weight[:, tap_index, :],
            (((1,), (1,)), ((), ())),
            preferred_element_type=jnp.float32,
        )
    return summed.reshape(size_z, size_x, size_y, weight.shape[0])


def pool_features(fine, kernel):
    size_z, size_x, size_y, channels = fine.shape
    blocks = fine.reshape(size_z // 2, 2, size_x // 2, 2, size_y // 2, 2, channels)
    kernel_cube = kernel.reshape(2, 2, 2, kernel.shape[1], kernel.shape[2])
    return jnp.einsum(
        "zaxbycf,abcfg->zxyg", blocks, kernel_cube, preferred_element_type=jnp.float32
    )


def pool_adjoint(coarse_in, kernel):
    size_z, size_x, size_y, wide_channels = coarse_in.shape
    kernel_cube = kernel.reshape(2, 2, 2, kernel.shape[1], kernel.shape[2])
    result = jnp.einsum(
        "zxyg,abcfg->zaxbycf", coarse_in, kernel_cube, preferred_element_type=jnp.float32
    )
    return result.reshape(2 * size_z, 2 * size_x, 2 * size_y, kernel.shape[1])


def lift_features(coarse_in, kernel):
    size_z, size_x, size_y, wide_channels = coarse_in.shape
    kernel_cube = kernel.reshape(2, 2, 2, kernel.shape[1], kernel.shape[2])
    result = jnp.einsum(
        "zxyg,abcgf->zaxbycf", coarse_in, kernel_cube, preferred_element_type=jnp.float32
    )
    return result.reshape(2 * size_z, 2 * size_x, 2 * size_y, kernel.shape[2])


def lift_adjoint(fine, kernel):
    size_z, size_x, size_y, channels = fine.shape
    blocks = fine.reshape(size_z // 2, 2, size_x // 2, 2, size_y // 2, 2, channels)
    kernel_cube = kernel.reshape(2, 2, 2, kernel.shape[1], kernel.shape[2])
    return jnp.einsum(
        "zaxbycf,abcgf->zxyg", blocks, kernel_cube, preferred_element_type=jnp.float32
    )


def column_body(volume, cotangent, w_conv, w_down, w_bottle, w_up):
    size_z, size_x, size_y, channels = volume.shape
    group_channels = w_bottle.shape[2]
    half_x = size_x // 2
    half_y = size_y // 2
    padded = with_halo(volume, (("gx", 1), ("gy", 2), ("gz", 0)), 1)
    pre_hidden = conv_forward(padded, w_conv, (size_z, size_x, size_y))
    hidden = jax.nn.silu(pre_hidden).astype(jnp.bfloat16)
    hidden_slope = silu_slope(pre_hidden)
    coarse = pool_features(hidden, w_down).astype(jnp.bfloat16)
    stacked = lax.all_gather(coarse, "gz", axis=0, tiled=True)
    rimmed = with_halo(stacked, (("gx", 1), ("gy", 2)), 1)
    column_z = rimmed.shape[0]
    coarse_pad = jnp.pad(rimmed, ((1, 1), (0, 0), (0, 0), (0, 0)))
    pre_bottle = conv_forward(coarse_pad, w_bottle, (column_z, half_x, half_y))
    bottle = jax.nn.silu(pre_bottle).astype(jnp.bfloat16)
    bottle_slope = silu_slope(pre_bottle)
    own_start = lax.axis_index("gz") * group_channels
    own_up = lax.dynamic_slice_in_dim(w_up, own_start, group_channels, 1)
    lifted = lax.psum_scatter(
        lift_features(bottle, own_up).astype(jnp.bfloat16), "gz", scatter_dimension=0, tiled=True
    ).astype(jnp.float32)
    output = (lifted + hidden.astype(jnp.float32)).astype(jnp.bfloat16)
    back_bottle = lift_adjoint(cotangent, w_up).astype(jnp.bfloat16)
    split_grad = lax.all_to_all(back_bottle, "gz", split_axis=3, concat_axis=0, tiled=True)
    bottle_grad = (split_grad.astype(jnp.float32) * bottle_slope).astype(jnp.bfloat16)
    grad_bottle = lax.psum_scatter(
        conv_weight_grad(coarse_pad, bottle_grad, (column_z, half_x, half_y)),
        ("gx", "gy"),
        scatter_dimension=0,
        tiled=True,
    )
    grad_rimmed = with_halo(bottle_grad, (("gx", 1), ("gy", 2)), 1)
    grad_pad = jnp.pad(grad_rimmed, ((1, 1), (0, 0), (0, 0), (0, 0)))
    coarse_grad = lax.psum_scatter(
        conv_input_grad(
            grad_pad, w_bottle, (lax.axis_size("gz") * (size_z // 2), half_x, half_y)
        ).astype(jnp.bfloat16),
        "gz",
        scatter_dimension=0,
        tiled=True,
    )
    hidden_grad = (
        (pool_adjoint(coarse_grad, w_down) + cotangent.astype(jnp.float32)) * hidden_slope
    ).astype(jnp.bfloat16)
    full_term = conv_weight_grad(padded, hidden_grad, (size_z, size_x, size_y))
    depth_summed = lax.psum(full_term.astype(jnp.bfloat16), "gz").astype(jnp.float32)
    grad_conv = lax.psum_scatter(depth_summed, ("gx", "gy"), scatter_dimension=0, tiled=True)
    return (output, grad_conv, grad_bottle)


def fits_one_plane(counts, brick, wide):
    count_p = counts[0] * counts[1]
    size_z, size_x, size_y, channels = brick
    return (
        counts == (2, 4, 4)
        and count_p * (size_x // 2) * (size_y // 2) == 128
        and wide // count_p == 64
        and (size_z, size_x, size_y, channels) == (8, 8, 8, 128)
    )


def solution(mesh):
    in_specs = (
        P("gz", "gx", "gy", None),
        P("gz", "gx", "gy", None),
        P(),
        P(),
        P(None, None, "gz"),
        P(),
    )
    out_specs = (
        P("gz", "gx", "gy", None),
        P(("gx", "gy"), None, None),
        P(("gx", "gy"), None, "gz"),
    )
    counts = (mesh.shape["gx"], mesh.shape["gy"], mesh.shape["gz"])

    def body(volume, cotangent, w_conv, w_down, w_bottle, w_up):
        if fits_one_plane(counts, volume.shape, w_down.shape[2]):
            return gathered_body(counts, volume, cotangent, w_conv, w_down, w_bottle, w_up)
        return column_body(volume, cotangent, w_conv, w_down, w_bottle, w_up)

    return jax.shard_map(body, mesh=mesh, in_specs=in_specs, out_specs=out_specs, check_vma=False)
```

```python
import numpy as np
import jax
import jax.numpy as jnp
from jax import lax
from jax.experimental import pallas as pl
from jax.experimental.pallas import tpu as pltpu
from jax.sharding import PartitionSpec as P

BF16 = jnp.bfloat16
F32 = jnp.float32
VMEM_LIMIT = 24 * 1024 * 1024


def local_call(kernel, name, out_shapes, scratch=()):
    whole = pl.BlockSpec(memory_space=pltpu.VMEM)

    def call(*operands):
        return pl.pallas_call(
            kernel,
            name=name,
            out_shape=out_shapes,
            in_specs=[whole] * len(operands),
            out_specs=jax.tree.map(lambda _: whole, out_shapes),
            scratch_shapes=list(scratch),
            compiler_params=pltpu.CompilerParams(vmem_limit_bytes=VMEM_LIMIT),
        )(*operands)

    return call


def matmul(left, right):
    return jnp.dot(left, right, preferred_element_type=F32)


def matmul_nt(left, right):
    return lax.dot_general(left, right, (((1,), (1,)), ((), ())), preferred_element_type=F32)


def sub_order(size_x, size_y):
    half_x, half_y = size_x // 2, size_y // 2
    return {
        (2 * kx + b, 2 * ky + c): ((2 * b + c) * half_x + kx) * half_y + ky
        for b in range(2)
        for c in range(2)
        for kx in range(half_x)
        for ky in range(half_y)
    }


def fine_maps(size_x, size_y):
    own = size_x * size_y
    rows = sub_order(size_x, size_y)
    order = np.zeros((own, own), np.float32)
    taps = np.zeros((9, own, 2 * own), np.float32)
    for (x, y), row in rows.items():
        order[row, x * size_y + y] = 1
        for b in range(3):
            for c in range(3):
                sx, sy = x + b - 1, y + c - 1
                if sx < 0:
                    part = 0 if 0 <= sy < size_y else (4 if sy < 0 else 5)
                    source = own + 8 * part + sy % size_y
                elif sx >= size_x:
                    part = 1 if 0 <= sy < size_y else (6 if sy < 0 else 7)
                    source = own + 8 * part + sy % size_y
                elif sy < 0:
                    source = own + 16 + sx
                elif sy >= size_y:
                    source = own + 24 + sx
                else:
                    source = sx * size_y + sy
                taps[3 * b + c, row, source] = 1
    return order, taps


def coarse_maps(count_x, count_y, half_x, half_y):
    wide_x, wide_y = count_x * half_x, count_y * half_y

    def row_of(x, y):
        brick = (x // half_x) * count_y + y // half_y
        return (brick * half_x + x % half_x) * half_y + y % half_y

    shift = np.zeros((9, wide_x * wide_y, wide_x * wide_y), np.float32)
    for x in range(wide_x):
        for y in range(wide_y):
            for b in range(3):
                for c in range(3):
                    sx, sy = x + b - 1, y + c - 1
                    if 0 <= sx < wide_x and 0 <= sy < wide_y:
                        shift[3 * b + c, row_of(x, y), row_of(sx, sy)] = 1
    return shift


def column_maps(half_x, half_y, depth):
    quarter = half_x * half_y
    rows = depth * quarter
    send = np.zeros((2, depth * (half_y + 2 * half_x + 2), rows), np.float32)
    rim = np.zeros((2, 9, 4, quarter, 8 * quarter), np.float32)
    for px in range(2):
        out_x = 0 if px else half_x - 1
        for z in range(depth):
            base = z * quarter
            row = z * half_y
            for ky in range(half_y):
                send[px, row + ky, base + out_x * half_y + ky] = 1
            for side, ky in enumerate((0, half_y - 1)):
                row = depth * (half_y + side * half_x) + z * half_x
                for kx in range(half_x):
                    send[px, row + kx, base + kx * half_y + ky] = 1
                row = depth * (half_y + 2 * half_x + side) + z
                send[px, row, base + out_x * half_y + ky] = 1
        for b in range(3):
            for c in range(3):
                for kx in range(half_x):
                    for ky in range(half_y):
                        sx, sy = kx + b - 1, ky + c - 1
                        beyond = sx < 0 if px else sx >= half_x
                        if (sx < 0 or sx >= half_x) and not beyond:
                            continue
                        for z in range(4):
                            if beyond and 0 <= sy < half_y:
                                source = 4 * quarter + z * half_y + sy
                            elif beyond:
                                source = 7 * quarter + 4 * (sy >= half_y) + z
                            elif sy < 0:
                                source = 5 * quarter + z * half_x + sx
                            elif sy >= half_y:
                                source = 6 * quarter + z * half_x + sx
                            else:
                                source = z * quarter + sx * half_y + sy
                            rim[px, 3 * b + c, z, kx * half_y + ky, source] = 1
    return send, rim


def swap(block, axes, count, distance):
    return lax.ppermute(block, axes, [(i, i ^ distance) for i in range(count)])


def trade(blocks, axes, count):
    got = {d: swap(blocks[d], axes, count, d) for d in reversed(range(1, count))}
    return [blocks[0]] + [got[d] for d in range(1, count)]


def near_kernel(count, *refs):
    copies = [pltpu.make_async_copy(refs[i], refs[count + i], refs[2 * count].at[i]) for i in range(count)]
    for copy in copies:
        copy.start()
    for copy in copies:
        copy.wait()


def bring_near(*arrays):
    count = len(arrays)
    return pl.pallas_call(
        lambda *refs: near_kernel(count, *refs),
        name="near",
        out_shape=[jax.ShapeDtypeStruct(array.shape, array.dtype) for array in arrays],
        in_specs=[pl.BlockSpec(memory_space=pltpu.HBM)] * count,
        out_specs=[pl.BlockSpec(memory_space=pltpu.VMEM)] * count,
        scratch_shapes=[pltpu.SemaphoreType.DMA((count,))],
        compiler_params=pltpu.CompilerParams(vmem_limit_bytes=VMEM_LIMIT),
    )(*arrays)


def plane_index(count_y):
    return lax.axis_index("gx") * count_y + lax.axis_index("gy")


def plane_rows(ref, z):
    _, size_x, size_y, channels = ref.shape
    return ref[z].astype(F32).reshape(size_x * size_y, channels)


def hand_out(blocks, outs, me):
    for d, out in enumerate(outs):
        out[...] = blocks[me ^ d]


def take_in(parts, blocks, me):
    for d, part in enumerate(parts):
        blocks[me ^ d] = part[...]


def total_of(parts):
    terms = [part[...].astype(F32) for part in parts]
    while len(terms) > 1:
        terms = [terms[i] + terms[i + 1] for i in range(0, len(terms), 2)]
    return terms[0]


def back_of(cotangent, w_up, order, ordered):
    size_z, size_x, size_y, channels = cotangent.shape
    quarter = size_x * size_y // 4
    for z in range(size_z):
        ordered[z] = matmul(order[...], plane_rows(cotangent, z).astype(BF16)).astype(BF16)
    back = None
    for s in range(8):
        a, bc = s // 4, s % 4
        cells = jnp.concatenate(
            [ordered[2 * kz + a, bc * quarter : (bc + 1) * quarter, :] for kz in range(size_z // 2)], axis=0
        )
        term = matmul_nt(cells, w_up[s])
        back = term if back is None else back + term
    return back.astype(BF16)


def depth_rim(volume, below, above, z):
    size_z, size_x, size_y, channels = volume.shape
    if z < 0:
        return below[...].astype(F32).reshape(size_x * size_y, channels)
    if z >= size_z:
        return above[...].astype(F32).reshape(size_x * size_y, channels)
    return plane_rows(volume, z)


def faces_kernel(volume, below, above, x_send, y_low_send, y_high_send, deep):
    size_z, size_x, size_y, channels = volume.shape
    own = size_x * size_y
    planes = size_z + 2
    for z in range(planes):
        deep[z * own : (z + 1) * own, :] = depth_rim(volume, below, above, z - 1)

    def x_face(x):
        return jnp.concatenate(
            [deep[z * own + x * size_y : z * own + (x + 1) * size_y, :] for z in range(planes)], axis=0
        ).astype(BF16)

    x_send[...] = jnp.where(lax.axis_index("gx") == 0, x_face(size_x - 1), x_face(0))
    y_low_send[...] = deep[pl.ds(0, planes * size_x, stride=size_y), :].astype(BF16)
    y_high_send[...] = deep[pl.ds(size_y - 1, planes * size_x, stride=size_y), :].astype(BF16)


def hidden_kernel(
    count_z, volume, below, above, x_rim, y_low, y_high, xy_low, xy_high, taps, w_conv, w_down, cotangent, w_up,
    order, *refs,
):
    (hidden, slope, rim, ordered), sends, (rim32, cells, blocks) = refs[:4], refs[4:-3], refs[-3:]
    size_z, size_x, size_y, channels = volume.shape
    own = size_x * size_y
    quarter = own // 4
    planes = size_z + 2
    first = lax.axis_index("gx") == 0
    for z in range(planes):
        rim32[z, :own, :] = depth_rim(volume, below, above, z - 1)
    sides = (
        (x_rim, False),
        (x_rim, True),
        (y_low, None),
        (y_high, None),
        (xy_low, False),
        (xy_high, False),
        (xy_low, True),
        (xy_high, True),
    )
    for part, (block, high) in enumerate(sides):
        rows = block[...].astype(F32).reshape(planes, 8, channels)
        if high is not None:
            rows = jnp.where(first == high, rows, 0.0)
        rim32[:, own + 8 * part : own + 8 * (part + 1), :] = rows
    for z in range(planes):
        rows = rim32[z].astype(BF16)
        rim[z] = rows
        moved = matmul(taps[...], rows).astype(BF16)
        for bc in range(9):
            cells[z, :, bc * channels : (bc + 1) * channels] = moved[bc * own : (bc + 1) * own, :]
    pre = None
    for a in range(3):
        window = cells[a : a + size_z].reshape(size_z * own, 9 * channels)
        weight = w_conv[9 * a : 9 * (a + 1)].reshape(9 * channels, channels)
        term = matmul(window, weight)
        pre = term if pre is None else pre + term
    sig = jax.nn.sigmoid(pre)
    slope[...] = (sig * (1.0 + pre * (1.0 - sig))).reshape(size_z, own, channels)
    hidden[...] = (pre * sig).astype(BF16).reshape(size_z, own, channels)
    parts = []
    for s in range(8):
        a, bc = s // 4, s % 4
        parts.append(
            jnp.concatenate(
                [hidden[2 * kz + a, bc * quarter : (bc + 1) * quarter, :] for kz in range(size_z // 2)], axis=0
            )
        )
    coarse = matmul(jnp.concatenate(parts, axis=1), w_down[...].reshape(8 * channels, w_down.shape[2]))
    coarse = coarse.astype(BF16)
    wide = coarse.shape[1]
    back = back_of(cotangent, w_up, order, ordered)
    group = wide // count_z
    for q in range(count_z):
        blocks[q] = back[:, q * group : (q + 1) * group]
    pz = lax.axis_index("gz")
    for d, send in enumerate(sends):
        send[:, :wide] = coarse
        send[:, wide:] = blocks[pz ^ d]


def rim_transpose_kernel(rim, taps_t, turned):
    planes, rows, channels = rim.shape
    for pair in range(planes // 2):
        sides = [rim[2 * pair + i].astype(F32).T for i in range(2)]
        moved = matmul(jnp.concatenate(sides, axis=1).astype(BF16), taps_t[...]).astype(BF16)
        for bc in range(9):
            turned[bc * channels : (bc + 1) * channels, pair * rows : (pair + 1) * rows] = moved[
                :, bc * rows : (bc + 1) * rows
            ]


def column_kernel(count_z, *refs):
    parts, picks, (column, back, x_send, y_low_send, y_high_send, low_send, high_send) = (
        refs[:count_z],
        refs[count_z],
        refs[count_z + 1 :],
    )
    own_cells = parts[0].shape[0]
    wide = column.shape[1]
    pz = lax.axis_index("gz")
    for d, part in enumerate(parts):
        rows = pl.ds(pl.multiple_of((pz ^ d) * own_cells, own_cells), own_cells)
        column[rows, :] = part[:, :wide]
        back[rows, :] = part[:, wide:]
    rims = matmul(picks[lax.axis_index("gx")], column[...]).astype(BF16)
    start = 0
    for send in (x_send, y_low_send, y_high_send, low_send, high_send):
        send[...] = rims[start : start + send.shape[0], :]
        start += send.shape[0]


def bottle_kernel(count_y, column, back, x_rim, y_low, y_high, low, high, shift, w_bottle, *refs):
    bottle, sends, (rim32, window, slices) = refs[0], refs[1:-3], refs[-3:]
    cells, wide = column.shape
    outs = w_bottle.shape[2]
    side = x_rim.shape[0]
    depth = low.shape[0]
    quarter = cells // depth
    span = 4 * quarter
    picks = shift[lax.axis_index("gx")]
    window[:quarter, :] = jnp.zeros((quarter, 9 * wide), BF16)
    window[(depth + 1) * quarter :, :] = jnp.zeros((quarter, 9 * wide), BF16)
    edge = side // (depth // 4)
    for g in range(depth // 4):
        rim32[g, :span, :] = column[g * span : (g + 1) * span, :].astype(F32)
        for part, block in enumerate((x_rim, y_low, y_high)):
            start = span + part * edge
            rim32[g, start : start + edge, :] = block[g * edge : (g + 1) * edge, :].astype(F32)
        start = span + 3 * edge
        rim32[g, start + 8 :, :] = jnp.zeros((rim32.shape[1] - start - 8, wide), F32)
    lows, highs = low[...].astype(F32), high[...].astype(F32)
    for g in range(depth // 4):
        start = span + 3 * edge
        rim32[g, start : start + 4, :] = lows[4 * g : 4 * g + 4, :]
        rim32[g, start + 4 : start + 8, :] = highs[4 * g : 4 * g + 4, :]
        moved = matmul(picks, rim32[g].astype(BF16)).astype(BF16)
        for bc in range(9):
            window[quarter + g * span : quarter + (g + 1) * span, bc * wide : (bc + 1) * wide] = moved[
                bc * span : (bc + 1) * span, :
            ]
    pre = None
    for a in range(3):
        term = matmul(
            window[a * quarter : a * quarter + cells, :], w_bottle[9 * a : 9 * (a + 1)].reshape(9 * wide, outs)
        )
        pre = term if pre is None else pre + term
    sig = jax.nn.sigmoid(pre)
    bottle[...] = (pre * sig).astype(BF16)
    slope = sig * (1.0 + pre * (1.0 - sig))
    grad = (back[...].astype(F32) * slope).astype(BF16)
    p = plane_index(count_y)
    half = span // 2
    lane = lax.broadcasted_iota(jnp.int32, (half, 128), 1)
    for pair in range(wide // 128):
        for g in range(depth // 4):
            top = column[g * span : g * span + half, pair * 128 : (pair + 1) * 128].astype(F32)
            end = column[g * span + half : (g + 1) * span, pair * 128 : (pair + 1) * 128].astype(F32)
            rows = slice(g * half, (g + 1) * half)
            slices[2 * pair, rows, :] = jnp.where(lane < 64, top, pltpu.roll(end, 64, 1)).astype(BF16)
            slices[2 * pair + 1, rows, :] = jnp.where(lane < 64, pltpu.roll(top, 64, 1), end).astype(BF16)
    middle = cells + slices.shape[1]
    for i, send in enumerate(sends):
        send[:cells, :] = grad
        send[cells:middle, :] = slices[p ^ (2 * i)]
        send[middle:, :] = slices[p ^ (2 * i + 1)]


def coarse_grad_kernel(count_y, count_z, quarter, *refs):
    grads, (bottle, shift, w_bottle) = refs[: -count_z - 6], refs[-count_z - 6 : -count_z - 3]
    sends, (window, gathered, blocks) = refs[-count_z - 3 : -3], refs[-3:]
    count_p = len(grads)
    cells, outs = bottle.shape
    rows = count_p * quarter
    depth = cells // quarter
    own_cells = cells // count_z
    inputs = w_bottle.shape[1]
    p = plane_index(count_y)
    for d, part in enumerate(grads):
        gathered[p ^ d] = part[:cells, :]
    mine = pl.multiple_of(p * quarter, quarter)
    picks = jnp.concatenate([shift[pl.ds((8 - bc) * rows + mine, quarter), :] for bc in range(9)], axis=0)
    window[:quarter, :] = jnp.zeros((quarter, 9 * outs), BF16)
    window[(depth + 1) * quarter :, :] = jnp.zeros((quarter, 9 * outs), BF16)
    for z in range(depth):
        plane = jnp.concatenate([gathered[q, z * quarter : (z + 1) * quarter, :] for q in range(count_p)], axis=0)
        moved = matmul(picks, plane).astype(BF16)
        for bc in range(9):
            window[(z + 1) * quarter : (z + 2) * quarter, bc * outs : (bc + 1) * outs] = moved[
                bc * quarter : (bc + 1) * quarter, :
            ]
    total = None
    for a in range(3):
        for bc in range(9):
            term = matmul_nt(
                window[(2 - a) * quarter : (2 - a + depth) * quarter, bc * outs : (bc + 1) * outs],
                w_bottle[9 * a + bc],
            )
            total = term if total is None else total + term
    total = total.astype(BF16)
    for q in range(count_z):
        blocks[q, :, :inputs] = total[q * own_cells : (q + 1) * own_cells, :]
        blocks[q, :, inputs:] = bottle[q * own_cells : (q + 1) * own_cells, :]
    hand_out(blocks, sends, lax.axis_index("gz"))


def grad_bottle_kernel(count_y, shift, *refs):
    parts, (out, turned, wide, grads, slices) = refs[:-5], refs[-5:]
    count_p, cells, outs = grads.shape
    lines = slices.shape[1]
    rows = shift.shape[1]
    quarter = rows // count_p
    depth = cells // quarter
    channels = out.shape[1]
    p = plane_index(count_y)
    for d, part in enumerate(parts):
        start = cells + d % 2 * lines
        grads[p ^ d] = part[:cells, :]
        slices[p ^ d] = part[start : start + lines, :]
    wide[...] = jnp.zeros_like(wide)
    planes = [
        jnp.concatenate([grads[q, z * quarter : (z + 1) * quarter, :] for q in range(count_p)], axis=0)
        for z in range(depth)
    ]
    for j in range(depth // 2):
        plane = jnp.concatenate([slices[q, j * quarter : (j + 1) * quarter, :] for q in range(count_p)], axis=0)
        plane = plane.astype(F32).T.astype(BF16)
        for bc in range(9):
            turned[bc * 128 : (bc + 1) * 128, j * rows : (j + 1) * rows] = matmul(
                plane, shift[(8 - bc) * rows : (9 - bc) * rows, :]
            ).astype(BF16)
        for slot in range(5):
            z = j // 2 * 4 + j % 2 + slot - 1
            if 0 <= z < depth:
                wide[j * rows : (j + 1) * rows, slot * outs : (slot + 1) * outs] = planes[z]
    full = matmul(turned[...], wide[...])
    for bc in range(9):
        top = full[bc * 128 : bc * 128 + channels, :]
        end = full[bc * 128 + channels : (bc + 1) * 128, :]
        for a in range(3):
            out[9 * a + bc] = top[:, (2 - a) * outs : (3 - a) * outs] + end[:, (4 - a) * outs : (5 - a) * outs]


def hidden_grad_kernel(count_y, count_z, *refs):
    parts, (hidden, slope, ordered, w_up, w_down, turned, order_t) = refs[:count_z], refs[count_z : count_z + 7]
    output, keep, give, (shifted, rows_out, bottles, blocks) = *refs[count_z + 7 : count_z + 10], refs[-4:]
    count_p = blocks.shape[0]
    size_z, own, channels = hidden.shape
    quarter = own // 4
    inputs = w_down.shape[2]
    pz = lax.axis_index("gz")
    grad = parts[0][:, :inputs].astype(F32)
    for part in parts[1:]:
        grad = grad + part[:, :inputs].astype(F32)
    grad = grad.astype(BF16)
    for d, part in enumerate(parts):
        bottles[pz ^ d] = part[:, inputs:]
    bottle = jnp.concatenate([bottles[q] for q in range(count_z)], axis=1)
    shifted[...] = jnp.zeros_like(shifted)
    for s in range(8):
        a, bc = s // 4, s % 4
        lifted = matmul(bottle, w_up[s])
        spread_grad = matmul_nt(grad, w_down[s])
        for kz in range(size_z // 2):
            z = 2 * kz + a
            part = slice(bc * quarter, (bc + 1) * quarter)
            line = slice(kz * quarter, (kz + 1) * quarter)
            rows_out[z, part, :] = (lifted[line, :] + hidden[z, part, :].astype(F32)).astype(BF16)
            value = ((spread_grad[line, :] + ordered[z, part, :].astype(F32)) * slope[z, part, :]).astype(BF16)
            for t in range(3):
                start = (z + t) * own + bc * quarter
                shifted[start : start + quarter, t * channels : (t + 1) * channels] = value
    for z in range(size_z):
        plane = matmul(order_t[...], rows_out[z])
        output[z] = plane.reshape(output.shape[1:]).astype(BF16)
    full = matmul(turned[...], shifted[...])
    group = channels // count_p
    for bc in range(9):
        for a in range(3):
            t = 9 * a + bc
            block = full[bc * channels : (bc + 1) * channels, a * channels : (a + 1) * channels].astype(BF16)
            for p in range(count_p):
                blocks[p, t * group : (t + 1) * group, :] = block[p * group : (p + 1) * group, :]
    p = plane_index(count_y)
    for i in range(count_p // 2):
        keep[i] = blocks[p ^ (2 * i)]
        give[i] = blocks[p ^ (2 * i + 1)]


def pair_sum_kernel(keep, got, *sends):
    for i, send in enumerate(sends):
        send[...] = (keep[i].astype(F32) + got[i].astype(F32)).astype(BF16)


def plane_sum_kernel(count, *refs):
    sends, blocks = refs[count:-1], refs[-1]
    total = total_of(refs[:count]).astype(BF16)
    share = blocks.shape[1]
    for q in range(blocks.shape[0]):
        size = min(share, total.shape[0] - q * share)
        blocks[q, :size, :] = total[q * share : q * share + size, :]
        if size < share:
            blocks[q, size:, :] = jnp.zeros((share - size, total.shape[1]), BF16)
    hand_out(blocks, sends, lax.axis_index("gz"))


def depth_sum_kernel(*refs):
    refs[-1][...] = total_of(refs[:-1]).astype(BF16)


def grad_conv_kernel(*refs):
    parts, (out, blocks) = refs[:-2], refs[-2:]
    take_in(parts, blocks, lax.axis_index("gz"))
    share = blocks.shape[1]
    taps, group, _ = out.shape
    for t in range(taps):
        q, start = t * group // share, t * group % share
        out[t] = blocks[q, start : start + group, :].astype(F32)


def shape_of(shape, dtype=BF16):
    return jax.ShapeDtypeStruct(shape, dtype)


def gathered_body(counts, volume, cotangent, w_conv, w_down, w_bottle, w_up):
    count_x, count_y, count_z = counts
    count_p = count_x * count_y
    size_z, size_x, size_y, channels = volume.shape
    wide = w_down.shape[2]
    group = w_bottle.shape[2]
    half_x, half_y = size_x // 2, size_y // 2
    own = size_x * size_y
    quarter = half_x * half_y
    own_cells = size_z // 2 * quarter
    cells = count_z * own_cells
    depth = count_z * size_z // 2
    rows = count_p * quarter
    planes = size_z + 2
    share_c = channels // count_p
    share_w = wide // count_p
    plane_axes = ("gx", "gy")

    order, taps = fine_maps(size_x, size_y)
    pair_taps = np.zeros((2, 2 * own, 9, 2, own), np.float32)
    for i in range(2):
        pair_taps[i, :, :, i, :] = taps.transpose(2, 0, 1)
    shift = coarse_maps(count_x, count_y, half_x, half_y)
    order_m = jnp.asarray(order, BF16)
    order_t = jnp.asarray(order.T, BF16)
    taps_m = jnp.asarray(taps.reshape(9 * own, 2 * own), BF16)
    taps_t = jnp.asarray(pair_taps.reshape(4 * own, 18 * own), BF16)
    shift_m = jnp.asarray(shift.reshape(9 * rows, rows), BF16)

    send_maps, rim_maps = column_maps(half_x, half_y, depth)
    send_m = jnp.asarray(send_maps, BF16)
    rim_m = jnp.asarray(rim_maps.reshape(count_x, 36 * quarter, 8 * quarter), BF16)
    w_bottle_t = jnp.transpose(w_bottle, (1, 0, 2))
    up_z = [(i, i + 1) for i in range(count_z - 1)]
    below = lax.ppermute(volume[size_z - 1], "gz", up_z)
    above = lax.ppermute(volume[0], "gz", [(j, i) for i, j in up_z])
    near = bring_near(
        volume,
        cotangent,
        jnp.transpose(w_conv, (1, 0, 2)),
        w_down,
        w_up,
        order_m,
        order_t,
        taps_m,
        taps_t,
        send_m,
        rim_m,
        shift_m,
    )
    volume, cotangent, w_conv_t, w_down, w_up, order_m, order_t, taps_m, taps_t, send_m, rim_m, shift_m = near
    x_send, y_low_send, y_high_send = local_call(
        faces_kernel,
        "faces",
        [shape_of((planes * 8, channels))] * 3,
        [pltpu.VMEM((planes * own, channels), F32)],
    )(volume, below, above)
    ups = [(x * count_y + y, x * count_y + y + 1) for x in range(count_x) for y in range(count_y - 1)]
    downs = [(j, i) for i, j in ups]
    cross_ups = [((1 - i // count_y) * count_y + i % count_y, j) for i, j in ups]
    cross_downs = [(j, i) for i, j in cross_ups]
    xy_low = lax.ppermute(x_send, plane_axes, cross_ups)
    xy_high = lax.ppermute(x_send, plane_axes, cross_downs)
    x_rim = lax.ppermute(x_send, "gx", [(0, 1), (1, 0)])
    y_low = lax.ppermute(y_high_send, plane_axes, ups)
    y_high = lax.ppermute(y_low_send, plane_axes, downs)
    hidden, slope, rim, ordered, *sends = local_call(
        lambda *refs: hidden_kernel(count_z, *refs),
        "hidden",
        [
            shape_of((size_z, own, channels)),
            shape_of((size_z, own, channels), F32),
            shape_of((planes, 2 * own, channels)),
            shape_of((size_z, own, channels)),
        ]
        + [shape_of((own_cells, wide + group))] * count_z,
        [
            pltpu.VMEM((planes, 2 * own, channels), F32),
            pltpu.VMEM((planes, own, 9 * channels), BF16),
            pltpu.VMEM((count_z, own_cells, group), BF16),
        ],
    )(
        volume, below, above, x_rim, y_low, y_high, xy_low, xy_high, taps_m, w_conv_t, w_down, cotangent, w_up, order_m
    )
    parts = trade(sends, "gz", count_z)
    turned = local_call(
        rim_transpose_kernel,
        "rim_transpose",
        shape_of((9 * channels, planes * own)),
    )(rim, taps_t)
    column, back, x_send, y_low_send, y_high_send, low_send, high_send = local_call(
        lambda *refs: column_kernel(count_z, *refs),
        "column",
        [
            shape_of((cells, wide)),
            shape_of((cells, group)),
            shape_of((depth * half_y, wide)),
            shape_of((depth * half_x, wide)),
            shape_of((depth * half_x, wide)),
            shape_of((depth, wide)),
            shape_of((depth, wide)),
        ],
    )(*parts, send_m)
    low = lax.ppermute(high_send, plane_axes, cross_ups)
    high = lax.ppermute(low_send, plane_axes, cross_downs)
    x_rim = lax.ppermute(x_send, "gx", [(0, 1), (1, 0)])
    y_low = lax.ppermute(y_high_send, plane_axes, ups)
    y_high = lax.ppermute(y_low_send, plane_axes, downs)
    bottle, *sends = local_call(
        lambda *refs: bottle_kernel(count_y, *refs),
        "bottle",
        [shape_of((cells, group))] + [shape_of((2 * cells, group))] * (count_p // 2),
        [
            pltpu.VMEM((depth // 4, 8 * quarter, wide), F32),
            pltpu.VMEM(((depth + 2) * quarter, 9 * wide), BF16),
            pltpu.VMEM((count_p, cells // 2, 128), BF16),
        ],
    )(column, back, x_rim, y_low, y_high, low, high, rim_m, w_bottle_t)
    grads = [None] * count_p
    grads[0] = sends[0]
    for d in (6, 4, 2):
        grads[d] = swap(sends[d // 2], plane_axes, count_p, d)
    for d in (0, 2, 4, 6):
        grads[d + 1] = swap(grads[d], plane_axes, count_p, 1)
    sends = local_call(
        lambda *refs: coarse_grad_kernel(count_y, count_z, quarter, *refs),
        "coarse_grad",
        [shape_of((own_cells, wide + group))] * count_z,
        [
            pltpu.VMEM(((depth + 2) * quarter, 9 * group), BF16),
            pltpu.VMEM((count_p, cells, group), BF16),
            pltpu.VMEM((count_z, own_cells, wide + group), BF16),
        ],
    )(*grads, bottle, shift_m, w_bottle_t)
    parts = trade(sends, "gz", count_z)
    output, keep, give = local_call(
        lambda *refs: hidden_grad_kernel(count_y, count_z, *refs),
        "hidden_grad",
        [shape_of(volume.shape)] + [shape_of((count_p // 2, 27 * share_c, channels))] * 2,
        [
            pltpu.VMEM((planes * own, 3 * channels), BF16),
            pltpu.VMEM((size_z, own, channels), BF16),
            pltpu.VMEM((count_z, own_cells, group), BF16),
            pltpu.VMEM((count_p, 27 * share_c, channels), BF16),
        ],
    )(*parts, hidden, slope, ordered, w_up, w_down, turned, order_t)
    got = swap(give, plane_axes, count_p, 1)
    sends = local_call(
        pair_sum_kernel,
        "pair_sum",
        [shape_of((27 * share_c, channels))] * (count_p // 2),
    )(keep, got)
    parts = [sends[0]] + [swap(sends[d // 2], plane_axes, count_p, d) for d in (6, 4, 2)]
    share = -(-27 * share_c // (16 * count_z)) * 16
    sends = local_call(
        lambda *refs: plane_sum_kernel(count_p // 2, *refs),
        "plane_sum",
        [shape_of((share, channels))] * count_z,
        [pltpu.VMEM((count_z, share, channels), BF16)],
    )(*parts)
    parts = trade(sends, "gz", count_z)
    part = local_call(depth_sum_kernel, "depth_sum", shape_of((share, channels)))(*parts)
    parts = trade([part] * count_z, "gz", count_z)
    grad_bottle = local_call(
        lambda *refs: grad_bottle_kernel(count_y, *refs),
        "grad_bottle",
        shape_of((27, share_w, group), F32),
        [
            pltpu.VMEM((18 * share_w, depth // 2 * rows), BF16),
            pltpu.VMEM((depth // 2 * rows, 5 * group), BF16),
            pltpu.VMEM((count_p, cells, group), BF16),
            pltpu.VMEM((count_p, cells // 2, 128), BF16),
        ],
    )(shift_m, *grads)
    grad_conv = local_call(
        grad_conv_kernel,
        "grad_conv",
        shape_of((27, share_c, channels), F32),
        [pltpu.VMEM((count_z, share, channels), BF16)],
    )(*parts)
    return (output, jnp.transpose(grad_conv, (1, 0, 2)), jnp.transpose(grad_bottle, (1, 0, 2)))


def with_halo(cells, sides, width):
    for axis, dim in sides:
        count = lax.axis_size(axis)
        ends = count - 1
        head = lax.slice_in_dim(cells, 0, width, axis=dim)
        tail = lax.slice_in_dim(cells, cells.shape[dim] - width, cells.shape[dim], axis=dim)
        cells = jnp.concatenate(
            [
                lax.ppermute(tail, axis, [(i, (i + 1) % count) for i in range(ends)]),
                cells,
                lax.ppermute(head, axis, [((i + 1) % count, i) for i in range(ends)]),
            ],
            axis=dim,
        )
    return cells


def silu_slope(values):
    sig = jax.nn.sigmoid(values)
    return sig * (1.0 + values * (1.0 - sig))


def conv_forward(padded, weight, extent):
    size_z, size_x, size_y = extent
    count_cells = size_z * size_x * size_y
    summed = jnp.zeros((count_cells, weight.shape[2]), jnp.float32)
    for tap_index in range(27):
        shift_z, shift_x, shift_y = (tap_index // 9, tap_index // 3 % 3, tap_index % 3)
        window = padded[
            shift_z : shift_z + size_z, shift_x : shift_x + size_x, shift_y : shift_y + size_y, :
        ]
        window = window.reshape(count_cells, padded.shape[3])
        summed = summed + jnp.dot(
            window, weight[:, tap_index, :], preferred_element_type=jnp.float32
        )
    return summed.reshape(size_z, size_x, size_y, weight.shape[2])


def conv_weight_grad(padded, gradient, extent):
    size_z, size_x, size_y = extent
    count_cells = size_z * size_x * size_y
    flat_gradient = gradient.reshape(count_cells, gradient.shape[3])
    pieces = []
    for tap_index in range(27):
        shift_z, shift_x, shift_y = (tap_index // 9, tap_index // 3 % 3, tap_index % 3)
        window = padded[
            shift_z : shift_z + size_z, shift_x : shift_x + size_x, shift_y : shift_y + size_y, :
        ]
        window = window.reshape(count_cells, padded.shape[3])
        pieces.append(
            lax.dot_general(
                window, flat_gradient, (((0,), (0,)), ((), ())), preferred_element_type=jnp.float32
            )
        )
    return jnp.stack(pieces, axis=1)


def conv_input_grad(padded, weight, extent):
    size_z, size_x, size_y = extent
    count_cells = size_z * size_x * size_y
    summed = jnp.zeros((count_cells, weight.shape[0]), jnp.float32)
    for tap_index in range(27):
        shift_z, shift_x, shift_y = (2 - tap_index // 9, 2 - tap_index // 3 % 3, 2 - tap_index % 3)
        window = padded[
            shift_z : shift_z + size_z, shift_x : shift_x + size_x, shift_y : shift_y + size_y, :
        ]
        window = window.reshape(count_cells, padded.shape[3])
        summed = summed + lax.dot_general(
            window,
            weight[:, tap_index, :],
            (((1,), (1,)), ((), ())),
            preferred_element_type=jnp.float32,
        )
    return summed.reshape(size_z, size_x, size_y, weight.shape[0])


def pool_features(fine, kernel):
    size_z, size_x, size_y, channels = fine.shape
    blocks = fine.reshape(size_z // 2, 2, size_x // 2, 2, size_y // 2, 2, channels)
    kernel_cube = kernel.reshape(2, 2, 2, kernel.shape[1], kernel.shape[2])
    return jnp.einsum(
        "zaxbycf,abcfg->zxyg", blocks, kernel_cube, preferred_element_type=jnp.float32
    )


def pool_adjoint(coarse_in, kernel):
    size_z, size_x, size_y, wide_channels = coarse_in.shape
    kernel_cube = kernel.reshape(2, 2, 2, kernel.shape[1], kernel.shape[2])
    result = jnp.einsum(
        "zxyg,abcfg->zaxbycf", coarse_in, kernel_cube, preferred_element_type=jnp.float32
    )
    return result.reshape(2 * size_z, 2 * size_x, 2 * size_y, kernel.shape[1])


def lift_features(coarse_in, kernel):
    size_z, size_x, size_y, wide_channels = coarse_in.shape
    kernel_cube = kernel.reshape(2, 2, 2, kernel.shape[1], kernel.shape[2])
    result = jnp.einsum(
        "zxyg,abcgf->zaxbycf", coarse_in, kernel_cube, preferred_element_type=jnp.float32
    )
    return result.reshape(2 * size_z, 2 * size_x, 2 * size_y, kernel.shape[2])


def lift_adjoint(fine, kernel):
    size_z, size_x, size_y, channels = fine.shape
    blocks = fine.reshape(size_z // 2, 2, size_x // 2, 2, size_y // 2, 2, channels)
    kernel_cube = kernel.reshape(2, 2, 2, kernel.shape[1], kernel.shape[2])
    return jnp.einsum(
        "zaxbycf,abcgf->zxyg", blocks, kernel_cube, preferred_element_type=jnp.float32
    )


def column_body(volume, cotangent, w_conv, w_down, w_bottle, w_up):
    size_z, size_x, size_y, channels = volume.shape
    group_channels = w_bottle.shape[2]
    half_x = size_x // 2
    half_y = size_y // 2
    padded = with_halo(volume, (("gx", 1), ("gy", 2), ("gz", 0)), 1)
    pre_hidden = conv_forward(padded, w_conv, (size_z, size_x, size_y))
    hidden = jax.nn.silu(pre_hidden).astype(jnp.bfloat16)
    hidden_slope = silu_slope(pre_hidden)
    coarse = pool_features(hidden, w_down).astype(jnp.bfloat16)
    stacked = lax.all_gather(coarse, "gz", axis=0, tiled=True)
    rimmed = with_halo(stacked, (("gx", 1), ("gy", 2)), 1)
    column_z = rimmed.shape[0]
    coarse_pad = jnp.pad(rimmed, ((1, 1), (0, 0), (0, 0), (0, 0)))
    pre_bottle = conv_forward(coarse_pad, w_bottle, (column_z, half_x, half_y))
    bottle = jax.nn.silu(pre_bottle).astype(jnp.bfloat16)
    bottle_slope = silu_slope(pre_bottle)
    own_start = lax.axis_index("gz") * group_channels
    own_up = lax.dynamic_slice_in_dim(w_up, own_start, group_channels, 1)
    lifted = lax.psum_scatter(
        lift_features(bottle, own_up).astype(jnp.bfloat16), "gz", scatter_dimension=0, tiled=True
    ).astype(jnp.float32)
    output = (lifted + hidden.astype(jnp.float32)).astype(jnp.bfloat16)
    back_bottle = lift_adjoint(cotangent, w_up).astype(jnp.bfloat16)
    split_grad = lax.all_to_all(back_bottle, "gz", split_axis=3, concat_axis=0, tiled=True)
    bottle_grad = (split_grad.astype(jnp.float32) * bottle_slope).astype(jnp.bfloat16)
    grad_bottle = lax.psum_scatter(
        conv_weight_grad(coarse_pad, bottle_grad, (column_z, half_x, half_y)),
        ("gx", "gy"),
        scatter_dimension=0,
        tiled=True,
    )
    grad_rimmed = with_halo(bottle_grad, (("gx", 1), ("gy", 2)), 1)
    grad_pad = jnp.pad(grad_rimmed, ((1, 1), (0, 0), (0, 0), (0, 0)))
    coarse_grad = lax.psum_scatter(
        conv_input_grad(
            grad_pad, w_bottle, (lax.axis_size("gz") * (size_z // 2), half_x, half_y)
        ).astype(jnp.bfloat16),
        "gz",
        scatter_dimension=0,
        tiled=True,
    )
    hidden_grad = (
        (pool_adjoint(coarse_grad, w_down) + cotangent.astype(jnp.float32)) * hidden_slope
    ).astype(jnp.bfloat16)
    full_term = conv_weight_grad(padded, hidden_grad, (size_z, size_x, size_y))
    depth_summed = lax.psum(full_term.astype(jnp.bfloat16), "gz").astype(jnp.float32)
    grad_conv = lax.psum_scatter(depth_summed, ("gx", "gy"), scatter_dimension=0, tiled=True)
    return (output, grad_conv, grad_bottle)


def fits_one_plane(counts, brick, wide):
    count_p = counts[0] * counts[1]
    size_z, size_x, size_y, channels = brick
    return (
        counts == (2, 4, 4)
        and count_p * (size_x // 2) * (size_y // 2) == 128
        and wide // count_p == 64
        and (size_z, size_x, size_y, channels) == (8, 8, 8, 128)
    )


def solution(mesh):
    in_specs = (
        P("gz", "gx", "gy", None),
        P("gz", "gx", "gy", None),
        P(),
        P(),
        P(None, None, "gz"),
        P(),
    )
    out_specs = (
        P("gz", "gx", "gy", None),
        P(("gx", "gy"), None, None),
        P(("gx", "gy"), None, "gz"),
    )
    counts = (mesh.shape["gx"], mesh.shape["gy"], mesh.shape["gz"])

    def body(volume, cotangent, w_conv, w_down, w_bottle, w_up):
        if fits_one_plane(counts, volume.shape, w_down.shape[2]):
            return gathered_body(counts, volume, cotangent, w_conv, w_down, w_bottle, w_up)
        return column_body(volume, cotangent, w_conv, w_down, w_bottle, w_up)

    return jax.shard_map(body, mesh=mesh, in_specs=in_specs, out_specs=out_specs, check_vma=False)
```

```python
import numpy as np
import jax
import jax.numpy as jnp
from jax import lax
from jax.experimental import pallas as pl
from jax.experimental.pallas import tpu as pltpu
from jax.sharding import PartitionSpec as P

BF16 = jnp.bfloat16
F32 = jnp.float32
VMEM_LIMIT = 24 * 1024 * 1024


def local_call(kernel, name, out_shapes, scratch=(), flops=1_000_000_000):
    whole = pl.BlockSpec(memory_space=pltpu.VMEM)

    def call(*operands):
        return pl.pallas_call(
            kernel,
            name=name,
            out_shape=out_shapes,
            in_specs=[whole] * len(operands),
            out_specs=jax.tree.map(lambda _: whole, out_shapes),
            scratch_shapes=list(scratch),
            compiler_params=pltpu.CompilerParams(vmem_limit_bytes=VMEM_LIMIT),
            cost_estimate=pl.CostEstimate(flops=flops, bytes_accessed=flops // 1000, transcendentals=0),
        )(*operands)

    return call


def matmul(left, right):
    return jnp.dot(left, right, preferred_element_type=F32)


def matmul_nt(left, right):
    return lax.dot_general(left, right, (((1,), (1,)), ((), ())), preferred_element_type=F32)


def sub_order(size_x, size_y):
    half_x, half_y = size_x // 2, size_y // 2
    return {
        (2 * kx + b, 2 * ky + c): ((2 * b + c) * half_x + kx) * half_y + ky
        for b in range(2)
        for c in range(2)
        for kx in range(half_x)
        for ky in range(half_y)
    }


def fine_maps(size_x, size_y):
    own = size_x * size_y
    rows = sub_order(size_x, size_y)
    order = np.zeros((own, own), np.float32)
    taps = np.zeros((9, own, 2 * own), np.float32)
    for (x, y), row in rows.items():
        order[row, x * size_y + y] = 1
        for b in range(3):
            for c in range(3):
                sx, sy = x + b - 1, y + c - 1
                if sx < 0:
                    part = 0 if 0 <= sy < size_y else (4 if sy < 0 else 5)
                    source = own + 8 * part + sy % size_y
                elif sx >= size_x:
                    part = 1 if 0 <= sy < size_y else (6 if sy < 0 else 7)
                    source = own + 8 * part + sy % size_y
                elif sy < 0:
                    source = own + 16 + sx
                elif sy >= size_y:
                    source = own + 24 + sx
                else:
                    source = sx * size_y + sy
                taps[3 * b + c, row, source] = 1
    return order, taps


def coarse_maps(count_x, count_y, half_x, half_y):
    wide_x, wide_y = count_x * half_x, count_y * half_y

    def row_of(x, y):
        brick = (x // half_x) * count_y + y // half_y
        return (brick * half_x + x % half_x) * half_y + y % half_y

    shift = np.zeros((9, wide_x * wide_y, wide_x * wide_y), np.float32)
    for x in range(wide_x):
        for y in range(wide_y):
            for b in range(3):
                for c in range(3):
                    sx, sy = x + b - 1, y + c - 1
                    if 0 <= sx < wide_x and 0 <= sy < wide_y:
                        shift[3 * b + c, row_of(x, y), row_of(sx, sy)] = 1
    return shift


def column_maps(half_x, half_y, depth):
    quarter = half_x * half_y
    rows = depth * quarter
    x_out = np.zeros((2, depth * half_y, rows), np.float32)
    y_out = np.zeros((2, depth * (half_x + 1), rows + depth * half_y), np.float32)
    rim = np.zeros((2, 9, 4, quarter, 8 * quarter), np.float32)
    for z in range(depth):
        for ky in range(half_y):
            x_out[0, z * half_y + ky, z * quarter + (half_x - 1) * half_y + ky] = 1
            x_out[1, z * half_y + ky, z * quarter + ky] = 1
        for side, ky in enumerate((0, half_y - 1)):
            for kx in range(half_x):
                y_out[side, z * half_x + kx, z * quarter + kx * half_y + ky] = 1
            y_out[side, depth * half_x + z, rows + z * half_y + ky] = 1
    for px in range(2):
        for b in range(3):
            for c in range(3):
                for kx in range(half_x):
                    for ky in range(half_y):
                        sx, sy = kx + b - 1, ky + c - 1
                        beyond = sx < 0 if px else sx >= half_x
                        if (sx < 0 or sx >= half_x) and not beyond:
                            continue
                        for z in range(4):
                            if beyond and 0 <= sy < half_y:
                                source = 4 * quarter + z * half_y + sy
                            elif beyond:
                                source = 7 * quarter + 4 * (sy >= half_y) + z
                            elif sy < 0:
                                source = 5 * quarter + z * half_x + sx
                            elif sy >= half_y:
                                source = 6 * quarter + z * half_x + sx
                            else:
                                source = z * quarter + sx * half_y + sy
                            rim[px, 3 * b + c, z, kx * half_y + ky, source] = 1
    return x_out, y_out, rim


def swap(block, axes, count, distance):
    return lax.ppermute(block, axes, [(i, i ^ distance) for i in range(count)])


def trade(blocks, axes, count):
    got = {d: swap(blocks[d], axes, count, d) for d in reversed(range(1, count))}
    return [blocks[0]] + [got[d] for d in range(1, count)]


def swap_lines(pair_a, pair_b, axis):
    length = lax.axis_size(axis)
    first = [(i, i ^ 1) for i in range(length)]
    second = [(i, i + 1 if i % 2 else i - 1) for i in range(1, length - 1)]
    return lax.ppermute(pair_a, axis, first), lax.ppermute(pair_b, axis, second)


def line_sides(axis, pair_a, pair_b):
    even = lax.axis_index(axis) % 2 == 0
    return jnp.where(even, pair_b, pair_a), jnp.where(even, pair_a, pair_b)


def plane_index(count_y):
    return lax.axis_index("gx") * count_y + lax.axis_index("gy")


def plane_rows(ref, z):
    _, size_x, size_y, channels = ref.shape
    return ref[z].astype(F32).reshape(size_x * size_y, channels)


def hand_out(blocks, outs, me):
    for d, out in enumerate(outs):
        out[...] = blocks[me ^ d]


def take_in(parts, blocks, me):
    for d, part in enumerate(parts):
        blocks[me ^ d] = part[...]


def total_of(parts):
    terms = [part[...].astype(F32) for part in parts]
    while len(terms) > 1:
        terms = [terms[i] + terms[i + 1] for i in range(0, len(terms), 2)]
    return terms[0]


def back_kernel(count_z, cotangent, w_up, order, *refs):
    sends, (ordered, blocks) = refs[:count_z], refs[count_z:]
    size_z, size_x, size_y, channels = cotangent.shape
    own = size_x * size_y
    quarter = own // 4
    for z in range(size_z):
        ordered[z] = matmul(order[...], plane_rows(cotangent, z).astype(BF16)).astype(BF16)
    back = None
    for s in range(8):
        a, bc = s // 4, s % 4
        cells = jnp.concatenate(
            [ordered[2 * kz + a, bc * quarter : (bc + 1) * quarter, :] for kz in range(size_z // 2)], axis=0
        )
        term = matmul_nt(cells, w_up[s])
        back = term if back is None else back + term
    back = back.astype(BF16)
    group = back.shape[1] // count_z
    for q in range(count_z):
        blocks[q] = back[:, q * group : (q + 1) * group]
    hand_out(blocks, sends, lax.axis_index("gz"))


def deepen(volume, z_a, z_b, deep, pitch):
    size_z, size_x, size_y, channels = volume.shape
    own = size_x * size_y
    below, above = line_sides("gz", z_a[...], z_b[...])
    deep[:own, :] = below.astype(F32).reshape(own, channels)
    for z in range(size_z):
        deep[(z + 1) * pitch : (z + 1) * pitch + own, :] = plane_rows(volume, z)
    deep[(size_z + 1) * pitch : (size_z + 1) * pitch + own, :] = above.astype(F32).reshape(own, channels)


def x_face_kernel(volume, z_a, z_b, x_send, deep):
    size_z, size_x, size_y, channels = volume.shape
    own = size_x * size_y
    deepen(volume, z_a, z_b, deep, own)
    edge = jnp.where(lax.axis_index("gx") == 0, size_x - 1, 0)
    for z in range(size_z + 2):
        start = pl.multiple_of(z * own + edge * size_y, size_y)
        rows = deep[pl.ds(start, size_y), :]
        deep[z * size_y : (z + 1) * size_y, :] = rows
    x_send[...] = deep[: x_send.shape[0], :].astype(BF16)


def y_face_kernel(volume, z_a, z_b, x_rim, send_a, send_b, deep, side):
    size_z, size_x, size_y, channels = volume.shape
    planes = size_z + 2
    deepen(volume, z_a, z_b, deep, size_x * size_y)
    side[: planes * size_y, :] = x_rim[...].astype(F32)
    side[planes * size_y :, :] = jnp.zeros((side.shape[0] - planes * size_y, channels), F32)
    lines = send_a.shape[0] - planes * size_x

    def face(y):
        return jnp.concatenate(
            [deep[pl.ds(y, planes * size_x, stride=size_y), :], side[pl.ds(y, lines, stride=size_y), :]], axis=0
        ).astype(BF16)

    send_b[...], send_a[...] = line_sides("gy", face(size_y - 1), face(0))


def hidden_kernel(count_z, volume, z_a, z_b, x_rim, y_a, y_b, taps, w_conv, w_down, *refs):
    backs, (hidden, slope, rim), sends, (rim32, cells) = (
        refs[:count_z],
        refs[count_z : count_z + 3],
        refs[count_z + 3 : -2],
        refs[-2:],
    )
    size_z, size_x, size_y, channels = volume.shape
    own = size_x * size_y
    quarter = own // 4
    planes = size_z + 2
    pitch = 2 * own
    first = lax.axis_index("gx") == 0
    deepen(volume, z_a, z_b, rim32, pitch)
    y_low, y_high = (block.astype(F32) for block in line_sides("gy", y_a[...], y_b[...]))
    x_side = x_rim[...].astype(F32)
    x_low, x_high = jnp.where(first, 0.0, x_side), jnp.where(first, x_side, 0.0)
    faces = (x_low, x_high, y_low, y_high)
    for z in range(planes):
        for part, block in enumerate(faces):
            start = z * pitch + own + 8 * part
            rim32[start : start + 8, :] = block[8 * z : 8 * (z + 1), :]
        rim32[z * pitch + own + 32 : (z + 1) * pitch, :] = jnp.zeros((own - 32, channels), F32)
    for part, (block, row, low) in enumerate(((y_low, 7, True), (y_high, 0, True), (y_low, 7, False), (y_high, 0, False))):
        corner = block[planes * size_x : planes * size_x + 8, :]
        rest = block[planes * size_x + 8 : planes * size_x + 16, :]
        start = own + 32 + 8 * part + row
        rim32[pl.ds(start, 8, stride=pitch), :] = jnp.where(first == low, 0.0, corner)
        for z in range(8, planes):
            rim32[z * pitch + start : z * pitch + start + 1, :] = jnp.where(first == low, 0.0, rest[z - 8 : z - 7, :])
    for z in range(planes):
        rows = rim32[z * pitch : (z + 1) * pitch, :].astype(BF16)
        rim[z] = rows
        moved = matmul(taps[...], rows).astype(BF16)
        for bc in range(9):
            cells[z, :, bc * channels : (bc + 1) * channels] = moved[bc * own : (bc + 1) * own, :]
    pre = None
    for a in range(3):
        window = cells[a : a + size_z].reshape(size_z * own, 9 * channels)
        weight = w_conv[9 * a : 9 * (a + 1)].reshape(9 * channels, channels)
        term = matmul(window, weight)
        pre = term if pre is None else pre + term
    sig = jax.nn.sigmoid(pre)
    slope[...] = (sig * (1.0 + pre * (1.0 - sig))).reshape(size_z, own, channels)
    hidden[...] = (pre * sig).astype(BF16).reshape(size_z, own, channels)
    parts = []
    for s in range(8):
        a, bc = s // 4, s % 4
        parts.append(
            jnp.concatenate(
                [hidden[2 * kz + a, bc * quarter : (bc + 1) * quarter, :] for kz in range(size_z // 2)], axis=0
            )
        )
    coarse = matmul(jnp.concatenate(parts, axis=1), w_down[...].reshape(8 * channels, w_down.shape[2]))
    coarse = coarse.astype(BF16)
    wide = coarse.shape[1]
    for send, back in zip(sends, backs):
        send[:, :wide] = coarse
        send[:, wide:] = back[...]


def rim_transpose_kernel(rim, taps_t, turned):
    planes, rows, channels = rim.shape
    for pair in range(planes // 2):
        sides = [rim[2 * pair + i].astype(F32).T for i in range(2)]
        moved = matmul(jnp.concatenate(sides, axis=1).astype(BF16), taps_t[...]).astype(BF16)
        for bc in range(9):
            turned[bc * channels : (bc + 1) * channels, pair * rows : (pair + 1) * rows] = moved[
                :, bc * rows : (bc + 1) * rows
            ]


def column_kernel(count_z, *refs):
    parts, x_out, (column, back, x_send) = refs[:count_z], refs[count_z], refs[count_z + 1 :]
    own_cells = parts[0].shape[0]
    wide = column.shape[1]
    pz = lax.axis_index("gz")
    for d, part in enumerate(parts):
        rows = pl.ds(pl.multiple_of((pz ^ d) * own_cells, own_cells), own_cells)
        column[rows, :] = part[:, :wide]
        back[rows, :] = part[:, wide:]
    x_send[...] = matmul(x_out[lax.axis_index("gx")], column[...]).astype(BF16)


def column_face_kernel(column, x_rim, y_out, send_a, send_b):
    rows = jnp.concatenate([column[...], x_rim[...]], axis=0)
    low, high = (matmul(y_out[side], rows).astype(BF16) for side in range(2))
    send_b[...], send_a[...] = line_sides("gy", high, low)


def bottle_kernel(count_y, column, back, x_rim, y_a, y_b, shift, w_bottle, *refs):
    bottle, sends, (rim32, window, slices) = refs[0], refs[1:-3], refs[-3:]
    cells, wide = column.shape
    outs = w_bottle.shape[2]
    side = x_rim.shape[0]
    depth = y_a.shape[0] - side
    quarter = cells // depth
    span = 4 * quarter
    picks = shift[lax.axis_index("gx")]
    window[:quarter, :] = jnp.zeros((quarter, 9 * wide), BF16)
    window[(depth + 1) * quarter :, :] = jnp.zeros((quarter, 9 * wide), BF16)
    edge = side // (depth // 4)
    y_low, y_high = (block.astype(F32) for block in line_sides("gy", y_a[...], y_b[...]))
    for g in range(depth // 4):
        rim32[g, :span, :] = column[g * span : (g + 1) * span, :].astype(F32)
        for part, block in enumerate((x_rim, y_low, y_high)):
            start = span + part * edge
            rim32[g, start : start + edge, :] = block[g * edge : (g + 1) * edge, :].astype(F32)
        start = span + 3 * edge
        rim32[g, start : start + 4, :] = y_low[side + 4 * g : side + 4 * g + 4, :]
        rim32[g, start + 4 : start + 8, :] = y_high[side + 4 * g : side + 4 * g + 4, :]
        rim32[g, start + 8 :, :] = jnp.zeros((rim32.shape[1] - start - 8, wide), F32)
        moved = matmul(picks, rim32[g].astype(BF16)).astype(BF16)
        for bc in range(9):
            window[quarter + g * span : quarter + (g + 1) * span, bc * wide : (bc + 1) * wide] = moved[
                bc * span : (bc + 1) * span, :
            ]
    pre = None
    for a in range(3):
        term = matmul(
            window[a * quarter : a * quarter + cells, :], w_bottle[9 * a : 9 * (a + 1)].reshape(9 * wide, outs)
        )
        pre = term if pre is None else pre + term
    sig = jax.nn.sigmoid(pre)
    bottle[...] = (pre * sig).astype(BF16)
    slope = sig * (1.0 + pre * (1.0 - sig))
    grad = (back[...].astype(F32) * slope).astype(BF16)
    p = plane_index(count_y)
    half = span // 2
    lane = lax.broadcasted_iota(jnp.int32, (half, 128), 1)
    for pair in range(wide // 128):
        for g in range(depth // 4):
            top = column[g * span : g * span + half, pair * 128 : (pair + 1) * 128].astype(F32)
            end = column[g * span + half : (g + 1) * span, pair * 128 : (pair + 1) * 128].astype(F32)
            rows = slice(g * half, (g + 1) * half)
            slices[2 * pair, rows, :] = jnp.where(lane < 64, top, pltpu.roll(end, 64, 1)).astype(BF16)
            slices[2 * pair + 1, rows, :] = jnp.where(lane < 64, pltpu.roll(top, 64, 1), end).astype(BF16)
    middle = cells + slices.shape[1]
    for i, send in enumerate(sends):
        send[:cells, :] = grad
        send[cells:middle, :] = slices[p ^ (2 * i)]
        send[middle:, :] = slices[p ^ (2 * i + 1)]


def coarse_grad_kernel(count_y, count_z, quarter, *refs):
    grads, (bottle, shift, w_bottle) = refs[: -count_z - 6], refs[-count_z - 6 : -count_z - 3]
    sends, (window, gathered, blocks) = refs[-count_z - 3 : -3], refs[-3:]
    count_p = len(grads)
    cells, outs = bottle.shape
    rows = count_p * quarter
    depth = cells // quarter
    own_cells = cells // count_z
    inputs = w_bottle.shape[1]
    p = plane_index(count_y)
    for d, part in enumerate(grads):
        gathered[p ^ d] = part[:cells, :]
    mine = pl.multiple_of(p * quarter, quarter)
    picks = jnp.concatenate([shift[pl.ds((8 - bc) * rows + mine, quarter), :] for bc in range(9)], axis=0)
    window[:quarter, :] = jnp.zeros((quarter, 9 * outs), BF16)
    window[(depth + 1) * quarter :, :] = jnp.zeros((quarter, 9 * outs), BF16)
    for z in range(depth):
        plane = jnp.concatenate([gathered[q, z * quarter : (z + 1) * quarter, :] for q in range(count_p)], axis=0)
        moved = matmul(picks, plane).astype(BF16)
        for bc in range(9):
            window[(z + 1) * quarter : (z + 2) * quarter, bc * outs : (bc + 1) * outs] = moved[
                bc * quarter : (bc + 1) * quarter, :
            ]
    total = None
    for a in range(3):
        for bc in range(9):
            term = matmul_nt(
                window[(2 - a) * quarter : (2 - a + depth) * quarter, bc * outs : (bc + 1) * outs],
                w_bottle[9 * a + bc],
            )
            total = term if total is None else total + term
    total = total.astype(BF16)
    for q in range(count_z):
        blocks[q, :, :inputs] = total[q * own_cells : (q + 1) * own_cells, :]
        blocks[q, :, inputs:] = bottle[q * own_cells : (q + 1) * own_cells, :]
    hand_out(blocks, sends, lax.axis_index("gz"))


def grad_bottle_kernel(count_y, shift, *refs):
    parts, (out, turned, wide, grads, slices) = refs[:-5], refs[-5:]
    count_p, cells, outs = grads.shape
    lines = slices.shape[1]
    rows = shift.shape[1]
    quarter = rows // count_p
    depth = cells // quarter
    channels = out.shape[1]
    p = plane_index(count_y)
    for d, part in enumerate(parts):
        start = cells + d % 2 * lines
        grads[p ^ d] = part[:cells, :]
        slices[p ^ d] = part[start : start + lines, :]
    wide[...] = jnp.zeros_like(wide)
    planes = [
        jnp.concatenate([grads[q, z * quarter : (z + 1) * quarter, :] for q in range(count_p)], axis=0)
        for z in range(depth)
    ]
    for j in range(depth // 2):
        plane = jnp.concatenate([slices[q, j * quarter : (j + 1) * quarter, :] for q in range(count_p)], axis=0)
        plane = plane.astype(F32).T.astype(BF16)
        for bc in range(9):
            turned[bc * 128 : (bc + 1) * 128, j * rows : (j + 1) * rows] = matmul(
                plane, shift[(8 - bc) * rows : (9 - bc) * rows, :]
            ).astype(BF16)
        for slot in range(5):
            z = j // 2 * 4 + j % 2 + slot - 1
            if 0 <= z < depth:
                wide[j * rows : (j + 1) * rows, slot * outs : (slot + 1) * outs] = planes[z]
    full = matmul(turned[...], wide[...])
    for bc in range(9):
        top = full[bc * 128 : bc * 128 + channels, :]
        end = full[bc * 128 + channels : (bc + 1) * 128, :]
        for a in range(3):
            out[9 * a + bc] = top[:, (2 - a) * outs : (3 - a) * outs] + end[:, (4 - a) * outs : (5 - a) * outs]


def hidden_grad_kernel(count_y, count_z, *refs):
    parts, (hidden, slope, ordered, w_up, w_down, turned, order_t) = refs[:count_z], refs[count_z : count_z + 7]
    output, keep, give, (shifted, rows_out, bottles, blocks) = *refs[count_z + 7 : count_z + 10], refs[-4:]
    count_p = blocks.shape[0]
    size_z, own, channels = hidden.shape
    quarter = own // 4
    inputs = w_down.shape[2]
    pz = lax.axis_index("gz")
    grad = parts[0][:, :inputs].astype(F32)
    for part in parts[1:]:
        grad = grad + part[:, :inputs].astype(F32)
    grad = grad.astype(BF16)
    for d, part in enumerate(parts):
        bottles[pz ^ d] = part[:, inputs:]
    bottle = jnp.concatenate([bottles[q] for q in range(count_z)], axis=1)
    shifted[...] = jnp.zeros_like(shifted)
    for s in range(8):
        a, bc = s // 4, s % 4
        lifted = matmul(bottle, w_up[s])
        spread_grad = matmul_nt(grad, w_down[s])
        for kz in range(size_z // 2):
            z = 2 * kz + a
            part = slice(bc * quarter, (bc + 1) * quarter)
            line = slice(kz * quarter, (kz + 1) * quarter)
            rows_out[z, part, :] = (lifted[line, :] + hidden[z, part, :].astype(F32)).astype(BF16)
            value = ((spread_grad[line, :] + ordered[z, part, :].astype(F32)) * slope[z, part, :]).astype(BF16)
            for t in range(3):
                start = (z + t) * own + bc * quarter
                shifted[start : start + quarter, t * channels : (t + 1) * channels] = value
    for z in range(size_z):
        plane = matmul(order_t[...], rows_out[z])
        output[z] = plane.reshape(output.shape[1:]).astype(BF16)
    full = matmul(turned[...], shifted[...])
    group = channels // count_p
    for bc in range(9):
        for a in range(3):
            t = 9 * a + bc
            block = full[bc * channels : (bc + 1) * channels, a * channels : (a + 1) * channels].astype(BF16)
            for p in range(count_p):
                blocks[p, t * group : (t + 1) * group, :] = block[p * group : (p + 1) * group, :]
    p = plane_index(count_y)
    for i in range(count_p // 2):
        keep[i] = blocks[p ^ (2 * i)]
        give[i] = blocks[p ^ (2 * i + 1)]


def pair_sum_kernel(keep, got, *sends):
    for i, send in enumerate(sends):
        send[...] = (keep[i].astype(F32) + got[i].astype(F32)).astype(BF16)


def sum_kernel(*refs):
    out = refs[-1]
    out[...] = total_of(refs[:-1]).reshape(out.shape).astype(out.dtype)


def shape_of(shape, dtype=BF16):
    return jax.ShapeDtypeStruct(shape, dtype)


def gathered_body(counts, volume, cotangent, w_conv, w_down, w_bottle, w_up):
    count_x, count_y, count_z = counts
    count_p = count_x * count_y
    size_z, size_x, size_y, channels = volume.shape
    wide = w_down.shape[2]
    group = w_bottle.shape[2]
    half_x, half_y = size_x // 2, size_y // 2
    own = size_x * size_y
    quarter = half_x * half_y
    own_cells = size_z // 2 * quarter
    cells = count_z * own_cells
    depth = count_z * size_z // 2
    rows = count_p * quarter
    planes = size_z + 2
    share_c = channels // count_p
    share_w = wide // count_p
    plane_axes = ("gx", "gy")

    order, taps = fine_maps(size_x, size_y)
    pair_taps = np.zeros((2, 2 * own, 9, 2, own), np.float32)
    for i in range(2):
        pair_taps[i, :, :, i, :] = taps.transpose(2, 0, 1)
    shift = coarse_maps(count_x, count_y, half_x, half_y)
    order_m = jnp.asarray(order, BF16)
    order_t = jnp.asarray(order.T, BF16)
    taps_m = jnp.asarray(taps.reshape(9 * own, 2 * own), BF16)
    taps_t = jnp.asarray(pair_taps.reshape(4 * own, 18 * own), BF16)
    shift_m = jnp.asarray(shift.reshape(9 * rows, rows), BF16)

    x_out, y_out, rim_maps = column_maps(half_x, half_y, depth)
    x_out = jnp.asarray(x_out, BF16)
    y_out = jnp.asarray(y_out, BF16)
    rim_m = jnp.asarray(rim_maps.reshape(count_x, 36 * quarter, 8 * quarter), BF16)

    w_conv_t = jnp.transpose(w_conv, (1, 0, 2))
    w_bottle_t = jnp.transpose(w_bottle, (1, 0, 2))
    even_z = lax.axis_index("gz") % 2 == 0
    low_z, high_z = volume[0], volume[size_z - 1]
    z_a, z_b = swap_lines(jnp.where(even_z, high_z, low_z), jnp.where(even_z, low_z, high_z), "gz")
    *backs, ordered = local_call(
        lambda *refs: back_kernel(count_z, *refs),
        "back",
        [shape_of((own_cells, group))] * count_z + [shape_of((size_z, own, channels))],
        [pltpu.VMEM((count_z, own_cells, group), BF16)],
    )(cotangent, w_up, order_m)
    x_send = local_call(
        x_face_kernel,
        "x_face",
        shape_of((planes * size_y, channels)),
        [pltpu.VMEM((planes * own, channels), F32)],
    )(volume, z_a, z_b)
    x_rim = swap(x_send, plane_axes, count_p, count_y)
    send_a, send_b = local_call(
        y_face_kernel,
        "y_face",
        [shape_of((planes * size_x + 16, channels))] * 2,
        [pltpu.VMEM((planes * own, channels), F32), pltpu.VMEM((16 * size_y, channels), F32)],
    )(volume, z_a, z_b, x_rim)
    y_a, y_b = swap_lines(send_a, send_b, "gy")
    hidden, slope, rim, *sends = local_call(
        lambda *refs: hidden_kernel(count_z, *refs),
        "hidden",
        [
            shape_of((size_z, own, channels)),
            shape_of((size_z, own, channels), F32),
            shape_of((planes, 2 * own, channels)),
        ]
        + [shape_of((own_cells, wide + group))] * count_z,
        [
            pltpu.VMEM((planes * 2 * own, channels), F32),
            pltpu.VMEM((planes, own, 9 * channels), BF16),
        ],
        flops=2_000_000_000,
    )(volume, z_a, z_b, x_rim, y_a, y_b, taps_m, w_conv_t, w_down, *backs)
    parts = trade(sends, "gz", count_z)
    turned = local_call(
        rim_transpose_kernel,
        "rim_transpose",
        shape_of((9 * channels, planes * own)),
    )(rim, taps_t)
    column, back, x_send = local_call(
        lambda *refs: column_kernel(count_z, *refs),
        "column",
        [shape_of((cells, wide)), shape_of((cells, group)), shape_of((depth * half_y, wide))],
    )(*parts, x_out)
    x_rim = swap(x_send, plane_axes, count_p, count_y)
    send_a, send_b = local_call(
        column_face_kernel,
        "column_face",
        [shape_of((depth * (half_x + 1), wide))] * 2,
    )(column, x_rim, y_out)
    y_a, y_b = swap_lines(send_a, send_b, "gy")
    bottle, *sends = local_call(
        lambda *refs: bottle_kernel(count_y, *refs),
        "bottle",
        [shape_of((cells, group))] + [shape_of((2 * cells, group))] * (count_p // 2),
        [
            pltpu.VMEM((depth // 4, 8 * quarter, wide), F32),
            pltpu.VMEM(((depth + 2) * quarter, 9 * wide), BF16),
            pltpu.VMEM((count_p, cells // 2, 128), BF16),
        ],
        flops=2_000_000_000,
    )(column, back, x_rim, y_a, y_b, rim_m, w_bottle_t)
    grads = [None] * count_p
    grads[0] = sends[0]
    for d in (6, 4, 2):
        grads[d] = swap(sends[d // 2], plane_axes, count_p, d)
    for d in (0, 2, 4, 6):
        grads[d + 1] = swap(grads[d], plane_axes, count_p, 1)
    sends = local_call(
        lambda *refs: coarse_grad_kernel(count_y, count_z, quarter, *refs),
        "coarse_grad",
        [shape_of((own_cells, wide + group))] * count_z,
        [
            pltpu.VMEM(((depth + 2) * quarter, 9 * group), BF16),
            pltpu.VMEM((count_p, cells, group), BF16),
            pltpu.VMEM((count_z, own_cells, wide + group), BF16),
        ],
    )(*grads, bottle, shift_m, w_bottle_t)
    parts = trade(sends, "gz", count_z)
    output, keep, give = local_call(
        lambda *refs: hidden_grad_kernel(count_y, count_z, *refs),
        "hidden_grad",
        [shape_of(volume.shape)] + [shape_of((count_p // 2, 27 * share_c, channels))] * 2,
        [
            pltpu.VMEM((planes * own, 3 * channels), BF16),
            pltpu.VMEM((size_z, own, channels), BF16),
            pltpu.VMEM((count_z, own_cells, group), BF16),
            pltpu.VMEM((count_p, 27 * share_c, channels), BF16),
        ],
    )(*parts, hidden, slope, ordered, w_up, w_down, turned, order_t)
    got = swap(give, plane_axes, count_p, 1)
    sends = local_call(
        pair_sum_kernel,
        "pair_sum",
        [shape_of((27 * share_c, channels))] * (count_p // 2),
    )(keep, got)
    parts = [sends[0]] + [swap(sends[d // 2], plane_axes, count_p, d) for d in (6, 4, 2)]
    part = local_call(sum_kernel, "plane_sum", shape_of((27 * share_c, channels)))(*parts)
    got = swap(part, "gz", count_z, 1)
    part = local_call(sum_kernel, "depth_sum", shape_of((27 * share_c, channels)))(part, got)
    got = swap(part, "gz", count_z, 2)
    grad_bottle = local_call(
        lambda *refs: grad_bottle_kernel(count_y, *refs),
        "grad_bottle",
        shape_of((27, share_w, group), F32),
        [
            pltpu.VMEM((18 * share_w, depth // 2 * rows), BF16),
            pltpu.VMEM((depth // 2 * rows, 5 * group), BF16),
            pltpu.VMEM((count_p, cells, group), BF16),
            pltpu.VMEM((count_p, cells // 2, 128), BF16),
        ],
        flops=4_000_000_000,
    )(shift_m, *grads)
    grad_conv = local_call(
        sum_kernel,
        "grad_conv",
        shape_of((27, share_c, channels), F32),
    )(part, got)
    return (output, jnp.transpose(grad_conv, (1, 0, 2)), jnp.transpose(grad_bottle, (1, 0, 2)))


def with_halo(cells, sides, width):
    for axis, dim in sides:
        count = lax.axis_size(axis)
        ends = count - 1
        head = lax.slice_in_dim(cells, 0, width, axis=dim)
        tail = lax.slice_in_dim(cells, cells.shape[dim] - width, cells.shape[dim], axis=dim)
        cells = jnp.concatenate(
            [
                lax.ppermute(tail, axis, [(i, (i + 1) % count) for i in range(ends)]),
                cells,
                lax.ppermute(head, axis, [((i + 1) % count, i) for i in range(ends)]),
            ],
            axis=dim,
        )
    return cells


def silu_slope(values):
    sig = jax.nn.sigmoid(values)
    return sig * (1.0 + values * (1.0 - sig))


def conv_forward(padded, weight, extent):
    size_z, size_x, size_y = extent
    count_cells = size_z * size_x * size_y
    summed = jnp.zeros((count_cells, weight.shape[2]), jnp.float32)
    for tap_index in range(27):
        shift_z, shift_x, shift_y = (tap_index // 9, tap_index // 3 % 3, tap_index % 3)
        window = padded[
            shift_z : shift_z + size_z, shift_x : shift_x + size_x, shift_y : shift_y + size_y, :
        ]
        window = window.reshape(count_cells, padded.shape[3])
        summed = summed + jnp.dot(
            window, weight[:, tap_index, :], preferred_element_type=jnp.float32
        )
    return summed.reshape(size_z, size_x, size_y, weight.shape[2])


def conv_weight_grad(padded, gradient, extent):
    size_z, size_x, size_y = extent
    count_cells = size_z * size_x * size_y
    flat_gradient = gradient.reshape(count_cells, gradient.shape[3])
    pieces = []
    for tap_index in range(27):
        shift_z, shift_x, shift_y = (tap_index // 9, tap_index // 3 % 3, tap_index % 3)
        window = padded[
            shift_z : shift_z + size_z, shift_x : shift_x + size_x, shift_y : shift_y + size_y, :
        ]
        window = window.reshape(count_cells, padded.shape[3])
        pieces.append(
            lax.dot_general(
                window, flat_gradient, (((0,), (0,)), ((), ())), preferred_element_type=jnp.float32
            )
        )
    return jnp.stack(pieces, axis=1)


def conv_input_grad(padded, weight, extent):
    size_z, size_x, size_y = extent
    count_cells = size_z * size_x * size_y
    summed = jnp.zeros((count_cells, weight.shape[0]), jnp.float32)
    for tap_index in range(27):
        shift_z, shift_x, shift_y = (2 - tap_index // 9, 2 - tap_index // 3 % 3, 2 - tap_index % 3)
        window = padded[
            shift_z : shift_z + size_z, shift_x : shift_x + size_x, shift_y : shift_y + size_y, :
        ]
        window = window.reshape(count_cells, padded.shape[3])
        summed = summed + lax.dot_general(
            window,
            weight[:, tap_index, :],
            (((1,), (1,)), ((), ())),
            preferred_element_type=jnp.float32,
        )
    return summed.reshape(size_z, size_x, size_y, weight.shape[0])


def pool_features(fine, kernel):
    size_z, size_x, size_y, channels = fine.shape
    blocks = fine.reshape(size_z // 2, 2, size_x // 2, 2, size_y // 2, 2, channels)
    kernel_cube = kernel.reshape(2, 2, 2, kernel.shape[1], kernel.shape[2])
    return jnp.einsum(
        "zaxbycf,abcfg->zxyg", blocks, kernel_cube, preferred_element_type=jnp.float32
    )


def pool_adjoint(coarse_in, kernel):
    size_z, size_x, size_y, wide_channels = coarse_in.shape
    kernel_cube = kernel.reshape(2, 2, 2, kernel.shape[1], kernel.shape[2])
    result = jnp.einsum(
        "zxyg,abcfg->zaxbycf", coarse_in, kernel_cube, preferred_element_type=jnp.float32
    )
    return result.reshape(2 * size_z, 2 * size_x, 2 * size_y, kernel.shape[1])


def lift_features(coarse_in, kernel):
    size_z, size_x, size_y, wide_channels = coarse_in.shape
    kernel_cube = kernel.reshape(2, 2, 2, kernel.shape[1], kernel.shape[2])
    result = jnp.einsum(
        "zxyg,abcgf->zaxbycf", coarse_in, kernel_cube, preferred_element_type=jnp.float32
    )
    return result.reshape(2 * size_z, 2 * size_x, 2 * size_y, kernel.shape[2])


def lift_adjoint(fine, kernel):
    size_z, size_x, size_y, channels = fine.shape
    blocks = fine.reshape(size_z // 2, 2, size_x // 2, 2, size_y // 2, 2, channels)
    kernel_cube = kernel.reshape(2, 2, 2, kernel.shape[1], kernel.shape[2])
    return jnp.einsum(
        "zaxbycf,abcgf->zxyg", blocks, kernel_cube, preferred_element_type=jnp.float32
    )


def column_body(volume, cotangent, w_conv, w_down, w_bottle, w_up):
    size_z, size_x, size_y, channels = volume.shape
    group_channels = w_bottle.shape[2]
    half_x = size_x // 2
    half_y = size_y // 2
    padded = with_halo(volume, (("gx", 1), ("gy", 2), ("gz", 0)), 1)
    pre_hidden = conv_forward(padded, w_conv, (size_z, size_x, size_y))
    hidden = jax.nn.silu(pre_hidden).astype(jnp.bfloat16)
    hidden_slope = silu_slope(pre_hidden)
    coarse = pool_features(hidden, w_down).astype(jnp.bfloat16)
    stacked = lax.all_gather(coarse, "gz", axis=0, tiled=True)
    rimmed = with_halo(stacked, (("gx", 1), ("gy", 2)), 1)
    column_z = rimmed.shape[0]
    coarse_pad = jnp.pad(rimmed, ((1, 1), (0, 0), (0, 0), (0, 0)))
    pre_bottle = conv_forward(coarse_pad, w_bottle, (column_z, half_x, half_y))
    bottle = jax.nn.silu(pre_bottle).astype(jnp.bfloat16)
    bottle_slope = silu_slope(pre_bottle)
    own_start = lax.axis_index("gz") * group_channels
    own_up = lax.dynamic_slice_in_dim(w_up, own_start, group_channels, 1)
    lifted = lax.psum_scatter(
        lift_features(bottle, own_up).astype(jnp.bfloat16), "gz", scatter_dimension=0, tiled=True
    ).astype(jnp.float32)
    output = (lifted + hidden.astype(jnp.float32)).astype(jnp.bfloat16)
    back_bottle = lift_adjoint(cotangent, w_up).astype(jnp.bfloat16)
    split_grad = lax.all_to_all(back_bottle, "gz", split_axis=3, concat_axis=0, tiled=True)
    bottle_grad = (split_grad.astype(jnp.float32) * bottle_slope).astype(jnp.bfloat16)
    grad_bottle = lax.psum_scatter(
        conv_weight_grad(coarse_pad, bottle_grad, (column_z, half_x, half_y)),
        ("gx", "gy"),
        scatter_dimension=0,
        tiled=True,
    )
    grad_rimmed = with_halo(bottle_grad, (("gx", 1), ("gy", 2)), 1)
    grad_pad = jnp.pad(grad_rimmed, ((1, 1), (0, 0), (0, 0), (0, 0)))
    coarse_grad = lax.psum_scatter(
        conv_input_grad(
            grad_pad, w_bottle, (lax.axis_size("gz") * (size_z // 2), half_x, half_y)
        ).astype(jnp.bfloat16),
        "gz",
        scatter_dimension=0,
        tiled=True,
    )
    hidden_grad = (
        (pool_adjoint(coarse_grad, w_down) + cotangent.astype(jnp.float32)) * hidden_slope
    ).astype(jnp.bfloat16)
    full_term = conv_weight_grad(padded, hidden_grad, (size_z, size_x, size_y))
    depth_summed = lax.psum(full_term.astype(jnp.bfloat16), "gz").astype(jnp.float32)
    grad_conv = lax.psum_scatter(depth_summed, ("gx", "gy"), scatter_dimension=0, tiled=True)
    return (output, grad_conv, grad_bottle)


def fits_one_plane(counts, brick, wide):
    count_p = counts[0] * counts[1]
    size_z, size_x, size_y, channels = brick
    return (
        counts == (2, 4, 4)
        and count_p * (size_x // 2) * (size_y // 2) == 128
        and wide // count_p == 64
        and (size_z, size_x, size_y, channels) == (8, 8, 8, 128)
    )


def solution(mesh):
    in_specs = (
        P("gz", "gx", "gy", None),
        P("gz", "gx", "gy", None),
        P(),
        P(),
        P(None, None, "gz"),
        P(),
    )
    out_specs = (
        P("gz", "gx", "gy", None),
        P(("gx", "gy"), None, None),
        P(("gx", "gy"), None, "gz"),
    )
    counts = (mesh.shape["gx"], mesh.shape["gy"], mesh.shape["gz"])

    def body(volume, cotangent, w_conv, w_down, w_bottle, w_up):
        if fits_one_plane(counts, volume.shape, w_down.shape[2]):
            return gathered_body(counts, volume, cotangent, w_conv, w_down, w_bottle, w_up)
        return column_body(volume, cotangent, w_conv, w_down, w_bottle, w_up)

    return jax.shard_map(body, mesh=mesh, in_specs=in_specs, out_specs=out_specs, check_vma=False)
```

```python
import numpy as np
import jax
import jax.numpy as jnp
from jax import lax
from jax.experimental import pallas as pl
from jax.experimental.pallas import tpu as pltpu
from jax.sharding import PartitionSpec as P

BF16 = jnp.bfloat16
F32 = jnp.float32
VMEM_LIMIT = 24 * 1024 * 1024


def local_call(kernel, name, out_shapes, scratch=(), flops=1_000_000_000):
    whole = pl.BlockSpec(memory_space=pltpu.VMEM)

    def call(*operands):
        return pl.pallas_call(
            kernel,
            name=name,
            out_shape=out_shapes,
            in_specs=[whole] * len(operands),
            out_specs=jax.tree.map(lambda _: whole, out_shapes),
            scratch_shapes=list(scratch),
            compiler_params=pltpu.CompilerParams(vmem_limit_bytes=VMEM_LIMIT),
            cost_estimate=pl.CostEstimate(flops=flops, bytes_accessed=flops // 1000, transcendentals=0),
        )(*operands)

    return call


def matmul(left, right):
    return jnp.dot(left, right, preferred_element_type=F32)


def matmul_nt(left, right):
    return lax.dot_general(left, right, (((1,), (1,)), ((), ())), preferred_element_type=F32)


def sub_order(size_x, size_y):
    half_x, half_y = size_x // 2, size_y // 2
    return {
        (2 * kx + b, 2 * ky + c): ((2 * b + c) * half_x + kx) * half_y + ky
        for b in range(2)
        for c in range(2)
        for kx in range(half_x)
        for ky in range(half_y)
    }


def fine_maps(size_x, size_y):
    own = size_x * size_y
    rows = sub_order(size_x, size_y)
    order = np.zeros((own, own), np.float32)
    taps = np.zeros((9, own, 2 * own), np.float32)
    for (x, y), row in rows.items():
        order[row, x * size_y + y] = 1
        for b in range(3):
            for c in range(3):
                sx, sy = x + b - 1, y + c - 1
                if sx < 0:
                    part = 0 if 0 <= sy < size_y else (4 if sy < 0 else 5)
                    source = own + 8 * part + sy % size_y
                elif sx >= size_x:
                    part = 1 if 0 <= sy < size_y else (6 if sy < 0 else 7)
                    source = own + 8 * part + sy % size_y
                elif sy < 0:
                    source = own + 16 + sx
                elif sy >= size_y:
                    source = own + 24 + sx
                else:
                    source = sx * size_y + sy
                taps[3 * b + c, row, source] = 1
    return order, taps


def coarse_maps(count_x, count_y, half_x, half_y):
    wide_x, wide_y = count_x * half_x, count_y * half_y

    def row_of(x, y):
        brick = (x // half_x) * count_y + y // half_y
        return (brick * half_x + x % half_x) * half_y + y % half_y

    shift = np.zeros((9, wide_x * wide_y, wide_x * wide_y), np.float32)
    for x in range(wide_x):
        for y in range(wide_y):
            for b in range(3):
                for c in range(3):
                    sx, sy = x + b - 1, y + c - 1
                    if 0 <= sx < wide_x and 0 <= sy < wide_y:
                        shift[3 * b + c, row_of(x, y), row_of(sx, sy)] = 1
    return shift


def column_maps(half_x, half_y, depth):
    quarter = half_x * half_y
    rows = depth * quarter
    send = np.zeros((2, depth * (half_y + 2 * half_x + 2), rows), np.float32)
    rim = np.zeros((2, 9, 4, quarter, 8 * quarter), np.float32)
    for px in range(2):
        out_x = 0 if px else half_x - 1
        for z in range(depth):
            base = z * quarter
            for ky in range(half_y):
                send[px, z * half_y + ky, base + out_x * half_y + ky] = 1
            for side, ky in enumerate((0, half_y - 1)):
                row = depth * (half_y + side * half_x) + z * half_x
                for kx in range(half_x):
                    send[px, row + kx, base + kx * half_y + ky] = 1
                row = depth * (half_y + 2 * half_x + side) + z
                send[px, row, base + out_x * half_y + ky] = 1
    for px in range(2):
        for b in range(3):
            for c in range(3):
                for kx in range(half_x):
                    for ky in range(half_y):
                        sx, sy = kx + b - 1, ky + c - 1
                        beyond = sx < 0 if px else sx >= half_x
                        if (sx < 0 or sx >= half_x) and not beyond:
                            continue
                        for z in range(4):
                            if beyond and 0 <= sy < half_y:
                                source = 4 * quarter + z * half_y + sy
                            elif beyond:
                                source = 7 * quarter + 4 * (sy >= half_y) + z
                            elif sy < 0:
                                source = 5 * quarter + z * half_x + sx
                            elif sy >= half_y:
                                source = 6 * quarter + z * half_x + sx
                            else:
                                source = z * quarter + sx * half_y + sy
                            rim[px, 3 * b + c, z, kx * half_y + ky, source] = 1
    return send, rim


def swap(block, axes, count, distance):
    return lax.ppermute(block, axes, [(i, i ^ distance) for i in range(count)])


def trade(blocks, axes, count):
    got = {d: swap(blocks[d], axes, count, d) for d in reversed(range(1, count))}
    return [blocks[0]] + [got[d] for d in range(1, count)]


def line_pairs(length):
    first = [(i, i ^ 1) for i in range(length)]
    second = [(i, i + 1 if i % 2 else i - 1) for i in range(1, length - 1)]
    return first, second


def swap_rims(x_send, sends, corners, counts):
    count_x, count_y, _ = counts
    axes = ("gx", "gy")
    pairs = line_pairs(count_y)
    straight = [[(x * count_y + i, x * count_y + j) for x in range(count_x) for i, j in pair] for pair in pairs]
    across = [[(x * count_y + i, (x ^ 1) * count_y + j) for x in range(count_x) for i, j in pair] for pair in pairs]
    corner_b = lax.ppermute(corners[1], axes, across[1])
    corner_a = lax.ppermute(corners[0], axes, across[0])
    x_rim = swap(x_send, axes, count_x * count_y, count_y)
    face_b = lax.ppermute(sends[1], axes, straight[1])
    face_a = lax.ppermute(sends[0], axes, straight[0])
    return x_rim, face_a, face_b, corner_a, corner_b


def line_sides(axis, pair_a, pair_b):
    even = lax.axis_index(axis) % 2 == 0
    return jnp.where(even, pair_b, pair_a), jnp.where(even, pair_a, pair_b)


def plane_index(count_y):
    return lax.axis_index("gx") * count_y + lax.axis_index("gy")


def plane_rows(ref, z):
    _, size_x, size_y, channels = ref.shape
    return ref[z].astype(F32).reshape(size_x * size_y, channels)


def hand_out(blocks, outs, me):
    for d, out in enumerate(outs):
        out[...] = blocks[me ^ d]


def take_in(parts, blocks, me):
    for d, part in enumerate(parts):
        blocks[me ^ d] = part[...]


def total_of(parts):
    terms = [part[...].astype(F32) for part in parts]
    while len(terms) > 1:
        terms = [terms[i] + terms[i + 1] for i in range(0, len(terms), 2)]
    return terms[0]


def back_kernel(count_z, cotangent, w_up, order, *refs):
    sends, (ordered, blocks) = refs[:count_z], refs[count_z:]
    size_z, size_x, size_y, channels = cotangent.shape
    own = size_x * size_y
    quarter = own // 4
    for z in range(size_z):
        ordered[z] = matmul(order[...], plane_rows(cotangent, z).astype(BF16)).astype(BF16)
    back = None
    for s in range(8):
        a, bc = s // 4, s % 4
        cells = jnp.concatenate(
            [ordered[2 * kz + a, bc * quarter : (bc + 1) * quarter, :] for kz in range(size_z // 2)], axis=0
        )
        term = matmul_nt(cells, w_up[s])
        back = term if back is None else back + term
    back = back.astype(BF16)
    group = back.shape[1] // count_z
    for q in range(count_z):
        blocks[q] = back[:, q * group : (q + 1) * group]
    hand_out(blocks, sends, lax.axis_index("gz"))


def deepen(volume, z_a, z_b, deep, pitch):
    size_z, size_x, size_y, channels = volume.shape
    own = size_x * size_y
    below, above = line_sides("gz", z_a[...], z_b[...])
    deep[:own, :] = below.astype(F32).reshape(own, channels)
    for z in range(size_z):
        deep[(z + 1) * pitch : (z + 1) * pitch + own, :] = plane_rows(volume, z)
    deep[(size_z + 1) * pitch : (size_z + 1) * pitch + own, :] = above.astype(F32).reshape(own, channels)


def ends_kernel(volume, send_a, send_b):
    below, above = volume[0], volume[volume.shape[0] - 1]
    send_b[...], send_a[...] = line_sides("gz", above, below)


def faces_kernel(volume, z_a, z_b, x_send, send_a, send_b, corner_a, corner_b, deep):
    size_z, size_x, size_y, channels = volume.shape
    own = size_x * size_y
    planes = size_z + 2
    deepen(volume, z_a, z_b, deep, own)
    deep[planes * own :, :] = jnp.zeros((deep.shape[0] - planes * own, channels), F32)
    first = lax.axis_index("gx") == 0
    far = (size_x - 1) * size_y

    def x_face(start):
        return jnp.concatenate([deep[z * own + start : z * own + start + size_y, :] for z in range(planes)], axis=0)

    x_send[...] = jnp.where(first, x_face(far), x_face(0)).astype(BF16)
    faces, corners = [], []
    for y in (0, size_y - 1):
        faces.append(deep[pl.ds(y, planes * size_x, stride=size_y), :].astype(BF16))
        ends = [deep[pl.ds(start + y, corner_a.shape[0], stride=own), :] for start in (far, 0)]
        corners.append(jnp.where(first, ends[0], ends[1]).astype(BF16))
    send_b[...], send_a[...] = line_sides("gy", faces[1], faces[0])
    corner_b[...], corner_a[...] = line_sides("gy", corners[1], corners[0])


def hidden_kernel(count_z, volume, z_a, z_b, x_rim, y_a, y_b, xy_a, xy_b, taps, w_conv, w_down, *refs):
    backs, (hidden, slope, rim), sends, (rim32, cells) = (
        refs[:count_z],
        refs[count_z : count_z + 3],
        refs[count_z + 3 : -2],
        refs[-2:],
    )
    size_z, size_x, size_y, channels = volume.shape
    own = size_x * size_y
    quarter = own // 4
    planes = size_z + 2
    pitch = 2 * own
    first = lax.axis_index("gx") == 0
    deepen(volume, z_a, z_b, rim32, pitch)
    y_low, y_high = (block.astype(F32) for block in line_sides("gy", y_a[...], y_b[...]))
    xy_low, xy_high = (block.astype(F32) for block in line_sides("gy", xy_a[...], xy_b[...]))
    x_side = x_rim[...].astype(F32)
    x_low, x_high = jnp.where(first, 0.0, x_side), jnp.where(first, x_side, 0.0)
    faces = (x_low, x_high, y_low, y_high)
    for z in range(planes):
        for part, block in enumerate(faces):
            start = z * pitch + own + 8 * part
            rim32[start : start + 8, :] = block[8 * z : 8 * (z + 1), :]
        rim32[z * pitch + own + 32 : (z + 1) * pitch, :] = jnp.zeros((own - 32, channels), F32)
    corners = ((xy_low, 7, True), (xy_high, 0, True), (xy_low, 7, False), (xy_high, 0, False))
    for part, (block, row, low) in enumerate(corners):
        start = own + 32 + 8 * part + row
        value = jnp.where(first == low, 0.0, block)
        rim32[pl.ds(start, 8, stride=pitch), :] = value[:8, :]
        for z in range(8, planes):
            rim32[z * pitch + start : z * pitch + start + 1, :] = value[z : z + 1, :]
    for z in range(planes):
        rows = rim32[z * pitch : (z + 1) * pitch, :].astype(BF16)
        rim[z] = rows
        moved = matmul(taps[...], rows).astype(BF16)
        for bc in range(9):
            cells[z, :, bc * channels : (bc + 1) * channels] = moved[bc * own : (bc + 1) * own, :]
    pre = None
    for a in range(3):
        window = cells[a : a + size_z].reshape(size_z * own, 9 * channels)
        weight = w_conv[9 * a : 9 * (a + 1)].reshape(9 * channels, channels)
        term = matmul(window, weight)
        pre = term if pre is None else pre + term
    sig = jax.nn.sigmoid(pre)
    slope[...] = (sig * (1.0 + pre * (1.0 - sig))).reshape(size_z, own, channels)
    hidden[...] = (pre * sig).astype(BF16).reshape(size_z, own, channels)
    parts = []
    for s in range(8):
        a, bc = s // 4, s % 4
        parts.append(
            jnp.concatenate(
                [hidden[2 * kz + a, bc * quarter : (bc + 1) * quarter, :] for kz in range(size_z // 2)], axis=0
            )
        )
    coarse = matmul(jnp.concatenate(parts, axis=1), w_down[...].reshape(8 * channels, w_down.shape[2]))
    coarse = coarse.astype(BF16)
    wide = coarse.shape[1]
    for send, back in zip(sends, backs):
        send[:, :wide] = coarse
        send[:, wide:] = back[...]


def rim_transpose_kernel(count_p, rim, taps_t, turned):
    planes, rows, channels = rim.shape
    share = channels // count_p
    for pair in range(planes // 2):
        sides = [rim[2 * pair + i].astype(F32).T for i in range(2)]
        moved = matmul(jnp.concatenate(sides, axis=1).astype(BF16), taps_t[...]).astype(BF16)
        for bc in range(9):
            for p in range(count_p):
                start = (bc * count_p // 2 + p // 2) * share
                turned[p % 2, start : start + share, pair * rows : (pair + 1) * rows] = moved[
                    p * share : (p + 1) * share, bc * rows : (bc + 1) * rows
                ]


def column_kernel(count_z, *refs):
    parts, picks, (column, back, x_send, send_a, send_b, corner_a, corner_b) = (
        refs[:count_z],
        refs[count_z],
        refs[count_z + 1 :],
    )
    own_cells = parts[0].shape[0]
    wide = column.shape[1]
    pz = lax.axis_index("gz")
    for d, part in enumerate(parts):
        rows = pl.ds(pl.multiple_of((pz ^ d) * own_cells, own_cells), own_cells)
        column[rows, :] = part[:, :wide]
        back[rows, :] = part[:, wide:]
    rims = matmul(picks[lax.axis_index("gx")], column[...]).astype(BF16)
    cuts, start = [], 0
    for size in (x_send.shape[0], *[send_a.shape[0]] * 2, *[corner_a.shape[0]] * 2):
        cuts.append(rims[start : start + size, :])
        start += size
    x_send[...] = cuts[0]
    send_b[...], send_a[...] = line_sides("gy", cuts[2], cuts[1])
    corner_b[...], corner_a[...] = line_sides("gy", cuts[4], cuts[3])


def bottle_kernel(count_y, column, back, x_rim, y_a, y_b, xy_a, xy_b, shift, w_bottle, *refs):
    bottle, sends, (rim32, window, slices) = refs[0], refs[1:-3], refs[-3:]
    cells, wide = column.shape
    outs = w_bottle.shape[2]
    side = x_rim.shape[0]
    depth = xy_a.shape[0]
    quarter = cells // depth
    span = 4 * quarter
    picks = shift[lax.axis_index("gx")]
    window[:quarter, :] = jnp.zeros((quarter, 9 * wide), BF16)
    window[(depth + 1) * quarter :, :] = jnp.zeros((quarter, 9 * wide), BF16)
    edge = side // (depth // 4)
    y_low, y_high = (block.astype(F32) for block in line_sides("gy", y_a[...], y_b[...]))
    xy_low, xy_high = (block.astype(F32) for block in line_sides("gy", xy_a[...], xy_b[...]))
    for g in range(depth // 4):
        rim32[g, :span, :] = column[g * span : (g + 1) * span, :].astype(F32)
        for part, block in enumerate((x_rim, y_low, y_high)):
            start = span + part * edge
            rim32[g, start : start + edge, :] = block[g * edge : (g + 1) * edge, :].astype(F32)
        start = span + 3 * edge
        rim32[g, start : start + 4, :] = xy_low[4 * g : 4 * g + 4, :]
        rim32[g, start + 4 : start + 8, :] = xy_high[4 * g : 4 * g + 4, :]
        rim32[g, start + 8 :, :] = jnp.zeros((rim32.shape[1] - start - 8, wide), F32)
        moved = matmul(picks, rim32[g].astype(BF16)).astype(BF16)
        for bc in range(9):
            window[quarter + g * span : quarter + (g + 1) * span, bc * wide : (bc + 1) * wide] = moved[
                bc * span : (bc + 1) * span, :
            ]
    pre = None
    for a in range(3):
        term = matmul(
            window[a * quarter : a * quarter + cells, :], w_bottle[9 * a : 9 * (a + 1)].reshape(9 * wide, outs)
        )
        pre = term if pre is None else pre + term
    sig = jax.nn.sigmoid(pre)
    bottle[...] = (pre * sig).astype(BF16)
    slope = sig * (1.0 + pre * (1.0 - sig))
    grad = (back[...].astype(F32) * slope).astype(BF16)
    p = plane_index(count_y)
    half = span // 2
    lane = lax.broadcasted_iota(jnp.int32, (half, 128), 1)
    for pair in range(wide // 128):
        for g in range(depth // 4):
            top = column[g * span : g * span + half, pair * 128 : (pair + 1) * 128].astype(F32)
            end = column[g * span + half : (g + 1) * span, pair * 128 : (pair + 1) * 128].astype(F32)
            rows = slice(g * half, (g + 1) * half)
            slices[2 * pair, rows, :] = jnp.where(lane < 64, top, pltpu.roll(end, 64, 1)).astype(BF16)
            slices[2 * pair + 1, rows, :] = jnp.where(lane < 64, pltpu.roll(top, 64, 1), end).astype(BF16)
    middle = cells + slices.shape[1]
    for i, send in enumerate(sends):
        send[:cells, :] = grad
        send[cells:middle, :] = slices[p ^ (2 * i)]
        send[middle:, :] = slices[p ^ (2 * i + 1)]


def coarse_grad_kernel(count_y, count_z, quarter, *refs):
    grads, (bottle, shift, w_bottle) = refs[: -count_z - 6], refs[-count_z - 6 : -count_z - 3]
    sends, (window, gathered, blocks) = refs[-count_z - 3 : -3], refs[-3:]
    count_p = len(grads)
    cells, outs = bottle.shape
    rows = count_p * quarter
    depth = cells // quarter
    own_cells = cells // count_z
    inputs = w_bottle.shape[1]
    p = plane_index(count_y)
    for d, part in enumerate(grads):
        gathered[p ^ d] = part[:cells, :]
    mine = pl.multiple_of(p * quarter, quarter)
    picks = jnp.concatenate([shift[pl.ds((8 - bc) * rows + mine, quarter), :] for bc in range(9)], axis=0)
    window[:quarter, :] = jnp.zeros((quarter, 9 * outs), BF16)
    window[(depth + 1) * quarter :, :] = jnp.zeros((quarter, 9 * outs), BF16)
    for z in range(depth):
        plane = jnp.concatenate([gathered[q, z * quarter : (z + 1) * quarter, :] for q in range(count_p)], axis=0)
        moved = matmul(picks, plane).astype(BF16)
        for bc in range(9):
            window[(z + 1) * quarter : (z + 2) * quarter, bc * outs : (bc + 1) * outs] = moved[
                bc * quarter : (bc + 1) * quarter, :
            ]
    total = None
    for a in range(3):
        for bc in range(9):
            term = matmul_nt(
                window[(2 - a) * quarter : (2 - a + depth) * quarter, bc * outs : (bc + 1) * outs],
                w_bottle[9 * a + bc],
            )
            total = term if total is None else total + term
    total = total.astype(BF16)
    for q in range(count_z):
        blocks[q, :, :inputs] = total[q * own_cells : (q + 1) * own_cells, :]
        blocks[q, :, inputs:] = bottle[q * own_cells : (q + 1) * own_cells, :]
    hand_out(blocks, sends, lax.axis_index("gz"))


def grad_bottle_kernel(count_y, shift, *refs):
    parts, (out, turned, wide, grads, slices) = refs[:-5], refs[-5:]
    count_p, cells, outs = grads.shape
    lines = slices.shape[1]
    rows = shift.shape[1]
    quarter = rows // count_p
    depth = cells // quarter
    channels = out.shape[1]
    p = plane_index(count_y)
    for d, part in enumerate(parts):
        start = cells + d % 2 * lines
        grads[p ^ d] = part[:cells, :]
        slices[p ^ d] = part[start : start + lines, :]
    wide[...] = jnp.zeros_like(wide)
    planes = [
        jnp.concatenate([grads[q, z * quarter : (z + 1) * quarter, :] for q in range(count_p)], axis=0)
        for z in range(depth)
    ]
    for j in range(depth // 2):
        plane = jnp.concatenate([slices[q, j * quarter : (j + 1) * quarter, :] for q in range(count_p)], axis=0)
        plane = plane.astype(F32).T.astype(BF16)
        for bc in range(9):
            turned[bc * 128 : (bc + 1) * 128, j * rows : (j + 1) * rows] = matmul(
                plane, shift[(8 - bc) * rows : (9 - bc) * rows, :]
            ).astype(BF16)
        for slot in range(5):
            z = j // 2 * 4 + j % 2 + slot - 1
            if 0 <= z < depth:
                wide[j * rows : (j + 1) * rows, slot * outs : (slot + 1) * outs] = planes[z]
    full = matmul(turned[...], wide[...])
    for bc in range(9):
        top = full[bc * 128 : bc * 128 + channels, :]
        end = full[bc * 128 + channels : (bc + 1) * 128, :]
        for a in range(3):
            out[9 * a + bc] = top[:, (2 - a) * outs : (3 - a) * outs] + end[:, (4 - a) * outs : (5 - a) * outs]


def half_grad(turned, shifted, parity, chip, out, blocks):
    chips, rows, channels = blocks.shape
    group = rows // 27
    full = matmul(turned[parity], shifted[...])
    for bc in range(9):
        for a in range(3):
            t = 9 * a + bc
            for q in range(chips):
                start = (bc * chips + q) * group
                blocks[q, t * group : (t + 1) * group, :] = full[
                    start : start + group, a * channels : (a + 1) * channels
                ].astype(BF16)
    for i in range(chips):
        out[i] = blocks[chip ^ i]


def hidden_grad_kernel(count_y, count_z, *refs):
    parts, (slope, ordered, w_down, turned) = refs[:count_z], refs[count_z : count_z + 4]
    shifted, bottle, give, bottles, blocks = refs[count_z + 4 :]
    size_z, own, channels = ordered.shape
    quarter = own // 4
    inputs = w_down.shape[2]
    pz = lax.axis_index("gz")
    grad = total_of([part.at[:, :inputs] for part in parts]).astype(BF16)
    for d, part in enumerate(parts):
        bottles[pz ^ d] = part[:, inputs:]
    bottle[...] = jnp.concatenate([bottles[q] for q in range(count_z)], axis=1)
    shifted[...] = jnp.zeros_like(shifted)
    for s in range(8):
        a, bc = s // 4, s % 4
        spread_grad = matmul_nt(grad, w_down[s])
        for kz in range(size_z // 2):
            z = 2 * kz + a
            part = slice(bc * quarter, (bc + 1) * quarter)
            line = slice(kz * quarter, (kz + 1) * quarter)
            value = ((spread_grad[line, :] + ordered[z, part, :].astype(F32)) * slope[z, part, :]).astype(BF16)
            for t in range(3):
                start = (z + t) * own + bc * quarter
                shifted[start : start + quarter, t * channels : (t + 1) * channels] = value
    p = plane_index(count_y)
    half_grad(turned, shifted, 1 - p % 2, p // 2, give, blocks)


def keep_kernel(count_y, shifted, turned, keep, blocks):
    p = plane_index(count_y)
    half_grad(turned, shifted, p % 2, p // 2, keep, blocks)


def output_kernel(bottle, hidden, w_up, order_t, output, rows_out):
    size_z, own, channels = hidden.shape
    quarter = own // 4
    for s in range(8):
        a, bc = s // 4, s % 4
        lifted = matmul(bottle[...], w_up[s])
        for kz in range(size_z // 2):
            z = 2 * kz + a
            part = slice(bc * quarter, (bc + 1) * quarter)
            line = slice(kz * quarter, (kz + 1) * quarter)
            rows_out[z, part, :] = (lifted[line, :] + hidden[z, part, :].astype(F32)).astype(BF16)
    for z in range(size_z):
        plane = matmul(order_t[...], rows_out[z])
        output[z] = plane.reshape(output.shape[1:]).astype(BF16)


def pair_sum_kernel(keep, got, *sends):
    for i, send in enumerate(sends):
        send[...] = (keep[i].astype(F32) + got[i].astype(F32)).astype(BF16)


def sum_kernel(*refs):
    out = refs[-1]
    out[...] = total_of(refs[:-1]).reshape(out.shape).astype(out.dtype)


def shape_of(shape, dtype=BF16):
    return jax.ShapeDtypeStruct(shape, dtype)


def gathered_body(counts, volume, cotangent, w_conv, w_down, w_bottle, w_up):
    count_x, count_y, count_z = counts
    count_p = count_x * count_y
    size_z, size_x, size_y, channels = volume.shape
    wide = w_down.shape[2]
    group = w_bottle.shape[2]
    half_x, half_y = size_x // 2, size_y // 2
    own = size_x * size_y
    quarter = half_x * half_y
    own_cells = size_z // 2 * quarter
    cells = count_z * own_cells
    depth = count_z * size_z // 2
    rows = count_p * quarter
    planes = size_z + 2
    share_c = channels // count_p
    share_w = wide // count_p
    plane_axes = ("gx", "gy")

    order, taps = fine_maps(size_x, size_y)
    pair_taps = np.zeros((2, 2 * own, 9, 2, own), np.float32)
    for i in range(2):
        pair_taps[i, :, :, i, :] = taps.transpose(2, 0, 1)
    shift = coarse_maps(count_x, count_y, half_x, half_y)
    order_m = jnp.asarray(order, BF16)
    order_t = jnp.asarray(order.T, BF16)
    taps_m = jnp.asarray(taps.reshape(9 * own, 2 * own), BF16)
    taps_t = jnp.asarray(pair_taps.reshape(4 * own, 18 * own), BF16)
    shift_m = jnp.asarray(shift.reshape(9 * rows, rows), BF16)

    send_maps, rim_maps = column_maps(half_x, half_y, depth)
    send_m = jnp.asarray(send_maps, BF16)
    rim_m = jnp.asarray(rim_maps.reshape(count_x, 36 * quarter, 8 * quarter), BF16)

    w_conv_t = jnp.transpose(w_conv, (1, 0, 2))
    w_bottle_t = jnp.transpose(w_bottle, (1, 0, 2))
    send_a, send_b = local_call(ends_kernel, "ends", [shape_of((size_x, size_y, channels))] * 2)(volume)
    z_pairs = line_pairs(count_z)
    z_b = lax.ppermute(send_b, "gz", z_pairs[1])
    z_a = lax.ppermute(send_a, "gz", z_pairs[0])
    *backs, ordered = local_call(
        lambda *refs: back_kernel(count_z, *refs),
        "back",
        [shape_of((own_cells, group))] * count_z + [shape_of((size_z, own, channels))],
        [pltpu.VMEM((count_z, own_cells, group), BF16)],
    )(cotangent, w_up, order_m)
    x_send, *sends = local_call(
        faces_kernel,
        "faces",
        [shape_of((planes * size_y, channels))] + [shape_of((planes * size_x, channels))] * 2 + [shape_of((16, channels))] * 2,
        [pltpu.VMEM((16 * own, channels), F32)],
    )(volume, z_a, z_b)
    rims = swap_rims(x_send, sends[:2], sends[2:], counts)
    hidden, slope, rim, *sends = local_call(
        lambda *refs: hidden_kernel(count_z, *refs),
        "hidden",
        [
            shape_of((size_z, own, channels)),
            shape_of((size_z, own, channels), F32),
            shape_of((planes, 2 * own, channels)),
        ]
        + [shape_of((own_cells, wide + group))] * count_z,
        [
            pltpu.VMEM((planes * 2 * own, channels), F32),
            pltpu.VMEM((planes, own, 9 * channels), BF16),
        ],
        flops=2_000_000_000,
    )(volume, z_a, z_b, *rims, taps_m, w_conv_t, w_down, *backs)
    parts = trade(sends, "gz", count_z)
    turned = local_call(
        lambda *refs: rim_transpose_kernel(count_p, *refs),
        "rim_transpose",
        shape_of((2, 9 * channels // 2, planes * own)),
    )(rim, taps_t)
    column, back, x_send, *sends = local_call(
        lambda *refs: column_kernel(count_z, *refs),
        "column",
        [shape_of((cells, wide)), shape_of((cells, group)), shape_of((depth * half_y, wide))]
        + [shape_of((depth * half_x, wide))] * 2
        + [shape_of((depth, wide))] * 2,
    )(*parts, send_m)
    rims = swap_rims(x_send, sends[:2], sends[2:], counts)
    bottle, *sends = local_call(
        lambda *refs: bottle_kernel(count_y, *refs),
        "bottle",
        [shape_of((cells, group))] + [shape_of((2 * cells, group))] * (count_p // 2),
        [
            pltpu.VMEM((depth // 4, 8 * quarter, wide), F32),
            pltpu.VMEM(((depth + 2) * quarter, 9 * wide), BF16),
            pltpu.VMEM((count_p, cells // 2, 128), BF16),
        ],
        flops=2_000_000_000,
    )(column, back, *rims, rim_m, w_bottle_t)
    grads = [None] * count_p
    grads[0] = sends[0]
    for d in (6, 4, 2):
        grads[d] = swap(sends[d // 2], plane_axes, count_p, d)
    for d in (0, 2, 4, 6):
        grads[d + 1] = swap(grads[d], plane_axes, count_p, 1)
    sends = local_call(
        lambda *refs: coarse_grad_kernel(count_y, count_z, quarter, *refs),
        "coarse_grad",
        [shape_of((own_cells, wide + group))] * count_z,
        [
            pltpu.VMEM(((depth + 2) * quarter, 9 * group), BF16),
            pltpu.VMEM((count_p, cells, group), BF16),
            pltpu.VMEM((count_z, own_cells, wide + group), BF16),
        ],
    )(*grads, bottle, shift_m, w_bottle_t)
    parts = trade(sends, "gz", count_z)
    shifted, bottle, give = local_call(
        lambda *refs: hidden_grad_kernel(count_y, count_z, *refs),
        "hidden_grad",
        [
            shape_of((planes * own, 3 * channels)),
            shape_of((own_cells, wide)),
            shape_of((count_p // 2, 27 * share_c, channels)),
        ],
        [
            pltpu.VMEM((count_z, own_cells, group), BF16),
            pltpu.VMEM((count_p // 2, 27 * share_c, channels), BF16),
        ],
    )(*parts, slope, ordered, w_down, turned)
    got = swap(give, plane_axes, count_p, 1)
    keep = local_call(
        lambda *refs: keep_kernel(count_y, *refs),
        "keep",
        shape_of((count_p // 2, 27 * share_c, channels)),
        [pltpu.VMEM((count_p // 2, 27 * share_c, channels), BF16)],
    )(shifted, turned)
    output = local_call(
        output_kernel,
        "output",
        shape_of(volume.shape),
        [pltpu.VMEM((size_z, own, channels), BF16)],
    )(bottle, hidden, w_up, order_t)
    sends = local_call(
        pair_sum_kernel,
        "pair_sum",
        [shape_of((27 * share_c, channels))] * (count_p // 2),
    )(keep, got)
    parts = [sends[0]] + [swap(sends[d // 2], plane_axes, count_p, d) for d in (6, 4, 2)]
    part = local_call(sum_kernel, "plane_sum", shape_of((27 * share_c, channels)))(*parts)
    got = swap(part, "gz", count_z, 1)
    part = local_call(sum_kernel, "depth_sum", shape_of((27 * share_c, channels)))(part, got)
    got = swap(part, "gz", count_z, 2)
    grad_bottle = local_call(
        lambda *refs: grad_bottle_kernel(count_y, *refs),
        "grad_bottle",
        shape_of((27, share_w, group), F32),
        [
            pltpu.VMEM((18 * share_w, depth // 2 * rows), BF16),
            pltpu.VMEM((depth // 2 * rows, 5 * group), BF16),
            pltpu.VMEM((count_p, cells, group), BF16),
            pltpu.VMEM((count_p, cells // 2, 128), BF16),
        ],
        flops=4_000_000_000,
    )(shift_m, *grads)
    grad_conv = local_call(
        sum_kernel,
        "grad_conv",
        shape_of((27, share_c, channels), F32),
    )(part, got)
    return (output, jnp.transpose(grad_conv, (1, 0, 2)), jnp.transpose(grad_bottle, (1, 0, 2)))


def with_halo(cells, sides, width):
    for axis, dim in sides:
        count = lax.axis_size(axis)
        ends = count - 1
        head = lax.slice_in_dim(cells, 0, width, axis=dim)
        tail = lax.slice_in_dim(cells, cells.shape[dim] - width, cells.shape[dim], axis=dim)
        cells = jnp.concatenate(
            [
                lax.ppermute(tail, axis, [(i, (i + 1) % count) for i in range(ends)]),
                cells,
                lax.ppermute(head, axis, [((i + 1) % count, i) for i in range(ends)]),
            ],
            axis=dim,
        )
    return cells


def silu_slope(values):
    sig = jax.nn.sigmoid(values)
    return sig * (1.0 + values * (1.0 - sig))


def conv_forward(padded, weight, extent):
    size_z, size_x, size_y = extent
    count_cells = size_z * size_x * size_y
    summed = jnp.zeros((count_cells, weight.shape[2]), jnp.float32)
    for tap_index in range(27):
        shift_z, shift_x, shift_y = (tap_index // 9, tap_index // 3 % 3, tap_index % 3)
        window = padded[
            shift_z : shift_z + size_z, shift_x : shift_x + size_x, shift_y : shift_y + size_y, :
        ]
        window = window.reshape(count_cells, padded.shape[3])
        summed = summed + jnp.dot(
            window, weight[:, tap_index, :], preferred_element_type=jnp.float32
        )
    return summed.reshape(size_z, size_x, size_y, weight.shape[2])


def conv_weight_grad(padded, gradient, extent):
    size_z, size_x, size_y = extent
    count_cells = size_z * size_x * size_y
    flat_gradient = gradient.reshape(count_cells, gradient.shape[3])
    pieces = []
    for tap_index in range(27):
        shift_z, shift_x, shift_y = (tap_index // 9, tap_index // 3 % 3, tap_index % 3)
        window = padded[
            shift_z : shift_z + size_z, shift_x : shift_x + size_x, shift_y : shift_y + size_y, :
        ]
        window = window.reshape(count_cells, padded.shape[3])
        pieces.append(
            lax.dot_general(
                window, flat_gradient, (((0,), (0,)), ((), ())), preferred_element_type=jnp.float32
            )
        )
    return jnp.stack(pieces, axis=1)


def conv_input_grad(padded, weight, extent):
    size_z, size_x, size_y = extent
    count_cells = size_z * size_x * size_y
    summed = jnp.zeros((count_cells, weight.shape[0]), jnp.float32)
    for tap_index in range(27):
        shift_z, shift_x, shift_y = (2 - tap_index // 9, 2 - tap_index // 3 % 3, 2 - tap_index % 3)
        window = padded[
            shift_z : shift_z + size_z, shift_x : shift_x + size_x, shift_y : shift_y + size_y, :
        ]
        window = window.reshape(count_cells, padded.shape[3])
        summed = summed + lax.dot_general(
            window,
            weight[:, tap_index, :],
            (((1,), (1,)), ((), ())),
            preferred_element_type=jnp.float32,
        )
    return summed.reshape(size_z, size_x, size_y, weight.shape[0])


def pool_features(fine, kernel):
    size_z, size_x, size_y, channels = fine.shape
    blocks = fine.reshape(size_z // 2, 2, size_x // 2, 2, size_y // 2, 2, channels)
    kernel_cube = kernel.reshape(2, 2, 2, kernel.shape[1], kernel.shape[2])
    return jnp.einsum(
        "zaxbycf,abcfg->zxyg", blocks, kernel_cube, preferred_element_type=jnp.float32
    )


def pool_adjoint(coarse_in, kernel):
    size_z, size_x, size_y, wide_channels = coarse_in.shape
    kernel_cube = kernel.reshape(2, 2, 2, kernel.shape[1], kernel.shape[2])
    result = jnp.einsum(
        "zxyg,abcfg->zaxbycf", coarse_in, kernel_cube, preferred_element_type=jnp.float32
    )
    return result.reshape(2 * size_z, 2 * size_x, 2 * size_y, kernel.shape[1])


def lift_features(coarse_in, kernel):
    size_z, size_x, size_y, wide_channels = coarse_in.shape
    kernel_cube = kernel.reshape(2, 2, 2, kernel.shape[1], kernel.shape[2])
    result = jnp.einsum(
        "zxyg,abcgf->zaxbycf", coarse_in, kernel_cube, preferred_element_type=jnp.float32
    )
    return result.reshape(2 * size_z, 2 * size_x, 2 * size_y, kernel.shape[2])


def lift_adjoint(fine, kernel):
    size_z, size_x, size_y, channels = fine.shape
    blocks = fine.reshape(size_z // 2, 2, size_x // 2, 2, size_y // 2, 2, channels)
    kernel_cube = kernel.reshape(2, 2, 2, kernel.shape[1], kernel.shape[2])
    return jnp.einsum(
        "zaxbycf,abcgf->zxyg", blocks, kernel_cube, preferred_element_type=jnp.float32
    )


def column_body(volume, cotangent, w_conv, w_down, w_bottle, w_up):
    size_z, size_x, size_y, channels = volume.shape
    group_channels = w_bottle.shape[2]
    half_x = size_x // 2
    half_y = size_y // 2
    padded = with_halo(volume, (("gx", 1), ("gy", 2), ("gz", 0)), 1)
    pre_hidden = conv_forward(padded, w_conv, (size_z, size_x, size_y))
    hidden = jax.nn.silu(pre_hidden).astype(jnp.bfloat16)
    hidden_slope = silu_slope(pre_hidden)
    coarse = pool_features(hidden, w_down).astype(jnp.bfloat16)
    stacked = lax.all_gather(coarse, "gz", axis=0, tiled=True)
    rimmed = with_halo(stacked, (("gx", 1), ("gy", 2)), 1)
    column_z = rimmed.shape[0]
    coarse_pad = jnp.pad(rimmed, ((1, 1), (0, 0), (0, 0), (0, 0)))
    pre_bottle = conv_forward(coarse_pad, w_bottle, (column_z, half_x, half_y))
    bottle = jax.nn.silu(pre_bottle).astype(jnp.bfloat16)
    bottle_slope = silu_slope(pre_bottle)
    own_start = lax.axis_index("gz") * group_channels
    own_up = lax.dynamic_slice_in_dim(w_up, own_start, group_channels, 1)
    lifted = lax.psum_scatter(
        lift_features(bottle, own_up).astype(jnp.bfloat16), "gz", scatter_dimension=0, tiled=True
    ).astype(jnp.float32)
    output = (lifted + hidden.astype(jnp.float32)).astype(jnp.bfloat16)
    back_bottle = lift_adjoint(cotangent, w_up).astype(jnp.bfloat16)
    split_grad = lax.all_to_all(back_bottle, "gz", split_axis=3, concat_axis=0, tiled=True)
    bottle_grad = (split_grad.astype(jnp.float32) * bottle_slope).astype(jnp.bfloat16)
    grad_bottle = lax.psum_scatter(
        conv_weight_grad(coarse_pad, bottle_grad, (column_z, half_x, half_y)),
        ("gx", "gy"),
        scatter_dimension=0,
        tiled=True,
    )
    grad_rimmed = with_halo(bottle_grad, (("gx", 1), ("gy", 2)), 1)
    grad_pad = jnp.pad(grad_rimmed, ((1, 1), (0, 0), (0, 0), (0, 0)))
    coarse_grad = lax.psum_scatter(
        conv_input_grad(
            grad_pad, w_bottle, (lax.axis_size("gz") * (size_z // 2), half_x, half_y)
        ).astype(jnp.bfloat16),
        "gz",
        scatter_dimension=0,
        tiled=True,
    )
    hidden_grad = (
        (pool_adjoint(coarse_grad, w_down) + cotangent.astype(jnp.float32)) * hidden_slope
    ).astype(jnp.bfloat16)
    full_term = conv_weight_grad(padded, hidden_grad, (size_z, size_x, size_y))
    depth_summed = lax.psum(full_term.astype(jnp.bfloat16), "gz").astype(jnp.float32)
    grad_conv = lax.psum_scatter(depth_summed, ("gx", "gy"), scatter_dimension=0, tiled=True)
    return (output, grad_conv, grad_bottle)


def fits_one_plane(counts, brick, wide):
    count_p = counts[0] * counts[1]
    size_z, size_x, size_y, channels = brick
    return (
        counts == (2, 4, 4)
        and count_p * (size_x // 2) * (size_y // 2) == 128
        and wide // count_p == 64
        and (size_z, size_x, size_y, channels) == (8, 8, 8, 128)
    )


def solution(mesh):
    in_specs = (
        P("gz", "gx", "gy", None),
        P("gz", "gx", "gy", None),
        P(),
        P(),
        P(None, None, "gz"),
        P(),
    )
    out_specs = (
        P("gz", "gx", "gy", None),
        P(("gx", "gy"), None, None),
        P(("gx", "gy"), None, "gz"),
    )
    counts = (mesh.shape["gx"], mesh.shape["gy"], mesh.shape["gz"])

    def body(volume, cotangent, w_conv, w_down, w_bottle, w_up):
        if fits_one_plane(counts, volume.shape, w_down.shape[2]):
            return gathered_body(counts, volume, cotangent, w_conv, w_down, w_bottle, w_up)
        return column_body(volume, cotangent, w_conv, w_down, w_bottle, w_up)

    return jax.shard_map(body, mesh=mesh, in_specs=in_specs, out_specs=out_specs, check_vma=False)
```

```python
import numpy as np
import jax
import jax.numpy as jnp
from jax import lax
from jax.experimental import pallas as pl
from jax.experimental.pallas import tpu as pltpu
from jax.sharding import PartitionSpec as P

BF16 = jnp.bfloat16
F32 = jnp.float32
VMEM_LIMIT = 24 * 1024 * 1024


def local_call(kernel, name, out_shapes, scratch=(), flops=1_000_000_000):
    whole = pl.BlockSpec(memory_space=pltpu.VMEM)

    def call(*operands):
        return pl.pallas_call(
            kernel,
            name=name,
            out_shape=out_shapes,
            in_specs=[whole] * len(operands),
            out_specs=jax.tree.map(lambda _: whole, out_shapes),
            scratch_shapes=list(scratch),
            compiler_params=pltpu.CompilerParams(vmem_limit_bytes=VMEM_LIMIT),
            cost_estimate=pl.CostEstimate(flops=flops, bytes_accessed=flops // 1000, transcendentals=0),
        )(*operands)

    return call


def matmul(left, right):
    return jnp.dot(left, right, preferred_element_type=F32)


def matmul_nt(left, right):
    return lax.dot_general(left, right, (((1,), (1,)), ((), ())), preferred_element_type=F32)


def sub_order(size_x, size_y):
    half_x, half_y = size_x // 2, size_y // 2
    return {
        (2 * kx + b, 2 * ky + c): ((2 * b + c) * half_x + kx) * half_y + ky
        for b in range(2)
        for c in range(2)
        for kx in range(half_x)
        for ky in range(half_y)
    }


def fine_maps(size_x, size_y):
    own = size_x * size_y
    rows = sub_order(size_x, size_y)
    order = np.zeros((own, own), np.float32)
    taps = np.zeros((9, own, 2 * own), np.float32)
    for (x, y), row in rows.items():
        order[row, x * size_y + y] = 1
        for b in range(3):
            for c in range(3):
                sx, sy = x + b - 1, y + c - 1
                if sx < 0:
                    part = 0 if 0 <= sy < size_y else (4 if sy < 0 else 5)
                    source = own + 8 * part + sy % size_y
                elif sx >= size_x:
                    part = 1 if 0 <= sy < size_y else (6 if sy < 0 else 7)
                    source = own + 8 * part + sy % size_y
                elif sy < 0:
                    source = own + 16 + sx
                elif sy >= size_y:
                    source = own + 24 + sx
                else:
                    source = sx * size_y + sy
                taps[3 * b + c, row, source] = 1
    return order, taps


def coarse_maps(count_x, count_y, half_x, half_y):
    wide_x, wide_y = count_x * half_x, count_y * half_y

    def row_of(x, y):
        brick = (x // half_x) * count_y + y // half_y
        return (brick * half_x + x % half_x) * half_y + y % half_y

    shift = np.zeros((9, wide_x * wide_y, wide_x * wide_y), np.float32)
    for x in range(wide_x):
        for y in range(wide_y):
            for b in range(3):
                for c in range(3):
                    sx, sy = x + b - 1, y + c - 1
                    if 0 <= sx < wide_x and 0 <= sy < wide_y:
                        shift[3 * b + c, row_of(x, y), row_of(sx, sy)] = 1
    return shift


def column_maps(half_x, half_y, depth):
    quarter = half_x * half_y
    rows = depth * quarter
    y_out = np.zeros((2, 2 * depth * (half_x + 1), rows), np.float32)
    x_out = np.zeros((2, depth * (half_y + 1), rows + depth * half_x), np.float32)
    rim = np.zeros((2, 9, 4, quarter, 8 * quarter), np.float32)
    for px in range(2):
        edge = 0 if px else half_x - 1
        for z in range(depth):
            base = z * quarter
            for ky in range(half_y):
                x_out[px, z * half_y + ky, base + edge * half_y + ky] = 1
            x_out[px, depth * half_y + z, rows + z * half_x + edge] = 1
            for side, ky in enumerate((0, half_y - 1)):
                for kx in range(half_x):
                    y_out[px, depth * half_x * side + z * half_x + kx, base + kx * half_y + ky] = 1
                y_out[px, depth * (2 * half_x + side) + z, base + edge * half_y + ky] = 1
    for px in range(2):
        for b in range(3):
            for c in range(3):
                for kx in range(half_x):
                    for ky in range(half_y):
                        sx, sy = kx + b - 1, ky + c - 1
                        beyond = sx < 0 if px else sx >= half_x
                        if (sx < 0 or sx >= half_x) and not beyond:
                            continue
                        for z in range(4):
                            if beyond and 0 <= sy < half_y:
                                source = 4 * quarter + z * half_y + sy
                            elif beyond:
                                source = 7 * quarter + 4 * (sy >= half_y) + z
                            elif sy < 0:
                                source = 5 * quarter + z * half_x + sx
                            elif sy >= half_y:
                                source = 6 * quarter + z * half_x + sx
                            else:
                                source = z * quarter + sx * half_y + sy
                            rim[px, 3 * b + c, z, kx * half_y + ky, source] = 1
    return y_out, x_out, rim


def swap(block, axes, count, distance):
    return lax.ppermute(block, axes, [(i, i ^ distance) for i in range(count)])


def trade(blocks, axes, count):
    got = {d: swap(blocks[d], axes, count, d) for d in reversed(range(1, count))}
    return [blocks[0]] + [got[d] for d in range(1, count)]


def line_pairs(length):
    first = [(i, i ^ 1) for i in range(length)]
    second = [(i, i + 1 if i % 2 else i - 1) for i in range(1, length - 1)]
    return first, second


def swap_y_rims(send_a, send_b, corner_b, counts):
    count_x, count_y, _ = counts
    axes = ("gx", "gy")
    pair_a, pair_b = line_pairs(count_y)
    face_a = lax.ppermute(send_a, "gy", pair_a)
    face_b = lax.ppermute(send_b, "gy", pair_b)
    across = [(x * count_y + i, (x ^ 1) * count_y + j) for x in range(count_x) for i, j in pair_b]
    return face_a, face_b, lax.ppermute(corner_b, axes, across)


def line_sides(axis, pair_a, pair_b):
    even = lax.axis_index(axis) % 2 == 0
    return jnp.where(even, pair_b, pair_a), jnp.where(even, pair_a, pair_b)


def plane_index(count_y):
    return lax.axis_index("gx") * count_y + lax.axis_index("gy")


def plane_rows(ref, z):
    _, size_x, size_y, channels = ref.shape
    return ref[z].astype(F32).reshape(size_x * size_y, channels)


def hand_out(blocks, outs, me):
    for d, out in enumerate(outs):
        out[...] = blocks[me ^ d]


def take_in(parts, blocks, me):
    for d, part in enumerate(parts):
        blocks[me ^ d] = part[...]


def total_of(parts):
    terms = [part[...].astype(F32) for part in parts]
    while len(terms) > 1:
        terms = [terms[i] + terms[i + 1] for i in range(0, len(terms), 2)]
    return terms[0]


def back_kernel(count_z, cotangent, w_up, order, *refs):
    sends, (ordered, blocks) = refs[:count_z], refs[count_z:]
    size_z, size_x, size_y, channels = cotangent.shape
    own = size_x * size_y
    quarter = own // 4
    for z in range(size_z):
        ordered[z] = matmul(order[...], plane_rows(cotangent, z).astype(BF16)).astype(BF16)
    back = None
    for s in range(8):
        a, bc = s // 4, s % 4
        cells = jnp.concatenate(
            [ordered[2 * kz + a, bc * quarter : (bc + 1) * quarter, :] for kz in range(size_z // 2)], axis=0
        )
        term = matmul_nt(cells, w_up[s])
        back = term if back is None else back + term
    back = back.astype(BF16)
    group = back.shape[1] // count_z
    for q in range(count_z):
        blocks[q] = back[:, q * group : (q + 1) * group]
    hand_out(blocks, sends, lax.axis_index("gz"))


def deepen(volume, z_a, z_b, deep, pitch):
    size_z, size_x, size_y, channels = volume.shape
    own = size_x * size_y
    below, above = line_sides("gz", z_a[...], z_b[...])
    deep[:own, :] = below.astype(F32).reshape(own, channels)
    for z in range(size_z):
        deep[(z + 1) * pitch : (z + 1) * pitch + own, :] = plane_rows(volume, z)
    deep[(size_z + 1) * pitch : (size_z + 1) * pitch + own, :] = above.astype(F32).reshape(own, channels)


def ends_kernel(volume, send_a, send_b):
    below, above = volume[0], volume[volume.shape[0] - 1]
    send_b[...], send_a[...] = line_sides("gz", above, below)


def y_face_kernel(volume, z_a, z_b, send_a, send_b, corner_b, deep):
    size_z, size_x, size_y, channels = volume.shape
    own = size_x * size_y
    planes = size_z + 2
    deepen(volume, z_a, z_b, deep, own)
    deep[planes * own :, :] = jnp.zeros((deep.shape[0] - planes * own, channels), F32)
    first = lax.axis_index("gx") == 0
    faces, corners = [], []
    for y in (0, size_y - 1):
        faces.append(deep[pl.ds(y, planes * size_x, stride=size_y), :].astype(BF16))
        ends = [deep[pl.ds(x * size_y + y, corner_b.shape[0], stride=own), :] for x in (size_x - 1, 0)]
        corners.append(jnp.where(first, ends[0], ends[1]).astype(BF16))
    send_b[...], send_a[...] = line_sides("gy", faces[1], faces[0])
    corner_b[...], _ = line_sides("gy", corners[1], corners[0])


def x_face_kernel(volume, z_a, z_b, y_a, x_send, deep, side):
    size_z, size_x, size_y, channels = volume.shape
    own = size_x * size_y
    planes = size_z + 2
    deepen(volume, z_a, z_b, deep, own)
    side[: planes * size_x, :] = y_a[...].astype(F32)
    side[planes * size_x :, :] = jnp.zeros((side.shape[0] - planes * size_x, channels), F32)
    lines = x_send.shape[0] - planes * size_y

    def face(x):
        start = x * size_y
        cuts = [deep[z * own + start : z * own + start + size_y, :] for z in range(planes)]
        return jnp.concatenate(cuts + [side[pl.ds(x, lines, stride=size_x), :]], axis=0)

    x_send[...] = jnp.where(lax.axis_index("gx") == 0, face(size_x - 1), face(0)).astype(BF16)


def hidden_kernel(count_z, volume, z_a, z_b, x_rim, y_a, y_b, xy_b, taps, w_conv, w_down, *refs):
    backs, (hidden, slope, rim), sends, (rim32, cells) = (
        refs[:count_z],
        refs[count_z : count_z + 3],
        refs[count_z + 3 : -2],
        refs[-2:],
    )
    size_z, size_x, size_y, channels = volume.shape
    own = size_x * size_y
    quarter = own // 4
    planes = size_z + 2
    pitch = 2 * own
    first = lax.axis_index("gx") == 0
    deepen(volume, z_a, z_b, rim32, pitch)
    y_low, y_high = (block.astype(F32) for block in line_sides("gy", y_a[...], y_b[...]))
    x_side = x_rim[...].astype(F32)
    xy_a = x_side[planes * size_y :, :]
    xy_low, xy_high = line_sides("gy", xy_a, xy_b[...].astype(F32))
    x_low, x_high = jnp.where(first, 0.0, x_side), jnp.where(first, x_side, 0.0)
    faces = (x_low, x_high, y_low, y_high)
    for z in range(planes):
        for part, block in enumerate(faces):
            start = z * pitch + own + 8 * part
            rim32[start : start + 8, :] = block[8 * z : 8 * (z + 1), :]
        rim32[z * pitch + own + 32 : (z + 1) * pitch, :] = jnp.zeros((own - 32, channels), F32)
    corners = ((xy_low, 7, True), (xy_high, 0, True), (xy_low, 7, False), (xy_high, 0, False))
    for part, (block, row, low) in enumerate(corners):
        start = own + 32 + 8 * part + row
        value = jnp.where(first == low, 0.0, block)
        rim32[pl.ds(start, 8, stride=pitch), :] = value[:8, :]
        for z in range(8, planes):
            rim32[z * pitch + start : z * pitch + start + 1, :] = value[z : z + 1, :]
    for z in range(planes):
        rows = rim32[z * pitch : (z + 1) * pitch, :].astype(BF16)
        rim[z] = rows
        moved = matmul(taps[...], rows).astype(BF16)
        for bc in range(9):
            cells[z, :, bc * channels : (bc + 1) * channels] = moved[bc * own : (bc + 1) * own, :]
    pre = None
    for a in range(3):
        window = cells[a : a + size_z].reshape(size_z * own, 9 * channels)
        weight = w_conv[9 * a : 9 * (a + 1)].reshape(9 * channels, channels)
        term = matmul(window, weight)
        pre = term if pre is None else pre + term
    sig = jax.nn.sigmoid(pre)
    slope[...] = (sig * (1.0 + pre * (1.0 - sig))).reshape(size_z, own, channels)
    hidden[...] = (pre * sig).astype(BF16).reshape(size_z, own, channels)
    parts = []
    for s in range(8):
        a, bc = s // 4, s % 4
        parts.append(
            jnp.concatenate(
                [hidden[2 * kz + a, bc * quarter : (bc + 1) * quarter, :] for kz in range(size_z // 2)], axis=0
            )
        )
    coarse = matmul(jnp.concatenate(parts, axis=1), w_down[...].reshape(8 * channels, w_down.shape[2]))
    coarse = coarse.astype(BF16)
    wide = coarse.shape[1]
    for send, back in zip(sends, backs):
        send[:, :wide] = coarse
        send[:, wide:] = back[...]


def rim_transpose_kernel(count_p, rim, taps_t, turned):
    planes, rows, channels = rim.shape
    share = channels // count_p
    for pair in range(planes // 2):
        sides = [rim[2 * pair + i].astype(F32).T for i in range(2)]
        moved = matmul(jnp.concatenate(sides, axis=1).astype(BF16), taps_t[...]).astype(BF16)
        for bc in range(9):
            for p in range(count_p):
                start = (bc * count_p // 2 + p // 2) * share
                turned[p % 2, start : start + share, pair * rows : (pair + 1) * rows] = moved[
                    p * share : (p + 1) * share, bc * rows : (bc + 1) * rows
                ]


def column_kernel(count_z, *refs):
    parts, picks, (column, back, send_a, send_b, corner_b) = refs[:count_z], refs[count_z], refs[count_z + 1 :]
    own_cells = parts[0].shape[0]
    wide = column.shape[1]
    pz = lax.axis_index("gz")
    for d, part in enumerate(parts):
        rows = pl.ds(pl.multiple_of((pz ^ d) * own_cells, own_cells), own_cells)
        column[rows, :] = part[:, :wide]
        back[rows, :] = part[:, wide:]
    rims = matmul(picks[lax.axis_index("gx")], column[...]).astype(BF16)
    side, depth = send_a.shape[0], corner_b.shape[0]
    send_b[...], send_a[...] = line_sides("gy", rims[side : 2 * side, :], rims[:side, :])
    corner_b[...], _ = line_sides("gy", rims[2 * side + depth :, :], rims[2 * side : 2 * side + depth, :])


def column_face_kernel(column, y_a, picks, x_send):
    rows = jnp.concatenate([column[...], y_a[...]], axis=0)
    x_send[...] = matmul(picks[lax.axis_index("gx")], rows).astype(BF16)


def bottle_kernel(column, back, x_rim, y_a, y_b, xy_b, shift, w_bottle, bottle, grad, rim32, window):
    cells, wide = column.shape
    outs = w_bottle.shape[2]
    side = y_a.shape[0]
    depth = xy_b.shape[0]
    quarter = cells // depth
    span = 4 * quarter
    picks = shift[lax.axis_index("gx")]
    window[:quarter, :] = jnp.zeros((quarter, 9 * wide), BF16)
    window[(depth + 1) * quarter :, :] = jnp.zeros((quarter, 9 * wide), BF16)
    edge = side // (depth // 4)
    y_low, y_high = (block.astype(F32) for block in line_sides("gy", y_a[...], y_b[...]))
    xy_low, xy_high = (block.astype(F32) for block in line_sides("gy", x_rim[side:, :], xy_b[...]))
    for g in range(depth // 4):
        rim32[g, :span, :] = column[g * span : (g + 1) * span, :].astype(F32)
        for part, block in enumerate((x_rim, y_low, y_high)):
            start = span + part * edge
            rim32[g, start : start + edge, :] = block[g * edge : (g + 1) * edge, :].astype(F32)
        start = span + 3 * edge
        rim32[g, start : start + 4, :] = xy_low[4 * g : 4 * g + 4, :]
        rim32[g, start + 4 : start + 8, :] = xy_high[4 * g : 4 * g + 4, :]
        rim32[g, start + 8 :, :] = jnp.zeros((rim32.shape[1] - start - 8, wide), F32)
        moved = matmul(picks, rim32[g].astype(BF16)).astype(BF16)
        for bc in range(9):
            window[quarter + g * span : quarter + (g + 1) * span, bc * wide : (bc + 1) * wide] = moved[
                bc * span : (bc + 1) * span, :
            ]
    spread_out = None
    for bc in range(9):
        weight = jnp.concatenate([w_bottle[9 * a + bc] for a in range(3)], axis=1)
        term = matmul(window[:, bc * wide : (bc + 1) * wide], weight)
        spread_out = term if spread_out is None else spread_out + term
    pre = spread_out[:cells, :outs]
    for a in range(1, 3):
        pre = pre + spread_out[a * quarter : a * quarter + cells, a * outs : (a + 1) * outs]
    sig = jax.nn.sigmoid(pre)
    bottle[...] = (pre * sig).astype(BF16)
    slope = sig * (1.0 + pre * (1.0 - sig))
    grad[...] = (back[...].astype(F32) * slope).astype(BF16)


def slices_kernel(count_y, quarter, column, *refs):
    sends, slices = refs[:-1], refs[-1]
    cells, wide = column.shape
    span = 4 * quarter
    half = 2 * quarter
    lane = lax.broadcasted_iota(jnp.int32, (half, 128), 1)
    for pair in range(wide // 128):
        for g in range(cells // span):
            top = column[g * span : g * span + half, pair * 128 : (pair + 1) * 128].astype(F32)
            end = column[g * span + half : (g + 1) * span, pair * 128 : (pair + 1) * 128].astype(F32)
            rows = slice(g * half, (g + 1) * half)
            slices[2 * pair, rows, :] = jnp.where(lane < 64, top, pltpu.roll(end, 64, 1)).astype(BF16)
            slices[2 * pair + 1, rows, :] = jnp.where(lane < 64, pltpu.roll(top, 64, 1), end).astype(BF16)
    p = plane_index(count_y)
    lines = slices.shape[1]
    for i, send in enumerate(sends):
        send[:lines, :] = slices[p ^ (2 * i)]
        send[lines:, :] = slices[p ^ (2 * i + 1)]


def relay_kernel(*refs):
    parts, send = refs[:-1], refs[-1]
    lines = send.shape[0] // len(parts)
    for i, part in enumerate(parts):
        send[i * lines : (i + 1) * lines, :] = part[lines:, :]


def coarse_grad_kernel(count_y, count_z, quarter, *refs):
    grads, (bottle, shift, w_bottle) = refs[: -count_z - 6], refs[-count_z - 6 : -count_z - 3]
    sends, (window, gathered, blocks) = refs[-count_z - 3 : -3], refs[-3:]
    count_p = len(grads)
    cells, outs = bottle.shape
    rows = count_p * quarter
    depth = cells // quarter
    own_cells = cells // count_z
    inputs = w_bottle.shape[1]
    p = plane_index(count_y)
    take_in(grads, gathered, p)
    mine = pl.multiple_of(p * quarter, quarter)
    picks = jnp.concatenate([shift[pl.ds((8 - bc) * rows + mine, quarter), :] for bc in range(9)], axis=0)
    window[:quarter, :] = jnp.zeros((quarter, 9 * outs), BF16)
    window[(depth + 1) * quarter :, :] = jnp.zeros((quarter, 9 * outs), BF16)
    for z in range(depth):
        plane = jnp.concatenate([gathered[q, z * quarter : (z + 1) * quarter, :] for q in range(count_p)], axis=0)
        moved = matmul(picks, plane).astype(BF16)
        for bc in range(9):
            window[(z + 1) * quarter : (z + 2) * quarter, bc * outs : (bc + 1) * outs] = moved[
                bc * quarter : (bc + 1) * quarter, :
            ]
    total = None
    for a in range(3):
        weight = jnp.concatenate([w_bottle[9 * a + bc] for bc in range(9)], axis=1)
        term = matmul_nt(window[(2 - a) * quarter : (2 - a + depth) * quarter, :], weight)
        total = term if total is None else total + term
    total = total.astype(BF16)
    for q in range(count_z):
        blocks[q, :, :inputs] = total[q * own_cells : (q + 1) * own_cells, :]
        blocks[q, :, inputs:] = bottle[q * own_cells : (q + 1) * own_cells, :]
    hand_out(blocks, sends, lax.axis_index("gz"))


def grad_bottle_kernel(count_y, shift, *refs):
    out, turned, wide, grads, slices = refs[-5:]
    count_p, cells, outs = grads.shape
    parts, firsts, relayed = refs[:count_p], refs[count_p:-6], refs[-6]
    lines = slices.shape[1]
    rows = shift.shape[1]
    quarter = rows // count_p
    depth = cells // quarter
    channels = out.shape[1]
    p = plane_index(count_y)
    take_in(parts, grads, p)
    for i, part in enumerate(firsts):
        slices[p ^ (2 * i)] = part[:lines, :]
        slices[p ^ (2 * i + 1)] = relayed[i * lines : (i + 1) * lines, :]
    wide[...] = jnp.zeros_like(wide)
    planes = [
        jnp.concatenate([grads[q, z * quarter : (z + 1) * quarter, :] for q in range(count_p)], axis=0)
        for z in range(depth)
    ]
    for j in range(depth // 2):
        plane = jnp.concatenate([slices[q, j * quarter : (j + 1) * quarter, :] for q in range(count_p)], axis=0)
        plane = plane.astype(F32).T.astype(BF16)
        for bc in range(9):
            turned[bc * 128 : (bc + 1) * 128, j * rows : (j + 1) * rows] = matmul(
                plane, shift[(8 - bc) * rows : (9 - bc) * rows, :]
            ).astype(BF16)
        for slot in range(5):
            z = j // 2 * 4 + j % 2 + slot - 1
            if 0 <= z < depth:
                wide[j * rows : (j + 1) * rows, slot * outs : (slot + 1) * outs] = planes[z]
    full = matmul(turned[...], wide[...])
    for bc in range(9):
        top = full[bc * 128 : bc * 128 + channels, :]
        end = full[bc * 128 + channels : (bc + 1) * 128, :]
        for a in range(3):
            out[9 * a + bc] = top[:, (2 - a) * outs : (3 - a) * outs] + end[:, (4 - a) * outs : (5 - a) * outs]


def half_grad(turned, shifted, parity, chip, out, blocks):
    chips, rows, channels = blocks.shape
    group = rows // 27
    full = matmul(turned[parity], shifted[...])
    for bc in range(9):
        for a in range(3):
            t = 9 * a + bc
            for q in range(chips):
                start = (bc * chips + q) * group
                blocks[q, t * group : (t + 1) * group, :] = full[
                    start : start + group, a * channels : (a + 1) * channels
                ].astype(BF16)
    for i in range(chips):
        out[i] = blocks[chip ^ i]


def hidden_grad_kernel(count_y, count_z, *refs):
    parts, (slope, ordered, w_down, turned) = refs[:count_z], refs[count_z : count_z + 4]
    shifted, bottle, give, bottles, blocks = refs[count_z + 4 :]
    size_z, own, channels = ordered.shape
    quarter = own // 4
    inputs = w_down.shape[2]
    pz = lax.axis_index("gz")
    grad = total_of([part.at[:, :inputs] for part in parts]).astype(BF16)
    for d, part in enumerate(parts):
        bottles[pz ^ d] = part[:, inputs:]
    bottle[...] = jnp.concatenate([bottles[q] for q in range(count_z)], axis=1)
    shifted[...] = jnp.zeros_like(shifted)
    for s in range(8):
        a, bc = s // 4, s % 4
        spread_grad = matmul_nt(grad, w_down[s])
        for kz in range(size_z // 2):
            z = 2 * kz + a
            part = slice(bc * quarter, (bc + 1) * quarter)
            line = slice(kz * quarter, (kz + 1) * quarter)
            value = ((spread_grad[line, :] + ordered[z, part, :].astype(F32)) * slope[z, part, :]).astype(BF16)
            for t in range(3):
                start = (z + t) * own + bc * quarter
                shifted[start : start + quarter, t * channels : (t + 1) * channels] = value
    p = plane_index(count_y)
    half_grad(turned, shifted, 1 - p % 2, p // 2, give, blocks)


def keep_kernel(count_y, shifted, turned, keep, blocks):
    p = plane_index(count_y)
    half_grad(turned, shifted, p % 2, p // 2, keep, blocks)


def output_kernel(bottle, hidden, w_up, order_t, output, rows_out):
    size_z, own, channels = hidden.shape
    quarter = own // 4
    for s in range(8):
        a, bc = s // 4, s % 4
        lifted = matmul(bottle[...], w_up[s])
        for kz in range(size_z // 2):
            z = 2 * kz + a
            part = slice(bc * quarter, (bc + 1) * quarter)
            line = slice(kz * quarter, (kz + 1) * quarter)
            rows_out[z, part, :] = (lifted[line, :] + hidden[z, part, :].astype(F32)).astype(BF16)
    for z in range(size_z):
        plane = matmul(order_t[...], rows_out[z])
        output[z] = plane.reshape(output.shape[1:]).astype(BF16)


def pair_sum_kernel(keep, got, *sends):
    for i, send in enumerate(sends):
        send[...] = (keep[i].astype(F32) + got[i].astype(F32)).astype(BF16)


def sum_kernel(*refs):
    out = refs[-1]
    out[...] = total_of(refs[:-1]).reshape(out.shape).astype(out.dtype)


def shape_of(shape, dtype=BF16):
    return jax.ShapeDtypeStruct(shape, dtype)


def gathered_body(counts, volume, cotangent, w_conv, w_down, w_bottle, w_up):
    count_x, count_y, count_z = counts
    count_p = count_x * count_y
    size_z, size_x, size_y, channels = volume.shape
    wide = w_down.shape[2]
    group = w_bottle.shape[2]
    half_x, half_y = size_x // 2, size_y // 2
    own = size_x * size_y
    quarter = half_x * half_y
    own_cells = size_z // 2 * quarter
    cells = count_z * own_cells
    depth = count_z * size_z // 2
    rows = count_p * quarter
    planes = size_z + 2
    share_c = channels // count_p
    share_w = wide // count_p
    plane_axes = ("gx", "gy")

    order, taps = fine_maps(size_x, size_y)
    pair_taps = np.zeros((2, 2 * own, 9, 2, own), np.float32)
    for i in range(2):
        pair_taps[i, :, :, i, :] = taps.transpose(2, 0, 1)
    shift = coarse_maps(count_x, count_y, half_x, half_y)
    order_m = jnp.asarray(order, BF16)
    order_t = jnp.asarray(order.T, BF16)
    taps_m = jnp.asarray(taps.reshape(9 * own, 2 * own), BF16)
    taps_t = jnp.asarray(pair_taps.reshape(4 * own, 18 * own), BF16)
    shift_m = jnp.asarray(shift.reshape(9 * rows, rows), BF16)

    y_out, x_out, rim_maps = column_maps(half_x, half_y, depth)
    y_out = jnp.asarray(y_out, BF16)
    x_out = jnp.asarray(x_out, BF16)
    rim_m = jnp.asarray(rim_maps.reshape(count_x, 36 * quarter, 8 * quarter), BF16)

    w_conv_t = jnp.transpose(w_conv, (1, 0, 2))
    w_bottle_t = jnp.transpose(w_bottle, (1, 0, 2))
    send_a, send_b = local_call(ends_kernel, "ends", [shape_of((size_x, size_y, channels))] * 2)(volume)
    z_pairs = line_pairs(count_z)
    z_b = lax.ppermute(send_b, "gz", z_pairs[1])
    z_a = lax.ppermute(send_a, "gz", z_pairs[0])
    *backs, ordered = local_call(
        lambda *refs: back_kernel(count_z, *refs),
        "back",
        [shape_of((own_cells, group))] * count_z + [shape_of((size_z, own, channels))],
        [pltpu.VMEM((count_z, own_cells, group), BF16)],
    )(cotangent, w_up, order_m)
    send_a, send_b, corner_b = local_call(
        y_face_kernel,
        "y_face",
        [shape_of((planes * size_x, channels))] * 2 + [shape_of((16, channels))],
        [pltpu.VMEM((16 * own, channels), F32)],
    )(volume, z_a, z_b)
    y_a, y_b, xy_b = swap_y_rims(send_a, send_b, corner_b, counts)
    x_send = local_call(
        x_face_kernel,
        "x_face",
        shape_of((planes * size_y + 16, channels)),
        [pltpu.VMEM((planes * own, channels), F32), pltpu.VMEM((16 * size_x, channels), F32)],
    )(volume, z_a, z_b, y_a)
    x_rim = swap(x_send, plane_axes, count_p, count_y)
    hidden, slope, rim, *sends = local_call(
        lambda *refs: hidden_kernel(count_z, *refs),
        "hidden",
        [
            shape_of((size_z, own, channels)),
            shape_of((size_z, own, channels), F32),
            shape_of((planes, 2 * own, channels)),
        ]
        + [shape_of((own_cells, wide + group))] * count_z,
        [
            pltpu.VMEM((planes * 2 * own, channels), F32),
            pltpu.VMEM((planes, own, 9 * channels), BF16),
        ],
        flops=2_000_000_000,
    )(volume, z_a, z_b, x_rim, y_a, y_b, xy_b, taps_m, w_conv_t, w_down, *backs)
    parts = trade(sends, "gz", count_z)
    column, back, send_a, send_b, corner_b = local_call(
        lambda *refs: column_kernel(count_z, *refs),
        "column",
        [shape_of((cells, wide)), shape_of((cells, group))]
        + [shape_of((depth * half_x, wide))] * 2
        + [shape_of((depth, wide))],
    )(*parts, y_out)
    y_a, y_b, xy_b = swap_y_rims(send_a, send_b, corner_b, counts)
    x_send = local_call(
        column_face_kernel,
        "column_face",
        shape_of((depth * (half_y + 1), wide)),
    )(column, y_a, x_out)
    x_rim = swap(x_send, plane_axes, count_p, count_y)
    slices = local_call(
        lambda *refs: slices_kernel(count_y, quarter, *refs),
        "slices",
        [shape_of((cells, 128))] * (count_p // 2),
        [pltpu.VMEM((count_p, cells // 2, 128), BF16)],
    )(column)
    column, *slices = lax.optimization_barrier((column, *slices))
    bottle, grad = local_call(
        bottle_kernel,
        "bottle",
        [shape_of((cells, group))] * 2,
        [
            pltpu.VMEM((depth // 4, 8 * quarter, wide), F32),
            pltpu.VMEM(((depth + 2) * quarter, 9 * wide), BF16),
        ],
        flops=2_000_000_000,
    )(column, back, x_rim, y_a, y_b, xy_b, rim_m, w_bottle_t)
    grads = [None] * count_p
    grads[0] = grad
    for d in (6, 4, 2):
        grads[d] = swap(grad, plane_axes, count_p, d)
    for d in (0, 2, 4, 6):
        grads[d + 1] = swap(grads[d], plane_axes, count_p, 1)
    sends = local_call(
        lambda *refs: coarse_grad_kernel(count_y, count_z, quarter, *refs),
        "coarse_grad",
        [shape_of((own_cells, wide + group))] * count_z,
        [
            pltpu.VMEM(((depth + 2) * quarter, 9 * group), BF16),
            pltpu.VMEM((count_p, cells, group), BF16),
            pltpu.VMEM((count_z, own_cells, wide + group), BF16),
        ],
    )(*grads, bottle, shift_m, w_bottle_t)
    parts = trade(sends, "gz", count_z)
    rim, _ = lax.optimization_barrier((rim, sends[1]))
    turned = local_call(
        lambda *refs: rim_transpose_kernel(count_p, *refs),
        "rim_transpose",
        shape_of((2, 9 * channels // 2, planes * own)),
    )(rim, taps_t)
    *slices, _ = lax.optimization_barrier((*slices, parts[1]))
    firsts = [slices[0]] + [swap(slices[d // 2], plane_axes, count_p, d) for d in (2, 4, 6)]
    *parts, _ = lax.optimization_barrier((*parts, *firsts))[: count_z + 1]
    shifted, bottle, give = local_call(
        lambda *refs: hidden_grad_kernel(count_y, count_z, *refs),
        "hidden_grad",
        [
            shape_of((planes * own, 3 * channels)),
            shape_of((own_cells, wide)),
            shape_of((count_p // 2, 27 * share_c, channels)),
        ],
        [
            pltpu.VMEM((count_z, own_cells, group), BF16),
            pltpu.VMEM((count_p // 2, 27 * share_c, channels), BF16),
        ],
    )(*parts, slope, ordered, w_down, turned)
    got = swap(give, plane_axes, count_p, 1)
    *late, _ = lax.optimization_barrier((*firsts, give))
    relay = local_call(relay_kernel, "relay", shape_of((count_p // 2 * (cells // 2), 128)))(*late)
    relayed = swap(relay, plane_axes, count_p, 1)
    keep = local_call(
        lambda *refs: keep_kernel(count_y, *refs),
        "keep",
        shape_of((count_p // 2, 27 * share_c, channels)),
        [pltpu.VMEM((count_p // 2, 27 * share_c, channels), BF16)],
    )(shifted, turned)
    output = local_call(
        output_kernel,
        "output",
        shape_of(volume.shape),
        [pltpu.VMEM((size_z, own, channels), BF16)],
    )(bottle, hidden, w_up, order_t)
    sends = local_call(
        pair_sum_kernel,
        "pair_sum",
        [shape_of((27 * share_c, channels))] * (count_p // 2),
    )(keep, got)
    parts = [sends[0]] + [swap(sends[d // 2], plane_axes, count_p, d) for d in (6, 4, 2)]
    part = local_call(sum_kernel, "plane_sum", shape_of((27 * share_c, channels)))(*parts)
    part, output = lax.optimization_barrier((part, output))
    got = swap(part, "gz", count_z, 1)
    part = local_call(sum_kernel, "depth_sum", shape_of((27 * share_c, channels)))(part, got)
    got = swap(part, "gz", count_z, 2)
    grad_bottle = local_call(
        lambda *refs: grad_bottle_kernel(count_y, *refs),
        "grad_bottle",
        shape_of((27, share_w, group), F32),
        [
            pltpu.VMEM((18 * share_w, depth // 2 * rows), BF16),
            pltpu.VMEM((depth // 2 * rows, 5 * group), BF16),
            pltpu.VMEM((count_p, cells, group), BF16),
            pltpu.VMEM((count_p, cells // 2, 128), BF16),
        ],
        flops=4_000_000_000,
    )(shift_m, *grads, *firsts, relayed)
    grad_conv = local_call(
        sum_kernel,
        "grad_conv",
        shape_of((27, share_c, channels), F32),
    )(part, got)
    return (output, jnp.transpose(grad_conv, (1, 0, 2)), jnp.transpose(grad_bottle, (1, 0, 2)))


def with_halo(cells, sides, width):
    for axis, dim in sides:
        count = lax.axis_size(axis)
        ends = count - 1
        head = lax.slice_in_dim(cells, 0, width, axis=dim)
        tail = lax.slice_in_dim(cells, cells.shape[dim] - width, cells.shape[dim], axis=dim)
        cells = jnp.concatenate(
            [
                lax.ppermute(tail, axis, [(i, (i + 1) % count) for i in range(ends)]),
                cells,
                lax.ppermute(head, axis, [((i + 1) % count, i) for i in range(ends)]),
            ],
            axis=dim,
        )
    return cells


def silu_slope(values):
    sig = jax.nn.sigmoid(values)
    return sig * (1.0 + values * (1.0 - sig))


def conv_forward(padded, weight, extent):
    size_z, size_x, size_y = extent
    count_cells = size_z * size_x * size_y
    summed = jnp.zeros((count_cells, weight.shape[2]), jnp.float32)
    for tap_index in range(27):
        shift_z, shift_x, shift_y = (tap_index // 9, tap_index // 3 % 3, tap_index % 3)
        window = padded[
            shift_z : shift_z + size_z, shift_x : shift_x + size_x, shift_y : shift_y + size_y, :
        ]
        window = window.reshape(count_cells, padded.shape[3])
        summed = summed + jnp.dot(
            window, weight[:, tap_index, :], preferred_element_type=jnp.float32
        )
    return summed.reshape(size_z, size_x, size_y, weight.shape[2])


def conv_weight_grad(padded, gradient, extent):
    size_z, size_x, size_y = extent
    count_cells = size_z * size_x * size_y
    flat_gradient = gradient.reshape(count_cells, gradient.shape[3])
    pieces = []
    for tap_index in range(27):
        shift_z, shift_x, shift_y = (tap_index // 9, tap_index // 3 % 3, tap_index % 3)
        window = padded[
            shift_z : shift_z + size_z, shift_x : shift_x + size_x, shift_y : shift_y + size_y, :
        ]
        window = window.reshape(count_cells, padded.shape[3])
        pieces.append(
            lax.dot_general(
                window, flat_gradient, (((0,), (0,)), ((), ())), preferred_element_type=jnp.float32
            )
        )
    return jnp.stack(pieces, axis=1)


def conv_input_grad(padded, weight, extent):
    size_z, size_x, size_y = extent
    count_cells = size_z * size_x * size_y
    summed = jnp.zeros((count_cells, weight.shape[0]), jnp.float32)
    for tap_index in range(27):
        shift_z, shift_x, shift_y = (2 - tap_index // 9, 2 - tap_index // 3 % 3, 2 - tap_index % 3)
        window = padded[
            shift_z : shift_z + size_z, shift_x : shift_x + size_x, shift_y : shift_y + size_y, :
        ]
        window = window.reshape(count_cells, padded.shape[3])
        summed = summed + lax.dot_general(
            window,
            weight[:, tap_index, :],
            (((1,), (1,)), ((), ())),
            preferred_element_type=jnp.float32,
        )
    return summed.reshape(size_z, size_x, size_y, weight.shape[0])


def pool_features(fine, kernel):
    size_z, size_x, size_y, channels = fine.shape
    blocks = fine.reshape(size_z // 2, 2, size_x // 2, 2, size_y // 2, 2, channels)
    kernel_cube = kernel.reshape(2, 2, 2, kernel.shape[1], kernel.shape[2])
    return jnp.einsum(
        "zaxbycf,abcfg->zxyg", blocks, kernel_cube, preferred_element_type=jnp.float32
    )


def pool_adjoint(coarse_in, kernel):
    size_z, size_x, size_y, wide_channels = coarse_in.shape
    kernel_cube = kernel.reshape(2, 2, 2, kernel.shape[1], kernel.shape[2])
    result = jnp.einsum(
        "zxyg,abcfg->zaxbycf", coarse_in, kernel_cube, preferred_element_type=jnp.float32
    )
    return result.reshape(2 * size_z, 2 * size_x, 2 * size_y, kernel.shape[1])


def lift_features(coarse_in, kernel):
    size_z, size_x, size_y, wide_channels = coarse_in.shape
    kernel_cube = kernel.reshape(2, 2, 2, kernel.shape[1], kernel.shape[2])
    result = jnp.einsum(
        "zxyg,abcgf->zaxbycf", coarse_in, kernel_cube, preferred_element_type=jnp.float32
    )
    return result.reshape(2 * size_z, 2 * size_x, 2 * size_y, kernel.shape[2])


def lift_adjoint(fine, kernel):
    size_z, size_x, size_y, channels = fine.shape
    blocks = fine.reshape(size_z // 2, 2, size_x // 2, 2, size_y // 2, 2, channels)
    kernel_cube = kernel.reshape(2, 2, 2, kernel.shape[1], kernel.shape[2])
    return jnp.einsum(
        "zaxbycf,abcgf->zxyg", blocks, kernel_cube, preferred_element_type=jnp.float32
    )


def column_body(volume, cotangent, w_conv, w_down, w_bottle, w_up):
    size_z, size_x, size_y, channels = volume.shape
    group_channels = w_bottle.shape[2]
    half_x = size_x // 2
    half_y = size_y // 2
    padded = with_halo(volume, (("gx", 1), ("gy", 2), ("gz", 0)), 1)
    pre_hidden = conv_forward(padded, w_conv, (size_z, size_x, size_y))
    hidden = jax.nn.silu(pre_hidden).astype(jnp.bfloat16)
    hidden_slope = silu_slope(pre_hidden)
    coarse = pool_features(hidden, w_down).astype(jnp.bfloat16)
    stacked = lax.all_gather(coarse, "gz", axis=0, tiled=True)
    rimmed = with_halo(stacked, (("gx", 1), ("gy", 2)), 1)
    column_z = rimmed.shape[0]
    coarse_pad = jnp.pad(rimmed, ((1, 1), (0, 0), (0, 0), (0, 0)))
    pre_bottle = conv_forward(coarse_pad, w_bottle, (column_z, half_x, half_y))
    bottle = jax.nn.silu(pre_bottle).astype(jnp.bfloat16)
    bottle_slope = silu_slope(pre_bottle)
    own_start = lax.axis_index("gz") * group_channels
    own_up = lax.dynamic_slice_in_dim(w_up, own_start, group_channels, 1)
    lifted = lax.psum_scatter(
        lift_features(bottle, own_up).astype(jnp.bfloat16), "gz", scatter_dimension=0, tiled=True
    ).astype(jnp.float32)
    output = (lifted + hidden.astype(jnp.float32)).astype(jnp.bfloat16)
    back_bottle = lift_adjoint(cotangent, w_up).astype(jnp.bfloat16)
    split_grad = lax.all_to_all(back_bottle, "gz", split_axis=3, concat_axis=0, tiled=True)
    bottle_grad = (split_grad.astype(jnp.float32) * bottle_slope).astype(jnp.bfloat16)
    grad_bottle = lax.psum_scatter(
        conv_weight_grad(coarse_pad, bottle_grad, (column_z, half_x, half_y)),
        ("gx", "gy"),
        scatter_dimension=0,
        tiled=True,
    )
    grad_rimmed = with_halo(bottle_grad, (("gx", 1), ("gy", 2)), 1)
    grad_pad = jnp.pad(grad_rimmed, ((1, 1), (0, 0), (0, 0), (0, 0)))
    coarse_grad = lax.psum_scatter(
        conv_input_grad(
            grad_pad, w_bottle, (lax.axis_size("gz") * (size_z // 2), half_x, half_y)
        ).astype(jnp.bfloat16),
        "gz",
        scatter_dimension=0,
        tiled=True,
    )
    hidden_grad = (
        (pool_adjoint(coarse_grad, w_down) + cotangent.astype(jnp.float32)) * hidden_slope
    ).astype(jnp.bfloat16)
    full_term = conv_weight_grad(padded, hidden_grad, (size_z, size_x, size_y))
    depth_summed = lax.psum(full_term.astype(jnp.bfloat16), "gz").astype(jnp.float32)
    grad_conv = lax.psum_scatter(depth_summed, ("gx", "gy"), scatter_dimension=0, tiled=True)
    return (output, grad_conv, grad_bottle)


def fits_one_plane(counts, brick, wide):
    count_p = counts[0] * counts[1]
    size_z, size_x, size_y, channels = brick
    return (
        counts == (2, 4, 4)
        and count_p * (size_x // 2) * (size_y // 2) == 128
        and wide // count_p == 64
        and (size_z, size_x, size_y, channels) == (8, 8, 8, 128)
    )


def solution(mesh):
    in_specs = (
        P("gz", "gx", "gy", None),
        P("gz", "gx", "gy", None),
        P(),
        P(),
        P(None, None, "gz"),
        P(),
    )
    out_specs = (
        P("gz", "gx", "gy", None),
        P(("gx", "gy"), None, None),
        P(("gx", "gy"), None, "gz"),
    )
    counts = (mesh.shape["gx"], mesh.shape["gy"], mesh.shape["gz"])

    def body(volume, cotangent, w_conv, w_down, w_bottle, w_up):
        if fits_one_plane(counts, volume.shape, w_down.shape[2]):
            return gathered_body(counts, volume, cotangent, w_conv, w_down, w_bottle, w_up)
        return column_body(volume, cotangent, w_conv, w_down, w_bottle, w_up)

    return jax.shard_map(body, mesh=mesh, in_specs=in_specs, out_specs=out_specs, check_vma=False)
```

```python
import numpy as np
import jax
import jax.numpy as jnp
from jax import lax
from jax.experimental import pallas as pl
from jax.experimental.pallas import tpu as pltpu
from jax.sharding import PartitionSpec as P

BF16 = jnp.bfloat16
F32 = jnp.float32
VMEM_LIMIT = 24 * 1024 * 1024


def local_call(kernel, name, out_shapes, scratch=(), flops=1_000_000_000):
    whole = pl.BlockSpec(memory_space=pltpu.VMEM)

    def call(*operands):
        return pl.pallas_call(
            kernel,
            name=name,
            out_shape=out_shapes,
            in_specs=[whole] * len(operands),
            out_specs=jax.tree.map(lambda _: whole, out_shapes),
            scratch_shapes=list(scratch),
            compiler_params=pltpu.CompilerParams(vmem_limit_bytes=VMEM_LIMIT),
            cost_estimate=pl.CostEstimate(flops=flops, bytes_accessed=flops // 1000, transcendentals=0),
        )(*operands)

    return call


def matmul(left, right):
    return jnp.dot(left, right, preferred_element_type=F32)


def matmul_nt(left, right):
    return lax.dot_general(left, right, (((1,), (1,)), ((), ())), preferred_element_type=F32)


def sub_order(size_x, size_y):
    half_x, half_y = size_x // 2, size_y // 2
    return {
        (2 * kx + b, 2 * ky + c): ((2 * b + c) * half_x + kx) * half_y + ky
        for b in range(2)
        for c in range(2)
        for kx in range(half_x)
        for ky in range(half_y)
    }


def fine_maps(size_x, size_y):
    own = size_x * size_y
    rows = sub_order(size_x, size_y)
    order = np.zeros((own, own), np.float32)
    taps = np.zeros((9, own, 2 * own), np.float32)
    for (x, y), row in rows.items():
        order[row, x * size_y + y] = 1
        for b in range(3):
            for c in range(3):
                sx, sy = x + b - 1, y + c - 1
                if sx < 0:
                    part = 0 if 0 <= sy < size_y else (4 if sy < 0 else 5)
                    source = own + 8 * part + sy % size_y
                elif sx >= size_x:
                    part = 1 if 0 <= sy < size_y else (6 if sy < 0 else 7)
                    source = own + 8 * part + sy % size_y
                elif sy < 0:
                    source = own + 16 + sx
                elif sy >= size_y:
                    source = own + 24 + sx
                else:
                    source = sx * size_y + sy
                taps[3 * b + c, row, source] = 1
    return order, taps


def coarse_maps(count_x, count_y, half_x, half_y):
    wide_x, wide_y = count_x * half_x, count_y * half_y

    def row_of(x, y):
        brick = (x // half_x) * count_y + y // half_y
        return (brick * half_x + x % half_x) * half_y + y % half_y

    shift = np.zeros((9, wide_x * wide_y, wide_x * wide_y), np.float32)
    for x in range(wide_x):
        for y in range(wide_y):
            for b in range(3):
                for c in range(3):
                    sx, sy = x + b - 1, y + c - 1
                    if 0 <= sx < wide_x and 0 <= sy < wide_y:
                        shift[3 * b + c, row_of(x, y), row_of(sx, sy)] = 1
    return shift


def column_maps(half_x, half_y, depth):
    quarter = half_x * half_y
    rows = depth * quarter
    send = np.zeros((2, depth * (half_y + 2 * half_x + 2), rows), np.float32)
    rim = np.zeros((2, 9, 4, quarter, 8 * quarter), np.float32)
    for px in range(2):
        edge = 0 if px else half_x - 1
        for z in range(depth):
            base = z * quarter
            for ky in range(half_y):
                send[px, z * half_y + ky, base + edge * half_y + ky] = 1
            for side, ky in enumerate((0, half_y - 1)):
                row = depth * (half_y + side * half_x) + z * half_x
                for kx in range(half_x):
                    send[px, row + kx, base + kx * half_y + ky] = 1
                send[px, depth * (half_y + 2 * half_x + side) + z, base + edge * half_y + ky] = 1
    for px in range(2):
        for b in range(3):
            for c in range(3):
                for kx in range(half_x):
                    for ky in range(half_y):
                        sx, sy = kx + b - 1, ky + c - 1
                        beyond = sx < 0 if px else sx >= half_x
                        if (sx < 0 or sx >= half_x) and not beyond:
                            continue
                        for z in range(4):
                            if beyond and 0 <= sy < half_y:
                                source = 4 * quarter + z * half_y + sy
                            elif beyond:
                                source = 7 * quarter + 4 * (sy >= half_y) + z
                            elif sy < 0:
                                source = 5 * quarter + z * half_x + sx
                            elif sy >= half_y:
                                source = 6 * quarter + z * half_x + sx
                            else:
                                source = z * quarter + sx * half_y + sy
                            rim[px, 3 * b + c, z, kx * half_y + ky, source] = 1
    return send, rim


def swap(block, axes, count, distance):
    return lax.ppermute(block, axes, [(i, i ^ distance) for i in range(count)])


def trade(blocks, axes, count):
    got = {d: swap(blocks[d], axes, count, d) for d in reversed(range(1, count))}
    return [blocks[0]] + [got[d] for d in range(1, count)]


def line_pairs(length):
    first = [(i, i ^ 1) for i in range(length)]
    second = [(i, i + 1 if i % 2 else i - 1) for i in range(1, length - 1)]
    return first, second


def swap_rims(x_send, send_b, corner_b, counts):
    count_x, count_y, _ = counts
    axes, count = ("gx", "gy"), count_x * count_y
    corner = swap(corner_b, axes, count, count_y + 2)
    x_rim = swap(x_send, axes, count, count_y)
    across = swap(send_b, axes, count, 2)
    return x_rim, across, corner


def line_sides(axis, pair_a, pair_b):
    even = lax.axis_index(axis) % 2 == 0
    return jnp.where(even, pair_b, pair_a), jnp.where(even, pair_a, pair_b)


def relay_rims_kernel(x_rim, across, corner, send_a, send, side):
    face, lines = across.shape[0], corner.shape[0]
    pitch = x_rim.shape[0] // lines
    even = lax.axis_index("gy") % 2 == 0
    for part in range(0, x_rim.shape[1], 128):
        columns = slice(part, part + 128)
        side[...] = x_rim[:, columns].astype(F32)
        ends = [side[pl.ds(y, lines, stride=pitch), :] for y in (pitch - 1, 0)]
        send[face + lines : face + 2 * lines, columns] = jnp.where(even, ends[0], ends[1]).astype(BF16)
    send[face + 2 * lines :, :] = send_a[...]
    send[:face, :] = across[...]
    send[face : face + lines, :] = corner[...]


def relay_rims(x_rim, across, corner, send_a, counts):
    rows = 2 * (across.shape[0] + corner.shape[0])
    send = local_call(
        relay_rims_kernel,
        "relay_rims",
        shape_of((rows, across.shape[1])),
        [pltpu.VMEM((x_rim.shape[0], 128), F32)],
    )(x_rim, across, corner, send_a)
    return swap(send, ("gx", "gy"), counts[0] * counts[1], 1)


def y_rims(relayed, lines):
    py = lax.axis_index("gy")
    face = relayed.shape[0] // 2 - lines
    inner = (py > 0) & (py < lax.axis_size("gy") - 1)
    face_b = jnp.where(inner, relayed[:face, :].astype(F32), 0.0)
    corner_b = jnp.where(inner, relayed[face : face + lines, :].astype(F32), 0.0)
    corner_a = relayed[face + lines : face + 2 * lines, :].astype(F32)
    face_a = relayed[face + 2 * lines :, :].astype(F32)
    return *line_sides("gy", face_a, face_b), *line_sides("gy", corner_a, corner_b)


def plane_index(count_y):
    return lax.axis_index("gx") * count_y + lax.axis_index("gy")


def plane_rows(ref, z):
    _, size_x, size_y, channels = ref.shape
    return ref[z].astype(F32).reshape(size_x * size_y, channels)


def hand_out(blocks, outs, me):
    for d, out in enumerate(outs):
        out[...] = blocks[me ^ d]


def take_in(parts, blocks, me):
    for d, part in enumerate(parts):
        blocks[me ^ d] = part[...]


def total_of(parts):
    terms = [part[...].astype(F32) for part in parts]
    while len(terms) > 1:
        terms = [terms[i] + terms[i + 1] for i in range(0, len(terms), 2)]
    return terms[0]


def back_kernel(count_z, cotangent, w_up, order, *refs):
    sends, (ordered, blocks) = refs[:count_z], refs[count_z:]
    size_z, size_x, size_y, channels = cotangent.shape
    own = size_x * size_y
    quarter = own // 4
    for z in range(size_z):
        ordered[z] = matmul(order[...], plane_rows(cotangent, z).astype(BF16)).astype(BF16)
    back = None
    for s in range(8):
        a, bc = s // 4, s % 4
        cells = jnp.concatenate(
            [ordered[2 * kz + a, bc * quarter : (bc + 1) * quarter, :] for kz in range(size_z // 2)], axis=0
        )
        term = matmul_nt(cells, w_up[s])
        back = term if back is None else back + term
    back = back.astype(BF16)
    group = back.shape[1] // count_z
    for q in range(count_z):
        blocks[q] = back[:, q * group : (q + 1) * group]
    hand_out(blocks, sends, lax.axis_index("gz"))


def deepen(volume, z_a, z_b, deep, pitch):
    size_z, size_x, size_y, channels = volume.shape
    own = size_x * size_y
    below, above = line_sides("gz", z_a[...], z_b[...])
    deep[:own, :] = below.astype(F32).reshape(own, channels)
    for z in range(size_z):
        deep[(z + 1) * pitch : (z + 1) * pitch + own, :] = plane_rows(volume, z)
    deep[(size_z + 1) * pitch : (size_z + 1) * pitch + own, :] = above.astype(F32).reshape(own, channels)


def ends_kernel(volume, send_a, send_b):
    below, above = volume[0], volume[volume.shape[0] - 1]
    send_b[...], send_a[...] = line_sides("gz", above, below)


def faces_kernel(volume, z_a, z_b, x_send, send_a, send_b, corner_b, deep):
    size_z, size_x, size_y, channels = volume.shape
    own = size_x * size_y
    planes = x_send.shape[0] // size_y
    deepen(volume, z_a, z_b, deep, own)
    start = (size_z + 2) * own
    deep[start:, :] = jnp.zeros((deep.shape[0] - start, channels), F32)
    first = lax.axis_index("gx") == 0
    far = (size_x - 1) * size_y

    def x_face(start):
        return jnp.concatenate([deep[z * own + start : z * own + start + size_y, :] for z in range(planes)], axis=0)

    x_send[...] = jnp.where(first, x_face(far), x_face(0)).astype(BF16)
    faces, corners = [], []
    for y in (0, size_y - 1):
        faces.append(deep[pl.ds(y, send_a.shape[0], stride=size_y), :].astype(BF16))
        ends = [deep[pl.ds(start + y, planes, stride=own), :] for start in (far, 0)]
        corners.append(jnp.where(first, ends[0], ends[1]).astype(BF16))
    send_b[...], send_a[...] = line_sides("gy", faces[1], faces[0])
    corner_b[...], _ = line_sides("gy", corners[1], corners[0])


def hidden_kernel(count_z, volume, z_a, z_b, x_rim, relayed, taps, w_conv, w_down, *refs):
    backs, (hidden, slope, rim), sends, (rim32, cells) = (
        refs[:count_z],
        refs[count_z : count_z + 3],
        refs[count_z + 3 : -2],
        refs[-2:],
    )
    size_z, size_x, size_y, channels = volume.shape
    own = size_x * size_y
    quarter = own // 4
    planes = size_z + 2
    pitch = 2 * own
    first = lax.axis_index("gx") == 0
    deepen(volume, z_a, z_b, rim32, pitch)
    y_low, y_high, xy_low, xy_high = y_rims(relayed, x_rim.shape[0] // size_y)
    x_side = x_rim[...].astype(F32)
    x_low, x_high = jnp.where(first, 0.0, x_side), jnp.where(first, x_side, 0.0)
    faces = (x_low, x_high, y_low, y_high)
    for z in range(planes):
        for part, block in enumerate(faces):
            start = z * pitch + own + 8 * part
            rim32[start : start + 8, :] = block[8 * z : 8 * (z + 1), :]
        rim32[z * pitch + own + 32 : (z + 1) * pitch, :] = jnp.zeros((own - 32, channels), F32)
    corners = ((xy_low, 7, True), (xy_high, 0, True), (xy_low, 7, False), (xy_high, 0, False))
    for part, (block, row, low) in enumerate(corners):
        start = own + 32 + 8 * part + row
        value = jnp.where(first == low, 0.0, block)
        rim32[pl.ds(start, 8, stride=pitch), :] = value[:8, :]
        for z in range(8, planes):
            rim32[z * pitch + start : z * pitch + start + 1, :] = value[z : z + 1, :]
    for z in range(0, planes, 2):
        pair = [rim32[(z + i) * pitch : (z + i + 1) * pitch, :].astype(BF16) for i in range(2)]
        moved = matmul(taps[...], jnp.concatenate(pair, axis=1)).astype(BF16)
        for i in range(2):
            rim[z + i] = pair[i]
            for bc in range(9):
                cells[z + i, :, bc * channels : (bc + 1) * channels] = moved[
                    bc * own : (bc + 1) * own, i * channels : (i + 1) * channels
                ]
    pre = None
    for a in range(3):
        window = cells[a : a + size_z].reshape(size_z * own, 9 * channels)
        weight = w_conv[9 * a : 9 * (a + 1)].reshape(9 * channels, channels)
        term = matmul(window, weight)
        pre = term if pre is None else pre + term
    sig = jax.nn.sigmoid(pre)
    slope[...] = (sig * (1.0 + pre * (1.0 - sig))).reshape(size_z, own, channels)
    hidden[...] = (pre * sig).astype(BF16).reshape(size_z, own, channels)
    parts = []
    for s in range(8):
        a, bc = s // 4, s % 4
        parts.append(
            jnp.concatenate(
                [hidden[2 * kz + a, bc * quarter : (bc + 1) * quarter, :] for kz in range(size_z // 2)], axis=0
            )
        )
    coarse = matmul(jnp.concatenate(parts, axis=1), w_down[...].reshape(8 * channels, w_down.shape[2]))
    coarse = coarse.astype(BF16)
    wide = coarse.shape[1]
    for send, back in zip(sends, backs):
        send[:, :wide] = coarse
        send[:, wide:] = back[...]


def rim_transpose_kernel(count_p, rim, taps_t, turned):
    planes, rows, channels = rim.shape
    share = channels // count_p
    for pair in range(planes // 2):
        sides = [rim[2 * pair + i].astype(F32).T for i in range(2)]
        moved = matmul(jnp.concatenate(sides, axis=1).astype(BF16), taps_t[...]).astype(BF16)
        for bc in range(9):
            for p in range(count_p):
                start = (bc * count_p // 2 + p // 2) * share
                turned[p % 2, start : start + share, pair * rows : (pair + 1) * rows] = moved[
                    p * share : (p + 1) * share, bc * rows : (bc + 1) * rows
                ]


def column_kernel(count_z, *refs):
    parts, picks, (column, back, x_send, send_a, send_b, corner_b) = refs[:count_z], refs[count_z], refs[count_z + 1 :]
    own_cells = parts[0].shape[0]
    wide = column.shape[1]
    pz = lax.axis_index("gz")
    for d, part in enumerate(parts):
        rows = pl.ds(pl.multiple_of((pz ^ d) * own_cells, own_cells), own_cells)
        column[rows, :] = part[:, :wide]
        back[rows, :] = part[:, wide:]
    rims = matmul(picks[lax.axis_index("gx")], column[...]).astype(BF16)
    cuts, start = [], 0
    for size in (x_send.shape[0], *[send_a.shape[0]] * 2, *[corner_b.shape[0]] * 2):
        cuts.append(rims[start : start + size, :])
        start += size
    x_send[...] = cuts[0]
    send_b[...], send_a[...] = line_sides("gy", cuts[2], cuts[1])
    corner_b[...], _ = line_sides("gy", cuts[4], cuts[3])


def bottle_kernel(quarter, column, back, x_rim, relayed, shift, w_bottle, bottle, grad, rim32, window):
    cells, wide = column.shape
    outs = w_bottle.shape[2]
    side = x_rim.shape[0]
    depth = cells // quarter
    span = 4 * quarter
    picks = shift[lax.axis_index("gx")]
    window[:quarter, :] = jnp.zeros((quarter, 9 * wide), BF16)
    window[(depth + 1) * quarter :, :] = jnp.zeros((quarter, 9 * wide), BF16)
    edge = side // (depth // 4)
    y_low, y_high, xy_low, xy_high = y_rims(relayed, depth)
    for g in range(depth // 4):
        rim32[g, :span, :] = column[g * span : (g + 1) * span, :].astype(F32)
        for part, block in enumerate((x_rim, y_low, y_high)):
            start = span + part * edge
            rim32[g, start : start + edge, :] = block[g * edge : (g + 1) * edge, :].astype(F32)
        start = span + 3 * edge
        rim32[g, start : start + 4, :] = xy_low[4 * g : 4 * g + 4, :]
        rim32[g, start + 4 : start + 8, :] = xy_high[4 * g : 4 * g + 4, :]
        rim32[g, start + 8 :, :] = jnp.zeros((rim32.shape[1] - start - 8, wide), F32)
        moved = matmul(picks, rim32[g].astype(BF16)).astype(BF16)
        for bc in range(9):
            window[quarter + g * span : quarter + (g + 1) * span, bc * wide : (bc + 1) * wide] = moved[
                bc * span : (bc + 1) * span, :
            ]
    spread_out = None
    for bc in range(9):
        weight = jnp.concatenate([w_bottle[9 * a + bc] for a in range(3)], axis=1)
        term = matmul(window[:, bc * wide : (bc + 1) * wide], weight)
        spread_out = term if spread_out is None else spread_out + term
    pre = spread_out[:cells, :outs]
    for a in range(1, 3):
        pre = pre + spread_out[a * quarter : a * quarter + cells, a * outs : (a + 1) * outs]
    sig = jax.nn.sigmoid(pre)
    bottle[...] = (pre * sig).astype(BF16)
    slope = sig * (1.0 + pre * (1.0 - sig))
    grad[...] = (back[...].astype(F32) * slope).astype(BF16)


def slices_kernel(count_y, quarter, column, *refs):
    sends, slices = refs[:-1], refs[-1]
    cells, wide = column.shape
    span = 4 * quarter
    half = 2 * quarter
    lane = lax.broadcasted_iota(jnp.int32, (half, 128), 1)
    for pair in range(wide // 128):
        for g in range(cells // span):
            top = column[g * span : g * span + half, pair * 128 : (pair + 1) * 128].astype(F32)
            end = column[g * span + half : (g + 1) * span, pair * 128 : (pair + 1) * 128].astype(F32)
            rows = slice(g * half, (g + 1) * half)
            slices[2 * pair, rows, :] = jnp.where(lane < 64, top, pltpu.roll(end, 64, 1)).astype(BF16)
            slices[2 * pair + 1, rows, :] = jnp.where(lane < 64, pltpu.roll(top, 64, 1), end).astype(BF16)
    p = plane_index(count_y)
    lines = slices.shape[1]
    for i, send in enumerate(sends):
        send[:lines, :] = slices[p ^ (2 * i)]
        send[lines:, :] = slices[p ^ (2 * i + 1)]


def relay_kernel(*refs):
    parts, send = refs[:-1], refs[-1]
    lines = send.shape[0] // len(parts)
    for i, part in enumerate(parts):
        send[i * lines : (i + 1) * lines, :] = part[lines:, :]


def coarse_grad_kernel(count_y, count_z, quarter, *refs):
    grads, (bottle, shift, w_bottle) = refs[: -count_z - 6], refs[-count_z - 6 : -count_z - 3]
    sends, (window, gathered, blocks) = refs[-count_z - 3 : -3], refs[-3:]
    count_p = len(grads)
    cells, outs = bottle.shape
    rows = count_p * quarter
    depth = cells // quarter
    own_cells = cells // count_z
    inputs = w_bottle.shape[1]
    p = plane_index(count_y)
    take_in(grads, gathered, p)
    mine = pl.multiple_of(p * quarter, quarter)
    picks = jnp.concatenate([shift[pl.ds((8 - bc) * rows + mine, quarter), :] for bc in range(9)], axis=0)
    window[:quarter, :] = jnp.zeros((quarter, 9 * outs), BF16)
    window[(depth + 1) * quarter :, :] = jnp.zeros((quarter, 9 * outs), BF16)
    for z in range(depth):
        plane = jnp.concatenate([gathered[q, z * quarter : (z + 1) * quarter, :] for q in range(count_p)], axis=0)
        moved = matmul(picks, plane).astype(BF16)
        for bc in range(9):
            window[(z + 1) * quarter : (z + 2) * quarter, bc * outs : (bc + 1) * outs] = moved[
                bc * quarter : (bc + 1) * quarter, :
            ]
    total = None
    for a in range(3):
        weight = jnp.concatenate([w_bottle[9 * a + bc] for bc in range(9)], axis=1)
        term = matmul_nt(window[(2 - a) * quarter : (2 - a + depth) * quarter, :], weight)
        total = term if total is None else total + term
    total = total.astype(BF16)
    for q in range(count_z):
        blocks[q, :, :inputs] = total[q * own_cells : (q + 1) * own_cells, :]
        blocks[q, :, inputs:] = bottle[q * own_cells : (q + 1) * own_cells, :]
    hand_out(blocks, sends, lax.axis_index("gz"))


def grad_bottle_kernel(count_y, shift, *refs):
    out, turned, wide, grads, slices = refs[-5:]
    count_p, cells, outs = grads.shape
    parts, firsts, relayed = refs[:count_p], refs[count_p:-6], refs[-6]
    lines = slices.shape[1]
    rows = shift.shape[1]
    quarter = rows // count_p
    depth = cells // quarter
    channels = out.shape[1]
    p = plane_index(count_y)
    take_in(parts, grads, p)
    for i, part in enumerate(firsts):
        slices[p ^ (2 * i)] = part[:lines, :]
        slices[p ^ (2 * i + 1)] = relayed[i * lines : (i + 1) * lines, :]
    wide[...] = jnp.zeros_like(wide)
    planes = [
        jnp.concatenate([grads[q, z * quarter : (z + 1) * quarter, :] for q in range(count_p)], axis=0)
        for z in range(depth)
    ]
    for j in range(depth // 2):
        plane = jnp.concatenate([slices[q, j * quarter : (j + 1) * quarter, :] for q in range(count_p)], axis=0)
        plane = plane.astype(F32).T.astype(BF16)
        for bc in range(9):
            turned[bc * 128 : (bc + 1) * 128, j * rows : (j + 1) * rows] = matmul(
                plane, shift[(8 - bc) * rows : (9 - bc) * rows, :]
            ).astype(BF16)
        for slot in range(5):
            z = j // 2 * 4 + j % 2 + slot - 1
            if 0 <= z < depth:
                wide[j * rows : (j + 1) * rows, slot * outs : (slot + 1) * outs] = planes[z]
    full = matmul(turned[...], wide[...])
    for bc in range(9):
        top = full[bc * 128 : bc * 128 + channels, :]
        end = full[bc * 128 + channels : (bc + 1) * 128, :]
        for a in range(3):
            out[9 * a + bc] = top[:, (2 - a) * outs : (3 - a) * outs] + end[:, (4 - a) * outs : (5 - a) * outs]


def half_grad(turned, shifted, parity, chip, out, blocks):
    chips, rows, channels = blocks.shape
    group = rows // 27
    full = matmul(turned[parity], shifted[...])
    for bc in range(9):
        for a in range(3):
            t = 9 * a + bc
            for q in range(chips):
                start = (bc * chips + q) * group
                blocks[q, t * group : (t + 1) * group, :] = full[
                    start : start + group, a * channels : (a + 1) * channels
                ].astype(BF16)
    for i in range(chips):
        out[i] = blocks[chip ^ i]


def hidden_grad_kernel(count_y, count_z, *refs):
    parts, (slope, ordered, w_down, turned) = refs[:count_z], refs[count_z : count_z + 4]
    shifted, bottle, give, bottles, blocks = refs[count_z + 4 :]
    size_z, own, channels = ordered.shape
    quarter = own // 4
    inputs = w_down.shape[2]
    pz = lax.axis_index("gz")
    grad = total_of([part.at[:, :inputs] for part in parts]).astype(BF16)
    for d, part in enumerate(parts):
        bottles[pz ^ d] = part[:, inputs:]
    bottle[...] = jnp.concatenate([bottles[q] for q in range(count_z)], axis=1)
    shifted[...] = jnp.zeros_like(shifted)
    for s in range(8):
        a, bc = s // 4, s % 4
        spread_grad = matmul_nt(grad, w_down[s])
        for kz in range(size_z // 2):
            z = 2 * kz + a
            part = slice(bc * quarter, (bc + 1) * quarter)
            line = slice(kz * quarter, (kz + 1) * quarter)
            value = ((spread_grad[line, :] + ordered[z, part, :].astype(F32)) * slope[z, part, :]).astype(BF16)
            for t in range(3):
                start = (z + t) * own + bc * quarter
                shifted[start : start + quarter, t * channels : (t + 1) * channels] = value
    p = plane_index(count_y)
    half_grad(turned, shifted, 1 - p % 2, p // 2, give, blocks)


def keep_kernel(count_y, shifted, turned, keep, blocks):
    p = plane_index(count_y)
    half_grad(turned, shifted, p % 2, p // 2, keep, blocks)


def output_kernel(bottle, hidden, w_up, order_t, output, rows_out):
    size_z, own, channels = hidden.shape
    quarter = own // 4
    for s in range(8):
        a, bc = s // 4, s % 4
        lifted = matmul(bottle[...], w_up[s])
        for kz in range(size_z // 2):
            z = 2 * kz + a
            part = slice(bc * quarter, (bc + 1) * quarter)
            line = slice(kz * quarter, (kz + 1) * quarter)
            rows_out[z, part, :] = (lifted[line, :] + hidden[z, part, :].astype(F32)).astype(BF16)
    for z in range(size_z):
        plane = matmul(order_t[...], rows_out[z])
        output[z] = plane.reshape(output.shape[1:]).astype(BF16)


def pair_sum_kernel(keep, got, *sends):
    for i, send in enumerate(sends):
        send[...] = (keep[i].astype(F32) + got[i].astype(F32)).astype(BF16)


def sum_kernel(*refs):
    out = refs[-1]
    out[...] = total_of(refs[:-1]).reshape(out.shape).astype(out.dtype)


def shape_of(shape, dtype=BF16):
    return jax.ShapeDtypeStruct(shape, dtype)


def gathered_body(counts, volume, cotangent, w_conv, w_down, w_bottle, w_up):
    count_x, count_y, count_z = counts
    count_p = count_x * count_y
    size_z, size_x, size_y, channels = volume.shape
    wide = w_down.shape[2]
    group = w_bottle.shape[2]
    half_x, half_y = size_x // 2, size_y // 2
    own = size_x * size_y
    quarter = half_x * half_y
    own_cells = size_z // 2 * quarter
    cells = count_z * own_cells
    depth = count_z * size_z // 2
    rows = count_p * quarter
    planes = size_z + 2
    share_c = channels // count_p
    share_w = wide // count_p
    plane_axes = ("gx", "gy")

    order, taps = fine_maps(size_x, size_y)
    pair_taps = np.zeros((2, 2 * own, 9, 2, own), np.float32)
    for i in range(2):
        pair_taps[i, :, :, i, :] = taps.transpose(2, 0, 1)
    shift = coarse_maps(count_x, count_y, half_x, half_y)
    order_m = jnp.asarray(order, BF16)
    order_t = jnp.asarray(order.T, BF16)
    taps_m = jnp.asarray(taps.reshape(9 * own, 2 * own), BF16)
    taps_t = jnp.asarray(pair_taps.reshape(4 * own, 18 * own), BF16)
    shift_m = jnp.asarray(shift.reshape(9 * rows, rows), BF16)

    send_maps, rim_maps = column_maps(half_x, half_y, depth)
    send_m = jnp.asarray(send_maps, BF16)
    rim_m = jnp.asarray(rim_maps.reshape(count_x, 36 * quarter, 8 * quarter), BF16)

    w_conv_t = jnp.transpose(w_conv, (1, 0, 2))
    w_bottle_t = jnp.transpose(w_bottle, (1, 0, 2))
    send_a, send_b = local_call(ends_kernel, "ends", [shape_of((size_x, size_y, channels))] * 2)(volume)
    z_pairs = line_pairs(count_z)
    z_b = lax.ppermute(send_b, "gz", z_pairs[1])
    z_a = lax.ppermute(send_a, "gz", z_pairs[0])
    *backs, ordered = local_call(
        lambda *refs: back_kernel(count_z, *refs),
        "back",
        [shape_of((own_cells, group))] * count_z + [shape_of((size_z, own, channels))],
        [pltpu.VMEM((count_z, own_cells, group), BF16)],
    )(cotangent, w_up, order_m)
    sends = local_call(
        faces_kernel,
        "faces",
        [shape_of((16 * size_y, channels))] + [shape_of((planes * size_x, channels))] * 2 + [shape_of((16, channels))],
        [pltpu.VMEM((16 * own, channels), F32)],
    )(volume, z_a, z_b)
    x_send, send_a, send_b, corner_b = sends
    x_rim, across, corner = swap_rims(x_send, send_b, corner_b, counts)
    relayed = relay_rims(x_rim, across, corner, send_a, counts)
    hidden, slope, rim, *sends = local_call(
        lambda *refs: hidden_kernel(count_z, *refs),
        "hidden",
        [
            shape_of((size_z, own, channels)),
            shape_of((size_z, own, channels), F32),
            shape_of((planes, 2 * own, channels)),
        ]
        + [shape_of((own_cells, wide + group))] * count_z,
        [
            pltpu.VMEM((planes * 2 * own, channels), F32),
            pltpu.VMEM((planes, own, 9 * channels), BF16),
        ],
        flops=2_000_000_000,
    )(volume, z_a, z_b, x_rim, relayed, taps_m, w_conv_t, w_down, *backs)
    parts = trade(sends, "gz", count_z)
    column, back, *sends = local_call(
        lambda *refs: column_kernel(count_z, *refs),
        "column",
        [shape_of((cells, wide)), shape_of((cells, group)), shape_of((depth * half_y, wide))]
        + [shape_of((depth * half_x, wide))] * 2
        + [shape_of((depth, wide))],
    )(*parts, send_m)
    x_send, send_a, send_b, corner_b = sends
    x_rim, across, corner = swap_rims(x_send, send_b, corner_b, counts)
    relayed = relay_rims(x_rim, across, corner, send_a, counts)
    slices = local_call(
        lambda *refs: slices_kernel(count_y, quarter, *refs),
        "slices",
        [shape_of((cells, 128))] * (count_p // 2),
        [pltpu.VMEM((count_p, cells // 2, 128), BF16)],
    )(column)
    column, *slices = lax.optimization_barrier((column, *slices))
    bottle, grad = local_call(
        lambda *refs: bottle_kernel(quarter, *refs),
        "bottle",
        [shape_of((cells, group))] * 2,
        [
            pltpu.VMEM((depth // 4, 8 * quarter, wide), F32),
            pltpu.VMEM(((depth + 2) * quarter, 9 * wide), BF16),
        ],
        flops=2_000_000_000,
    )(column, back, x_rim, relayed, rim_m, w_bottle_t)
    grads = [None] * count_p
    grads[0] = grad
    for d in (6, 4, 2):
        grads[d] = swap(grad, plane_axes, count_p, d)
    for d in (0, 2, 4, 6):
        grads[d + 1] = swap(grads[d], plane_axes, count_p, 1)
    sends = local_call(
        lambda *refs: coarse_grad_kernel(count_y, count_z, quarter, *refs),
        "coarse_grad",
        [shape_of((own_cells, wide + group))] * count_z,
        [
            pltpu.VMEM(((depth + 2) * quarter, 9 * group), BF16),
            pltpu.VMEM((count_p, cells, group), BF16),
            pltpu.VMEM((count_z, own_cells, wide + group), BF16),
        ],
    )(*grads, bottle, shift_m, w_bottle_t)
    parts = trade(sends, "gz", count_z)
    rim, _ = lax.optimization_barrier((rim, sends[1]))
    turned = local_call(
        lambda *refs: rim_transpose_kernel(count_p, *refs),
        "rim_transpose",
        shape_of((2, 9 * channels // 2, planes * own)),
    )(rim, taps_t)
    *slices, _ = lax.optimization_barrier((*slices, parts[1]))
    firsts = [slices[0]] + [swap(slices[d // 2], plane_axes, count_p, d) for d in (2, 4, 6)]
    *parts, _ = lax.optimization_barrier((*parts, *firsts))[: count_z + 1]
    shifted, bottle, give = local_call(
        lambda *refs: hidden_grad_kernel(count_y, count_z, *refs),
        "hidden_grad",
        [
            shape_of((planes * own, 3 * channels)),
            shape_of((own_cells, wide)),
            shape_of((count_p // 2, 27 * share_c, channels)),
        ],
        [
            pltpu.VMEM((count_z, own_cells, group), BF16),
            pltpu.VMEM((count_p // 2, 27 * share_c, channels), BF16),
        ],
    )(*parts, slope, ordered, w_down, turned)
    got = swap(give, plane_axes, count_p, 1)
    *late, _ = lax.optimization_barrier((*firsts, give))
    relay = local_call(relay_kernel, "relay", shape_of((count_p // 2 * (cells // 2), 128)))(*late)
    relayed = swap(relay, plane_axes, count_p, 1)
    keep = local_call(
        lambda *refs: keep_kernel(count_y, *refs),
        "keep",
        shape_of((count_p // 2, 27 * share_c, channels)),
        [pltpu.VMEM((count_p // 2, 27 * share_c, channels), BF16)],
    )(shifted, turned)
    output = local_call(
        output_kernel,
        "output",
        shape_of(volume.shape),
        [pltpu.VMEM((size_z, own, channels), BF16)],
    )(bottle, hidden, w_up, order_t)
    sends = local_call(
        pair_sum_kernel,
        "pair_sum",
        [shape_of((27 * share_c, channels))] * (count_p // 2),
    )(keep, got)
    parts = [sends[0]] + [swap(sends[d // 2], plane_axes, count_p, d) for d in (6, 4, 2)]
    part = local_call(sum_kernel, "plane_sum", shape_of((27 * share_c, channels)))(*parts)
    part, output = lax.optimization_barrier((part, output))
    got = swap(part, "gz", count_z, 1)
    part = local_call(sum_kernel, "depth_sum", shape_of((27 * share_c, channels)))(part, got)
    got = swap(part, "gz", count_z, 2)
    grad_bottle = local_call(
        lambda *refs: grad_bottle_kernel(count_y, *refs),
        "grad_bottle",
        shape_of((27, share_w, group), F32),
        [
            pltpu.VMEM((18 * share_w, depth // 2 * rows), BF16),
            pltpu.VMEM((depth // 2 * rows, 5 * group), BF16),
            pltpu.VMEM((count_p, cells, group), BF16),
            pltpu.VMEM((count_p, cells // 2, 128), BF16),
        ],
        flops=4_000_000_000,
    )(shift_m, *grads, *firsts, relayed)
    grad_conv = local_call(
        sum_kernel,
        "grad_conv",
        shape_of((27, share_c, channels), F32),
    )(part, got)
    return (output, jnp.transpose(grad_conv, (1, 0, 2)), jnp.transpose(grad_bottle, (1, 0, 2)))


def with_halo(cells, sides, width):
    for axis, dim in sides:
        count = lax.axis_size(axis)
        ends = count - 1
        head = lax.slice_in_dim(cells, 0, width, axis=dim)
        tail = lax.slice_in_dim(cells, cells.shape[dim] - width, cells.shape[dim], axis=dim)
        cells = jnp.concatenate(
            [
                lax.ppermute(tail, axis, [(i, (i + 1) % count) for i in range(ends)]),
                cells,
                lax.ppermute(head, axis, [((i + 1) % count, i) for i in range(ends)]),
            ],
            axis=dim,
        )
    return cells


def silu_slope(values):
    sig = jax.nn.sigmoid(values)
    return sig * (1.0 + values * (1.0 - sig))


def conv_forward(padded, weight, extent):
    size_z, size_x, size_y = extent
    count_cells = size_z * size_x * size_y
    summed = jnp.zeros((count_cells, weight.shape[2]), jnp.float32)
    for tap_index in range(27):
        shift_z, shift_x, shift_y = (tap_index // 9, tap_index // 3 % 3, tap_index % 3)
        window = padded[
            shift_z : shift_z + size_z, shift_x : shift_x + size_x, shift_y : shift_y + size_y, :
        ]
        window = window.reshape(count_cells, padded.shape[3])
        summed = summed + jnp.dot(
            window, weight[:, tap_index, :], preferred_element_type=jnp.float32
        )
    return summed.reshape(size_z, size_x, size_y, weight.shape[2])


def conv_weight_grad(padded, gradient, extent):
    size_z, size_x, size_y = extent
    count_cells = size_z * size_x * size_y
    flat_gradient = gradient.reshape(count_cells, gradient.shape[3])
    pieces = []
    for tap_index in range(27):
        shift_z, shift_x, shift_y = (tap_index // 9, tap_index // 3 % 3, tap_index % 3)
        window = padded[
            shift_z : shift_z + size_z, shift_x : shift_x + size_x, shift_y : shift_y + size_y, :
        ]
        window = window.reshape(count_cells, padded.shape[3])
        pieces.append(
            lax.dot_general(
                window, flat_gradient, (((0,), (0,)), ((), ())), preferred_element_type=jnp.float32
            )
        )
    return jnp.stack(pieces, axis=1)


def conv_input_grad(padded, weight, extent):
    size_z, size_x, size_y = extent
    count_cells = size_z * size_x * size_y
    summed = jnp.zeros((count_cells, weight.shape[0]), jnp.float32)
    for tap_index in range(27):
        shift_z, shift_x, shift_y = (2 - tap_index // 9, 2 - tap_index // 3 % 3, 2 - tap_index % 3)
        window = padded[
            shift_z : shift_z + size_z, shift_x : shift_x + size_x, shift_y : shift_y + size_y, :
        ]
        window = window.reshape(count_cells, padded.shape[3])
        summed = summed + lax.dot_general(
            window,
            weight[:, tap_index, :],
            (((1,), (1,)), ((), ())),
            preferred_element_type=jnp.float32,
        )
    return summed.reshape(size_z, size_x, size_y, weight.shape[0])


def pool_features(fine, kernel):
    size_z, size_x, size_y, channels = fine.shape
    blocks = fine.reshape(size_z // 2, 2, size_x // 2, 2, size_y // 2, 2, channels)
    kernel_cube = kernel.reshape(2, 2, 2, kernel.shape[1], kernel.shape[2])
    return jnp.einsum(
        "zaxbycf,abcfg->zxyg", blocks, kernel_cube, preferred_element_type=jnp.float32
    )


def pool_adjoint(coarse_in, kernel):
    size_z, size_x, size_y, wide_channels = coarse_in.shape
    kernel_cube = kernel.reshape(2, 2, 2, kernel.shape[1], kernel.shape[2])
    result = jnp.einsum(
        "zxyg,abcfg->zaxbycf", coarse_in, kernel_cube, preferred_element_type=jnp.float32
    )
    return result.reshape(2 * size_z, 2 * size_x, 2 * size_y, kernel.shape[1])


def lift_features(coarse_in, kernel):
    size_z, size_x, size_y, wide_channels = coarse_in.shape
    kernel_cube = kernel.reshape(2, 2, 2, kernel.shape[1], kernel.shape[2])
    result = jnp.einsum(
        "zxyg,abcgf->zaxbycf", coarse_in, kernel_cube, preferred_element_type=jnp.float32
    )
    return result.reshape(2 * size_z, 2 * size_x, 2 * size_y, kernel.shape[2])


def lift_adjoint(fine, kernel):
    size_z, size_x, size_y, channels = fine.shape
    blocks = fine.reshape(size_z // 2, 2, size_x // 2, 2, size_y // 2, 2, channels)
    kernel_cube = kernel.reshape(2, 2, 2, kernel.shape[1], kernel.shape[2])
    return jnp.einsum(
        "zaxbycf,abcgf->zxyg", blocks, kernel_cube, preferred_element_type=jnp.float32
    )


def column_body(volume, cotangent, w_conv, w_down, w_bottle, w_up):
    size_z, size_x, size_y, channels = volume.shape
    group_channels = w_bottle.shape[2]
    half_x = size_x // 2
    half_y = size_y // 2
    padded = with_halo(volume, (("gx", 1), ("gy", 2), ("gz", 0)), 1)
    pre_hidden = conv_forward(padded, w_conv, (size_z, size_x, size_y))
    hidden = jax.nn.silu(pre_hidden).astype(jnp.bfloat16)
    hidden_slope = silu_slope(pre_hidden)
    coarse = pool_features(hidden, w_down).astype(jnp.bfloat16)
    stacked = lax.all_gather(coarse, "gz", axis=0, tiled=True)
    rimmed = with_halo(stacked, (("gx", 1), ("gy", 2)), 1)
    column_z = rimmed.shape[0]
    coarse_pad = jnp.pad(rimmed, ((1, 1), (0, 0), (0, 0), (0, 0)))
    pre_bottle = conv_forward(coarse_pad, w_bottle, (column_z, half_x, half_y))
    bottle = jax.nn.silu(pre_bottle).astype(jnp.bfloat16)
    bottle_slope = silu_slope(pre_bottle)
    own_start = lax.axis_index("gz") * group_channels
    own_up = lax.dynamic_slice_in_dim(w_up, own_start, group_channels, 1)
    lifted = lax.psum_scatter(
        lift_features(bottle, own_up).astype(jnp.bfloat16), "gz", scatter_dimension=0, tiled=True
    ).astype(jnp.float32)
    output = (lifted + hidden.astype(jnp.float32)).astype(jnp.bfloat16)
    back_bottle = lift_adjoint(cotangent, w_up).astype(jnp.bfloat16)
    split_grad = lax.all_to_all(back_bottle, "gz", split_axis=3, concat_axis=0, tiled=True)
    bottle_grad = (split_grad.astype(jnp.float32) * bottle_slope).astype(jnp.bfloat16)
    grad_bottle = lax.psum_scatter(
        conv_weight_grad(coarse_pad, bottle_grad, (column_z, half_x, half_y)),
        ("gx", "gy"),
        scatter_dimension=0,
        tiled=True,
    )
    grad_rimmed = with_halo(bottle_grad, (("gx", 1), ("gy", 2)), 1)
    grad_pad = jnp.pad(grad_rimmed, ((1, 1), (0, 0), (0, 0), (0, 0)))
    coarse_grad = lax.psum_scatter(
        conv_input_grad(
            grad_pad, w_bottle, (lax.axis_size("gz") * (size_z // 2), half_x, half_y)
        ).astype(jnp.bfloat16),
        "gz",
        scatter_dimension=0,
        tiled=True,
    )
    hidden_grad = (
        (pool_adjoint(coarse_grad, w_down) + cotangent.astype(jnp.float32)) * hidden_slope
    ).astype(jnp.bfloat16)
    full_term = conv_weight_grad(padded, hidden_grad, (size_z, size_x, size_y))
    depth_summed = lax.psum(full_term.astype(jnp.bfloat16), "gz").astype(jnp.float32)
    grad_conv = lax.psum_scatter(depth_summed, ("gx", "gy"), scatter_dimension=0, tiled=True)
    return (output, grad_conv, grad_bottle)


def fits_one_plane(counts, brick, wide):
    count_p = counts[0] * counts[1]
    size_z, size_x, size_y, channels = brick
    return (
        counts == (2, 4, 4)
        and count_p * (size_x // 2) * (size_y // 2) == 128
        and wide // count_p == 64
        and (size_z, size_x, size_y, channels) == (8, 8, 8, 128)
    )


def solution(mesh):
    in_specs = (
        P("gz", "gx", "gy", None),
        P("gz", "gx", "gy", None),
        P(),
        P(),
        P(None, None, "gz"),
        P(),
    )
    out_specs = (
        P("gz", "gx", "gy", None),
        P(("gx", "gy"), None, None),
        P(("gx", "gy"), None, "gz"),
    )
    counts = (mesh.shape["gx"], mesh.shape["gy"], mesh.shape["gz"])

    def body(volume, cotangent, w_conv, w_down, w_bottle, w_up):
        if fits_one_plane(counts, volume.shape, w_down.shape[2]):
            return gathered_body(counts, volume, cotangent, w_conv, w_down, w_bottle, w_up)
        return column_body(volume, cotangent, w_conv, w_down, w_bottle, w_up)

    return jax.shard_map(body, mesh=mesh, in_specs=in_specs, out_specs=out_specs, check_vma=False)
```

```python
import numpy as np
import jax
import jax.numpy as jnp
from jax import lax
from jax.experimental import pallas as pl
from jax.experimental.pallas import tpu as pltpu
from jax.sharding import PartitionSpec as P

BF16 = jnp.bfloat16
F32 = jnp.float32
VMEM_LIMIT = 24 * 1024 * 1024


def local_call(kernel, name, out_shapes, scratch=(), flops=300_000_000):
    whole = pl.BlockSpec(memory_space=pltpu.VMEM)

    def call(*operands):
        return pl.pallas_call(
            kernel,
            name=name,
            out_shape=out_shapes,
            in_specs=[whole] * len(operands),
            out_specs=jax.tree.map(lambda _: whole, out_shapes),
            scratch_shapes=list(scratch),
            compiler_params=pltpu.CompilerParams(vmem_limit_bytes=VMEM_LIMIT),
            cost_estimate=pl.CostEstimate(flops=flops, bytes_accessed=flops // 1000, transcendentals=0),
        )(*operands)

    return call


def matmul(left, right):
    return jnp.dot(left, right, preferred_element_type=F32)


def matmul_nt(left, right):
    return lax.dot_general(left, right, (((1,), (1,)), ((), ())), preferred_element_type=F32)


def sub_order(size_x, size_y):
    half_x, half_y = size_x // 2, size_y // 2
    return {
        (2 * kx + b, 2 * ky + c): ((2 * b + c) * half_x + kx) * half_y + ky
        for b in range(2)
        for c in range(2)
        for kx in range(half_x)
        for ky in range(half_y)
    }


def fine_maps(size_x, size_y):
    own = size_x * size_y
    rows = sub_order(size_x, size_y)
    order = np.zeros((own, own), np.float32)
    taps = np.zeros((9, own, 2 * own), np.float32)
    for (x, y), row in rows.items():
        order[row, x * size_y + y] = 1
        for b in range(3):
            for c in range(3):
                sx, sy = x + b - 1, y + c - 1
                if sx < 0:
                    part = 0 if 0 <= sy < size_y else (4 if sy < 0 else 5)
                    source = own + 8 * part + sy % size_y
                elif sx >= size_x:
                    part = 1 if 0 <= sy < size_y else (6 if sy < 0 else 7)
                    source = own + 8 * part + sy % size_y
                elif sy < 0:
                    source = own + 16 + sx
                elif sy >= size_y:
                    source = own + 24 + sx
                else:
                    source = sx * size_y + sy
                taps[3 * b + c, row, source] = 1
    return order, taps


def coarse_maps(count_x, count_y, half_x, half_y):
    wide_x, wide_y = count_x * half_x, count_y * half_y

    def row_of(x, y):
        brick = (x // half_x) * count_y + y // half_y
        return (brick * half_x + x % half_x) * half_y + y % half_y

    shift = np.zeros((9, wide_x * wide_y, wide_x * wide_y), np.float32)
    for x in range(wide_x):
        for y in range(wide_y):
            for b in range(3):
                for c in range(3):
                    sx, sy = x + b - 1, y + c - 1
                    if 0 <= sx < wide_x and 0 <= sy < wide_y:
                        shift[3 * b + c, row_of(x, y), row_of(sx, sy)] = 1
    return shift


def column_maps(half_x, half_y, depth):
    quarter = half_x * half_y
    rows = depth * quarter
    send = np.zeros((2, depth * (half_y + 2 * half_x + 2), rows), np.float32)
    rim = np.zeros((2, 9, 4, quarter, 8 * quarter), np.float32)
    for px in range(2):
        edge = 0 if px else half_x - 1
        for z in range(depth):
            base = z * quarter
            for ky in range(half_y):
                send[px, z * half_y + ky, base + edge * half_y + ky] = 1
            for side, ky in enumerate((0, half_y - 1)):
                row = depth * (half_y + side * half_x) + z * half_x
                for kx in range(half_x):
                    send[px, row + kx, base + kx * half_y + ky] = 1
                send[px, depth * (half_y + 2 * half_x + side) + z, base + edge * half_y + ky] = 1
    for px in range(2):
        for b in range(3):
            for c in range(3):
                for kx in range(half_x):
                    for ky in range(half_y):
                        sx, sy = kx + b - 1, ky + c - 1
                        beyond = sx < 0 if px else sx >= half_x
                        if (sx < 0 or sx >= half_x) and not beyond:
                            continue
                        for z in range(4):
                            if beyond and 0 <= sy < half_y:
                                source = 4 * quarter + z * half_y + sy
                            elif beyond:
                                source = 7 * quarter + 4 * (sy >= half_y) + z
                            elif sy < 0:
                                source = 5 * quarter + z * half_x + sx
                            elif sy >= half_y:
                                source = 6 * quarter + z * half_x + sx
                            else:
                                source = z * quarter + sx * half_y + sy
                            rim[px, 3 * b + c, z, kx * half_y + ky, source] = 1
    return send, rim


def swap(block, axes, count, distance):
    return lax.ppermute(block, axes, [(i, i ^ distance) for i in range(count)])


def trade(blocks, axes, count):
    got = {d: swap(blocks[d], axes, count, d) for d in reversed(range(1, count))}
    return [blocks[0]] + [got[d] for d in range(1, count)]


def line_pairs(length):
    first = [(i, i ^ 1) for i in range(length)]
    second = [(i, i + 1 if i % 2 else i - 1) for i in range(1, length - 1)]
    return first, second


def swap_rims(x_send, send_b, corner_b, counts):
    count_x, count_y, _ = counts
    axes, count = ("gx", "gy"), count_x * count_y
    corner = swap(corner_b, axes, count, count_y + 2)
    x_rim = swap(x_send, axes, count, count_y)
    across = swap(send_b, axes, count, 2)
    return x_rim, across, corner


def line_sides(axis, pair_a, pair_b):
    even = lax.axis_index(axis) % 2 == 0
    return jnp.where(even, pair_b, pair_a), jnp.where(even, pair_a, pair_b)


def relay_rims_kernel(x_rim, across, corner, send_a, send, side):
    face, lines = across.shape[0], corner.shape[0]
    pitch = x_rim.shape[0] // lines
    even = lax.axis_index("gy") % 2 == 0
    for part in range(0, x_rim.shape[1], 128):
        columns = slice(part, part + 128)
        side[...] = x_rim[:, columns].astype(F32)
        ends = [side[pl.ds(y, lines, stride=pitch), :] for y in (pitch - 1, 0)]
        send[face + lines : face + 2 * lines, columns] = jnp.where(even, ends[0], ends[1]).astype(BF16)
    send[face + 2 * lines :, :] = send_a[...]
    send[:face, :] = across[...]
    send[face : face + lines, :] = corner[...]


def relay_rims(x_rim, across, corner, send_a, counts):
    rows = 2 * (across.shape[0] + corner.shape[0])
    send = local_call(
        relay_rims_kernel,
        "relay_rims",
        shape_of((rows, across.shape[1])),
        [pltpu.VMEM((x_rim.shape[0], 128), F32)],
    )(x_rim, across, corner, send_a)
    return swap(send, ("gx", "gy"), counts[0] * counts[1], 1)


def y_rims(relayed, lines):
    py = lax.axis_index("gy")
    face = relayed.shape[0] // 2 - lines
    inner = (py > 0) & (py < lax.axis_size("gy") - 1)
    face_b = jnp.where(inner, relayed[:face, :].astype(F32), 0.0)
    corner_b = jnp.where(inner, relayed[face : face + lines, :].astype(F32), 0.0)
    corner_a = relayed[face + lines : face + 2 * lines, :].astype(F32)
    face_a = relayed[face + 2 * lines :, :].astype(F32)
    return *line_sides("gy", face_a, face_b), *line_sides("gy", corner_a, corner_b)


def plane_index(count_y):
    return lax.axis_index("gx") * count_y + lax.axis_index("gy")


def plane_rows(ref, z):
    _, size_x, size_y, channels = ref.shape
    return ref[z].astype(F32).reshape(size_x * size_y, channels)


def hand_out(blocks, outs, me):
    for d, out in enumerate(outs):
        out[...] = blocks[me ^ d]


def take_in(parts, blocks, me):
    for d, part in enumerate(parts):
        blocks[me ^ d] = part[...]


def total_of(parts):
    terms = [part[...].astype(F32) for part in parts]
    while len(terms) > 1:
        terms = [terms[i] + terms[i + 1] for i in range(0, len(terms), 2)]
    return terms[0]


def back_kernel(count_z, cotangent, w_up, order, *refs):
    sends, (ordered, blocks) = refs[:count_z], refs[count_z:]
    size_z, size_x, size_y, channels = cotangent.shape
    own = size_x * size_y
    quarter = own // 4
    for z in range(size_z):
        ordered[z] = matmul(order[...], plane_rows(cotangent, z).astype(BF16)).astype(BF16)
    back = None
    for s in range(8):
        a, bc = s // 4, s % 4
        cells = jnp.concatenate(
            [ordered[2 * kz + a, bc * quarter : (bc + 1) * quarter, :] for kz in range(size_z // 2)], axis=0
        )
        term = matmul_nt(cells, w_up[s])
        back = term if back is None else back + term
    back = back.astype(BF16)
    group = back.shape[1] // count_z
    for q in range(count_z):
        blocks[q] = back[:, q * group : (q + 1) * group]
    hand_out(blocks, sends, lax.axis_index("gz"))


def deepen(volume, z_a, z_b, deep, pitch):
    size_z, size_x, size_y, channels = volume.shape
    own = size_x * size_y
    below, above = line_sides("gz", z_a[...], z_b[...])
    deep[:own, :] = below.astype(F32).reshape(own, channels)
    for z in range(size_z):
        deep[(z + 1) * pitch : (z + 1) * pitch + own, :] = plane_rows(volume, z)
    deep[(size_z + 1) * pitch : (size_z + 1) * pitch + own, :] = above.astype(F32).reshape(own, channels)


def ends_kernel(volume, send_a, send_b):
    below, above = volume[0], volume[volume.shape[0] - 1]
    send_b[...], send_a[...] = line_sides("gz", above, below)


def faces_kernel(volume, z_a, z_b, x_send, send_a, send_b, corner_b, deep):
    size_z, size_x, size_y, channels = volume.shape
    own = size_x * size_y
    planes = x_send.shape[0] // size_y
    deepen(volume, z_a, z_b, deep, own)
    start = (size_z + 2) * own
    deep[start:, :] = jnp.zeros((deep.shape[0] - start, channels), F32)
    first = lax.axis_index("gx") == 0
    far = (size_x - 1) * size_y

    def x_face(start):
        return jnp.concatenate([deep[z * own + start : z * own + start + size_y, :] for z in range(planes)], axis=0)

    x_send[...] = jnp.where(first, x_face(far), x_face(0)).astype(BF16)
    faces, corners = [], []
    for y in (0, size_y - 1):
        faces.append(deep[pl.ds(y, send_a.shape[0], stride=size_y), :].astype(BF16))
        ends = [deep[pl.ds(start + y, planes, stride=own), :] for start in (far, 0)]
        corners.append(jnp.where(first, ends[0], ends[1]).astype(BF16))
    send_b[...], send_a[...] = line_sides("gy", faces[1], faces[0])
    corner_b[...], _ = line_sides("gy", corners[1], corners[0])


def hidden_kernel(count_z, volume, z_a, z_b, x_rim, relayed, taps, w_conv, w_down, *refs):
    backs, (hidden, slope, rim), sends, (rim32, cells) = (
        refs[:count_z],
        refs[count_z : count_z + 3],
        refs[count_z + 3 : -2],
        refs[-2:],
    )
    size_z, size_x, size_y, channels = volume.shape
    own = size_x * size_y
    quarter = own // 4
    planes = size_z + 2
    pitch = 2 * own
    first = lax.axis_index("gx") == 0
    deepen(volume, z_a, z_b, rim32, pitch)
    y_low, y_high, xy_low, xy_high = y_rims(relayed, x_rim.shape[0] // size_y)
    x_side = x_rim[...].astype(F32)
    x_low, x_high = jnp.where(first, 0.0, x_side), jnp.where(first, x_side, 0.0)
    faces = (x_low, x_high, y_low, y_high)
    for z in range(planes):
        for part, block in enumerate(faces):
            start = z * pitch + own + 8 * part
            rim32[start : start + 8, :] = block[8 * z : 8 * (z + 1), :]
        rim32[z * pitch + own + 32 : (z + 1) * pitch, :] = jnp.zeros((own - 32, channels), F32)
    corners = ((xy_low, 7, True), (xy_high, 0, True), (xy_low, 7, False), (xy_high, 0, False))
    for part, (block, row, low) in enumerate(corners):
        start = own + 32 + 8 * part + row
        value = jnp.where(first == low, 0.0, block)
        rim32[pl.ds(start, 8, stride=pitch), :] = value[:8, :]
        for z in range(8, planes):
            rim32[z * pitch + start : z * pitch + start + 1, :] = value[z : z + 1, :]
    for z in range(0, planes, 2):
        pair = [rim32[(z + i) * pitch : (z + i + 1) * pitch, :].astype(BF16) for i in range(2)]
        moved = matmul(taps[...], jnp.concatenate(pair, axis=1)).astype(BF16)
        for i in range(2):
            rim[z + i] = pair[i]
            for bc in range(9):
                cells[z + i, :, bc * channels : (bc + 1) * channels] = moved[
                    bc * own : (bc + 1) * own, i * channels : (i + 1) * channels
                ]
    pre = None
    for a in range(3):
        window = cells[a : a + size_z].reshape(size_z * own, 9 * channels)
        weight = w_conv[9 * a : 9 * (a + 1)].reshape(9 * channels, channels)
        term = matmul(window, weight)
        pre = term if pre is None else pre + term
    sig = jax.nn.sigmoid(pre)
    slope[...] = (sig * (1.0 + pre * (1.0 - sig))).reshape(size_z, own, channels)
    hidden[...] = (pre * sig).astype(BF16).reshape(size_z, own, channels)
    parts = []
    for s in range(8):
        a, bc = s // 4, s % 4
        parts.append(
            jnp.concatenate(
                [hidden[2 * kz + a, bc * quarter : (bc + 1) * quarter, :] for kz in range(size_z // 2)], axis=0
            )
        )
    coarse = matmul(jnp.concatenate(parts, axis=1), w_down[...].reshape(8 * channels, w_down.shape[2]))
    coarse = coarse.astype(BF16)
    wide = coarse.shape[1]
    for send, back in zip(sends, backs):
        send[:, :wide] = coarse
        send[:, wide:] = back[...]


def rim_transpose_kernel(count_p, rim, taps_t, turned):
    planes, rows, channels = rim.shape
    share = channels // count_p
    for pair in range(planes // 2):
        sides = [rim[2 * pair + i].astype(F32).T for i in range(2)]
        moved = matmul(jnp.concatenate(sides, axis=1).astype(BF16), taps_t[...]).astype(BF16)
        for bc in range(9):
            for p in range(count_p):
                start = (bc * count_p // 2 + p // 2) * share
                turned[p % 2, start : start + share, pair * rows : (pair + 1) * rows] = moved[
                    p * share : (p + 1) * share, bc * rows : (bc + 1) * rows
                ]


def column_kernel(count_z, *refs):
    parts, picks, (column, back, x_send, send_a, send_b, corner_b) = refs[:count_z], refs[count_z], refs[count_z + 1 :]
    own_cells = parts[0].shape[0]
    wide = column.shape[1]
    pz = lax.axis_index("gz")
    for i, part in enumerate(parts):
        rows = pl.ds(pl.multiple_of((pz ^ (-i % count_z)) * own_cells, own_cells), own_cells)
        column[rows, :] = part[:, :wide]
        back[rows, :] = part[:, wide:]
    rims = matmul(picks[lax.axis_index("gx")], column[...]).astype(BF16)
    cuts, start = [], 0
    for size in (x_send.shape[0], *[send_a.shape[0]] * 2, *[corner_b.shape[0]] * 2):
        cuts.append(rims[start : start + size, :])
        start += size
    x_send[...] = cuts[0]
    send_b[...], send_a[...] = line_sides("gy", cuts[2], cuts[1])
    corner_b[...], _ = line_sides("gy", cuts[4], cuts[3])


def bottle_kernel(quarter, column, back, x_rim, relayed, shift, w_bottle, far, bottle, grad, grad_far, rim32, window):
    cells, wide = column.shape
    outs = w_bottle.shape[2]
    side = x_rim.shape[0]
    depth = cells // quarter
    span = 4 * quarter
    picks = shift[lax.axis_index("gx")]
    window[:quarter, :] = jnp.zeros((quarter, 9 * wide), BF16)
    window[(depth + 1) * quarter :, :] = jnp.zeros((quarter, 9 * wide), BF16)
    edge = side // (depth // 4)
    y_low, y_high, xy_low, xy_high = y_rims(relayed, depth)
    for g in range(depth // 4):
        rim32[g, :span, :] = column[g * span : (g + 1) * span, :].astype(F32)
        for part, block in enumerate((x_rim, y_low, y_high)):
            start = span + part * edge
            rim32[g, start : start + edge, :] = block[g * edge : (g + 1) * edge, :].astype(F32)
        start = span + 3 * edge
        rim32[g, start : start + 4, :] = xy_low[4 * g : 4 * g + 4, :]
        rim32[g, start + 4 : start + 8, :] = xy_high[4 * g : 4 * g + 4, :]
        rim32[g, start + 8 :, :] = jnp.zeros((rim32.shape[1] - start - 8, wide), F32)
        moved = matmul(picks, rim32[g].astype(BF16)).astype(BF16)
        for bc in range(9):
            window[quarter + g * span : quarter + (g + 1) * span, bc * wide : (bc + 1) * wide] = moved[
                bc * span : (bc + 1) * span, :
            ]
    spread_out = None
    for bc in range(9):
        weight = jnp.concatenate([w_bottle[9 * a + bc] for a in range(3)], axis=1)
        term = matmul(window[:, bc * wide : (bc + 1) * wide], weight)
        spread_out = term if spread_out is None else spread_out + term
    pre = spread_out[:cells, :outs]
    for a in range(1, 3):
        pre = pre + spread_out[a * quarter : a * quarter + cells, a * outs : (a + 1) * outs]
    sig = jax.nn.sigmoid(pre)
    bottle[...] = (pre * sig).astype(BF16)
    slope = sig * (1.0 + pre * (1.0 - sig))
    value = (back[...].astype(F32) * slope).astype(BF16)
    grad[...] = value
    grad_far[:cells, :] = value
    grad_far[cells:, :] = far[...]


def slices_kernel(count_y, quarter, column, *refs):
    sends, slices = refs[:-1], refs[-1]
    cells, wide = column.shape
    span = 4 * quarter
    half = 2 * quarter
    lane = lax.broadcasted_iota(jnp.int32, (half, 128), 1)
    for pair in range(wide // 128):
        for g in range(cells // span):
            top = column[g * span : g * span + half, pair * 128 : (pair + 1) * 128].astype(F32)
            end = column[g * span + half : (g + 1) * span, pair * 128 : (pair + 1) * 128].astype(F32)
            rows = slice(g * half, (g + 1) * half)
            slices[2 * pair, rows, :] = jnp.where(lane < 64, top, pltpu.roll(end, 64, 1)).astype(BF16)
            slices[2 * pair + 1, rows, :] = jnp.where(lane < 64, pltpu.roll(top, 64, 1), end).astype(BF16)
    p = plane_index(count_y)
    lines = slices.shape[1]
    for i, send in enumerate(sends):
        send[:lines, :] = slices[p ^ (2 * i)]
        send[lines:, :] = slices[p ^ (2 * i + 1)]


def relay_kernel(*refs):
    parts, send = refs[:-1], refs[-1]
    lines = send.shape[0] // len(parts)
    for i, part in enumerate(parts):
        send[i * lines : (i + 1) * lines, :] = part[lines:, :]


def coarse_grad_kernel(count_y, count_z, quarter, *refs):
    grads, (bottle, shift, w_bottle) = refs[: -count_z - 6], refs[-count_z - 6 : -count_z - 3]
    sends, (window, gathered, blocks) = refs[-count_z - 3 : -3], refs[-3:]
    count_p = len(grads)
    cells, outs = bottle.shape
    rows = count_p * quarter
    depth = cells // quarter
    own_cells = cells // count_z
    inputs = w_bottle.shape[1]
    p = plane_index(count_y)
    take_in([part.at[:cells, :] for part in grads], gathered, p)
    mine = pl.multiple_of(p * quarter, quarter)
    picks = jnp.concatenate([shift[pl.ds((8 - bc) * rows + mine, quarter), :] for bc in range(9)], axis=0)
    window[:quarter, :] = jnp.zeros((quarter, 9 * outs), BF16)
    window[(depth + 1) * quarter :, :] = jnp.zeros((quarter, 9 * outs), BF16)
    for z in range(depth):
        plane = jnp.concatenate([gathered[q, z * quarter : (z + 1) * quarter, :] for q in range(count_p)], axis=0)
        moved = matmul(picks, plane).astype(BF16)
        for bc in range(9):
            window[(z + 1) * quarter : (z + 2) * quarter, bc * outs : (bc + 1) * outs] = moved[
                bc * quarter : (bc + 1) * quarter, :
            ]
    total = None
    for a in range(3):
        weight = jnp.concatenate([w_bottle[9 * a + bc] for bc in range(9)], axis=1)
        term = matmul_nt(window[(2 - a) * quarter : (2 - a + depth) * quarter, :], weight)
        total = term if total is None else total + term
    total = total.astype(BF16)
    for q in range(count_z):
        blocks[q, :, :inputs] = total[q * own_cells : (q + 1) * own_cells, :]
        blocks[q, :, inputs:] = bottle[q * own_cells : (q + 1) * own_cells, :]
    hand_out(blocks, sends, lax.axis_index("gz"))


def wide_kernel(count_y, quarter, *refs):
    parts, (wide, grads) = refs[:-2], refs[-2:]
    count_p, cells, outs = grads.shape
    rows = count_p * quarter
    depth = cells // quarter
    take_in([part.at[:cells, :] for part in parts], grads, plane_index(count_y))
    planes = [
        jnp.concatenate([grads[q, z * quarter : (z + 1) * quarter, :] for q in range(count_p)], axis=0)
        for z in range(depth)
    ]
    zeros = jnp.zeros((rows, outs), BF16)
    for j in range(depth // 2):
        for slot in range(5):
            z = j // 2 * 4 + j % 2 + slot - 1
            wide[j * rows : (j + 1) * rows, slot * outs : (slot + 1) * outs] = planes[z] if 0 <= z < depth else zeros


def grad_bottle_kernel(count_y, shift, wide, *refs):
    out, turned, slices = refs[-3:]
    firsts, far, far_relayed, relayed = refs[:-6], *refs[-6:-3]
    count_p = slices.shape[0]
    outs = out.shape[2]
    lines = slices.shape[1]
    rows = shift.shape[1]
    quarter = rows // count_p
    depth = 2 * wide.shape[0] // rows
    channels = out.shape[1]
    p = plane_index(count_y)
    for i, part in enumerate(firsts):
        slices[p ^ (2 * i)] = part[:lines, :]
        slices[p ^ (2 * i + 1)] = relayed[i * lines : (i + 1) * lines, :]
    cells = far.shape[0] // 2
    slices[p ^ (count_p - 2)] = far[cells : cells + lines, :]
    slices[p ^ (count_p - 1)] = far_relayed[cells + lines :, :]
    for j in range(depth // 2):
        plane = jnp.concatenate([slices[q, j * quarter : (j + 1) * quarter, :] for q in range(count_p)], axis=0)
        plane = plane.astype(F32).T.astype(BF16)
        for bc in range(9):
            turned[bc * 128 : (bc + 1) * 128, j * rows : (j + 1) * rows] = matmul(
                plane, shift[(8 - bc) * rows : (9 - bc) * rows, :]
            ).astype(BF16)
    full = matmul(turned[...], wide[...])
    for bc in range(9):
        top = full[bc * 128 : bc * 128 + channels, :]
        end = full[bc * 128 + channels : (bc + 1) * 128, :]
        for a in range(3):
            out[9 * a + bc] = top[:, (2 - a) * outs : (3 - a) * outs] + end[:, (4 - a) * outs : (5 - a) * outs]


def half_grad(turned, shifted, parity, chip, out, blocks):
    chips, rows, channels = blocks.shape
    group = rows // 27
    full = matmul(turned[parity], shifted[...])
    for bc in range(9):
        for a in range(3):
            t = 9 * a + bc
            for q in range(chips):
                start = (bc * chips + q) * group
                blocks[q, t * group : (t + 1) * group, :] = full[
                    start : start + group, a * channels : (a + 1) * channels
                ].astype(BF16)
    for i in range(chips):
        out[i] = blocks[chip ^ i]


def hidden_grad_kernel(count_y, count_z, *refs):
    parts, (slope, ordered, w_down, turned) = refs[:count_z], refs[count_z : count_z + 4]
    shifted, bottle, give, bottles, blocks = refs[count_z + 4 :]
    size_z, own, channels = ordered.shape
    quarter = own // 4
    inputs = w_down.shape[2]
    pz = lax.axis_index("gz")
    grad = total_of([part.at[:, :inputs] for part in parts]).astype(BF16)
    for d, part in enumerate(parts):
        bottles[pz ^ d] = part[:, inputs:]
    bottle[...] = jnp.concatenate([bottles[q] for q in range(count_z)], axis=1)
    shifted[...] = jnp.zeros_like(shifted)
    for s in range(8):
        a, bc = s // 4, s % 4
        spread_grad = matmul_nt(grad, w_down[s])
        for kz in range(size_z // 2):
            z = 2 * kz + a
            part = slice(bc * quarter, (bc + 1) * quarter)
            line = slice(kz * quarter, (kz + 1) * quarter)
            value = ((spread_grad[line, :] + ordered[z, part, :].astype(F32)) * slope[z, part, :]).astype(BF16)
            for t in range(3):
                start = (z + t) * own + bc * quarter
                shifted[start : start + quarter, t * channels : (t + 1) * channels] = value
    p = plane_index(count_y)
    half_grad(turned, shifted, 1 - p % 2, p // 2, give, blocks)


def keep_kernel(count_y, shifted, turned, keep, blocks):
    p = plane_index(count_y)
    half_grad(turned, shifted, p % 2, p // 2, keep, blocks)


def output_kernel(bottle, hidden, w_up, order_t, output, rows_out):
    size_z, own, channels = hidden.shape
    quarter = own // 4
    for s in range(8):
        a, bc = s // 4, s % 4
        lifted = matmul(bottle[...], w_up[s])
        for kz in range(size_z // 2):
            z = 2 * kz + a
            part = slice(bc * quarter, (bc + 1) * quarter)
            line = slice(kz * quarter, (kz + 1) * quarter)
            rows_out[z, part, :] = (lifted[line, :] + hidden[z, part, :].astype(F32)).astype(BF16)
    for z in range(size_z):
        plane = matmul(order_t[...], rows_out[z])
        output[z] = plane.reshape(output.shape[1:]).astype(BF16)


def pair_sum_kernel(keep, got, *sends):
    for i, send in enumerate(sends):
        send[...] = (keep[i].astype(F32) + got[i].astype(F32)).astype(BF16)


def sum_kernel(*refs):
    out = refs[-1]
    out[...] = total_of(refs[:-1]).reshape(out.shape).astype(out.dtype)


def shape_of(shape, dtype=BF16):
    return jax.ShapeDtypeStruct(shape, dtype)


def gathered_body(counts, volume, cotangent, w_conv, w_down, w_bottle, w_up):
    count_x, count_y, count_z = counts
    count_p = count_x * count_y
    size_z, size_x, size_y, channels = volume.shape
    wide = w_down.shape[2]
    group = w_bottle.shape[2]
    half_x, half_y = size_x // 2, size_y // 2
    own = size_x * size_y
    quarter = half_x * half_y
    own_cells = size_z // 2 * quarter
    cells = count_z * own_cells
    depth = count_z * size_z // 2
    rows = count_p * quarter
    planes = size_z + 2
    share_c = channels // count_p
    share_w = wide // count_p
    plane_axes = ("gx", "gy")

    order, taps = fine_maps(size_x, size_y)
    pair_taps = np.zeros((2, 2 * own, 9, 2, own), np.float32)
    for i in range(2):
        pair_taps[i, :, :, i, :] = taps.transpose(2, 0, 1)
    shift = coarse_maps(count_x, count_y, half_x, half_y)
    order_m = jnp.asarray(order, BF16)
    order_t = jnp.asarray(order.T, BF16)
    taps_m = jnp.asarray(taps.reshape(9 * own, 2 * own), BF16)
    taps_t = jnp.asarray(pair_taps.reshape(4 * own, 18 * own), BF16)
    shift_m = jnp.asarray(shift.reshape(9 * rows, rows), BF16)

    send_maps, rim_maps = column_maps(half_x, half_y, depth)
    send_m = jnp.asarray(send_maps, BF16)
    rim_m = jnp.asarray(rim_maps.reshape(count_x, 36 * quarter, 8 * quarter), BF16)

    w_conv_t = jnp.transpose(w_conv, (1, 0, 2))
    w_bottle_t = jnp.transpose(w_bottle, (1, 0, 2))
    send_a, send_b = local_call(ends_kernel, "ends", [shape_of((size_x, size_y, channels))] * 2)(volume)
    z_pairs = line_pairs(count_z)
    z_b = lax.ppermute(send_b, "gz", z_pairs[1])
    z_a = lax.ppermute(send_a, "gz", z_pairs[0])
    *backs, ordered = local_call(
        lambda *refs: back_kernel(count_z, *refs),
        "back",
        [shape_of((own_cells, group))] * count_z + [shape_of((size_z, own, channels))],
        [pltpu.VMEM((count_z, own_cells, group), BF16)],
    )(cotangent, w_up, order_m)
    sends = local_call(
        faces_kernel,
        "faces",
        [shape_of((16 * size_y, channels))] + [shape_of((planes * size_x, channels))] * 2 + [shape_of((16, channels))],
        [pltpu.VMEM((16 * own, channels), F32)],
    )(volume, z_a, z_b)
    x_send, send_a, send_b, corner_b = sends
    x_rim, across, corner = swap_rims(x_send, send_b, corner_b, counts)
    relayed = relay_rims(x_rim, across, corner, send_a, counts)
    hidden, slope, rim, *sends = local_call(
        lambda *refs: hidden_kernel(count_z, *refs),
        "hidden",
        [
            shape_of((size_z, own, channels)),
            shape_of((size_z, own, channels), F32),
            shape_of((planes, 2 * own, channels)),
        ]
        + [shape_of((own_cells, wide + group))] * count_z,
        [
            pltpu.VMEM((planes * 2 * own, channels), F32),
            pltpu.VMEM((planes, own, 9 * channels), BF16),
        ],
        flops=2_000_000_000,
    )(volume, z_a, z_b, x_rim, relayed, taps_m, w_conv_t, w_down, *backs)
    parts = trade(sends, "gz", count_z)
    column, back, *sends = local_call(
        lambda *refs: column_kernel(count_z, *refs),
        "column",
        [shape_of((cells, wide)), shape_of((cells, group)), shape_of((depth * half_y, wide))]
        + [shape_of((depth * half_x, wide))] * 2
        + [shape_of((depth, wide))],
    )(parts[0], *parts[:0:-1], send_m)
    x_send, send_a, send_b, corner_b = sends
    x_rim, across, corner = swap_rims(x_send, send_b, corner_b, counts)
    relayed = relay_rims(x_rim, across, corner, send_a, counts)
    slices = local_call(
        lambda *refs: slices_kernel(count_y, quarter, *refs),
        "slices",
        [shape_of((cells, 128))] * (count_p // 2),
        [pltpu.VMEM((count_p, cells // 2, 128), BF16)],
    )(column)
    column, *slices, far = lax.optimization_barrier((column, *slices))
    bottle, grad, grad_far = local_call(
        lambda *refs: bottle_kernel(quarter, *refs),
        "bottle",
        [shape_of((cells, group))] * 2 + [shape_of((2 * cells, group))],
        [
            pltpu.VMEM((depth // 4, 8 * quarter, wide), F32),
            pltpu.VMEM(((depth + 2) * quarter, 9 * wide), BF16),
        ],
        flops=2_000_000_000,
    )(column, back, x_rim, relayed, rim_m, w_bottle_t, far)
    grads = [None] * count_p
    grads[0] = grad
    for d in (6, 4, 2):
        grads[d] = swap(grad_far if d == 6 else grad, plane_axes, count_p, d)
    for d in (0, 2, 4, 6):
        grads[d + 1] = swap(grads[d], plane_axes, count_p, 1)
    sends = local_call(
        lambda *refs: coarse_grad_kernel(count_y, count_z, quarter, *refs),
        "coarse_grad",
        [shape_of((own_cells, wide + group))] * count_z,
        [
            pltpu.VMEM(((depth + 2) * quarter, 9 * group), BF16),
            pltpu.VMEM((count_p, cells, group), BF16),
            pltpu.VMEM((count_z, own_cells, wide + group), BF16),
        ],
    )(*grads, bottle, shift_m, w_bottle_t)
    parts = trade(sends, "gz", count_z)
    rim, _ = lax.optimization_barrier((rim, sends[1]))
    turned = local_call(
        lambda *refs: rim_transpose_kernel(count_p, *refs),
        "rim_transpose",
        shape_of((2, 9 * channels // 2, planes * own)),
    )(rim, taps_t)
    *slices, _ = lax.optimization_barrier((*slices, parts[1]))
    firsts = [slices[0]] + [swap(slices[d // 2], plane_axes, count_p, d) for d in (2, 4)]
    parts = lax.optimization_barrier((*parts, *firsts))[:count_z]
    shifted, bottle, give = local_call(
        lambda *refs: hidden_grad_kernel(count_y, count_z, *refs),
        "hidden_grad",
        [
            shape_of((planes * own, 3 * channels)),
            shape_of((own_cells, wide)),
            shape_of((count_p // 2, 27 * share_c, channels)),
        ],
        [
            pltpu.VMEM((count_z, own_cells, group), BF16),
            pltpu.VMEM((count_p // 2, 27 * share_c, channels), BF16),
        ],
    )(*parts, slope, ordered, w_down, turned)
    got = swap(give, plane_axes, count_p, 1)
    *late, _ = lax.optimization_barrier((*firsts, give))
    relay = local_call(relay_kernel, "relay", shape_of((len(late) * (cells // 2), 128)))(*late)
    relayed = swap(relay, plane_axes, count_p, 1)
    keep = local_call(
        lambda *refs: keep_kernel(count_y, *refs),
        "keep",
        shape_of((count_p // 2, 27 * share_c, channels)),
        [pltpu.VMEM((count_p // 2, 27 * share_c, channels), BF16)],
    )(shifted, turned)
    output = local_call(
        output_kernel,
        "output",
        shape_of(volume.shape),
        [pltpu.VMEM((size_z, own, channels), BF16)],
    )(bottle, hidden, w_up, order_t)
    sends = local_call(
        pair_sum_kernel,
        "pair_sum",
        [shape_of((27 * share_c, channels))] * (count_p // 2),
    )(keep, got)
    parts = [sends[0]] + [swap(sends[d // 2], plane_axes, count_p, d) for d in (6, 4, 2)]
    part = local_call(sum_kernel, "plane_sum", shape_of((27 * share_c, channels)))(*parts)
    part, output = lax.optimization_barrier((part, output))
    got = swap(part, "gz", count_z, 1)
    wide_grads = local_call(
        lambda *refs: wide_kernel(count_y, quarter, *refs),
        "wide",
        shape_of((depth // 2 * rows, 5 * group)),
        [pltpu.VMEM((count_p, cells, group), BF16)],
    )(*grads)
    got, wide_grads = lax.optimization_barrier((got, wide_grads))
    part = local_call(sum_kernel, "depth_sum", shape_of((27 * share_c, channels)))(part, got)
    got = swap(part, "gz", count_z, 2)
    grad_bottle = local_call(
        lambda *refs: grad_bottle_kernel(count_y, *refs),
        "grad_bottle",
        shape_of((27, share_w, group), F32),
        [
            pltpu.VMEM((18 * share_w, depth // 2 * rows), BF16),
            pltpu.VMEM((count_p, cells // 2, 128), BF16),
        ],
        flops=4_000_000_000,
    )(shift_m, wide_grads, *firsts, *grads[-2:], relayed)
    grad_conv = local_call(
        sum_kernel,
        "grad_conv",
        shape_of((27, share_c, channels), F32),
    )(part, got)
    return (output, jnp.transpose(grad_conv, (1, 0, 2)), jnp.transpose(grad_bottle, (1, 0, 2)))


def with_halo(cells, sides, width):
    for axis, dim in sides:
        count = lax.axis_size(axis)
        ends = count - 1
        head = lax.slice_in_dim(cells, 0, width, axis=dim)
        tail = lax.slice_in_dim(cells, cells.shape[dim] - width, cells.shape[dim], axis=dim)
        cells = jnp.concatenate(
            [
                lax.ppermute(tail, axis, [(i, (i + 1) % count) for i in range(ends)]),
                cells,
                lax.ppermute(head, axis, [((i + 1) % count, i) for i in range(ends)]),
            ],
            axis=dim,
        )
    return cells


def silu_slope(values):
    sig = jax.nn.sigmoid(values)
    return sig * (1.0 + values * (1.0 - sig))


def conv_forward(padded, weight, extent):
    size_z, size_x, size_y = extent
    count_cells = size_z * size_x * size_y
    summed = jnp.zeros((count_cells, weight.shape[2]), jnp.float32)
    for tap_index in range(27):
        shift_z, shift_x, shift_y = (tap_index // 9, tap_index // 3 % 3, tap_index % 3)
        window = padded[
            shift_z : shift_z + size_z, shift_x : shift_x + size_x, shift_y : shift_y + size_y, :
        ]
        window = window.reshape(count_cells, padded.shape[3])
        summed = summed + jnp.dot(
            window, weight[:, tap_index, :], preferred_element_type=jnp.float32
        )
    return summed.reshape(size_z, size_x, size_y, weight.shape[2])


def conv_weight_grad(padded, gradient, extent):
    size_z, size_x, size_y = extent
    count_cells = size_z * size_x * size_y
    flat_gradient = gradient.reshape(count_cells, gradient.shape[3])
    pieces = []
    for tap_index in range(27):
        shift_z, shift_x, shift_y = (tap_index // 9, tap_index // 3 % 3, tap_index % 3)
        window = padded[
            shift_z : shift_z + size_z, shift_x : shift_x + size_x, shift_y : shift_y + size_y, :
        ]
        window = window.reshape(count_cells, padded.shape[3])
        pieces.append(
            lax.dot_general(
                window, flat_gradient, (((0,), (0,)), ((), ())), preferred_element_type=jnp.float32
            )
        )
    return jnp.stack(pieces, axis=1)


def conv_input_grad(padded, weight, extent):
    size_z, size_x, size_y = extent
    count_cells = size_z * size_x * size_y
    summed = jnp.zeros((count_cells, weight.shape[0]), jnp.float32)
    for tap_index in range(27):
        shift_z, shift_x, shift_y = (2 - tap_index // 9, 2 - tap_index // 3 % 3, 2 - tap_index % 3)
        window = padded[
            shift_z : shift_z + size_z, shift_x : shift_x + size_x, shift_y : shift_y + size_y, :
        ]
        window = window.reshape(count_cells, padded.shape[3])
        summed = summed + lax.dot_general(
            window,
            weight[:, tap_index, :],
            (((1,), (1,)), ((), ())),
            preferred_element_type=jnp.float32,
        )
    return summed.reshape(size_z, size_x, size_y, weight.shape[0])


def pool_features(fine, kernel):
    size_z, size_x, size_y, channels = fine.shape
    blocks = fine.reshape(size_z // 2, 2, size_x // 2, 2, size_y // 2, 2, channels)
    kernel_cube = kernel.reshape(2, 2, 2, kernel.shape[1], kernel.shape[2])
    return jnp.einsum(
        "zaxbycf,abcfg->zxyg", blocks, kernel_cube, preferred_element_type=jnp.float32
    )


def pool_adjoint(coarse_in, kernel):
    size_z, size_x, size_y, wide_channels = coarse_in.shape
    kernel_cube = kernel.reshape(2, 2, 2, kernel.shape[1], kernel.shape[2])
    result = jnp.einsum(
        "zxyg,abcfg->zaxbycf", coarse_in, kernel_cube, preferred_element_type=jnp.float32
    )
    return result.reshape(2 * size_z, 2 * size_x, 2 * size_y, kernel.shape[1])


def lift_features(coarse_in, kernel):
    size_z, size_x, size_y, wide_channels = coarse_in.shape
    kernel_cube = kernel.reshape(2, 2, 2, kernel.shape[1], kernel.shape[2])
    result = jnp.einsum(
        "zxyg,abcgf->zaxbycf", coarse_in, kernel_cube, preferred_element_type=jnp.float32
    )
    return result.reshape(2 * size_z, 2 * size_x, 2 * size_y, kernel.shape[2])


def lift_adjoint(fine, kernel):
    size_z, size_x, size_y, channels = fine.shape
    blocks = fine.reshape(size_z // 2, 2, size_x // 2, 2, size_y // 2, 2, channels)
    kernel_cube = kernel.reshape(2, 2, 2, kernel.shape[1], kernel.shape[2])
    return jnp.einsum(
        "zaxbycf,abcgf->zxyg", blocks, kernel_cube, preferred_element_type=jnp.float32
    )


def column_body(volume, cotangent, w_conv, w_down, w_bottle, w_up):
    size_z, size_x, size_y, channels = volume.shape
    group_channels = w_bottle.shape[2]
    half_x = size_x // 2
    half_y = size_y // 2
    padded = with_halo(volume, (("gx", 1), ("gy", 2), ("gz", 0)), 1)
    pre_hidden = conv_forward(padded, w_conv, (size_z, size_x, size_y))
    hidden = jax.nn.silu(pre_hidden).astype(jnp.bfloat16)
    hidden_slope = silu_slope(pre_hidden)
    coarse = pool_features(hidden, w_down).astype(jnp.bfloat16)
    stacked = lax.all_gather(coarse, "gz", axis=0, tiled=True)
    rimmed = with_halo(stacked, (("gx", 1), ("gy", 2)), 1)
    column_z = rimmed.shape[0]
    coarse_pad = jnp.pad(rimmed, ((1, 1), (0, 0), (0, 0), (0, 0)))
    pre_bottle = conv_forward(coarse_pad, w_bottle, (column_z, half_x, half_y))
    bottle = jax.nn.silu(pre_bottle).astype(jnp.bfloat16)
    bottle_slope = silu_slope(pre_bottle)
    own_start = lax.axis_index("gz") * group_channels
    own_up = lax.dynamic_slice_in_dim(w_up, own_start, group_channels, 1)
    lifted = lax.psum_scatter(
        lift_features(bottle, own_up).astype(jnp.bfloat16), "gz", scatter_dimension=0, tiled=True
    ).astype(jnp.float32)
    output = (lifted + hidden.astype(jnp.float32)).astype(jnp.bfloat16)
    back_bottle = lift_adjoint(cotangent, w_up).astype(jnp.bfloat16)
    split_grad = lax.all_to_all(back_bottle, "gz", split_axis=3, concat_axis=0, tiled=True)
    bottle_grad = (split_grad.astype(jnp.float32) * bottle_slope).astype(jnp.bfloat16)
    grad_bottle = lax.psum_scatter(
        conv_weight_grad(coarse_pad, bottle_grad, (column_z, half_x, half_y)),
        ("gx", "gy"),
        scatter_dimension=0,
        tiled=True,
    )
    grad_rimmed = with_halo(bottle_grad, (("gx", 1), ("gy", 2)), 1)
    grad_pad = jnp.pad(grad_rimmed, ((1, 1), (0, 0), (0, 0), (0, 0)))
    coarse_grad = lax.psum_scatter(
        conv_input_grad(
            grad_pad, w_bottle, (lax.axis_size("gz") * (size_z // 2), half_x, half_y)
        ).astype(jnp.bfloat16),
        "gz",
        scatter_dimension=0,
        tiled=True,
    )
    hidden_grad = (
        (pool_adjoint(coarse_grad, w_down) + cotangent.astype(jnp.float32)) * hidden_slope
    ).astype(jnp.bfloat16)
    full_term = conv_weight_grad(padded, hidden_grad, (size_z, size_x, size_y))
    depth_summed = lax.psum(full_term.astype(jnp.bfloat16), "gz").astype(jnp.float32)
    grad_conv = lax.psum_scatter(depth_summed, ("gx", "gy"), scatter_dimension=0, tiled=True)
    return (output, grad_conv, grad_bottle)


def fits_one_plane(counts, brick, wide):
    count_p = counts[0] * counts[1]
    size_z, size_x, size_y, channels = brick
    return (
        counts == (2, 4, 4)
        and count_p * (size_x // 2) * (size_y // 2) == 128
        and wide // count_p == 64
        and (size_z, size_x, size_y, channels) == (8, 8, 8, 128)
    )


def solution(mesh):
    in_specs = (
        P("gz", "gx", "gy", None),
        P("gz", "gx", "gy", None),
        P(),
        P(),
        P(None, None, "gz"),
        P(),
    )
    out_specs = (
        P("gz", "gx", "gy", None),
        P(("gx", "gy"), None, None),
        P(("gx", "gy"), None, "gz"),
    )
    counts = (mesh.shape["gx"], mesh.shape["gy"], mesh.shape["gz"])

    def body(volume, cotangent, w_conv, w_down, w_bottle, w_up):
        if fits_one_plane(counts, volume.shape, w_down.shape[2]):
            return gathered_body(counts, volume, cotangent, w_conv, w_down, w_bottle, w_up)
        return column_body(volume, cotangent, w_conv, w_down, w_bottle, w_up)

    return jax.shard_map(body, mesh=mesh, in_specs=in_specs, out_specs=out_specs, check_vma=False)
```

```python
import numpy as np
import jax
import jax.numpy as jnp
from jax import lax
from jax.experimental import pallas as pl
from jax.experimental.pallas import tpu as pltpu
from jax.sharding import PartitionSpec as P

BF16 = jnp.bfloat16
F32 = jnp.float32
VMEM_LIMIT = 24 * 1024 * 1024


def local_call(kernel, name, out_shapes, scratch=(), flops=300_000_000):
    whole = pl.BlockSpec(memory_space=pltpu.VMEM)

    def call(*operands):
        return pl.pallas_call(
            kernel,
            name=name,
            out_shape=out_shapes,
            in_specs=[whole] * len(operands),
            out_specs=jax.tree.map(lambda _: whole, out_shapes),
            scratch_shapes=list(scratch),
            compiler_params=pltpu.CompilerParams(vmem_limit_bytes=VMEM_LIMIT),
            cost_estimate=pl.CostEstimate(flops=flops, bytes_accessed=flops // 1000, transcendentals=0),
        )(*operands)

    return call


def matmul(left, right):
    return jnp.dot(left, right, preferred_element_type=F32)


def matmul_nt(left, right):
    return lax.dot_general(left, right, (((1,), (1,)), ((), ())), preferred_element_type=F32)


def sub_order(size_x, size_y):
    half_x, half_y = size_x // 2, size_y // 2
    return {
        (2 * kx + b, 2 * ky + c): ((2 * b + c) * half_x + kx) * half_y + ky
        for b in range(2)
        for c in range(2)
        for kx in range(half_x)
        for ky in range(half_y)
    }


def fine_maps(size_x, size_y):
    own = size_x * size_y
    rows = sub_order(size_x, size_y)
    order = np.zeros((own, own), np.float32)
    taps = np.zeros((9, own, 2 * own), np.float32)
    for (x, y), row in rows.items():
        order[row, x * size_y + y] = 1
        for b in range(3):
            for c in range(3):
                sx, sy = x + b - 1, y + c - 1
                if sx < 0:
                    part = 0 if 0 <= sy < size_y else (4 if sy < 0 else 5)
                    source = own + 8 * part + sy % size_y
                elif sx >= size_x:
                    part = 1 if 0 <= sy < size_y else (6 if sy < 0 else 7)
                    source = own + 8 * part + sy % size_y
                elif sy < 0:
                    source = own + 16 + sx
                elif sy >= size_y:
                    source = own + 24 + sx
                else:
                    source = sx * size_y + sy
                taps[3 * b + c, row, source] = 1
    return order, taps


def coarse_maps(count_x, count_y, half_x, half_y):
    wide_x, wide_y = count_x * half_x, count_y * half_y

    def row_of(x, y):
        brick = (x // half_x) * count_y + y // half_y
        return (brick * half_x + x % half_x) * half_y + y % half_y

    shift = np.zeros((9, wide_x * wide_y, wide_x * wide_y), np.float32)
    for x in range(wide_x):
        for y in range(wide_y):
            for b in range(3):
                for c in range(3):
                    sx, sy = x + b - 1, y + c - 1
                    if 0 <= sx < wide_x and 0 <= sy < wide_y:
                        shift[3 * b + c, row_of(x, y), row_of(sx, sy)] = 1
    return shift


def column_maps(half_x, half_y, depth):
    quarter = half_x * half_y
    rows = depth * quarter
    send = np.zeros((2, depth * (half_y + 2 * half_x + 2), rows), np.float32)
    rim = np.zeros((2, 9, 4, quarter, 8 * quarter), np.float32)
    for px in range(2):
        edge = 0 if px else half_x - 1
        for z in range(depth):
            base = z * quarter
            for ky in range(half_y):
                send[px, z * half_y + ky, base + edge * half_y + ky] = 1
            for side, ky in enumerate((0, half_y - 1)):
                row = depth * (half_y + side * half_x) + z * half_x
                for kx in range(half_x):
                    send[px, row + kx, base + kx * half_y + ky] = 1
                send[px, depth * (half_y + 2 * half_x + side) + z, base + edge * half_y + ky] = 1
    for px in range(2):
        for b in range(3):
            for c in range(3):
                for kx in range(half_x):
                    for ky in range(half_y):
                        sx, sy = kx + b - 1, ky + c - 1
                        beyond = sx < 0 if px else sx >= half_x
                        if (sx < 0 or sx >= half_x) and not beyond:
                            continue
                        for z in range(4):
                            if beyond and 0 <= sy < half_y:
                                source = 4 * quarter + z * half_y + sy
                            elif beyond:
                                source = 7 * quarter + 4 * (sy >= half_y) + z
                            elif sy < 0:
                                source = 5 * quarter + z * half_x + sx
                            elif sy >= half_y:
                                source = 6 * quarter + z * half_x + sx
                            else:
                                source = z * quarter + sx * half_y + sy
                            rim[px, 3 * b + c, z, kx * half_y + ky, source] = 1
    return send, rim


def swap(block, axes, count, distance):
    return lax.ppermute(block, axes, [(i, i ^ distance) for i in range(count)])


def trade(blocks, axes, count):
    got = {d: swap(blocks[d], axes, count, d) for d in reversed(range(1, count))}
    return [blocks[0]] + [got[d] for d in range(1, count)]


def line_pairs(length):
    first = [(i, i ^ 1) for i in range(length)]
    second = [(i, i + 1 if i % 2 else i - 1) for i in range(1, length - 1)]
    return first, second


def swap_rims(x_send, send_b, corner_b, counts):
    count_x, count_y, _ = counts
    axes, count = ("gx", "gy"), count_x * count_y
    corner = swap(corner_b, axes, count, count_y + 2)
    x_rim = swap(x_send, axes, count, count_y)
    across = swap(send_b, axes, count, 2)
    return x_rim, across, corner


def line_sides(axis, pair_a, pair_b):
    even = lax.axis_index(axis) % 2 == 0
    return jnp.where(even, pair_b, pair_a), jnp.where(even, pair_a, pair_b)


def relay_rims_kernel(x_rim, across, corner, send_a, send, side):
    face, lines = across.shape[0], corner.shape[0]
    pitch = x_rim.shape[0] // lines
    even = lax.axis_index("gy") % 2 == 0
    for part in range(0, x_rim.shape[1], 128):
        columns = slice(part, part + 128)
        side[...] = x_rim[:, columns].astype(F32)
        ends = [side[pl.ds(y, lines, stride=pitch), :] for y in (pitch - 1, 0)]
        send[face + lines : face + 2 * lines, columns] = jnp.where(even, ends[0], ends[1]).astype(BF16)
    send[face + 2 * lines :, :] = send_a[...]
    send[:face, :] = across[...]
    send[face : face + lines, :] = corner[...]


def relay_rims(x_rim, across, corner, send_a, counts):
    rows = 2 * (across.shape[0] + corner.shape[0])
    send = local_call(
        relay_rims_kernel,
        "relay_rims",
        shape_of((rows, across.shape[1])),
        [pltpu.VMEM((x_rim.shape[0], 128), F32)],
    )(x_rim, across, corner, send_a)
    return swap(send, ("gx", "gy"), counts[0] * counts[1], 1)


def y_rims(relayed, lines):
    py = lax.axis_index("gy")
    face = relayed.shape[0] // 2 - lines
    inner = (py > 0) & (py < lax.axis_size("gy") - 1)
    face_b = jnp.where(inner, relayed[:face, :].astype(F32), 0.0)
    corner_b = jnp.where(inner, relayed[face : face + lines, :].astype(F32), 0.0)
    corner_a = relayed[face + lines : face + 2 * lines, :].astype(F32)
    face_a = relayed[face + 2 * lines :, :].astype(F32)
    return *line_sides("gy", face_a, face_b), *line_sides("gy", corner_a, corner_b)


def plane_index(count_y):
    return lax.axis_index("gx") * count_y + lax.axis_index("gy")


def plane_rows(ref, z):
    _, size_x, size_y, channels = ref.shape
    return ref[z].astype(F32).reshape(size_x * size_y, channels)


def hand_out(blocks, outs, me):
    for d, out in enumerate(outs):
        out[...] = blocks[me ^ d]


def take_in(parts, blocks, me):
    for d, part in enumerate(parts):
        blocks[me ^ d] = part[...]


def total_of(parts):
    terms = [part[...].astype(F32) for part in parts]
    while len(terms) > 1:
        terms = [terms[i] + terms[i + 1] for i in range(0, len(terms), 2)]
    return terms[0]


def back_kernel(count_z, cotangent, w_up, order, *refs):
    sends, (ordered, blocks) = refs[:count_z], refs[count_z:]
    size_z, size_x, size_y, channels = cotangent.shape
    own = size_x * size_y
    quarter = own // 4
    for z in range(size_z):
        ordered[z] = matmul(order[...], plane_rows(cotangent, z).astype(BF16)).astype(BF16)
    back = None
    for s in range(8):
        a, bc = s // 4, s % 4
        cells = jnp.concatenate(
            [ordered[2 * kz + a, bc * quarter : (bc + 1) * quarter, :] for kz in range(size_z // 2)], axis=0
        )
        term = matmul_nt(cells, w_up[s])
        back = term if back is None else back + term
    back = back.astype(BF16)
    group = back.shape[1] // count_z
    for q in range(count_z):
        blocks[q] = back[:, q * group : (q + 1) * group]
    hand_out(blocks, sends, lax.axis_index("gz"))


def deepen(volume, z_a, z_b, deep, pitch):
    size_z, size_x, size_y, channels = volume.shape
    own = size_x * size_y
    below, above = line_sides("gz", z_a[...], z_b[...])
    deep[:own, :] = below.astype(F32).reshape(own, channels)
    for z in range(size_z):
        deep[(z + 1) * pitch : (z + 1) * pitch + own, :] = plane_rows(volume, z)
    deep[(size_z + 1) * pitch : (size_z + 1) * pitch + own, :] = above.astype(F32).reshape(own, channels)


def ends_kernel(volume, send_a, send_b):
    below, above = volume[0], volume[volume.shape[0] - 1]
    send_b[...], send_a[...] = line_sides("gz", above, below)


def faces_kernel(volume, z_a, z_b, x_send, send_a, send_b, corner_b, deep):
    size_z, size_x, size_y, channels = volume.shape
    own = size_x * size_y
    planes = x_send.shape[0] // size_y
    deepen(volume, z_a, z_b, deep, own)
    start = (size_z + 2) * own
    deep[start:, :] = jnp.zeros((deep.shape[0] - start, channels), F32)
    first = lax.axis_index("gx") == 0
    far = (size_x - 1) * size_y

    def x_face(start):
        return jnp.concatenate([deep[z * own + start : z * own + start + size_y, :] for z in range(planes)], axis=0)

    x_send[...] = jnp.where(first, x_face(far), x_face(0)).astype(BF16)
    faces, corners = [], []
    for y in (0, size_y - 1):
        faces.append(deep[pl.ds(y, send_a.shape[0], stride=size_y), :].astype(BF16))
        ends = [deep[pl.ds(start + y, planes, stride=own), :] for start in (far, 0)]
        corners.append(jnp.where(first, ends[0], ends[1]).astype(BF16))
    send_b[...], send_a[...] = line_sides("gy", faces[1], faces[0])
    corner_b[...], _ = line_sides("gy", corners[1], corners[0])


def hidden_kernel(count_z, volume, z_a, z_b, x_rim, relayed, taps, w_conv, w_down, *refs):
    backs, (hidden, slope, rim), sends, (rim32, cells) = (
        refs[:count_z],
        refs[count_z : count_z + 3],
        refs[count_z + 3 : -2],
        refs[-2:],
    )
    size_z, size_x, size_y, channels = volume.shape
    own = size_x * size_y
    quarter = own // 4
    planes = size_z + 2
    pitch = 2 * own
    first = lax.axis_index("gx") == 0
    deepen(volume, z_a, z_b, rim32, pitch)
    y_low, y_high, xy_low, xy_high = y_rims(relayed, x_rim.shape[0] // size_y)
    x_side = x_rim[...].astype(F32)
    x_low, x_high = jnp.where(first, 0.0, x_side), jnp.where(first, x_side, 0.0)
    faces = (x_low, x_high, y_low, y_high)
    for z in range(planes):
        for part, block in enumerate(faces):
            start = z * pitch + own + 8 * part
            rim32[start : start + 8, :] = block[8 * z : 8 * (z + 1), :]
        rim32[z * pitch + own + 32 : (z + 1) * pitch, :] = jnp.zeros((own - 32, channels), F32)
    corners = ((xy_low, 7, True), (xy_high, 0, True), (xy_low, 7, False), (xy_high, 0, False))
    for part, (block, row, low) in enumerate(corners):
        start = own + 32 + 8 * part + row
        value = jnp.where(first == low, 0.0, block)
        rim32[pl.ds(start, 8, stride=pitch), :] = value[:8, :]
        for z in range(8, planes):
            rim32[z * pitch + start : z * pitch + start + 1, :] = value[z : z + 1, :]
    for z in range(0, planes, 2):
        pair = [rim32[(z + i) * pitch : (z + i + 1) * pitch, :].astype(BF16) for i in range(2)]
        moved = matmul(taps[...], jnp.concatenate(pair, axis=1)).astype(BF16)
        for i in range(2):
            rim[z + i] = pair[i]
            for bc in range(9):
                cells[z + i, :, bc * channels : (bc + 1) * channels] = moved[
                    bc * own : (bc + 1) * own, i * channels : (i + 1) * channels
                ]
    pre = None
    for a in range(3):
        window = cells[a : a + size_z].reshape(size_z * own, 9 * channels)
        weight = w_conv[9 * a : 9 * (a + 1)].reshape(9 * channels, channels)
        term = matmul(window, weight)
        pre = term if pre is None else pre + term
    sig = jax.nn.sigmoid(pre)
    slope[...] = (sig * (1.0 + pre * (1.0 - sig))).reshape(size_z, own, channels)
    hidden[...] = (pre * sig).astype(BF16).reshape(size_z, own, channels)
    parts = []
    for s in range(8):
        a, bc = s // 4, s % 4
        parts.append(
            jnp.concatenate(
                [hidden[2 * kz + a, bc * quarter : (bc + 1) * quarter, :] for kz in range(size_z // 2)], axis=0
            )
        )
    coarse = matmul(jnp.concatenate(parts, axis=1), w_down[...].reshape(8 * channels, w_down.shape[2]))
    coarse = coarse.astype(BF16)
    wide = coarse.shape[1]
    for send, back in zip(sends, backs):
        send[:, :wide] = coarse
        send[:, wide:] = back[...]


def rim_transpose_kernel(count_p, rim, taps_t, turned):
    planes, rows, channels = rim.shape
    share = channels // count_p
    for pair in range(planes // 2):
        sides = [rim[2 * pair + i].astype(F32).T for i in range(2)]
        moved = matmul(jnp.concatenate(sides, axis=1).astype(BF16), taps_t[...]).astype(BF16)
        for bc in range(9):
            for p in range(count_p):
                start = (bc * count_p // 2 + p // 2) * share
                turned[p % 2, start : start + share, pair * rows : (pair + 1) * rows] = moved[
                    p * share : (p + 1) * share, bc * rows : (bc + 1) * rows
                ]


def column_kernel(count_z, *refs):
    parts, picks, (column, back, x_send, send_a, send_b, corner_b) = refs[:count_z], refs[count_z], refs[count_z + 1 :]
    own_cells = parts[0].shape[0]
    wide = column.shape[1]
    pz = lax.axis_index("gz")
    for i, part in enumerate(parts):
        rows = pl.ds(pl.multiple_of((pz ^ (-i % count_z)) * own_cells, own_cells), own_cells)
        column[rows, :] = part[:, :wide]
        back[rows, :] = part[:, wide:]
    rims = matmul(picks[lax.axis_index("gx")], column[...]).astype(BF16)
    cuts, start = [], 0
    for size in (x_send.shape[0], *[send_a.shape[0]] * 2, *[corner_b.shape[0]] * 2):
        cuts.append(rims[start : start + size, :])
        start += size
    x_send[...] = cuts[0]
    send_b[...], send_a[...] = line_sides("gy", cuts[2], cuts[1])
    corner_b[...], _ = line_sides("gy", cuts[4], cuts[3])


def bottle_kernel(quarter, column, back, x_rim, relayed, shift, w_bottle, *refs):
    count = len(refs) // 2 - 1
    slices, bottle, sends, (rim32, window) = refs[:count], refs[count], refs[count + 1 : -2], refs[-2:]
    cells, wide = column.shape
    outs = w_bottle.shape[2]
    side = x_rim.shape[0]
    depth = cells // quarter
    span = 4 * quarter
    picks = shift[lax.axis_index("gx")]
    window[:quarter, :] = jnp.zeros((quarter, 9 * wide), BF16)
    window[(depth + 1) * quarter :, :] = jnp.zeros((quarter, 9 * wide), BF16)
    edge = side // (depth // 4)
    y_low, y_high, xy_low, xy_high = y_rims(relayed, depth)
    for g in range(depth // 4):
        rim32[g, :span, :] = column[g * span : (g + 1) * span, :].astype(F32)
        for part, block in enumerate((x_rim, y_low, y_high)):
            start = span + part * edge
            rim32[g, start : start + edge, :] = block[g * edge : (g + 1) * edge, :].astype(F32)
        start = span + 3 * edge
        rim32[g, start : start + 4, :] = xy_low[4 * g : 4 * g + 4, :]
        rim32[g, start + 4 : start + 8, :] = xy_high[4 * g : 4 * g + 4, :]
        rim32[g, start + 8 :, :] = jnp.zeros((rim32.shape[1] - start - 8, wide), F32)
        moved = matmul(picks, rim32[g].astype(BF16)).astype(BF16)
        for bc in range(9):
            window[quarter + g * span : quarter + (g + 1) * span, bc * wide : (bc + 1) * wide] = moved[
                bc * span : (bc + 1) * span, :
            ]
    spread_out = None
    for bc in range(9):
        weight = jnp.concatenate([w_bottle[9 * a + bc] for a in range(3)], axis=1)
        term = matmul(window[:, bc * wide : (bc + 1) * wide], weight)
        spread_out = term if spread_out is None else spread_out + term
    pre = spread_out[:cells, :outs]
    for a in range(1, 3):
        pre = pre + spread_out[a * quarter : a * quarter + cells, a * outs : (a + 1) * outs]
    sig = jax.nn.sigmoid(pre)
    bottle[...] = (pre * sig).astype(BF16)
    slope = sig * (1.0 + pre * (1.0 - sig))
    value = (back[...].astype(F32) * slope).astype(BF16)
    for send, block in zip(sends, slices):
        send[:cells, :] = value
        send[cells:, :] = block[...]


def slices_kernel(count_y, quarter, column, *refs):
    sends, slices = refs[:-1], refs[-1]
    cells, wide = column.shape
    span = 4 * quarter
    half = 2 * quarter
    lane = lax.broadcasted_iota(jnp.int32, (half, 128), 1)
    for pair in range(wide // 128):
        for g in range(cells // span):
            top = column[g * span : g * span + half, pair * 128 : (pair + 1) * 128].astype(F32)
            end = column[g * span + half : (g + 1) * span, pair * 128 : (pair + 1) * 128].astype(F32)
            rows = slice(g * half, (g + 1) * half)
            slices[2 * pair, rows, :] = jnp.where(lane < 64, top, pltpu.roll(end, 64, 1)).astype(BF16)
            slices[2 * pair + 1, rows, :] = jnp.where(lane < 64, pltpu.roll(top, 64, 1), end).astype(BF16)
    p = plane_index(count_y)
    lines = slices.shape[1]
    for i, send in enumerate(sends):
        send[:lines, :] = slices[p ^ (2 * i)]
        send[lines:, :] = slices[p ^ (2 * i + 1)]


def coarse_grad_kernel(count_y, count_z, quarter, *refs):
    grads, (bottle, shift, w_bottle) = refs[: -count_z - 6], refs[-count_z - 6 : -count_z - 3]
    sends, (window, gathered, blocks) = refs[-count_z - 3 : -3], refs[-3:]
    count_p = len(grads)
    cells, outs = bottle.shape
    rows = count_p * quarter
    depth = cells // quarter
    own_cells = cells // count_z
    inputs = w_bottle.shape[1]
    p = plane_index(count_y)
    for i, part in enumerate(grads):
        gathered[p ^ (-i % count_p)] = part[:cells, :]
    mine = pl.multiple_of(p * quarter, quarter)
    picks = jnp.concatenate([shift[pl.ds((8 - bc) * rows + mine, quarter), :] for bc in range(9)], axis=0)
    window[:quarter, :] = jnp.zeros((quarter, 9 * outs), BF16)
    window[(depth + 1) * quarter :, :] = jnp.zeros((quarter, 9 * outs), BF16)
    for z in range(depth):
        plane = jnp.concatenate([gathered[q, z * quarter : (z + 1) * quarter, :] for q in range(count_p)], axis=0)
        moved = matmul(picks, plane).astype(BF16)
        for bc in range(9):
            window[(z + 1) * quarter : (z + 2) * quarter, bc * outs : (bc + 1) * outs] = moved[
                bc * quarter : (bc + 1) * quarter, :
            ]
    total = None
    for a in range(3):
        weight = jnp.concatenate([w_bottle[9 * a + bc] for bc in range(9)], axis=1)
        term = matmul_nt(window[(2 - a) * quarter : (2 - a + depth) * quarter, :], weight)
        total = term if total is None else total + term
    total = total.astype(BF16)
    for q in range(count_z):
        blocks[q, :, :inputs] = total[q * own_cells : (q + 1) * own_cells, :]
        blocks[q, :, inputs:] = bottle[q * own_cells : (q + 1) * own_cells, :]
    hand_out(blocks, sends, lax.axis_index("gz"))


def wide_kernel(count_y, quarter, *refs):
    parts, (wide, grads) = refs[:-2], refs[-2:]
    count_p, cells, outs = grads.shape
    rows = count_p * quarter
    depth = cells // quarter
    take_in([part.at[:cells, :] for part in parts], grads, plane_index(count_y))
    planes = [
        jnp.concatenate([grads[q, z * quarter : (z + 1) * quarter, :] for q in range(count_p)], axis=0)
        for z in range(depth)
    ]
    zeros = jnp.zeros((rows, outs), BF16)
    for j in range(depth // 2):
        for slot in range(5):
            z = j // 2 * 4 + j % 2 + slot - 1
            wide[j * rows : (j + 1) * rows, slot * outs : (slot + 1) * outs] = planes[z] if 0 <= z < depth else zeros


def coarse_transpose_kernel(count_y, shift, *refs):
    parts, (turned, slices) = refs[:-2], refs[-2:]
    count_p, lines, _ = slices.shape
    rows = shift.shape[1]
    quarter = rows // count_p
    p = plane_index(count_y)
    for d, part in enumerate(parts):
        start = (2 + d % 2) * lines
        slices[p ^ d] = part[start : start + lines, :]
    for j in range(lines // quarter):
        plane = jnp.concatenate([slices[q, j * quarter : (j + 1) * quarter, :] for q in range(count_p)], axis=0)
        plane = plane.astype(F32).T.astype(BF16)
        for bc in range(9):
            turned[bc * 128 : (bc + 1) * 128, j * rows : (j + 1) * rows] = matmul(
                plane, shift[(8 - bc) * rows : (9 - bc) * rows, :]
            ).astype(BF16)


def grad_bottle_kernel(turned, wide, out):
    _, channels, outs = out.shape
    full = matmul(turned[...], wide[...])
    for bc in range(9):
        top = full[bc * 128 : bc * 128 + channels, :]
        end = full[bc * 128 + channels : (bc + 1) * 128, :]
        for a in range(3):
            out[9 * a + bc] = top[:, (2 - a) * outs : (3 - a) * outs] + end[:, (4 - a) * outs : (5 - a) * outs]


def half_grad(turned, shifted, parity, chip, out, blocks):
    chips, rows, channels = blocks.shape
    group = rows // 27
    full = matmul(turned[parity], shifted[...])
    for bc in range(9):
        for a in range(3):
            t = 9 * a + bc
            for q in range(chips):
                start = (bc * chips + q) * group
                blocks[q, t * group : (t + 1) * group, :] = full[
                    start : start + group, a * channels : (a + 1) * channels
                ].astype(BF16)
    for i in range(chips):
        out[i] = blocks[chip ^ i]


def hidden_grad_kernel(count_y, count_z, *refs):
    parts, (slope, ordered, w_down, turned) = refs[:count_z], refs[count_z : count_z + 4]
    shifted, bottle, give, bottles, blocks = refs[count_z + 4 :]
    size_z, own, channels = ordered.shape
    quarter = own // 4
    inputs = w_down.shape[2]
    pz = lax.axis_index("gz")
    grad = total_of([part.at[:, :inputs] for part in parts]).astype(BF16)
    for i, part in enumerate(parts):
        bottles[pz ^ (-i % count_z)] = part[:, inputs:]
    bottle[...] = jnp.concatenate([bottles[q] for q in range(count_z)], axis=1)
    shifted[...] = jnp.zeros_like(shifted)
    for s in range(8):
        a, bc = s // 4, s % 4
        spread_grad = matmul_nt(grad, w_down[s])
        for kz in range(size_z // 2):
            z = 2 * kz + a
            part = slice(bc * quarter, (bc + 1) * quarter)
            line = slice(kz * quarter, (kz + 1) * quarter)
            value = ((spread_grad[line, :] + ordered[z, part, :].astype(F32)) * slope[z, part, :]).astype(BF16)
            for t in range(3):
                start = (z + t) * own + bc * quarter
                shifted[start : start + quarter, t * channels : (t + 1) * channels] = value
    p = plane_index(count_y)
    half_grad(turned, shifted, 1 - p % 2, p // 2, give, blocks)


def keep_kernel(count_y, shifted, turned, keep, blocks):
    p = plane_index(count_y)
    half_grad(turned, shifted, p % 2, p // 2, keep, blocks)


def output_kernel(bottle, hidden, w_up, order_t, output, rows_out):
    size_z, own, channels = hidden.shape
    quarter = own // 4
    for s in range(8):
        a, bc = s // 4, s % 4
        lifted = matmul(bottle[...], w_up[s])
        for kz in range(size_z // 2):
            z = 2 * kz + a
            part = slice(bc * quarter, (bc + 1) * quarter)
            line = slice(kz * quarter, (kz + 1) * quarter)
            rows_out[z, part, :] = (lifted[line, :] + hidden[z, part, :].astype(F32)).astype(BF16)
    for z in range(size_z):
        plane = matmul(order_t[...], rows_out[z])
        output[z] = plane.reshape(output.shape[1:]).astype(BF16)


def pair_sum_kernel(keep, got, *sends):
    for i, send in enumerate(sends):
        send[...] = (keep[i].astype(F32) + got[i].astype(F32)).astype(BF16)


def sum_kernel(*refs):
    out = refs[-1]
    out[...] = total_of(refs[:-1]).reshape(out.shape).astype(out.dtype)


def shape_of(shape, dtype=BF16):
    return jax.ShapeDtypeStruct(shape, dtype)


def gathered_body(counts, volume, cotangent, w_conv, w_down, w_bottle, w_up):
    count_x, count_y, count_z = counts
    count_p = count_x * count_y
    size_z, size_x, size_y, channels = volume.shape
    wide = w_down.shape[2]
    group = w_bottle.shape[2]
    half_x, half_y = size_x // 2, size_y // 2
    own = size_x * size_y
    quarter = half_x * half_y
    own_cells = size_z // 2 * quarter
    cells = count_z * own_cells
    depth = count_z * size_z // 2
    rows = count_p * quarter
    planes = size_z + 2
    share_c = channels // count_p
    share_w = wide // count_p
    plane_axes = ("gx", "gy")

    order, taps = fine_maps(size_x, size_y)
    pair_taps = np.zeros((2, 2 * own, 9, 2, own), np.float32)
    for i in range(2):
        pair_taps[i, :, :, i, :] = taps.transpose(2, 0, 1)
    shift = coarse_maps(count_x, count_y, half_x, half_y)
    order_m = jnp.asarray(order, BF16)
    order_t = jnp.asarray(order.T, BF16)
    taps_m = jnp.asarray(taps.reshape(9 * own, 2 * own), BF16)
    taps_t = jnp.asarray(pair_taps.reshape(4 * own, 18 * own), BF16)
    shift_m = jnp.asarray(shift.reshape(9 * rows, rows), BF16)

    send_maps, rim_maps = column_maps(half_x, half_y, depth)
    send_m = jnp.asarray(send_maps, BF16)
    rim_m = jnp.asarray(rim_maps.reshape(count_x, 36 * quarter, 8 * quarter), BF16)

    w_conv_t = jnp.transpose(w_conv, (1, 0, 2))
    w_bottle_t = jnp.transpose(w_bottle, (1, 0, 2))
    send_a, send_b = local_call(ends_kernel, "ends", [shape_of((size_x, size_y, channels))] * 2)(volume)
    z_pairs = line_pairs(count_z)
    z_b = lax.ppermute(send_b, "gz", z_pairs[1])
    z_a = lax.ppermute(send_a, "gz", z_pairs[0])
    *backs, ordered = local_call(
        lambda *refs: back_kernel(count_z, *refs),
        "back",
        [shape_of((own_cells, group))] * count_z + [shape_of((size_z, own, channels))],
        [pltpu.VMEM((count_z, own_cells, group), BF16)],
    )(cotangent, w_up, order_m)
    sends = local_call(
        faces_kernel,
        "faces",
        [shape_of((16 * size_y, channels))] + [shape_of((planes * size_x, channels))] * 2 + [shape_of((16, channels))],
        [pltpu.VMEM((16 * own, channels), F32)],
    )(volume, z_a, z_b)
    x_send, send_a, send_b, corner_b = sends
    x_rim, across, corner = swap_rims(x_send, send_b, corner_b, counts)
    relayed = relay_rims(x_rim, across, corner, send_a, counts)
    hidden, slope, rim, *sends = local_call(
        lambda *refs: hidden_kernel(count_z, *refs),
        "hidden",
        [
            shape_of((size_z, own, channels)),
            shape_of((size_z, own, channels), F32),
            shape_of((planes, 2 * own, channels)),
        ]
        + [shape_of((own_cells, wide + group))] * count_z,
        [
            pltpu.VMEM((planes * 2 * own, channels), F32),
            pltpu.VMEM((planes, own, 9 * channels), BF16),
        ],
        flops=2_000_000_000,
    )(volume, z_a, z_b, x_rim, relayed, taps_m, w_conv_t, w_down, *backs)
    parts = trade(sends, "gz", count_z)
    column, back, *sends = local_call(
        lambda *refs: column_kernel(count_z, *refs),
        "column",
        [shape_of((cells, wide)), shape_of((cells, group)), shape_of((depth * half_y, wide))]
        + [shape_of((depth * half_x, wide))] * 2
        + [shape_of((depth, wide))],
    )(parts[0], *parts[:0:-1], send_m)
    x_send, send_a, send_b, corner_b = sends
    x_rim, across, corner = swap_rims(x_send, send_b, corner_b, counts)
    relayed = relay_rims(x_rim, across, corner, send_a, counts)
    slices = local_call(
        lambda *refs: slices_kernel(count_y, quarter, *refs),
        "slices",
        [shape_of((cells, 128))] * (count_p // 2),
        [pltpu.VMEM((count_p, cells // 2, 128), BF16)],
    )(column)
    column, *slices = lax.optimization_barrier((column, *slices))
    bottle, *sends = local_call(
        lambda *refs: bottle_kernel(quarter, *refs),
        "bottle",
        [shape_of((cells, group))] + [shape_of((2 * cells, group))] * (count_p // 2),
        [
            pltpu.VMEM((depth // 4, 8 * quarter, wide), F32),
            pltpu.VMEM(((depth + 2) * quarter, 9 * wide), BF16),
        ],
        flops=2_000_000_000,
    )(column, back, x_rim, relayed, rim_m, w_bottle_t, *slices)
    grads = [None] * count_p
    grads[0] = sends[0]
    for d in (6, 4, 2):
        grads[d] = swap(sends[d // 2], plane_axes, count_p, d)
    for d in (0, 2, 4, 6):
        grads[d + 1] = swap(grads[d], plane_axes, count_p, 1)
    sends = local_call(
        lambda *refs: coarse_grad_kernel(count_y, count_z, quarter, *refs),
        "coarse_grad",
        [shape_of((own_cells, wide + group))] * count_z,
        [
            pltpu.VMEM(((depth + 2) * quarter, 9 * group), BF16),
            pltpu.VMEM((count_p, cells, group), BF16),
            pltpu.VMEM((count_z, own_cells, wide + group), BF16),
        ],
    )(grads[0], *grads[:0:-1], bottle, shift_m, w_bottle_t)
    parts = trade(sends, "gz", count_z)
    rim, late, _ = lax.optimization_barrier((rim, grads[0], sends[1]))
    turned = local_call(
        lambda *refs: rim_transpose_kernel(count_p, *refs),
        "rim_transpose",
        shape_of((2, 9 * channels // 2, planes * own)),
    )(rim, taps_t)
    coarse_turned = local_call(
        lambda *refs: coarse_transpose_kernel(count_y, *refs),
        "coarse_transpose",
        shape_of((18 * share_w, depth // 2 * rows)),
        [pltpu.VMEM((count_p, cells // 2, 128), BF16)],
    )(shift_m, late, *grads[1:])
    turned, coarse_turned = lax.optimization_barrier((turned, coarse_turned))
    shifted, bottle, give = local_call(
        lambda *refs: hidden_grad_kernel(count_y, count_z, *refs),
        "hidden_grad",
        [
            shape_of((planes * own, 3 * channels)),
            shape_of((own_cells, wide)),
            shape_of((count_p // 2, 27 * share_c, channels)),
        ],
        [
            pltpu.VMEM((count_z, own_cells, group), BF16),
            pltpu.VMEM((count_p // 2, 27 * share_c, channels), BF16),
        ],
    )(parts[0], *parts[:0:-1], slope, ordered, w_down, turned)
    got = swap(give, plane_axes, count_p, 1)
    keep = local_call(
        lambda *refs: keep_kernel(count_y, *refs),
        "keep",
        shape_of((count_p // 2, 27 * share_c, channels)),
        [pltpu.VMEM((count_p // 2, 27 * share_c, channels), BF16)],
    )(shifted, turned)
    output = local_call(
        output_kernel,
        "output",
        shape_of(volume.shape),
        [pltpu.VMEM((size_z, own, channels), BF16)],
    )(bottle, hidden, w_up, order_t)
    sends = local_call(
        pair_sum_kernel,
        "pair_sum",
        [shape_of((27 * share_c, channels))] * (count_p // 2),
    )(keep, got)
    parts = [sends[0]] + [swap(sends[d // 2], plane_axes, count_p, d) for d in (6, 4, 2)]
    part = local_call(sum_kernel, "plane_sum", shape_of((27 * share_c, channels)))(*parts)
    part, output = lax.optimization_barrier((part, output))
    got = swap(part, "gz", count_z, 1)
    wide_grads = local_call(
        lambda *refs: wide_kernel(count_y, quarter, *refs),
        "wide",
        shape_of((depth // 2 * rows, 5 * group)),
        [pltpu.VMEM((count_p, cells, group), BF16)],
    )(*grads)
    got, wide_grads = lax.optimization_barrier((got, wide_grads))
    part = local_call(sum_kernel, "depth_sum", shape_of((27 * share_c, channels)))(part, got)
    got = swap(part, "gz", count_z, 2)
    grad_bottle = local_call(
        grad_bottle_kernel,
        "grad_bottle",
        shape_of((27, share_w, group), F32),
        flops=4_000_000_000,
    )(coarse_turned, wide_grads)
    grad_conv = local_call(
        sum_kernel,
        "grad_conv",
        shape_of((27, share_c, channels), F32),
    )(part, got)
    return (output, jnp.transpose(grad_conv, (1, 0, 2)), jnp.transpose(grad_bottle, (1, 0, 2)))


def with_halo(cells, sides, width):
    for axis, dim in sides:
        count = lax.axis_size(axis)
        ends = count - 1
        head = lax.slice_in_dim(cells, 0, width, axis=dim)
        tail = lax.slice_in_dim(cells, cells.shape[dim] - width, cells.shape[dim], axis=dim)
        cells = jnp.concatenate(
            [
                lax.ppermute(tail, axis, [(i, (i + 1) % count) for i in range(ends)]),
                cells,
                lax.ppermute(head, axis, [((i + 1) % count, i) for i in range(ends)]),
            ],
            axis=dim,
        )
    return cells


def silu_slope(values):
    sig = jax.nn.sigmoid(values)
    return sig * (1.0 + values * (1.0 - sig))


def conv_forward(padded, weight, extent):
    size_z, size_x, size_y = extent
    count_cells = size_z * size_x * size_y
    summed = jnp.zeros((count_cells, weight.shape[2]), jnp.float32)
    for tap_index in range(27):
        shift_z, shift_x, shift_y = (tap_index // 9, tap_index // 3 % 3, tap_index % 3)
        window = padded[
            shift_z : shift_z + size_z, shift_x : shift_x + size_x, shift_y : shift_y + size_y, :
        ]
        window = window.reshape(count_cells, padded.shape[3])
        summed = summed + jnp.dot(
            window, weight[:, tap_index, :], preferred_element_type=jnp.float32
        )
    return summed.reshape(size_z, size_x, size_y, weight.shape[2])


def conv_weight_grad(padded, gradient, extent):
    size_z, size_x, size_y = extent
    count_cells = size_z * size_x * size_y
    flat_gradient = gradient.reshape(count_cells, gradient.shape[3])
    pieces = []
    for tap_index in range(27):
        shift_z, shift_x, shift_y = (tap_index // 9, tap_index // 3 % 3, tap_index % 3)
        window = padded[
            shift_z : shift_z + size_z, shift_x : shift_x + size_x, shift_y : shift_y + size_y, :
        ]
        window = window.reshape(count_cells, padded.shape[3])
        pieces.append(
            lax.dot_general(
                window, flat_gradient, (((0,), (0,)), ((), ())), preferred_element_type=jnp.float32
            )
        )
    return jnp.stack(pieces, axis=1)


def conv_input_grad(padded, weight, extent):
    size_z, size_x, size_y = extent
    count_cells = size_z * size_x * size_y
    summed = jnp.zeros((count_cells, weight.shape[0]), jnp.float32)
    for tap_index in range(27):
        shift_z, shift_x, shift_y = (2 - tap_index // 9, 2 - tap_index // 3 % 3, 2 - tap_index % 3)
        window = padded[
            shift_z : shift_z + size_z, shift_x : shift_x + size_x, shift_y : shift_y + size_y, :
        ]
        window = window.reshape(count_cells, padded.shape[3])
        summed = summed + lax.dot_general(
            window,
            weight[:, tap_index, :],
            (((1,), (1,)), ((), ())),
            preferred_element_type=jnp.float32,
        )
    return summed.reshape(size_z, size_x, size_y, weight.shape[0])


def pool_features(fine, kernel):
    size_z, size_x, size_y, channels = fine.shape
    blocks = fine.reshape(size_z // 2, 2, size_x // 2, 2, size_y // 2, 2, channels)
    kernel_cube = kernel.reshape(2, 2, 2, kernel.shape[1], kernel.shape[2])
    return jnp.einsum(
        "zaxbycf,abcfg->zxyg", blocks, kernel_cube, preferred_element_type=jnp.float32
    )


def pool_adjoint(coarse_in, kernel):
    size_z, size_x, size_y, wide_channels = coarse_in.shape
    kernel_cube = kernel.reshape(2, 2, 2, kernel.shape[1], kernel.shape[2])
    result = jnp.einsum(
        "zxyg,abcfg->zaxbycf", coarse_in, kernel_cube, preferred_element_type=jnp.float32
    )
    return result.reshape(2 * size_z, 2 * size_x, 2 * size_y, kernel.shape[1])


def lift_features(coarse_in, kernel):
    size_z, size_x, size_y, wide_channels = coarse_in.shape
    kernel_cube = kernel.reshape(2, 2, 2, kernel.shape[1], kernel.shape[2])
    result = jnp.einsum(
        "zxyg,abcgf->zaxbycf", coarse_in, kernel_cube, preferred_element_type=jnp.float32
    )
    return result.reshape(2 * size_z, 2 * size_x, 2 * size_y, kernel.shape[2])


def lift_adjoint(fine, kernel):
    size_z, size_x, size_y, channels = fine.shape
    blocks = fine.reshape(size_z // 2, 2, size_x // 2, 2, size_y // 2, 2, channels)
    kernel_cube = kernel.reshape(2, 2, 2, kernel.shape[1], kernel.shape[2])
    return jnp.einsum(
        "zaxbycf,abcgf->zxyg", blocks, kernel_cube, preferred_element_type=jnp.float32
    )


def column_body(volume, cotangent, w_conv, w_down, w_bottle, w_up):
    size_z, size_x, size_y, channels = volume.shape
    group_channels = w_bottle.shape[2]
    half_x = size_x // 2
    half_y = size_y // 2
    padded = with_halo(volume, (("gx", 1), ("gy", 2), ("gz", 0)), 1)
    pre_hidden = conv_forward(padded, w_conv, (size_z, size_x, size_y))
    hidden = jax.nn.silu(pre_hidden).astype(jnp.bfloat16)
    hidden_slope = silu_slope(pre_hidden)
    coarse = pool_features(hidden, w_down).astype(jnp.bfloat16)
    stacked = lax.all_gather(coarse, "gz", axis=0, tiled=True)
    rimmed = with_halo(stacked, (("gx", 1), ("gy", 2)), 1)
    column_z = rimmed.shape[0]
    coarse_pad = jnp.pad(rimmed, ((1, 1), (0, 0), (0, 0), (0, 0)))
    pre_bottle = conv_forward(coarse_pad, w_bottle, (column_z, half_x, half_y))
    bottle = jax.nn.silu(pre_bottle).astype(jnp.bfloat16)
    bottle_slope = silu_slope(pre_bottle)
    own_start = lax.axis_index("gz") * group_channels
    own_up = lax.dynamic_slice_in_dim(w_up, own_start, group_channels, 1)
    lifted = lax.psum_scatter(
        lift_features(bottle, own_up).astype(jnp.bfloat16), "gz", scatter_dimension=0, tiled=True
    ).astype(jnp.float32)
    output = (lifted + hidden.astype(jnp.float32)).astype(jnp.bfloat16)
    back_bottle = lift_adjoint(cotangent, w_up).astype(jnp.bfloat16)
    split_grad = lax.all_to_all(back_bottle, "gz", split_axis=3, concat_axis=0, tiled=True)
    bottle_grad = (split_grad.astype(jnp.float32) * bottle_slope).astype(jnp.bfloat16)
    grad_bottle = lax.psum_scatter(
        conv_weight_grad(coarse_pad, bottle_grad, (column_z, half_x, half_y)),
        ("gx", "gy"),
        scatter_dimension=0,
        tiled=True,
    )
    grad_rimmed = with_halo(bottle_grad, (("gx", 1), ("gy", 2)), 1)
    grad_pad = jnp.pad(grad_rimmed, ((1, 1), (0, 0), (0, 0), (0, 0)))
    coarse_grad = lax.psum_scatter(
        conv_input_grad(
            grad_pad, w_bottle, (lax.axis_size("gz") * (size_z // 2), half_x, half_y)
        ).astype(jnp.bfloat16),
        "gz",
        scatter_dimension=0,
        tiled=True,
    )
    hidden_grad = (
        (pool_adjoint(coarse_grad, w_down) + cotangent.astype(jnp.float32)) * hidden_slope
    ).astype(jnp.bfloat16)
    full_term = conv_weight_grad(padded, hidden_grad, (size_z, size_x, size_y))
    depth_summed = lax.psum(full_term.astype(jnp.bfloat16), "gz").astype(jnp.float32)
    grad_conv = lax.psum_scatter(depth_summed, ("gx", "gy"), scatter_dimension=0, tiled=True)
    return (output, grad_conv, grad_bottle)


def fits_one_plane(counts, brick, wide):
    count_p = counts[0] * counts[1]
    size_z, size_x, size_y, channels = brick
    return (
        counts == (2, 4, 4)
        and count_p * (size_x // 2) * (size_y // 2) == 128
        and wide // count_p == 64
        and (size_z, size_x, size_y, channels) == (8, 8, 8, 128)
    )


def solution(mesh):
    in_specs = (
        P("gz", "gx", "gy", None),
        P("gz", "gx", "gy", None),
        P(),
        P(),
        P(None, None, "gz"),
        P(),
    )
    out_specs = (
        P("gz", "gx", "gy", None),
        P(("gx", "gy"), None, None),
        P(("gx", "gy"), None, "gz"),
    )
    counts = (mesh.shape["gx"], mesh.shape["gy"], mesh.shape["gz"])

    def body(volume, cotangent, w_conv, w_down, w_bottle, w_up):
        if fits_one_plane(counts, volume.shape, w_down.shape[2]):
            return gathered_body(counts, volume, cotangent, w_conv, w_down, w_bottle, w_up)
        return column_body(volume, cotangent, w_conv, w_down, w_bottle, w_up)

    return jax.shard_map(body, mesh=mesh, in_specs=in_specs, out_specs=out_specs, check_vma=False)
```

```python
import numpy as np
import jax
import jax.numpy as jnp
from jax import lax
from jax.experimental import pallas as pl
from jax.experimental.pallas import tpu as pltpu
from jax.sharding import PartitionSpec as P

BF16 = jnp.bfloat16
F32 = jnp.float32
VMEM_LIMIT = 24 * 1024 * 1024


def local_call(kernel, name, out_shapes, scratch=(), flops=300_000_000):
    whole = pl.BlockSpec(memory_space=pltpu.VMEM)

    def call(*operands):
        return pl.pallas_call(
            kernel,
            name=name,
            out_shape=out_shapes,
            in_specs=[whole] * len(operands),
            out_specs=jax.tree.map(lambda _: whole, out_shapes),
            scratch_shapes=list(scratch),
            compiler_params=pltpu.CompilerParams(vmem_limit_bytes=VMEM_LIMIT),
            cost_estimate=pl.CostEstimate(flops=flops, bytes_accessed=flops // 1000, transcendentals=0),
        )(*operands)

    return call


def matmul(left, right):
    return jnp.dot(left, right, preferred_element_type=F32)


def matmul_nt(left, right):
    return lax.dot_general(left, right, (((1,), (1,)), ((), ())), preferred_element_type=F32)


def sub_order(size_x, size_y):
    half_x, half_y = size_x // 2, size_y // 2
    return {
        (2 * kx + b, 2 * ky + c): ((2 * b + c) * half_x + kx) * half_y + ky
        for b in range(2)
        for c in range(2)
        for kx in range(half_x)
        for ky in range(half_y)
    }


def fine_maps(size_x, size_y):
    own = size_x * size_y
    rows = sub_order(size_x, size_y)
    order = np.zeros((own, own), np.float32)
    taps = np.zeros((9, own, 2 * own), np.float32)
    for (x, y), row in rows.items():
        order[row, x * size_y + y] = 1
        for b in range(3):
            for c in range(3):
                sx, sy = x + b - 1, y + c - 1
                if sx < 0:
                    part = 0 if 0 <= sy < size_y else (4 if sy < 0 else 5)
                    source = own + 8 * part + sy % size_y
                elif sx >= size_x:
                    part = 1 if 0 <= sy < size_y else (6 if sy < 0 else 7)
                    source = own + 8 * part + sy % size_y
                elif sy < 0:
                    source = own + 16 + sx
                elif sy >= size_y:
                    source = own + 24 + sx
                else:
                    source = sx * size_y + sy
                taps[3 * b + c, row, source] = 1
    return order, taps


def coarse_maps(count_x, count_y, half_x, half_y):
    wide_x, wide_y = count_x * half_x, count_y * half_y

    def row_of(x, y):
        brick = (x // half_x) * count_y + y // half_y
        return (brick * half_x + x % half_x) * half_y + y % half_y

    shift = np.zeros((9, wide_x * wide_y, wide_x * wide_y), np.float32)
    for x in range(wide_x):
        for y in range(wide_y):
            for b in range(3):
                for c in range(3):
                    sx, sy = x + b - 1, y + c - 1
                    if 0 <= sx < wide_x and 0 <= sy < wide_y:
                        shift[3 * b + c, row_of(x, y), row_of(sx, sy)] = 1
    return shift


def column_maps(half_x, half_y, depth):
    quarter = half_x * half_y
    rows = depth * quarter
    send = np.zeros((2, depth * (half_y + 2 * half_x + 2), rows), np.float32)
    rim = np.zeros((2, 9, 4, quarter, 8 * quarter), np.float32)
    for px in range(2):
        edge = 0 if px else half_x - 1
        for z in range(depth):
            base = z * quarter
            for ky in range(half_y):
                send[px, z * half_y + ky, base + edge * half_y + ky] = 1
            for side, ky in enumerate((0, half_y - 1)):
                row = depth * (half_y + side * half_x) + z * half_x
                for kx in range(half_x):
                    send[px, row + kx, base + kx * half_y + ky] = 1
                send[px, depth * (half_y + 2 * half_x + side) + z, base + edge * half_y + ky] = 1
    for px in range(2):
        for b in range(3):
            for c in range(3):
                for kx in range(half_x):
                    for ky in range(half_y):
                        sx, sy = kx + b - 1, ky + c - 1
                        beyond = sx < 0 if px else sx >= half_x
                        if (sx < 0 or sx >= half_x) and not beyond:
                            continue
                        for z in range(4):
                            if beyond and 0 <= sy < half_y:
                                source = 4 * quarter + z * half_y + sy
                            elif beyond:
                                source = 7 * quarter + 4 * (sy >= half_y) + z
                            elif sy < 0:
                                source = 5 * quarter + z * half_x + sx
                            elif sy >= half_y:
                                source = 6 * quarter + z * half_x + sx
                            else:
                                source = z * quarter + sx * half_y + sy
                            rim[px, 3 * b + c, z, kx * half_y + ky, source] = 1
    return send, rim


def swap(block, axes, count, distance):
    return lax.ppermute(block, axes, [(i, i ^ distance) for i in range(count)])


def trade(blocks, axes, count):
    got = {d: swap(blocks[d], axes, count, d) for d in reversed(range(1, count))}
    return [blocks[0]] + [got[d] for d in range(1, count)]


def line_pairs(length):
    first = [(i, i ^ 1) for i in range(length)]
    second = [(i, i + 1 if i % 2 else i - 1) for i in range(1, length - 1)]
    return first, second


def swap_rims(x_send, send_b, corner_b, counts):
    count_x, count_y, _ = counts
    axes, count = ("gx", "gy"), count_x * count_y
    corner = swap(corner_b, axes, count, count_y + 2)
    x_rim = swap(x_send, axes, count, count_y)
    across = swap(send_b, axes, count, 2)
    return x_rim, across, corner


def line_sides(axis, pair_a, pair_b):
    even = lax.axis_index(axis) % 2 == 0
    return jnp.where(even, pair_b, pair_a), jnp.where(even, pair_a, pair_b)


def relay_rims_kernel(x_rim, across, corner, send_a, send, side):
    face, lines = across.shape[0], corner.shape[0]
    pitch = x_rim.shape[0] // lines
    even = lax.axis_index("gy") % 2 == 0
    for part in range(0, x_rim.shape[1], 128):
        columns = slice(part, part + 128)
        side[...] = x_rim[:, columns].astype(F32)
        ends = [side[pl.ds(y, lines, stride=pitch), :] for y in (pitch - 1, 0)]
        send[face + lines : face + 2 * lines, columns] = jnp.where(even, ends[0], ends[1]).astype(BF16)
    send[face + 2 * lines :, :] = send_a[...]
    send[:face, :] = across[...]
    send[face : face + lines, :] = corner[...]


def relay_rims(x_rim, across, corner, send_a, counts):
    rows = 2 * (across.shape[0] + corner.shape[0])
    send = local_call(
        relay_rims_kernel,
        "relay_rims",
        shape_of((rows, across.shape[1])),
        [pltpu.VMEM((x_rim.shape[0], 128), F32)],
    )(x_rim, across, corner, send_a)
    return swap(send, ("gx", "gy"), counts[0] * counts[1], 1)


def y_rims(relayed, lines):
    py = lax.axis_index("gy")
    face = relayed.shape[0] // 2 - lines
    inner = (py > 0) & (py < lax.axis_size("gy") - 1)
    face_b = jnp.where(inner, relayed[:face, :].astype(F32), 0.0)
    corner_b = jnp.where(inner, relayed[face : face + lines, :].astype(F32), 0.0)
    corner_a = relayed[face + lines : face + 2 * lines, :].astype(F32)
    face_a = relayed[face + 2 * lines :, :].astype(F32)
    return *line_sides("gy", face_a, face_b), *line_sides("gy", corner_a, corner_b)


def plane_index(count_y):
    return lax.axis_index("gx") * count_y + lax.axis_index("gy")


def plane_rows(ref, z):
    _, size_x, size_y, channels = ref.shape
    return ref[z].astype(F32).reshape(size_x * size_y, channels)


def hand_out(blocks, outs, me):
    for d, out in enumerate(outs):
        out[...] = blocks[me ^ d]


def take_in(parts, blocks, me):
    for d, part in enumerate(parts):
        blocks[me ^ d] = part[...]


def total_of(parts):
    terms = [part[...].astype(F32) for part in parts]
    while len(terms) > 1:
        terms = [terms[i] + terms[i + 1] for i in range(0, len(terms), 2)]
    return terms[0]


def back_kernel(count_z, cotangent, w_up, order, *refs):
    sends, (ordered, blocks) = refs[:count_z], refs[count_z:]
    size_z, size_x, size_y, channels = cotangent.shape
    own = size_x * size_y
    quarter = own // 4
    for z in range(size_z):
        ordered[z] = matmul(order[...], plane_rows(cotangent, z).astype(BF16)).astype(BF16)
    back = None
    for s in range(8):
        a, bc = s // 4, s % 4
        cells = jnp.concatenate(
            [ordered[2 * kz + a, bc * quarter : (bc + 1) * quarter, :] for kz in range(size_z // 2)], axis=0
        )
        term = matmul_nt(cells, w_up[s])
        back = term if back is None else back + term
    back = back.astype(BF16)
    group = back.shape[1] // count_z
    for q in range(count_z):
        blocks[q] = back[:, q * group : (q + 1) * group]
    hand_out(blocks, sends, lax.axis_index("gz"))


def deepen(volume, z_a, z_b, deep, pitch):
    size_z, size_x, size_y, channels = volume.shape
    own = size_x * size_y
    below, above = line_sides("gz", z_a[...], z_b[...])
    deep[:own, :] = below.astype(F32).reshape(own, channels)
    for z in range(size_z):
        deep[(z + 1) * pitch : (z + 1) * pitch + own, :] = plane_rows(volume, z)
    deep[(size_z + 1) * pitch : (size_z + 1) * pitch + own, :] = above.astype(F32).reshape(own, channels)


def ends_kernel(volume, send_a, send_b):
    below, above = volume[0], volume[volume.shape[0] - 1]
    send_b[...], send_a[...] = line_sides("gz", above, below)


def faces_kernel(volume, z_a, z_b, x_send, send_a, send_b, corner_b, deep):
    size_z, size_x, size_y, channels = volume.shape
    own = size_x * size_y
    planes = x_send.shape[0] // size_y
    deepen(volume, z_a, z_b, deep, own)
    start = (size_z + 2) * own
    deep[start:, :] = jnp.zeros((deep.shape[0] - start, channels), F32)
    first = lax.axis_index("gx") == 0
    far = (size_x - 1) * size_y

    def x_face(start):
        return jnp.concatenate([deep[z * own + start : z * own + start + size_y, :] for z in range(planes)], axis=0)

    x_send[...] = jnp.where(first, x_face(far), x_face(0)).astype(BF16)
    faces, corners = [], []
    for y in (0, size_y - 1):
        faces.append(deep[pl.ds(y, send_a.shape[0], stride=size_y), :].astype(BF16))
        ends = [deep[pl.ds(start + y, planes, stride=own), :] for start in (far, 0)]
        corners.append(jnp.where(first, ends[0], ends[1]).astype(BF16))
    send_b[...], send_a[...] = line_sides("gy", faces[1], faces[0])
    corner_b[...], _ = line_sides("gy", corners[1], corners[0])


def hidden_kernel(count_z, volume, z_a, z_b, x_rim, relayed, taps, w_conv, w_down, *refs):
    backs, (hidden, slope, rim), sends, (rim32, cells) = (
        refs[:count_z],
        refs[count_z : count_z + 3],
        refs[count_z + 3 : -2],
        refs[-2:],
    )
    size_z, size_x, size_y, channels = volume.shape
    own = size_x * size_y
    quarter = own // 4
    planes = size_z + 2
    pitch = 2 * own
    first = lax.axis_index("gx") == 0
    deepen(volume, z_a, z_b, rim32, pitch)
    y_low, y_high, xy_low, xy_high = y_rims(relayed, x_rim.shape[0] // size_y)
    x_side = x_rim[...].astype(F32)
    x_low, x_high = jnp.where(first, 0.0, x_side), jnp.where(first, x_side, 0.0)
    faces = (x_low, x_high, y_low, y_high)
    for z in range(planes):
        for part, block in enumerate(faces):
            start = z * pitch + own + 8 * part
            rim32[start : start + 8, :] = block[8 * z : 8 * (z + 1), :]
        rim32[z * pitch + own + 32 : (z + 1) * pitch, :] = jnp.zeros((own - 32, channels), F32)
    corners = ((xy_low, 7, True), (xy_high, 0, True), (xy_low, 7, False), (xy_high, 0, False))
    for part, (block, row, low) in enumerate(corners):
        start = own + 32 + 8 * part + row
        value = jnp.where(first == low, 0.0, block)
        rim32[pl.ds(start, 8, stride=pitch), :] = value[:8, :]
        for z in range(8, planes):
            rim32[z * pitch + start : z * pitch + start + 1, :] = value[z : z + 1, :]
    for z in range(0, planes, 2):
        pair = [rim32[(z + i) * pitch : (z + i + 1) * pitch, :].astype(BF16) for i in range(2)]
        moved = matmul(taps[...], jnp.concatenate(pair, axis=1)).astype(BF16)
        for i in range(2):
            rim[z + i] = pair[i]
            for bc in range(9):
                cells[z + i, :, bc * channels : (bc + 1) * channels] = moved[
                    bc * own : (bc + 1) * own, i * channels : (i + 1) * channels
                ]
    weights = [w_conv[9 * a : 9 * (a + 1)].reshape(9 * channels, channels) for a in range(3)]
    window = cells[: size_z + 1].reshape((size_z + 1) * own, 9 * channels)
    both = matmul(window, jnp.concatenate(weights[:2], axis=1))
    window = cells[2:].reshape(size_z * own, 9 * channels)
    pre = both[:-own, :channels] + both[own:, channels:] + matmul(window, weights[2])
    sig = jax.nn.sigmoid(pre)
    slope[...] = (sig * (1.0 + pre * (1.0 - sig))).reshape(size_z, own, channels)
    hidden[...] = (pre * sig).astype(BF16).reshape(size_z, own, channels)
    parts = []
    for s in range(8):
        a, bc = s // 4, s % 4
        parts.append(
            jnp.concatenate(
                [hidden[2 * kz + a, bc * quarter : (bc + 1) * quarter, :] for kz in range(size_z // 2)], axis=0
            )
        )
    coarse = matmul(jnp.concatenate(parts, axis=1), w_down[...].reshape(8 * channels, w_down.shape[2]))
    coarse = coarse.astype(BF16)
    wide = coarse.shape[1]
    for send, back in zip(sends, backs):
        send[:, :wide] = coarse
        send[:, wide:] = back[...]


def rim_transpose_kernel(count_p, rim, taps_t, turned):
    planes, rows, channels = rim.shape
    share = channels // count_p
    for pair in range(planes // 2):
        sides = [rim[2 * pair + i].astype(F32).T for i in range(2)]
        moved = matmul(jnp.concatenate(sides, axis=1).astype(BF16), taps_t[...]).astype(BF16)
        for bc in range(9):
            for p in range(count_p):
                start = (bc * count_p // 2 + p // 2) * share
                turned[p % 2, start : start + share, pair * rows : (pair + 1) * rows] = moved[
                    p * share : (p + 1) * share, bc * rows : (bc + 1) * rows
                ]


def column_kernel(count_z, *refs):
    parts, picks, (column, back, x_send, send_a, send_b, corner_b) = refs[:count_z], refs[count_z], refs[count_z + 1 :]
    own_cells = parts[0].shape[0]
    wide = column.shape[1]
    pz = lax.axis_index("gz")
    for i, part in enumerate(parts):
        rows = pl.ds(pl.multiple_of((pz ^ (-i % count_z)) * own_cells, own_cells), own_cells)
        column[rows, :] = part[:, :wide]
        back[rows, :] = part[:, wide:]
    rims = matmul(picks[lax.axis_index("gx")], column[...]).astype(BF16)
    cuts, start = [], 0
    for size in (x_send.shape[0], *[send_a.shape[0]] * 2, *[corner_b.shape[0]] * 2):
        cuts.append(rims[start : start + size, :])
        start += size
    x_send[...] = cuts[0]
    send_b[...], send_a[...] = line_sides("gy", cuts[2], cuts[1])
    corner_b[...], _ = line_sides("gy", cuts[4], cuts[3])


def bottle_kernel(quarter, column, back, x_rim, relayed, shift, w_bottle, bottle, grad, corners, window):
    cells, wide = column.shape
    outs = w_bottle.shape[2]
    side = x_rim.shape[0]
    depth = cells // quarter
    span = 4 * quarter
    picks = shift[lax.axis_index("gx")]
    window[:quarter, :] = jnp.zeros((quarter, 9 * wide), BF16)
    window[(depth + 1) * quarter :, :] = jnp.zeros((quarter, 9 * wide), BF16)
    edge = side // (depth // 4)
    y_low, y_high, xy_low, xy_high = y_rims(relayed, depth)
    y_low, y_high = y_low.astype(BF16), y_high.astype(BF16)
    for g in range(depth // 4):
        corners[g, :4, :] = xy_low[4 * g : 4 * g + 4, :]
        corners[g, 4:8, :] = xy_high[4 * g : 4 * g + 4, :]
        corners[g, 8:, :] = jnp.zeros((8, wide), F32)
        faces = [block[g * edge : (g + 1) * edge, :] for block in (x_rim, y_low, y_high)]
        rows = [column[g * span : (g + 1) * span, :], *faces, corners[g].astype(BF16)]
        moved = matmul(picks, jnp.concatenate(rows, axis=0)).astype(BF16)
        for bc in range(9):
            window[quarter + g * span : quarter + (g + 1) * span, bc * wide : (bc + 1) * wide] = moved[
                bc * span : (bc + 1) * span, :
            ]
    spread_out = None
    for bc in range(9):
        weight = jnp.concatenate([w_bottle[9 * a + bc] for a in range(3)], axis=1)
        term = matmul(window[:, bc * wide : (bc + 1) * wide], weight)
        spread_out = term if spread_out is None else spread_out + term
    pre = spread_out[:cells, :outs]
    for a in range(1, 3):
        pre = pre + spread_out[a * quarter : a * quarter + cells, a * outs : (a + 1) * outs]
    sig = jax.nn.sigmoid(pre)
    bottle[...] = (pre * sig).astype(BF16)
    slope = sig * (1.0 + pre * (1.0 - sig))
    grad[...] = (back[...].astype(F32) * slope).astype(BF16)


def slices_kernel(count_y, quarter, column, *refs):
    sends, slices = refs[:-1], refs[-1]
    cells, wide = column.shape
    span = 4 * quarter
    half = 2 * quarter
    lane = lax.broadcasted_iota(jnp.int32, (half, 128), 1)
    for pair in range(wide // 128):
        for g in range(cells // span):
            top = column[g * span : g * span + half, pair * 128 : (pair + 1) * 128].astype(F32)
            end = column[g * span + half : (g + 1) * span, pair * 128 : (pair + 1) * 128].astype(F32)
            rows = slice(g * half, (g + 1) * half)
            slices[2 * pair, rows, :] = jnp.where(lane < 64, top, pltpu.roll(end, 64, 1)).astype(BF16)
            slices[2 * pair + 1, rows, :] = jnp.where(lane < 64, pltpu.roll(top, 64, 1), end).astype(BF16)
    p = plane_index(count_y)
    lines = slices.shape[1]
    for i, send in enumerate(sends):
        send[:lines, :] = slices[p ^ (2 * i)]
        send[lines:, :] = slices[p ^ (2 * i + 1)]


def coarse_grad_kernel(count_y, count_z, quarter, *refs):
    grads, (bottle, shift, w_bottle) = refs[: -count_z - 6], refs[-count_z - 6 : -count_z - 3]
    sends, (window, gathered, blocks) = refs[-count_z - 3 : -3], refs[-3:]
    count_p = len(grads)
    cells, outs = bottle.shape
    rows = count_p * quarter
    depth = cells // quarter
    own_cells = cells // count_z
    inputs = w_bottle.shape[1]
    p = plane_index(count_y)
    for i, part in enumerate(grads):
        gathered[p ^ (-i % count_p)] = part[...]
    mine = pl.multiple_of(p * quarter, quarter)
    picks = jnp.concatenate([shift[pl.ds((8 - bc) * rows + mine, quarter), :] for bc in range(9)], axis=0)
    window[:quarter, :] = jnp.zeros((quarter, 9 * outs), BF16)
    window[(depth + 1) * quarter :, :] = jnp.zeros((quarter, 9 * outs), BF16)
    for z in range(depth):
        plane = jnp.concatenate([gathered[q, z * quarter : (z + 1) * quarter, :] for q in range(count_p)], axis=0)
        moved = matmul(picks, plane).astype(BF16)
        for bc in range(9):
            window[(z + 1) * quarter : (z + 2) * quarter, bc * outs : (bc + 1) * outs] = moved[
                bc * quarter : (bc + 1) * quarter, :
            ]
    total = None
    for a in range(3):
        weight = jnp.concatenate([w_bottle[9 * a + bc] for bc in range(9)], axis=1)
        term = matmul_nt(window[(2 - a) * quarter : (2 - a + depth) * quarter, :], weight)
        total = term if total is None else total + term
    total = total.astype(BF16)
    for q in range(count_z):
        blocks[q, :, :inputs] = total[q * own_cells : (q + 1) * own_cells, :]
        blocks[q, :, inputs:] = bottle[q * own_cells : (q + 1) * own_cells, :]
    hand_out(blocks, sends, lax.axis_index("gz"))


def wide_kernel(count_y, quarter, *refs):
    parts, (wide, grads) = refs[:-2], refs[-2:]
    count_p, cells, outs = grads.shape
    rows = count_p * quarter
    depth = cells // quarter
    take_in(parts, grads, plane_index(count_y))
    planes = [
        jnp.concatenate([grads[q, z * quarter : (z + 1) * quarter, :] for q in range(count_p)], axis=0)
        for z in range(depth)
    ]
    zeros = jnp.zeros((rows, outs), BF16)
    for j in range(depth // 2):
        for slot in range(5):
            z = j // 2 * 4 + j % 2 + slot - 1
            wide[j * rows : (j + 1) * rows, slot * outs : (slot + 1) * outs] = planes[z] if 0 <= z < depth else zeros


def coarse_transpose_kernel(count_y, shift, *refs):
    parts, relayed, (turned, slices) = refs[:-3], refs[-3], refs[-2:]
    count_p, lines, _ = slices.shape
    rows = shift.shape[1]
    quarter = rows // count_p
    p = plane_index(count_y)
    for i, part in enumerate(parts):
        start = part.shape[0] - 2 * lines
        slices[p ^ (2 * i)] = part[start : start + lines, :]
        slices[p ^ (2 * i + 1)] = relayed[i * lines : (i + 1) * lines, :]
    for j in range(lines // quarter):
        plane = jnp.concatenate([slices[q, j * quarter : (j + 1) * quarter, :] for q in range(count_p)], axis=0)
        plane = plane.astype(F32).T.astype(BF16)
        for bc in range(9):
            turned[bc * 128 : (bc + 1) * 128, j * rows : (j + 1) * rows] = matmul(
                plane, shift[(8 - bc) * rows : (9 - bc) * rows, :]
            ).astype(BF16)


def grad_bottle_kernel(turned, wide, out):
    _, channels, outs = out.shape
    full = matmul(turned[...], wide[...])
    for bc in range(9):
        top = full[bc * 128 : bc * 128 + channels, :]
        end = full[bc * 128 + channels : (bc + 1) * 128, :]
        for a in range(3):
            out[9 * a + bc] = top[:, (2 - a) * outs : (3 - a) * outs] + end[:, (4 - a) * outs : (5 - a) * outs]


def half_grad(turned, shifted, parity, chip, out, blocks):
    chips, rows, channels = blocks.shape
    group = rows // 27
    full = matmul(turned[parity], shifted[...])
    for bc in range(9):
        for a in range(3):
            t = 9 * a + bc
            for q in range(chips):
                start = (bc * chips + q) * group
                blocks[q, t * group : (t + 1) * group, :] = full[
                    start : start + group, a * channels : (a + 1) * channels
                ].astype(BF16)
    for i in range(chips):
        out[i] = blocks[chip ^ i]


def hidden_grad_kernel(count_y, count_z, *refs):
    parts, (slope, ordered, w_down, turned) = refs[:count_z], refs[count_z : count_z + 4]
    shifted, bottle, give, bottles, blocks = refs[count_z + 4 :]
    size_z, own, channels = ordered.shape
    quarter = own // 4
    inputs = w_down.shape[2]
    pz = lax.axis_index("gz")
    grad = total_of([part.at[:, :inputs] for part in parts]).astype(BF16)
    for i, part in enumerate(parts):
        bottles[pz ^ (-i % count_z)] = part[:, inputs:]
    bottle[...] = jnp.concatenate([bottles[q] for q in range(count_z)], axis=1)
    shifted[...] = jnp.zeros_like(shifted)
    for s in range(8):
        a, bc = s // 4, s % 4
        spread_grad = matmul_nt(grad, w_down[s])
        for kz in range(size_z // 2):
            z = 2 * kz + a
            part = slice(bc * quarter, (bc + 1) * quarter)
            line = slice(kz * quarter, (kz + 1) * quarter)
            value = ((spread_grad[line, :] + ordered[z, part, :].astype(F32)) * slope[z, part, :]).astype(BF16)
            for t in range(3):
                start = (z + t) * own + bc * quarter
                shifted[start : start + quarter, t * channels : (t + 1) * channels] = value
    p = plane_index(count_y)
    half_grad(turned, shifted, 1 - p % 2, p // 2, give, blocks)


def keep_kernel(count_y, shifted, turned, keep, blocks):
    p = plane_index(count_y)
    half_grad(turned, shifted, p % 2, p // 2, keep, blocks)


def output_kernel(bottle, hidden, w_up, order_t, output, rows_out):
    size_z, own, channels = hidden.shape
    quarter = own // 4
    for s in range(8):
        a, bc = s // 4, s % 4
        lifted = matmul(bottle[...], w_up[s])
        for kz in range(size_z // 2):
            z = 2 * kz + a
            part = slice(bc * quarter, (bc + 1) * quarter)
            line = slice(kz * quarter, (kz + 1) * quarter)
            rows_out[z, part, :] = (lifted[line, :] + hidden[z, part, :].astype(F32)).astype(BF16)
    for z in range(size_z):
        plane = matmul(order_t[...], rows_out[z])
        output[z] = plane.reshape(output.shape[1:]).astype(BF16)


def pair_sum_kernel(keep, got, *refs):
    slices, sends = refs[: len(refs) // 2], refs[len(refs) // 2 :]
    rows = keep.shape[1]
    for i, (send, block) in enumerate(zip(sends, slices)):
        send[:rows, :] = (keep[i].astype(F32) + got[i].astype(F32)).astype(BF16)
        send[rows:, :] = block[...]


def relay_kernel(*refs):
    parts, send = refs[:-1], refs[-1]
    lines = send.shape[0] // len(parts)
    for i, part in enumerate(parts):
        send[i * lines : (i + 1) * lines, :] = part[part.shape[0] - lines :, :]


def plane_sum_kernel(*refs):
    parts, out = refs[:-1], refs[-1]
    out[...] = total_of([part.at[: out.shape[0], :] for part in parts]).astype(BF16)


def sum_kernel(*refs):
    out = refs[-1]
    out[...] = total_of(refs[:-1]).reshape(out.shape).astype(out.dtype)


def shape_of(shape, dtype=BF16):
    return jax.ShapeDtypeStruct(shape, dtype)


def gathered_body(counts, volume, cotangent, w_conv, w_down, w_bottle, w_up):
    count_x, count_y, count_z = counts
    count_p = count_x * count_y
    size_z, size_x, size_y, channels = volume.shape
    wide = w_down.shape[2]
    group = w_bottle.shape[2]
    half_x, half_y = size_x // 2, size_y // 2
    own = size_x * size_y
    quarter = half_x * half_y
    own_cells = size_z // 2 * quarter
    cells = count_z * own_cells
    depth = count_z * size_z // 2
    rows = count_p * quarter
    planes = size_z + 2
    share_c = channels // count_p
    share_w = wide // count_p
    plane_axes = ("gx", "gy")

    order, taps = fine_maps(size_x, size_y)
    pair_taps = np.zeros((2, 2 * own, 9, 2, own), np.float32)
    for i in range(2):
        pair_taps[i, :, :, i, :] = taps.transpose(2, 0, 1)
    shift = coarse_maps(count_x, count_y, half_x, half_y)
    order_m = jnp.asarray(order, BF16)
    order_t = jnp.asarray(order.T, BF16)
    taps_m = jnp.asarray(taps.reshape(9 * own, 2 * own), BF16)
    taps_t = jnp.asarray(pair_taps.reshape(4 * own, 18 * own), BF16)
    shift_m = jnp.asarray(shift.reshape(9 * rows, rows), BF16)

    send_maps, rim_maps = column_maps(half_x, half_y, depth)
    send_m = jnp.asarray(send_maps, BF16)
    rim_m = jnp.asarray(rim_maps.reshape(count_x, 36 * quarter, 8 * quarter), BF16)

    w_conv_t = jnp.transpose(w_conv, (1, 0, 2))
    w_bottle_t = jnp.transpose(w_bottle, (1, 0, 2))
    send_a, send_b = local_call(ends_kernel, "ends", [shape_of((size_x, size_y, channels))] * 2)(volume)
    z_pairs = line_pairs(count_z)
    z_b = lax.ppermute(send_b, "gz", z_pairs[1])
    z_a = lax.ppermute(send_a, "gz", z_pairs[0])
    *backs, ordered = local_call(
        lambda *refs: back_kernel(count_z, *refs),
        "back",
        [shape_of((own_cells, group))] * count_z + [shape_of((size_z, own, channels))],
        [pltpu.VMEM((count_z, own_cells, group), BF16)],
    )(cotangent, w_up, order_m)
    sends = local_call(
        faces_kernel,
        "faces",
        [shape_of((16 * size_y, channels))] + [shape_of((planes * size_x, channels))] * 2 + [shape_of((16, channels))],
        [pltpu.VMEM((16 * own, channels), F32)],
    )(volume, z_a, z_b)
    x_send, send_a, send_b, corner_b = sends
    x_rim, across, corner = swap_rims(x_send, send_b, corner_b, counts)
    relayed = relay_rims(x_rim, across, corner, send_a, counts)
    hidden, slope, rim, *sends = local_call(
        lambda *refs: hidden_kernel(count_z, *refs),
        "hidden",
        [
            shape_of((size_z, own, channels)),
            shape_of((size_z, own, channels), F32),
            shape_of((planes, 2 * own, channels)),
        ]
        + [shape_of((own_cells, wide + group))] * count_z,
        [
            pltpu.VMEM((planes * 2 * own, channels), F32),
            pltpu.VMEM((planes, own, 9 * channels), BF16),
        ],
        flops=2_000_000_000,
    )(volume, z_a, z_b, x_rim, relayed, taps_m, w_conv_t, w_down, *backs)
    parts = trade(sends, "gz", count_z)
    column, back, *sends = local_call(
        lambda *refs: column_kernel(count_z, *refs),
        "column",
        [shape_of((cells, wide)), shape_of((cells, group)), shape_of((depth * half_y, wide))]
        + [shape_of((depth * half_x, wide))] * 2
        + [shape_of((depth, wide))],
    )(parts[0], *parts[:0:-1], send_m)
    x_send, send_a, send_b, corner_b = sends
    x_rim, across, corner = swap_rims(x_send, send_b, corner_b, counts)
    relayed = relay_rims(x_rim, across, corner, send_a, counts)
    slices = local_call(
        lambda *refs: slices_kernel(count_y, quarter, *refs),
        "slices",
        [shape_of((cells, 128))] * (count_p // 2),
        [pltpu.VMEM((count_p, cells // 2, 128), BF16)],
    )(column)
    column, *slices = lax.optimization_barrier((column, *slices))
    bottle, grad = local_call(
        lambda *refs: bottle_kernel(quarter, *refs),
        "bottle",
        [shape_of((cells, group))] * 2,
        [
            pltpu.VMEM((depth // 4, 16, wide), F32),
            pltpu.VMEM(((depth + 2) * quarter, 9 * wide), BF16),
        ],
        flops=2_000_000_000,
    )(column, back, x_rim, relayed, rim_m, w_bottle_t)
    grads = [None] * count_p
    grads[0] = grad
    for d in (6, 4, 2):
        grads[d] = swap(grad, plane_axes, count_p, d)
    for d in (0, 2, 4, 6):
        grads[d + 1] = swap(grads[d], plane_axes, count_p, 1)
    sends = local_call(
        lambda *refs: coarse_grad_kernel(count_y, count_z, quarter, *refs),
        "coarse_grad",
        [shape_of((own_cells, wide + group))] * count_z,
        [
            pltpu.VMEM(((depth + 2) * quarter, 9 * group), BF16),
            pltpu.VMEM((count_p, cells, group), BF16),
            pltpu.VMEM((count_z, own_cells, wide + group), BF16),
        ],
    )(grads[0], *grads[:0:-1], bottle, shift_m, w_bottle_t)
    parts = trade(sends, "gz", count_z)
    rim, _ = lax.optimization_barrier((rim, sends[1]))
    turned = local_call(
        lambda *refs: rim_transpose_kernel(count_p, *refs),
        "rim_transpose",
        shape_of((2, 9 * channels // 2, planes * own)),
    )(rim, taps_t)
    shifted, bottle, give = local_call(
        lambda *refs: hidden_grad_kernel(count_y, count_z, *refs),
        "hidden_grad",
        [
            shape_of((planes * own, 3 * channels)),
            shape_of((own_cells, wide)),
            shape_of((count_p // 2, 27 * share_c, channels)),
        ],
        [
            pltpu.VMEM((count_z, own_cells, group), BF16),
            pltpu.VMEM((count_p // 2, 27 * share_c, channels), BF16),
        ],
    )(parts[0], *parts[:0:-1], slope, ordered, w_down, turned)
    got = swap(give, plane_axes, count_p, 1)
    keep = local_call(
        lambda *refs: keep_kernel(count_y, *refs),
        "keep",
        shape_of((count_p // 2, 27 * share_c, channels)),
        [pltpu.VMEM((count_p // 2, 27 * share_c, channels), BF16)],
    )(shifted, turned)
    output = local_call(
        output_kernel,
        "output",
        shape_of(volume.shape),
        [pltpu.VMEM((size_z, own, channels), BF16)],
    )(bottle, hidden, w_up, order_t)
    sends = local_call(
        pair_sum_kernel,
        "pair_sum",
        [shape_of((27 * share_c + cells, channels))] * (count_p // 2),
    )(keep, got, *slices)
    parts = [sends[0]] + [swap(sends[d // 2], plane_axes, count_p, d) for d in (6, 4, 2)]
    *parts, output = lax.optimization_barrier((*parts, output))
    part = local_call(plane_sum_kernel, "plane_sum", shape_of((27 * share_c, channels)))(*parts)
    firsts = [parts[0], *parts[:0:-1]]
    *late, _ = lax.optimization_barrier((*firsts, part))
    relay = local_call(relay_kernel, "relay", shape_of((count_p // 2 * (cells // 2), 128)))(*late)
    relayed = swap(relay, plane_axes, count_p, 1)
    coarse_turned = local_call(
        lambda *refs: coarse_transpose_kernel(count_y, *refs),
        "coarse_transpose",
        shape_of((18 * share_w, depth // 2 * rows)),
        [pltpu.VMEM((count_p, cells // 2, 128), BF16)],
    )(shift_m, *late, relayed)
    got = swap(part, "gz", count_z, 1)
    wide_grads = local_call(
        lambda *refs: wide_kernel(count_y, quarter, *refs),
        "wide",
        shape_of((depth // 2 * rows, 5 * group)),
        [pltpu.VMEM((count_p, cells, group), BF16)],
    )(*grads)
    got, wide_grads, coarse_turned = lax.optimization_barrier((got, wide_grads, coarse_turned))
    part = local_call(sum_kernel, "depth_sum", shape_of((27 * share_c, channels)))(part, got)
    got = swap(part, "gz", count_z, 2)
    grad_bottle = local_call(
        grad_bottle_kernel,
        "grad_bottle",
        shape_of((27, share_w, group), F32),
        flops=4_000_000_000,
    )(coarse_turned, wide_grads)
    grad_conv = local_call(
        sum_kernel,
        "grad_conv",
        shape_of((27, share_c, channels), F32),
    )(part, got)
    return (output, jnp.transpose(grad_conv, (1, 0, 2)), jnp.transpose(grad_bottle, (1, 0, 2)))


def with_halo(cells, sides, width):
    for axis, dim in sides:
        count = lax.axis_size(axis)
        ends = count - 1
        head = lax.slice_in_dim(cells, 0, width, axis=dim)
        tail = lax.slice_in_dim(cells, cells.shape[dim] - width, cells.shape[dim], axis=dim)
        cells = jnp.concatenate(
            [
                lax.ppermute(tail, axis, [(i, (i + 1) % count) for i in range(ends)]),
                cells,
                lax.ppermute(head, axis, [((i + 1) % count, i) for i in range(ends)]),
            ],
            axis=dim,
        )
    return cells


def silu_slope(values):
    sig = jax.nn.sigmoid(values)
    return sig * (1.0 + values * (1.0 - sig))


def conv_forward(padded, weight, extent):
    size_z, size_x, size_y = extent
    count_cells = size_z * size_x * size_y
    summed = jnp.zeros((count_cells, weight.shape[2]), jnp.float32)
    for tap_index in range(27):
        shift_z, shift_x, shift_y = (tap_index // 9, tap_index // 3 % 3, tap_index % 3)
        window = padded[
            shift_z : shift_z + size_z, shift_x : shift_x + size_x, shift_y : shift_y + size_y, :
        ]
        window = window.reshape(count_cells, padded.shape[3])
        summed = summed + jnp.dot(
            window, weight[:, tap_index, :], preferred_element_type=jnp.float32
        )
    return summed.reshape(size_z, size_x, size_y, weight.shape[2])


def conv_weight_grad(padded, gradient, extent):
    size_z, size_x, size_y = extent
    count_cells = size_z * size_x * size_y
    flat_gradient = gradient.reshape(count_cells, gradient.shape[3])
    pieces = []
    for tap_index in range(27):
        shift_z, shift_x, shift_y = (tap_index // 9, tap_index // 3 % 3, tap_index % 3)
        window = padded[
            shift_z : shift_z + size_z, shift_x : shift_x + size_x, shift_y : shift_y + size_y, :
        ]
        window = window.reshape(count_cells, padded.shape[3])
        pieces.append(
            lax.dot_general(
                window, flat_gradient, (((0,), (0,)), ((), ())), preferred_element_type=jnp.float32
            )
        )
    return jnp.stack(pieces, axis=1)


def conv_input_grad(padded, weight, extent):
    size_z, size_x, size_y = extent
    count_cells = size_z * size_x * size_y
    summed = jnp.zeros((count_cells, weight.shape[0]), jnp.float32)
    for tap_index in range(27):
        shift_z, shift_x, shift_y = (2 - tap_index // 9, 2 - tap_index // 3 % 3, 2 - tap_index % 3)
        window = padded[
            shift_z : shift_z + size_z, shift_x : shift_x + size_x, shift_y : shift_y + size_y, :
        ]
        window = window.reshape(count_cells, padded.shape[3])
        summed = summed + lax.dot_general(
            window,
            weight[:, tap_index, :],
            (((1,), (1,)), ((), ())),
            preferred_element_type=jnp.float32,
        )
    return summed.reshape(size_z, size_x, size_y, weight.shape[0])


def pool_features(fine, kernel):
    size_z, size_x, size_y, channels = fine.shape
    blocks = fine.reshape(size_z // 2, 2, size_x // 2, 2, size_y // 2, 2, channels)
    kernel_cube = kernel.reshape(2, 2, 2, kernel.shape[1], kernel.shape[2])
    return jnp.einsum(
        "zaxbycf,abcfg->zxyg", blocks, kernel_cube, preferred_element_type=jnp.float32
    )


def pool_adjoint(coarse_in, kernel):
    size_z, size_x, size_y, wide_channels = coarse_in.shape
    kernel_cube = kernel.reshape(2, 2, 2, kernel.shape[1], kernel.shape[2])
    result = jnp.einsum(
        "zxyg,abcfg->zaxbycf", coarse_in, kernel_cube, preferred_element_type=jnp.float32
    )
    return result.reshape(2 * size_z, 2 * size_x, 2 * size_y, kernel.shape[1])


def lift_features(coarse_in, kernel):
    size_z, size_x, size_y, wide_channels = coarse_in.shape
    kernel_cube = kernel.reshape(2, 2, 2, kernel.shape[1], kernel.shape[2])
    result = jnp.einsum(
        "zxyg,abcgf->zaxbycf", coarse_in, kernel_cube, preferred_element_type=jnp.float32
    )
    return result.reshape(2 * size_z, 2 * size_x, 2 * size_y, kernel.shape[2])


def lift_adjoint(fine, kernel):
    size_z, size_x, size_y, channels = fine.shape
    blocks = fine.reshape(size_z // 2, 2, size_x // 2, 2, size_y // 2, 2, channels)
    kernel_cube = kernel.reshape(2, 2, 2, kernel.shape[1], kernel.shape[2])
    return jnp.einsum(
        "zaxbycf,abcgf->zxyg", blocks, kernel_cube, preferred_element_type=jnp.float32
    )


def column_body(volume, cotangent, w_conv, w_down, w_bottle, w_up):
    size_z, size_x, size_y, channels = volume.shape
    group_channels = w_bottle.shape[2]
    half_x = size_x // 2
    half_y = size_y // 2
    padded = with_halo(volume, (("gx", 1), ("gy", 2), ("gz", 0)), 1)
    pre_hidden = conv_forward(padded, w_conv, (size_z, size_x, size_y))
    hidden = jax.nn.silu(pre_hidden).astype(jnp.bfloat16)
    hidden_slope = silu_slope(pre_hidden)
    coarse = pool_features(hidden, w_down).astype(jnp.bfloat16)
    stacked = lax.all_gather(coarse, "gz", axis=0, tiled=True)
    rimmed = with_halo(stacked, (("gx", 1), ("gy", 2)), 1)
    column_z = rimmed.shape[0]
    coarse_pad = jnp.pad(rimmed, ((1, 1), (0, 0), (0, 0), (0, 0)))
    pre_bottle = conv_forward(coarse_pad, w_bottle, (column_z, half_x, half_y))
    bottle = jax.nn.silu(pre_bottle).astype(jnp.bfloat16)
    bottle_slope = silu_slope(pre_bottle)
    own_start = lax.axis_index("gz") * group_channels
    own_up = lax.dynamic_slice_in_dim(w_up, own_start, group_channels, 1)
    lifted = lax.psum_scatter(
        lift_features(bottle, own_up).astype(jnp.bfloat16), "gz", scatter_dimension=0, tiled=True
    ).astype(jnp.float32)
    output = (lifted + hidden.astype(jnp.float32)).astype(jnp.bfloat16)
    back_bottle = lift_adjoint(cotangent, w_up).astype(jnp.bfloat16)
    split_grad = lax.all_to_all(back_bottle, "gz", split_axis=3, concat_axis=0, tiled=True)
    bottle_grad = (split_grad.astype(jnp.float32) * bottle_slope).astype(jnp.bfloat16)
    grad_bottle = lax.psum_scatter(
        conv_weight_grad(coarse_pad, bottle_grad, (column_z, half_x, half_y)),
        ("gx", "gy"),
        scatter_dimension=0,
        tiled=True,
    )
    grad_rimmed = with_halo(bottle_grad, (("gx", 1), ("gy", 2)), 1)
    grad_pad = jnp.pad(grad_rimmed, ((1, 1), (0, 0), (0, 0), (0, 0)))
    coarse_grad = lax.psum_scatter(
        conv_input_grad(
            grad_pad, w_bottle, (lax.axis_size("gz") * (size_z // 2), half_x, half_y)
        ).astype(jnp.bfloat16),
        "gz",
        scatter_dimension=0,
        tiled=True,
    )
    hidden_grad = (
        (pool_adjoint(coarse_grad, w_down) + cotangent.astype(jnp.float32)) * hidden_slope
    ).astype(jnp.bfloat16)
    full_term = conv_weight_grad(padded, hidden_grad, (size_z, size_x, size_y))
    depth_summed = lax.psum(full_term.astype(jnp.bfloat16), "gz").astype(jnp.float32)
    grad_conv = lax.psum_scatter(depth_summed, ("gx", "gy"), scatter_dimension=0, tiled=True)
    return (output, grad_conv, grad_bottle)


def fits_one_plane(counts, brick, wide):
    count_p = counts[0] * counts[1]
    size_z, size_x, size_y, channels = brick
    return (
        counts == (2, 4, 4)
        and count_p * (size_x // 2) * (size_y // 2) == 128
        and wide // count_p == 64
        and (size_z, size_x, size_y, channels) == (8, 8, 8, 128)
    )


def solution(mesh):
    in_specs = (
        P("gz", "gx", "gy", None),
        P("gz", "gx", "gy", None),
        P(),
        P(),
        P(None, None, "gz"),
        P(),
    )
    out_specs = (
        P("gz", "gx", "gy", None),
        P(("gx", "gy"), None, None),
        P(("gx", "gy"), None, "gz"),
    )
    counts = (mesh.shape["gx"], mesh.shape["gy"], mesh.shape["gz"])

    def body(volume, cotangent, w_conv, w_down, w_bottle, w_up):
        if fits_one_plane(counts, volume.shape, w_down.shape[2]):
            return gathered_body(counts, volume, cotangent, w_conv, w_down, w_bottle, w_up)
        return column_body(volume, cotangent, w_conv, w_down, w_bottle, w_up)

    return jax.shard_map(body, mesh=mesh, in_specs=in_specs, out_specs=out_specs, check_vma=False)
```

```python
import numpy as np
import jax
import jax.numpy as jnp
from jax import lax
from jax.experimental import pallas as pl
from jax.experimental.pallas import tpu as pltpu
from jax.sharding import PartitionSpec as P

BF16 = jnp.bfloat16
F32 = jnp.float32
VMEM_LIMIT = 24 * 1024 * 1024


def local_call(kernel, name, out_shapes, scratch=(), flops=300_000_000):
    whole = pl.BlockSpec(memory_space=pltpu.VMEM)

    def call(*operands):
        return pl.pallas_call(
            kernel,
            name=name,
            out_shape=out_shapes,
            in_specs=[whole] * len(operands),
            out_specs=jax.tree.map(lambda _: whole, out_shapes),
            scratch_shapes=list(scratch),
            compiler_params=pltpu.CompilerParams(vmem_limit_bytes=VMEM_LIMIT),
            cost_estimate=pl.CostEstimate(flops=flops, bytes_accessed=flops // 1000, transcendentals=0),
        )(*operands)

    return call


def matmul(left, right):
    return jnp.dot(left, right, preferred_element_type=F32)


def matmul_nt(left, right):
    return lax.dot_general(left, right, (((1,), (1,)), ((), ())), preferred_element_type=F32)


def sub_order(size_x, size_y):
    half_x, half_y = size_x // 2, size_y // 2
    return {
        (2 * kx + b, 2 * ky + c): ((2 * b + c) * half_x + kx) * half_y + ky
        for b in range(2)
        for c in range(2)
        for kx in range(half_x)
        for ky in range(half_y)
    }


def fine_maps(size_x, size_y):
    own = size_x * size_y
    rows = sub_order(size_x, size_y)
    order = np.zeros((own, own), np.float32)
    taps = np.zeros((9, own, 2 * own), np.float32)
    for (x, y), row in rows.items():
        order[row, x * size_y + y] = 1
        for b in range(3):
            for c in range(3):
                sx, sy = x + b - 1, y + c - 1
                if sx < 0:
                    part = 0 if 0 <= sy < size_y else (4 if sy < 0 else 5)
                    source = own + 8 * part + sy % size_y
                elif sx >= size_x:
                    part = 1 if 0 <= sy < size_y else (6 if sy < 0 else 7)
                    source = own + 8 * part + sy % size_y
                elif sy < 0:
                    source = own + 16 + sx
                elif sy >= size_y:
                    source = own + 24 + sx
                else:
                    source = sx * size_y + sy
                taps[3 * b + c, row, source] = 1
    return order, taps


def coarse_maps(count_x, count_y, half_x, half_y):
    wide_x, wide_y = count_x * half_x, count_y * half_y

    def row_of(x, y):
        brick = (x // half_x) * count_y + y // half_y
        return (brick * half_x + x % half_x) * half_y + y % half_y

    shift = np.zeros((9, wide_x * wide_y, wide_x * wide_y), np.float32)
    for x in range(wide_x):
        for y in range(wide_y):
            for b in range(3):
                for c in range(3):
                    sx, sy = x + b - 1, y + c - 1
                    if 0 <= sx < wide_x and 0 <= sy < wide_y:
                        shift[3 * b + c, row_of(x, y), row_of(sx, sy)] = 1
    return shift


def column_maps(half_x, half_y, depth):
    quarter = half_x * half_y
    rows = depth * quarter
    send = np.zeros((2, depth * (half_y + 2 * half_x + 2), rows), np.float32)
    rim = np.zeros((2, 9, 4, quarter, 8 * quarter), np.float32)
    for px in range(2):
        edge = 0 if px else half_x - 1
        for z in range(depth):
            base = z * quarter
            for ky in range(half_y):
                send[px, z * half_y + ky, base + edge * half_y + ky] = 1
            for side, ky in enumerate((0, half_y - 1)):
                row = depth * (half_y + side * half_x) + z * half_x
                for kx in range(half_x):
                    send[px, row + kx, base + kx * half_y + ky] = 1
                send[px, depth * (half_y + 2 * half_x + side) + z, base + edge * half_y + ky] = 1
    for px in range(2):
        for b in range(3):
            for c in range(3):
                for kx in range(half_x):
                    for ky in range(half_y):
                        sx, sy = kx + b - 1, ky + c - 1
                        beyond = sx < 0 if px else sx >= half_x
                        if (sx < 0 or sx >= half_x) and not beyond:
                            continue
                        for z in range(4):
                            if beyond and 0 <= sy < half_y:
                                source = 4 * quarter + z * half_y + sy
                            elif beyond:
                                source = 7 * quarter + 4 * (sy >= half_y) + z
                            elif sy < 0:
                                source = 5 * quarter + z * half_x + sx
                            elif sy >= half_y:
                                source = 6 * quarter + z * half_x + sx
                            else:
                                source = z * quarter + sx * half_y + sy
                            rim[px, 3 * b + c, z, kx * half_y + ky, source] = 1
    return send, rim


def swap(block, axes, count, distance):
    return lax.ppermute(block, axes, [(i, i ^ distance) for i in range(count)])


def trade(blocks, axes, count):
    got = {d: swap(blocks[d], axes, count, d) for d in reversed(range(1, count))}
    return [blocks[0]] + [got[d] for d in range(1, count)]


def line_pairs(length):
    first = [(i, i ^ 1) for i in range(length)]
    second = [(i, i + 1 if i % 2 else i - 1) for i in range(1, length - 1)]
    return first, second


def swap_rims(x_send, send_b, corner_b, counts):
    count_x, count_y, _ = counts
    axes, count = ("gx", "gy"), count_x * count_y
    corner = swap(corner_b, axes, count, count_y + 2)
    x_rim = swap(x_send, axes, count, count_y)
    across = swap(send_b, axes, count, 2)
    return x_rim, across, corner


def line_sides(axis, pair_a, pair_b):
    even = lax.axis_index(axis) % 2 == 0
    return jnp.where(even, pair_b, pair_a), jnp.where(even, pair_a, pair_b)


def relay_rims_kernel(x_rim, across, corner, send_a, send, side):
    face, lines = across.shape[0], corner.shape[0]
    pitch = x_rim.shape[0] // lines
    even = lax.axis_index("gy") % 2 == 0
    for part in range(0, x_rim.shape[1], 128):
        columns = slice(part, part + 128)
        side[...] = x_rim[:, columns].astype(F32)
        ends = [side[pl.ds(y, lines, stride=pitch), :] for y in (pitch - 1, 0)]
        send[face + lines : face + 2 * lines, columns] = jnp.where(even, ends[0], ends[1]).astype(BF16)
    send[face + 2 * lines :, :] = send_a[...]
    send[:face, :] = across[...]
    send[face : face + lines, :] = corner[...]


def relay_rims(x_rim, across, corner, send_a, counts):
    rows = 2 * (across.shape[0] + corner.shape[0])
    send = local_call(
        relay_rims_kernel,
        "relay_rims",
        shape_of((rows, across.shape[1])),
        [pltpu.VMEM((x_rim.shape[0], 128), F32)],
    )(x_rim, across, corner, send_a)
    return swap(send, ("gx", "gy"), counts[0] * counts[1], 1)


def y_rims(relayed, lines):
    py = lax.axis_index("gy")
    face = relayed.shape[0] // 2 - lines
    inner = (py > 0) & (py < lax.axis_size("gy") - 1)
    face_b = jnp.where(inner, relayed[:face, :].astype(F32), 0.0)
    corner_b = jnp.where(inner, relayed[face : face + lines, :].astype(F32), 0.0)
    corner_a = relayed[face + lines : face + 2 * lines, :].astype(F32)
    face_a = relayed[face + 2 * lines :, :].astype(F32)
    return *line_sides("gy", face_a, face_b), *line_sides("gy", corner_a, corner_b)


def plane_index(count_y):
    return lax.axis_index("gx") * count_y + lax.axis_index("gy")


def plane_rows(ref, z):
    _, size_x, size_y, channels = ref.shape
    return ref[z].astype(F32).reshape(size_x * size_y, channels)


def hand_out(blocks, outs, me):
    for d, out in enumerate(outs):
        out[...] = blocks[me ^ d]


def take_in(parts, blocks, me):
    for d, part in enumerate(parts):
        blocks[me ^ d] = part[...]


def total_of(parts):
    terms = [part[...].astype(F32) for part in parts]
    while len(terms) > 1:
        terms = [terms[i] + terms[i + 1] for i in range(0, len(terms), 2)]
    return terms[0]


def back_kernel(count_z, cotangent, w_up, order, *refs):
    sends, (ordered, blocks) = refs[:count_z], refs[count_z:]
    size_z, size_x, size_y, channels = cotangent.shape
    own = size_x * size_y
    quarter = own // 4
    for z in range(size_z):
        ordered[z] = matmul(order[...], plane_rows(cotangent, z).astype(BF16)).astype(BF16)
    back = None
    for s in range(8):
        a, bc = s // 4, s % 4
        cells = jnp.concatenate(
            [ordered[2 * kz + a, bc * quarter : (bc + 1) * quarter, :] for kz in range(size_z // 2)], axis=0
        )
        term = matmul_nt(cells, w_up[s])
        back = term if back is None else back + term
    back = back.astype(BF16)
    group = back.shape[1] // count_z
    for q in range(count_z):
        blocks[q] = back[:, q * group : (q + 1) * group]
    hand_out(blocks, sends, lax.axis_index("gz"))


def deepen(volume, z_a, z_b, deep, pitch):
    size_z, size_x, size_y, channels = volume.shape
    own = size_x * size_y
    below, above = line_sides("gz", z_a[...], z_b[...])
    deep[:own, :] = below.astype(F32).reshape(own, channels)
    for z in range(size_z):
        deep[(z + 1) * pitch : (z + 1) * pitch + own, :] = plane_rows(volume, z)
    deep[(size_z + 1) * pitch : (size_z + 1) * pitch + own, :] = above.astype(F32).reshape(own, channels)


def ends_kernel(volume, send_a, send_b):
    below, above = volume[0], volume[volume.shape[0] - 1]
    send_b[...], send_a[...] = line_sides("gz", above, below)


def faces_kernel(volume, z_a, z_b, x_send, send_a, send_b, corner_b, deep):
    size_z, size_x, size_y, channels = volume.shape
    own = size_x * size_y
    planes = x_send.shape[0] // size_y
    deepen(volume, z_a, z_b, deep, own)
    start = (size_z + 2) * own
    deep[start:, :] = jnp.zeros((deep.shape[0] - start, channels), F32)
    first = lax.axis_index("gx") == 0
    far = (size_x - 1) * size_y

    def x_face(start):
        return jnp.concatenate([deep[z * own + start : z * own + start + size_y, :] for z in range(planes)], axis=0)

    x_send[...] = jnp.where(first, x_face(far), x_face(0)).astype(BF16)
    faces, corners = [], []
    for y in (0, size_y - 1):
        faces.append(deep[pl.ds(y, send_a.shape[0], stride=size_y), :].astype(BF16))
        ends = [deep[pl.ds(start + y, planes, stride=own), :] for start in (far, 0)]
        corners.append(jnp.where(first, ends[0], ends[1]).astype(BF16))
    send_b[...], send_a[...] = line_sides("gy", faces[1], faces[0])
    corner_b[...], _ = line_sides("gy", corners[1], corners[0])


def hidden_kernel(count_z, volume, z_a, z_b, x_rim, relayed, taps, w_conv, w_down, *refs):
    backs, (hidden, slope, rim), sends, (rim32, cells) = (
        refs[:count_z],
        refs[count_z : count_z + 3],
        refs[count_z + 3 : -2],
        refs[-2:],
    )
    size_z, size_x, size_y, channels = volume.shape
    own = size_x * size_y
    quarter = own // 4
    planes = size_z + 2
    pitch = 2 * own
    first = lax.axis_index("gx") == 0
    deepen(volume, z_a, z_b, rim32, pitch)
    y_low, y_high, xy_low, xy_high = y_rims(relayed, x_rim.shape[0] // size_y)
    x_side = x_rim[...].astype(F32)
    x_low, x_high = jnp.where(first, 0.0, x_side), jnp.where(first, x_side, 0.0)
    faces = (x_low, x_high, y_low, y_high)
    for z in range(planes):
        for part, block in enumerate(faces):
            start = z * pitch + own + 8 * part
            rim32[start : start + 8, :] = block[8 * z : 8 * (z + 1), :]
        rim32[z * pitch + own + 32 : (z + 1) * pitch, :] = jnp.zeros((own - 32, channels), F32)
    corners = ((xy_low, 7, True), (xy_high, 0, True), (xy_low, 7, False), (xy_high, 0, False))
    for part, (block, row, low) in enumerate(corners):
        start = own + 32 + 8 * part + row
        value = jnp.where(first == low, 0.0, block)
        rim32[pl.ds(start, 8, stride=pitch), :] = value[:8, :]
        for z in range(8, planes):
            rim32[z * pitch + start : z * pitch + start + 1, :] = value[z : z + 1, :]
    for z in range(0, planes, 2):
        pair = [rim32[(z + i) * pitch : (z + i + 1) * pitch, :].astype(BF16) for i in range(2)]
        moved = matmul(taps[...], jnp.concatenate(pair, axis=1)).astype(BF16)
        for i in range(2):
            rim[z + i] = pair[i]
            for bc in range(9):
                cells[z + i, :, bc * channels : (bc + 1) * channels] = moved[
                    bc * own : (bc + 1) * own, i * channels : (i + 1) * channels
                ]
    weights = [w_conv[9 * a : 9 * (a + 1)].reshape(9 * channels, channels) for a in range(3)]
    window = cells[: size_z + 1].reshape((size_z + 1) * own, 9 * channels)
    both = matmul(window, jnp.concatenate(weights[:2], axis=1))
    window = cells[2:].reshape(size_z * own, 9 * channels)
    pre = both[:-own, :channels] + both[own:, channels:] + matmul(window, weights[2])
    sig = jax.nn.sigmoid(pre)
    slope[...] = (sig * (1.0 + pre * (1.0 - sig))).reshape(size_z, own, channels)
    hidden[...] = (pre * sig).astype(BF16).reshape(size_z, own, channels)
    parts = []
    for s in range(8):
        a, bc = s // 4, s % 4
        parts.append(
            jnp.concatenate(
                [hidden[2 * kz + a, bc * quarter : (bc + 1) * quarter, :] for kz in range(size_z // 2)], axis=0
            )
        )
    coarse = matmul(jnp.concatenate(parts, axis=1), w_down[...].reshape(8 * channels, w_down.shape[2]))
    coarse = coarse.astype(BF16)
    wide = coarse.shape[1]
    for send, back in zip(sends, backs):
        send[:, :wide] = coarse
        send[:, wide:] = back[...]


def rim_transpose_kernel(count_p, rim, taps_t, turned):
    planes, rows, channels = rim.shape
    share = channels // count_p
    for pair in range(planes // 2):
        sides = [rim[2 * pair + i].astype(F32).T for i in range(2)]
        moved = matmul(jnp.concatenate(sides, axis=1).astype(BF16), taps_t[...]).astype(BF16)
        for bc in range(9):
            for p in range(count_p):
                start = (bc * count_p // 2 + p // 2) * share
                turned[p % 2, start : start + share, pair * rows : (pair + 1) * rows] = moved[
                    p * share : (p + 1) * share, bc * rows : (bc + 1) * rows
                ]


def column_kernel(count_z, *refs):
    parts, picks, (column, back, x_send, send_a, send_b, corner_b) = refs[:count_z], refs[count_z], refs[count_z + 1 :]
    own_cells = parts[0].shape[0]
    wide = column.shape[1]
    pz = lax.axis_index("gz")
    for i, part in enumerate(parts):
        rows = pl.ds(pl.multiple_of((pz ^ (-i % count_z)) * own_cells, own_cells), own_cells)
        column[rows, :] = part[:, :wide]
        back[rows, :] = part[:, wide:]
    rims = matmul(picks[lax.axis_index("gx")], column[...]).astype(BF16)
    cuts, start = [], 0
    for size in (x_send.shape[0], *[send_a.shape[0]] * 2, *[corner_b.shape[0]] * 2):
        cuts.append(rims[start : start + size, :])
        start += size
    x_send[...] = cuts[0]
    send_b[...], send_a[...] = line_sides("gy", cuts[2], cuts[1])
    corner_b[...], _ = line_sides("gy", cuts[4], cuts[3])


def bottle_kernel(quarter, column, back, x_rim, relayed, shift, w_bottle, *refs):
    count = len(refs) // 2 - 1
    slices, bottle, sends, (corners, window) = refs[:count], refs[count], refs[count + 1 : -2], refs[-2:]
    cells, wide = column.shape
    outs = w_bottle.shape[2]
    side = x_rim.shape[0]
    depth = cells // quarter
    span = 4 * quarter
    picks = shift[lax.axis_index("gx")]
    window[:quarter, :] = jnp.zeros((quarter, 9 * wide), BF16)
    window[(depth + 1) * quarter :, :] = jnp.zeros((quarter, 9 * wide), BF16)
    edge = side // (depth // 4)
    y_low, y_high, xy_low, xy_high = y_rims(relayed, depth)
    y_low, y_high = y_low.astype(BF16), y_high.astype(BF16)
    for g in range(depth // 4):
        corners[g, :4, :] = xy_low[4 * g : 4 * g + 4, :]
        corners[g, 4:8, :] = xy_high[4 * g : 4 * g + 4, :]
        corners[g, 8:, :] = jnp.zeros((8, wide), F32)
        faces = [block[g * edge : (g + 1) * edge, :] for block in (x_rim, y_low, y_high)]
        rows = [column[g * span : (g + 1) * span, :], *faces, corners[g].astype(BF16)]
        moved = matmul(picks, jnp.concatenate(rows, axis=0)).astype(BF16)
        for bc in range(9):
            window[quarter + g * span : quarter + (g + 1) * span, bc * wide : (bc + 1) * wide] = moved[
                bc * span : (bc + 1) * span, :
            ]
    spread_out = None
    for bc in range(9):
        weight = jnp.concatenate([w_bottle[9 * a + bc] for a in range(3)], axis=1)
        term = matmul(window[:, bc * wide : (bc + 1) * wide], weight)
        spread_out = term if spread_out is None else spread_out + term
    pre = spread_out[:cells, :outs]
    for a in range(1, 3):
        pre = pre + spread_out[a * quarter : a * quarter + cells, a * outs : (a + 1) * outs]
    sig = jax.nn.sigmoid(pre)
    bottle[...] = (pre * sig).astype(BF16)
    slope = sig * (1.0 + pre * (1.0 - sig))
    value = (back[...].astype(F32) * slope).astype(BF16)
    for send, block in zip(sends, slices):
        send[:cells, :] = value
        send[cells:, :] = block[...]


def slices_kernel(count_y, quarter, column, *refs):
    sends, slices = refs[:-1], refs[-1]
    cells, wide = column.shape
    span = 4 * quarter
    half = 2 * quarter
    lane = lax.broadcasted_iota(jnp.int32, (half, 128), 1)
    for pair in range(wide // 128):
        for g in range(cells // span):
            top = column[g * span : g * span + half, pair * 128 : (pair + 1) * 128].astype(F32)
            end = column[g * span + half : (g + 1) * span, pair * 128 : (pair + 1) * 128].astype(F32)
            rows = slice(g * half, (g + 1) * half)
            slices[2 * pair, rows, :] = jnp.where(lane < 64, top, pltpu.roll(end, 64, 1)).astype(BF16)
            slices[2 * pair + 1, rows, :] = jnp.where(lane < 64, pltpu.roll(top, 64, 1), end).astype(BF16)
    p = plane_index(count_y)
    lines = slices.shape[1]
    for i, send in enumerate(sends):
        send[:lines, :] = slices[p ^ (2 * i)]
        send[lines:, :] = slices[p ^ (2 * i + 1)]


def coarse_grad_kernel(count_y, count_z, quarter, *refs):
    grads, (bottle, shift, w_bottle) = refs[: -count_z - 6], refs[-count_z - 6 : -count_z - 3]
    sends, (window, gathered, blocks) = refs[-count_z - 3 : -3], refs[-3:]
    count_p = len(grads)
    cells, outs = bottle.shape
    rows = count_p * quarter
    depth = cells // quarter
    own_cells = cells // count_z
    inputs = w_bottle.shape[1]
    p = plane_index(count_y)
    for i, part in enumerate(grads):
        gathered[p ^ (-i % count_p)] = part[:cells, :]
    mine = pl.multiple_of(p * quarter, quarter)
    picks = jnp.concatenate([shift[pl.ds((8 - bc) * rows + mine, quarter), :] for bc in range(9)], axis=0)
    window[:quarter, :] = jnp.zeros((quarter, 9 * outs), BF16)
    window[(depth + 1) * quarter :, :] = jnp.zeros((quarter, 9 * outs), BF16)
    for z in range(depth):
        plane = jnp.concatenate([gathered[q, z * quarter : (z + 1) * quarter, :] for q in range(count_p)], axis=0)
        moved = matmul(picks, plane).astype(BF16)
        for bc in range(9):
            window[(z + 1) * quarter : (z + 2) * quarter, bc * outs : (bc + 1) * outs] = moved[
                bc * quarter : (bc + 1) * quarter, :
            ]
    total = None
    for a in range(3):
        weight = jnp.concatenate([w_bottle[9 * a + bc] for bc in range(9)], axis=1)
        term = matmul_nt(window[(2 - a) * quarter : (2 - a + depth) * quarter, :], weight)
        total = term if total is None else total + term
    total = total.astype(BF16)
    for q in range(count_z):
        blocks[q, :, :inputs] = total[q * own_cells : (q + 1) * own_cells, :]
        blocks[q, :, inputs:] = bottle[q * own_cells : (q + 1) * own_cells, :]
    hand_out(blocks, sends, lax.axis_index("gz"))


def wide_kernel(count_y, quarter, *refs):
    parts, (wide, grads) = refs[:-2], refs[-2:]
    count_p, cells, outs = grads.shape
    rows = count_p * quarter
    depth = cells // quarter
    take_in([part.at[:cells, :] for part in parts], grads, plane_index(count_y))
    planes = [
        jnp.concatenate([grads[q, z * quarter : (z + 1) * quarter, :] for q in range(count_p)], axis=0)
        for z in range(depth)
    ]
    zeros = jnp.zeros((rows, outs), BF16)
    for j in range(depth // 2):
        for slot in range(5):
            z = j // 2 * 4 + j % 2 + slot - 1
            wide[j * rows : (j + 1) * rows, slot * outs : (slot + 1) * outs] = planes[z] if 0 <= z < depth else zeros


def coarse_transpose_kernel(count_y, shift, *refs):
    parts, (turned, slices) = refs[:-2], refs[-2:]
    count_p, lines, _ = slices.shape
    rows = shift.shape[1]
    quarter = rows // count_p
    p = plane_index(count_y)
    for d, part in enumerate(parts):
        start = (2 + d % 2) * lines
        slices[p ^ d] = part[start : start + lines, :]
    for j in range(lines // quarter):
        plane = jnp.concatenate([slices[q, j * quarter : (j + 1) * quarter, :] for q in range(count_p)], axis=0)
        plane = plane.astype(F32).T.astype(BF16)
        for bc in range(9):
            turned[bc * 128 : (bc + 1) * 128, j * rows : (j + 1) * rows] = matmul(
                plane, shift[(8 - bc) * rows : (9 - bc) * rows, :]
            ).astype(BF16)


def grad_bottle_kernel(turned, wide, out):
    _, channels, outs = out.shape
    full = matmul(turned[...], wide[...])
    for bc in range(9):
        top = full[bc * 128 : bc * 128 + channels, :]
        end = full[bc * 128 + channels : (bc + 1) * 128, :]
        for a in range(3):
            out[9 * a + bc] = top[:, (2 - a) * outs : (3 - a) * outs] + end[:, (4 - a) * outs : (5 - a) * outs]


def half_grad(turned, shifted, parity, chip, out, blocks):
    chips, rows, channels = blocks.shape
    group = rows // 27
    full = matmul(turned[parity], shifted[...])
    for bc in range(9):
        for a in range(3):
            t = 9 * a + bc
            for q in range(chips):
                start = (bc * chips + q) * group
                blocks[q, t * group : (t + 1) * group, :] = full[
                    start : start + group, a * channels : (a + 1) * channels
                ].astype(BF16)
    for i in range(chips):
        out[i] = blocks[chip ^ i]


def hidden_grad_kernel(count_y, count_z, *refs):
    parts, (slope, ordered, w_down, turned) = refs[:count_z], refs[count_z : count_z + 4]
    shifted, bottle, give, bottles, blocks = refs[count_z + 4 :]
    size_z, own, channels = ordered.shape
    quarter = own // 4
    inputs = w_down.shape[2]
    pz = lax.axis_index("gz")
    grad = total_of([part.at[:, :inputs] for part in parts]).astype(BF16)
    for i, part in enumerate(parts):
        bottles[pz ^ (-i % count_z)] = part[:, inputs:]
    bottle[...] = jnp.concatenate([bottles[q] for q in range(count_z)], axis=1)
    shifted[...] = jnp.zeros_like(shifted)
    for s in range(8):
        a, bc = s // 4, s % 4
        spread_grad = matmul_nt(grad, w_down[s])
        for kz in range(size_z // 2):
            z = 2 * kz + a
            part = slice(bc * quarter, (bc + 1) * quarter)
            line = slice(kz * quarter, (kz + 1) * quarter)
            value = ((spread_grad[line, :] + ordered[z, part, :].astype(F32)) * slope[z, part, :]).astype(BF16)
            for t in range(3):
                start = (z + t) * own + bc * quarter
                shifted[start : start + quarter, t * channels : (t + 1) * channels] = value
    p = plane_index(count_y)
    half_grad(turned, shifted, 1 - p % 2, p // 2, give, blocks)


def keep_kernel(count_y, shifted, turned, keep, blocks):
    p = plane_index(count_y)
    half_grad(turned, shifted, p % 2, p // 2, keep, blocks)


def output_kernel(bottle, hidden, w_up, order_t, output, rows_out):
    size_z, own, channels = hidden.shape
    quarter = own // 4
    for s in range(8):
        a, bc = s // 4, s % 4
        lifted = matmul(bottle[...], w_up[s])
        for kz in range(size_z // 2):
            z = 2 * kz + a
            part = slice(bc * quarter, (bc + 1) * quarter)
            line = slice(kz * quarter, (kz + 1) * quarter)
            rows_out[z, part, :] = (lifted[line, :] + hidden[z, part, :].astype(F32)).astype(BF16)
    for z in range(size_z):
        plane = matmul(order_t[...], rows_out[z])
        output[z] = plane.reshape(output.shape[1:]).astype(BF16)


def pair_sum_kernel(keep, got, *sends):
    for i, send in enumerate(sends):
        send[...] = (keep[i].astype(F32) + got[i].astype(F32)).astype(BF16)


def sum_kernel(*refs):
    out = refs[-1]
    out[...] = total_of(refs[:-1]).reshape(out.shape).astype(out.dtype)


def shape_of(shape, dtype=BF16):
    return jax.ShapeDtypeStruct(shape, dtype)


def gathered_body(counts, volume, cotangent, w_conv, w_down, w_bottle, w_up):
    count_x, count_y, count_z = counts
    count_p = count_x * count_y
    size_z, size_x, size_y, channels = volume.shape
    wide = w_down.shape[2]
    group = w_bottle.shape[2]
    half_x, half_y = size_x // 2, size_y // 2
    own = size_x * size_y
    quarter = half_x * half_y
    own_cells = size_z // 2 * quarter
    cells = count_z * own_cells
    depth = count_z * size_z // 2
    rows = count_p * quarter
    planes = size_z + 2
    share_c = channels // count_p
    share_w = wide // count_p
    plane_axes = ("gx", "gy")

    order, taps = fine_maps(size_x, size_y)
    pair_taps = np.zeros((2, 2 * own, 9, 2, own), np.float32)
    for i in range(2):
        pair_taps[i, :, :, i, :] = taps.transpose(2, 0, 1)
    shift = coarse_maps(count_x, count_y, half_x, half_y)
    order_m = jnp.asarray(order, BF16)
    order_t = jnp.asarray(order.T, BF16)
    taps_m = jnp.asarray(taps.reshape(9 * own, 2 * own), BF16)
    taps_t = jnp.asarray(pair_taps.reshape(4 * own, 18 * own), BF16)
    shift_m = jnp.asarray(shift.reshape(9 * rows, rows), BF16)

    send_maps, rim_maps = column_maps(half_x, half_y, depth)
    send_m = jnp.asarray(send_maps, BF16)
    rim_m = jnp.asarray(rim_maps.reshape(count_x, 36 * quarter, 8 * quarter), BF16)

    w_conv_t = jnp.transpose(w_conv, (1, 0, 2))
    w_bottle_t = jnp.transpose(w_bottle, (1, 0, 2))
    send_a, send_b = local_call(ends_kernel, "ends", [shape_of((size_x, size_y, channels))] * 2)(volume)
    z_pairs = line_pairs(count_z)
    z_b = lax.ppermute(send_b, "gz", z_pairs[1])
    z_a = lax.ppermute(send_a, "gz", z_pairs[0])
    *backs, ordered = local_call(
        lambda *refs: back_kernel(count_z, *refs),
        "back",
        [shape_of((own_cells, group))] * count_z + [shape_of((size_z, own, channels))],
        [pltpu.VMEM((count_z, own_cells, group), BF16)],
    )(cotangent, w_up, order_m)
    sends = local_call(
        faces_kernel,
        "faces",
        [shape_of((16 * size_y, channels))] + [shape_of((planes * size_x, channels))] * 2 + [shape_of((16, channels))],
        [pltpu.VMEM((16 * own, channels), F32)],
    )(volume, z_a, z_b)
    x_send, send_a, send_b, corner_b = sends
    x_rim, across, corner = swap_rims(x_send, send_b, corner_b, counts)
    relayed = relay_rims(x_rim, across, corner, send_a, counts)
    hidden, slope, rim, *sends = local_call(
        lambda *refs: hidden_kernel(count_z, *refs),
        "hidden",
        [
            shape_of((size_z, own, channels)),
            shape_of((size_z, own, channels), F32),
            shape_of((planes, 2 * own, channels)),
        ]
        + [shape_of((own_cells, wide + group))] * count_z,
        [
            pltpu.VMEM((planes * 2 * own, channels), F32),
            pltpu.VMEM((planes, own, 9 * channels), BF16),
        ],
        flops=2_000_000_000,
    )(volume, z_a, z_b, x_rim, relayed, taps_m, w_conv_t, w_down, *backs)
    parts = trade(sends, "gz", count_z)
    column, back, *sends = local_call(
        lambda *refs: column_kernel(count_z, *refs),
        "column",
        [shape_of((cells, wide)), shape_of((cells, group)), shape_of((depth * half_y, wide))]
        + [shape_of((depth * half_x, wide))] * 2
        + [shape_of((depth, wide))],
    )(parts[0], *parts[:0:-1], send_m)
    x_send, send_a, send_b, corner_b = sends
    x_rim, across, corner = swap_rims(x_send, send_b, corner_b, counts)
    relayed = relay_rims(x_rim, across, corner, send_a, counts)
    slices = local_call(
        lambda *refs: slices_kernel(count_y, quarter, *refs),
        "slices",
        [shape_of((cells, 128))] * (count_p // 2),
        [pltpu.VMEM((count_p, cells // 2, 128), BF16)],
    )(column)
    column, *slices = lax.optimization_barrier((column, *slices))
    bottle, *sends = local_call(
        lambda *refs: bottle_kernel(quarter, *refs),
        "bottle",
        [shape_of((cells, group))] + [shape_of((2 * cells, group))] * (count_p // 2),
        [
            pltpu.VMEM((depth // 4, 16, wide), F32),
            pltpu.VMEM(((depth + 2) * quarter, 9 * wide), BF16),
        ],
        flops=2_000_000_000,
    )(column, back, x_rim, relayed, rim_m, w_bottle_t, *slices)
    grads = [None] * count_p
    grads[0] = sends[0]
    for d in (6, 4, 2):
        grads[d] = swap(sends[d // 2], plane_axes, count_p, d)
    for d in (0, 2, 4, 6):
        grads[d + 1] = swap(grads[d], plane_axes, count_p, 1)
    sends = local_call(
        lambda *refs: coarse_grad_kernel(count_y, count_z, quarter, *refs),
        "coarse_grad",
        [shape_of((own_cells, wide + group))] * count_z,
        [
            pltpu.VMEM(((depth + 2) * quarter, 9 * group), BF16),
            pltpu.VMEM((count_p, cells, group), BF16),
            pltpu.VMEM((count_z, own_cells, wide + group), BF16),
        ],
    )(grads[0], *grads[:0:-1], bottle, shift_m, w_bottle_t)
    parts = trade(sends, "gz", count_z)
    rim, late, _ = lax.optimization_barrier((rim, grads[0], sends[1]))
    turned = local_call(
        lambda *refs: rim_transpose_kernel(count_p, *refs),
        "rim_transpose",
        shape_of((2, 9 * channels // 2, planes * own)),
    )(rim, taps_t)
    coarse_turned = local_call(
        lambda *refs: coarse_transpose_kernel(count_y, *refs),
        "coarse_transpose",
        shape_of((18 * share_w, depth // 2 * rows)),
        [pltpu.VMEM((count_p, cells // 2, 128), BF16)],
    )(shift_m, late, *grads[1:])
    turned, coarse_turned = lax.optimization_barrier((turned, coarse_turned))
    shifted, bottle, give = local_call(
        lambda *refs: hidden_grad_kernel(count_y, count_z, *refs),
        "hidden_grad",
        [
            shape_of((planes * own, 3 * channels)),
            shape_of((own_cells, wide)),
            shape_of((count_p // 2, 27 * share_c, channels)),
        ],
        [
            pltpu.VMEM((count_z, own_cells, group), BF16),
            pltpu.VMEM((count_p // 2, 27 * share_c, channels), BF16),
        ],
    )(parts[0], *parts[:0:-1], slope, ordered, w_down, turned)
    got = swap(give, plane_axes, count_p, 1)
    keep = local_call(
        lambda *refs: keep_kernel(count_y, *refs),
        "keep",
        shape_of((count_p // 2, 27 * share_c, channels)),
        [pltpu.VMEM((count_p // 2, 27 * share_c, channels), BF16)],
    )(shifted, turned)
    output = local_call(
        output_kernel,
        "output",
        shape_of(volume.shape),
        [pltpu.VMEM((size_z, own, channels), BF16)],
    )(bottle, hidden, w_up, order_t)
    sends = local_call(
        pair_sum_kernel,
        "pair_sum",
        [shape_of((27 * share_c, channels))] * (count_p // 2),
    )(keep, got)
    parts = [sends[0]] + [swap(sends[d // 2], plane_axes, count_p, d) for d in (6, 4, 2)]
    part = local_call(sum_kernel, "plane_sum", shape_of((27 * share_c, channels)))(*parts)
    part, output = lax.optimization_barrier((part, output))
    got = swap(part, "gz", count_z, 1)
    wide_grads = local_call(
        lambda *refs: wide_kernel(count_y, quarter, *refs),
        "wide",
        shape_of((depth // 2 * rows, 5 * group)),
        [pltpu.VMEM((count_p, cells, group), BF16)],
    )(*grads)
    got, wide_grads = lax.optimization_barrier((got, wide_grads))
    part = local_call(sum_kernel, "depth_sum", shape_of((27 * share_c, channels)))(part, got)
    got = swap(part, "gz", count_z, 2)
    grad_bottle = local_call(
        grad_bottle_kernel,
        "grad_bottle",
        shape_of((27, share_w, group), F32),
        flops=4_000_000_000,
    )(coarse_turned, wide_grads)
    grad_conv = local_call(
        sum_kernel,
        "grad_conv",
        shape_of((27, share_c, channels), F32),
    )(part, got)
    return (output, jnp.transpose(grad_conv, (1, 0, 2)), jnp.transpose(grad_bottle, (1, 0, 2)))


def with_halo(cells, sides, width):
    for axis, dim in sides:
        count = lax.axis_size(axis)
        ends = count - 1
        head = lax.slice_in_dim(cells, 0, width, axis=dim)
        tail = lax.slice_in_dim(cells, cells.shape[dim] - width, cells.shape[dim], axis=dim)
        cells = jnp.concatenate(
            [
                lax.ppermute(tail, axis, [(i, (i + 1) % count) for i in range(ends)]),
                cells,
                lax.ppermute(head, axis, [((i + 1) % count, i) for i in range(ends)]),
            ],
            axis=dim,
        )
    return cells


def silu_slope(values):
    sig = jax.nn.sigmoid(values)
    return sig * (1.0 + values * (1.0 - sig))


def conv_forward(padded, weight, extent):
    size_z, size_x, size_y = extent
    count_cells = size_z * size_x * size_y
    summed = jnp.zeros((count_cells, weight.shape[2]), jnp.float32)
    for tap_index in range(27):
        shift_z, shift_x, shift_y = (tap_index // 9, tap_index // 3 % 3, tap_index % 3)
        window = padded[
            shift_z : shift_z + size_z, shift_x : shift_x + size_x, shift_y : shift_y + size_y, :
        ]
        window = window.reshape(count_cells, padded.shape[3])
        summed = summed + jnp.dot(
            window, weight[:, tap_index, :], preferred_element_type=jnp.float32
        )
    return summed.reshape(size_z, size_x, size_y, weight.shape[2])


def conv_weight_grad(padded, gradient, extent):
    size_z, size_x, size_y = extent
    count_cells = size_z * size_x * size_y
    flat_gradient = gradient.reshape(count_cells, gradient.shape[3])
    pieces = []
    for tap_index in range(27):
        shift_z, shift_x, shift_y = (tap_index // 9, tap_index // 3 % 3, tap_index % 3)
        window = padded[
            shift_z : shift_z + size_z, shift_x : shift_x + size_x, shift_y : shift_y + size_y, :
        ]
        window = window.reshape(count_cells, padded.shape[3])
        pieces.append(
            lax.dot_general(
                window, flat_gradient, (((0,), (0,)), ((), ())), preferred_element_type=jnp.float32
            )
        )
    return jnp.stack(pieces, axis=1)


def conv_input_grad(padded, weight, extent):
    size_z, size_x, size_y = extent
    count_cells = size_z * size_x * size_y
    summed = jnp.zeros((count_cells, weight.shape[0]), jnp.float32)
    for tap_index in range(27):
        shift_z, shift_x, shift_y = (2 - tap_index // 9, 2 - tap_index // 3 % 3, 2 - tap_index % 3)
        window = padded[
            shift_z : shift_z + size_z, shift_x : shift_x + size_x, shift_y : shift_y + size_y, :
        ]
        window = window.reshape(count_cells, padded.shape[3])
        summed = summed + lax.dot_general(
            window,
            weight[:, tap_index, :],
            (((1,), (1,)), ((), ())),
            preferred_element_type=jnp.float32,
        )
    return summed.reshape(size_z, size_x, size_y, weight.shape[0])


def pool_features(fine, kernel):
    size_z, size_x, size_y, channels = fine.shape
    blocks = fine.reshape(size_z // 2, 2, size_x // 2, 2, size_y // 2, 2, channels)
    kernel_cube = kernel.reshape(2, 2, 2, kernel.shape[1], kernel.shape[2])
    return jnp.einsum(
        "zaxbycf,abcfg->zxyg", blocks, kernel_cube, preferred_element_type=jnp.float32
    )


def pool_adjoint(coarse_in, kernel):
    size_z, size_x, size_y, wide_channels = coarse_in.shape
    kernel_cube = kernel.reshape(2, 2, 2, kernel.shape[1], kernel.shape[2])
    result = jnp.einsum(
        "zxyg,abcfg->zaxbycf", coarse_in, kernel_cube, preferred_element_type=jnp.float32
    )
    return result.reshape(2 * size_z, 2 * size_x, 2 * size_y, kernel.shape[1])


def lift_features(coarse_in, kernel):
    size_z, size_x, size_y, wide_channels = coarse_in.shape
    kernel_cube = kernel.reshape(2, 2, 2, kernel.shape[1], kernel.shape[2])
    result = jnp.einsum(
        "zxyg,abcgf->zaxbycf", coarse_in, kernel_cube, preferred_element_type=jnp.float32
    )
    return result.reshape(2 * size_z, 2 * size_x, 2 * size_y, kernel.shape[2])


def lift_adjoint(fine, kernel):
    size_z, size_x, size_y, channels = fine.shape
    blocks = fine.reshape(size_z // 2, 2, size_x // 2, 2, size_y // 2, 2, channels)
    kernel_cube = kernel.reshape(2, 2, 2, kernel.shape[1], kernel.shape[2])
    return jnp.einsum(
        "zaxbycf,abcgf->zxyg", blocks, kernel_cube, preferred_element_type=jnp.float32
    )


def column_body(volume, cotangent, w_conv, w_down, w_bottle, w_up):
    size_z, size_x, size_y, channels = volume.shape
    group_channels = w_bottle.shape[2]
    half_x = size_x // 2
    half_y = size_y // 2
    padded = with_halo(volume, (("gx", 1), ("gy", 2), ("gz", 0)), 1)
    pre_hidden = conv_forward(padded, w_conv, (size_z, size_x, size_y))
    hidden = jax.nn.silu(pre_hidden).astype(jnp.bfloat16)
    hidden_slope = silu_slope(pre_hidden)
    coarse = pool_features(hidden, w_down).astype(jnp.bfloat16)
    stacked = lax.all_gather(coarse, "gz", axis=0, tiled=True)
    rimmed = with_halo(stacked, (("gx", 1), ("gy", 2)), 1)
    column_z = rimmed.shape[0]
    coarse_pad = jnp.pad(rimmed, ((1, 1), (0, 0), (0, 0), (0, 0)))
    pre_bottle = conv_forward(coarse_pad, w_bottle, (column_z, half_x, half_y))
    bottle = jax.nn.silu(pre_bottle).astype(jnp.bfloat16)
    bottle_slope = silu_slope(pre_bottle)
    own_start = lax.axis_index("gz") * group_channels
    own_up = lax.dynamic_slice_in_dim(w_up, own_start, group_channels, 1)
    lifted = lax.psum_scatter(
        lift_features(bottle, own_up).astype(jnp.bfloat16), "gz", scatter_dimension=0, tiled=True
    ).astype(jnp.float32)
    output = (lifted + hidden.astype(jnp.float32)).astype(jnp.bfloat16)
    back_bottle = lift_adjoint(cotangent, w_up).astype(jnp.bfloat16)
    split_grad = lax.all_to_all(back_bottle, "gz", split_axis=3, concat_axis=0, tiled=True)
    bottle_grad = (split_grad.astype(jnp.float32) * bottle_slope).astype(jnp.bfloat16)
    grad_bottle = lax.psum_scatter(
        conv_weight_grad(coarse_pad, bottle_grad, (column_z, half_x, half_y)),
        ("gx", "gy"),
        scatter_dimension=0,
        tiled=True,
    )
    grad_rimmed = with_halo(bottle_grad, (("gx", 1), ("gy", 2)), 1)
    grad_pad = jnp.pad(grad_rimmed, ((1, 1), (0, 0), (0, 0), (0, 0)))
    coarse_grad = lax.psum_scatter(
        conv_input_grad(
            grad_pad, w_bottle, (lax.axis_size("gz") * (size_z // 2), half_x, half_y)
        ).astype(jnp.bfloat16),
        "gz",
        scatter_dimension=0,
        tiled=True,
    )
    hidden_grad = (
        (pool_adjoint(coarse_grad, w_down) + cotangent.astype(jnp.float32)) * hidden_slope
    ).astype(jnp.bfloat16)
    full_term = conv_weight_grad(padded, hidden_grad, (size_z, size_x, size_y))
    depth_summed = lax.psum(full_term.astype(jnp.bfloat16), "gz").astype(jnp.float32)
    grad_conv = lax.psum_scatter(depth_summed, ("gx", "gy"), scatter_dimension=0, tiled=True)
    return (output, grad_conv, grad_bottle)


def fits_one_plane(counts, brick, wide):
    count_p = counts[0] * counts[1]
    size_z, size_x, size_y, channels = brick
    return (
        counts == (2, 4, 4)
        and count_p * (size_x // 2) * (size_y // 2) == 128
        and wide // count_p == 64
        and (size_z, size_x, size_y, channels) == (8, 8, 8, 128)
    )


def solution(mesh):
    in_specs = (
        P("gz", "gx", "gy", None),
        P("gz", "gx", "gy", None),
        P(),
        P(),
        P(None, None, "gz"),
        P(),
    )
    out_specs = (
        P("gz", "gx", "gy", None),
        P(("gx", "gy"), None, None),
        P(("gx", "gy"), None, "gz"),
    )
    counts = (mesh.shape["gx"], mesh.shape["gy"], mesh.shape["gz"])

    def body(volume, cotangent, w_conv, w_down, w_bottle, w_up):
        if fits_one_plane(counts, volume.shape, w_down.shape[2]):
            return gathered_body(counts, volume, cotangent, w_conv, w_down, w_bottle, w_up)
        return column_body(volume, cotangent, w_conv, w_down, w_bottle, w_up)

    return jax.shard_map(body, mesh=mesh, in_specs=in_specs, out_specs=out_specs, check_vma=False)
```

```python
import numpy as np
import jax
import jax.numpy as jnp
from jax import lax
from jax.experimental import pallas as pl
from jax.experimental.pallas import tpu as pltpu
from jax.sharding import PartitionSpec as P

BF16 = jnp.bfloat16
F32 = jnp.float32
VMEM_LIMIT = 24 * 1024 * 1024


def local_call(kernel, name, out_shapes, scratch=(), flops=300_000_000):
    whole = pl.BlockSpec(memory_space=pltpu.VMEM)

    def call(*operands):
        return pl.pallas_call(
            kernel,
            name=name,
            out_shape=out_shapes,
            in_specs=[whole] * len(operands),
            out_specs=jax.tree.map(lambda _: whole, out_shapes),
            scratch_shapes=list(scratch),
            compiler_params=pltpu.CompilerParams(vmem_limit_bytes=VMEM_LIMIT),
            cost_estimate=pl.CostEstimate(flops=flops, bytes_accessed=flops // 1000, transcendentals=0),
        )(*operands)

    return call


def matmul(left, right):
    return jnp.dot(left, right, preferred_element_type=F32)


def matmul_nt(left, right):
    return lax.dot_general(left, right, (((1,), (1,)), ((), ())), preferred_element_type=F32)


def sub_order(size_x, size_y):
    half_x, half_y = size_x // 2, size_y // 2
    return {
        (2 * kx + b, 2 * ky + c): ((2 * b + c) * half_x + kx) * half_y + ky
        for b in range(2)
        for c in range(2)
        for kx in range(half_x)
        for ky in range(half_y)
    }


def fine_maps(size_x, size_y):
    own = size_x * size_y
    rows = sub_order(size_x, size_y)
    order = np.zeros((own, own), np.float32)
    taps = np.zeros((9, own, 2 * own), np.float32)
    for (x, y), row in rows.items():
        order[row, x * size_y + y] = 1
        for b in range(3):
            for c in range(3):
                sx, sy = x + b - 1, y + c - 1
                if sx < 0:
                    part = 0 if 0 <= sy < size_y else (4 if sy < 0 else 5)
                    source = own + 8 * part + sy % size_y
                elif sx >= size_x:
                    part = 1 if 0 <= sy < size_y else (6 if sy < 0 else 7)
                    source = own + 8 * part + sy % size_y
                elif sy < 0:
                    source = own + 16 + sx
                elif sy >= size_y:
                    source = own + 24 + sx
                else:
                    source = sx * size_y + sy
                taps[3 * b + c, row, source] = 1
    return order, taps


def coarse_maps(count_x, count_y, half_x, half_y):
    wide_x, wide_y = count_x * half_x, count_y * half_y

    def row_of(x, y):
        brick = (x // half_x) * count_y + y // half_y
        return (brick * half_x + x % half_x) * half_y + y % half_y

    shift = np.zeros((9, wide_x * wide_y, wide_x * wide_y), np.float32)
    for x in range(wide_x):
        for y in range(wide_y):
            for b in range(3):
                for c in range(3):
                    sx, sy = x + b - 1, y + c - 1
                    if 0 <= sx < wide_x and 0 <= sy < wide_y:
                        shift[3 * b + c, row_of(x, y), row_of(sx, sy)] = 1
    return shift


def column_maps(half_x, half_y, depth):
    quarter = half_x * half_y
    rows = depth * quarter
    send = np.zeros((2, depth * (half_y + 2 * half_x + 2), rows), np.float32)
    rim = np.zeros((2, 9, 4, quarter, 8 * quarter), np.float32)
    for px in range(2):
        edge = 0 if px else half_x - 1
        for z in range(depth):
            base = z * quarter
            for ky in range(half_y):
                send[px, z * half_y + ky, base + edge * half_y + ky] = 1
            for side, ky in enumerate((0, half_y - 1)):
                row = depth * (half_y + side * half_x) + z * half_x
                for kx in range(half_x):
                    send[px, row + kx, base + kx * half_y + ky] = 1
                send[px, depth * (half_y + 2 * half_x + side) + z, base + edge * half_y + ky] = 1
    for px in range(2):
        for b in range(3):
            for c in range(3):
                for kx in range(half_x):
                    for ky in range(half_y):
                        sx, sy = kx + b - 1, ky + c - 1
                        beyond = sx < 0 if px else sx >= half_x
                        if (sx < 0 or sx >= half_x) and not beyond:
                            continue
                        for z in range(4):
                            if beyond and 0 <= sy < half_y:
                                source = 4 * quarter + z * half_y + sy
                            elif beyond:
                                source = 7 * quarter + 4 * (sy >= half_y) + z
                            elif sy < 0:
                                source = 5 * quarter + z * half_x + sx
                            elif sy >= half_y:
                                source = 6 * quarter + z * half_x + sx
                            else:
                                source = z * quarter + sx * half_y + sy
                            rim[px, 3 * b + c, z, kx * half_y + ky, source] = 1
    return send, rim


def swap(block, axes, count, distance):
    return lax.ppermute(block, axes, [(i, i ^ distance) for i in range(count)])


def trade(blocks, axes, count):
    got = {d: swap(blocks[d], axes, count, d) for d in reversed(range(1, count))}
    return [blocks[0]] + [got[d] for d in range(1, count)]


def line_pairs(length):
    first = [(i, i ^ 1) for i in range(length)]
    second = [(i, i + 1 if i % 2 else i - 1) for i in range(1, length - 1)]
    return first, second


def swap_rims(x_send, send_b, corner_b, counts):
    count_x, count_y, _ = counts
    axes, count = ("gx", "gy"), count_x * count_y
    corner = swap(corner_b, axes, count, count_y + 2)
    x_rim = swap(x_send, axes, count, count_y)
    across = swap(send_b, axes, count, 2)
    return x_rim, across, corner


def line_sides(axis, pair_a, pair_b):
    even = lax.axis_index(axis) % 2 == 0
    return jnp.where(even, pair_b, pair_a), jnp.where(even, pair_a, pair_b)


def relay_rims_kernel(corner, across, x_rim, send_a, send, side):
    face, lines = across.shape[0], corner.shape[0]
    pitch = x_rim.shape[0] // lines
    even = lax.axis_index("gy") % 2 == 0
    for part in range(0, x_rim.shape[1], 128):
        columns = slice(part, part + 128)
        side[...] = x_rim[:, columns].astype(F32)
        ends = [side[pl.ds(y, lines, stride=pitch), :] for y in (pitch - 1, 0)]
        send[face + lines : face + 2 * lines, columns] = jnp.where(even, ends[0], ends[1]).astype(BF16)
    send[face + 2 * lines :, :] = send_a[...]
    send[:face, :] = across[...]
    send[face : face + lines, :] = corner[...]


def pass_kernel(block, out):
    out[...] = block[...]


def relay_rims(x_rim, across, corner, send_a, counts):
    rows = 2 * (across.shape[0] + corner.shape[0])
    corner = local_call(pass_kernel, "corner", shape_of(corner.shape), flops=5_000_000_000)(corner)
    send = local_call(
        relay_rims_kernel,
        "relay_rims",
        shape_of((rows, across.shape[1])),
        [pltpu.VMEM((x_rim.shape[0], 128), F32)],
    )(corner, across, x_rim, send_a)
    return swap(send, ("gx", "gy"), counts[0] * counts[1], 1)


def y_rims(relayed, lines):
    py = lax.axis_index("gy")
    face = relayed.shape[0] // 2 - lines
    inner = (py > 0) & (py < lax.axis_size("gy") - 1)
    face_b = jnp.where(inner, relayed[:face, :].astype(F32), 0.0)
    corner_b = jnp.where(inner, relayed[face : face + lines, :].astype(F32), 0.0)
    corner_a = relayed[face + lines : face + 2 * lines, :].astype(F32)
    face_a = relayed[face + 2 * lines :, :].astype(F32)
    return *line_sides("gy", face_a, face_b), *line_sides("gy", corner_a, corner_b)


def plane_index(count_y):
    return lax.axis_index("gx") * count_y + lax.axis_index("gy")


def plane_rows(ref, z):
    _, size_x, size_y, channels = ref.shape
    return ref[z].astype(F32).reshape(size_x * size_y, channels)


def hand_out(blocks, outs, me):
    for d, out in enumerate(outs):
        out[...] = blocks[me ^ d]


def take_in(parts, blocks, me):
    for d, part in enumerate(parts):
        blocks[me ^ d] = part[...]


def total_of(parts):
    terms = [part[...].astype(F32) for part in parts]
    while len(terms) > 1:
        terms = [terms[i] + terms[i + 1] for i in range(0, len(terms), 2)]
    return terms[0]


def back_kernel(count_z, cotangent, w_up, order, *refs):
    sends, (ordered, blocks) = refs[:count_z], refs[count_z:]
    size_z, size_x, size_y, channels = cotangent.shape
    own = size_x * size_y
    quarter = own // 4
    for z in range(size_z):
        ordered[z] = matmul(order[...], plane_rows(cotangent, z).astype(BF16)).astype(BF16)
    back = None
    for s in range(8):
        a, bc = s // 4, s % 4
        cells = jnp.concatenate(
            [ordered[2 * kz + a, bc * quarter : (bc + 1) * quarter, :] for kz in range(size_z // 2)], axis=0
        )
        term = matmul_nt(cells, w_up[s])
        back = term if back is None else back + term
    back = back.astype(BF16)
    group = back.shape[1] // count_z
    for q in range(count_z):
        blocks[q] = back[:, q * group : (q + 1) * group]
    hand_out(blocks, sends, lax.axis_index("gz"))


def deepen(volume, z_a, z_b, deep, pitch):
    size_z, size_x, size_y, channels = volume.shape
    own = size_x * size_y
    below, above = line_sides("gz", z_a[...], z_b[...])
    deep[:own, :] = below.astype(F32).reshape(own, channels)
    for z in range(size_z):
        deep[(z + 1) * pitch : (z + 1) * pitch + own, :] = plane_rows(volume, z)
    deep[(size_z + 1) * pitch : (size_z + 1) * pitch + own, :] = above.astype(F32).reshape(own, channels)


def ends_kernel(volume, send_a, send_b):
    below, above = volume[0], volume[volume.shape[0] - 1]
    send_b[...], send_a[...] = line_sides("gz", above, below)


def faces_kernel(volume, z_a, z_b, x_send, send_a, send_b, corner_b, deep):
    size_z, size_x, size_y, channels = volume.shape
    own = size_x * size_y
    planes = x_send.shape[0] // size_y
    deepen(volume, z_a, z_b, deep, own)
    start = (size_z + 2) * own
    deep[start:, :] = jnp.zeros((deep.shape[0] - start, channels), F32)
    first = lax.axis_index("gx") == 0
    far = (size_x - 1) * size_y

    def x_face(start):
        return jnp.concatenate([deep[z * own + start : z * own + start + size_y, :] for z in range(planes)], axis=0)

    x_send[...] = jnp.where(first, x_face(far), x_face(0)).astype(BF16)
    faces, corners = [], []
    for y in (0, size_y - 1):
        faces.append(deep[pl.ds(y, send_a.shape[0], stride=size_y), :].astype(BF16))
        ends = [deep[pl.ds(start + y, planes, stride=own), :] for start in (far, 0)]
        corners.append(jnp.where(first, ends[0], ends[1]).astype(BF16))
    send_b[...], send_a[...] = line_sides("gy", faces[1], faces[0])
    corner_b[...], _ = line_sides("gy", corners[1], corners[0])


def hidden_kernel(count_z, volume, z_a, z_b, x_rim, relayed, taps, w_conv, w_down, *refs):
    backs, (hidden, slope, rim), sends, (rim32, cells) = (
        refs[:count_z],
        refs[count_z : count_z + 3],
        refs[count_z + 3 : -2],
        refs[-2:],
    )
    size_z, size_x, size_y, channels = volume.shape
    own = size_x * size_y
    quarter = own // 4
    planes = size_z + 2
    pitch = 2 * own
    first = lax.axis_index("gx") == 0
    deepen(volume, z_a, z_b, rim32, pitch)
    y_low, y_high, xy_low, xy_high = y_rims(relayed, x_rim.shape[0] // size_y)
    x_side = x_rim[...].astype(F32)
    x_low, x_high = jnp.where(first, 0.0, x_side), jnp.where(first, x_side, 0.0)
    faces = (x_low, x_high, y_low, y_high)
    for z in range(planes):
        for part, block in enumerate(faces):
            start = z * pitch + own + 8 * part
            rim32[start : start + 8, :] = block[8 * z : 8 * (z + 1), :]
        rim32[z * pitch + own + 32 : (z + 1) * pitch, :] = jnp.zeros((own - 32, channels), F32)
    corners = ((xy_low, 7, True), (xy_high, 0, True), (xy_low, 7, False), (xy_high, 0, False))
    for part, (block, row, low) in enumerate(corners):
        start = own + 32 + 8 * part + row
        value = jnp.where(first == low, 0.0, block)
        rim32[pl.ds(start, 8, stride=pitch), :] = value[:8, :]
        for z in range(8, planes):
            rim32[z * pitch + start : z * pitch + start + 1, :] = value[z : z + 1, :]
    for z in range(0, planes, 2):
        pair = [rim32[(z + i) * pitch : (z + i + 1) * pitch, :].astype(BF16) for i in range(2)]
        moved = matmul(taps[...], jnp.concatenate(pair, axis=1)).astype(BF16)
        for i in range(2):
            rim[z + i] = pair[i]
            for bc in range(9):
                cells[z + i, :, bc * channels : (bc + 1) * channels] = moved[
                    bc * own : (bc + 1) * own, i * channels : (i + 1) * channels
                ]
    weights = [w_conv[9 * a : 9 * (a + 1)].reshape(9 * channels, channels) for a in range(3)]
    window = cells[: size_z + 1].reshape((size_z + 1) * own, 9 * channels)
    both = matmul(window, jnp.concatenate(weights[:2], axis=1))
    window = cells[2:].reshape(size_z * own, 9 * channels)
    pre = both[:-own, :channels] + both[own:, channels:] + matmul(window, weights[2])
    sig = jax.nn.sigmoid(pre)
    slope[...] = (sig * (1.0 + pre * (1.0 - sig))).reshape(size_z, own, channels)
    hidden[...] = (pre * sig).astype(BF16).reshape(size_z, own, channels)
    parts = []
    for s in range(8):
        a, bc = s // 4, s % 4
        parts.append(
            jnp.concatenate(
                [hidden[2 * kz + a, bc * quarter : (bc + 1) * quarter, :] for kz in range(size_z // 2)], axis=0
            )
        )
    coarse = matmul(jnp.concatenate(parts, axis=1), w_down[...].reshape(8 * channels, w_down.shape[2]))
    coarse = coarse.astype(BF16)
    wide = coarse.shape[1]
    for send, back in zip(sends, backs):
        send[:, :wide] = coarse
        send[:, wide:] = back[...]


def rim_transpose_kernel(count_p, rim, taps_t, turned):
    planes, rows, channels = rim.shape
    share = channels // count_p
    for pair in range(planes // 2):
        sides = [rim[2 * pair + i].astype(F32).T for i in range(2)]
        moved = matmul(jnp.concatenate(sides, axis=1).astype(BF16), taps_t[...]).astype(BF16)
        for bc in range(9):
            for p in range(count_p):
                start = (bc * count_p // 2 + p // 2) * share
                turned[p % 2, start : start + share, pair * rows : (pair + 1) * rows] = moved[
                    p * share : (p + 1) * share, bc * rows : (bc + 1) * rows
                ]


def column_kernel(count_z, *refs):
    parts, picks, (column, back, x_send, send_a, send_b, corner_b) = refs[:count_z], refs[count_z], refs[count_z + 1 :]
    own_cells = parts[0].shape[0]
    wide = column.shape[1]
    pz = lax.axis_index("gz")
    for i, part in enumerate(parts):
        rows = pl.ds(pl.multiple_of((pz ^ (-i % count_z)) * own_cells, own_cells), own_cells)
        column[rows, :] = part[:, :wide]
        back[rows, :] = part[:, wide:]
    rims = matmul(picks[lax.axis_index("gx")], column[...]).astype(BF16)
    cuts, start = [], 0
    for size in (x_send.shape[0], *[send_a.shape[0]] * 2, *[corner_b.shape[0]] * 2):
        cuts.append(rims[start : start + size, :])
        start += size
    x_send[...] = cuts[0]
    send_b[...], send_a[...] = line_sides("gy", cuts[2], cuts[1])
    corner_b[...], _ = line_sides("gy", cuts[4], cuts[3])


def bottle_kernel(quarter, column, back, x_rim, relayed, shift, w_bottle, *refs):
    count = len(refs) // 2 - 1
    slices, bottle, sends, (corners, window) = refs[:count], refs[count], refs[count + 1 : -2], refs[-2:]
    cells, wide = column.shape
    outs = w_bottle.shape[2]
    side = x_rim.shape[0]
    depth = cells // quarter
    span = 4 * quarter
    picks = shift[lax.axis_index("gx")]
    window[:quarter, :] = jnp.zeros((quarter, 9 * wide), BF16)
    window[(depth + 1) * quarter :, :] = jnp.zeros((quarter, 9 * wide), BF16)
    edge = side // (depth // 4)
    y_low, y_high, xy_low, xy_high = y_rims(relayed, depth)
    y_low, y_high = y_low.astype(BF16), y_high.astype(BF16)
    for g in range(depth // 4):
        corners[g, :4, :] = xy_low[4 * g : 4 * g + 4, :]
        corners[g, 4:8, :] = xy_high[4 * g : 4 * g + 4, :]
        corners[g, 8:, :] = jnp.zeros((8, wide), F32)
        faces = [block[g * edge : (g + 1) * edge, :] for block in (x_rim, y_low, y_high)]
        rows = [column[g * span : (g + 1) * span, :], *faces, corners[g].astype(BF16)]
        moved = matmul(picks, jnp.concatenate(rows, axis=0)).astype(BF16)
        for bc in range(9):
            window[quarter + g * span : quarter + (g + 1) * span, bc * wide : (bc + 1) * wide] = moved[
                bc * span : (bc + 1) * span, :
            ]
    spread_out = None
    for bc in range(9):
        weight = jnp.concatenate([w_bottle[9 * a + bc] for a in range(3)], axis=1)
        term = matmul(window[:, bc * wide : (bc + 1) * wide], weight)
        spread_out = term if spread_out is None else spread_out + term
    pre = spread_out[:cells, :outs]
    for a in range(1, 3):
        pre = pre + spread_out[a * quarter : a * quarter + cells, a * outs : (a + 1) * outs]
    sig = jax.nn.sigmoid(pre)
    bottle[...] = (pre * sig).astype(BF16)
    slope = sig * (1.0 + pre * (1.0 - sig))
    value = (back[...].astype(F32) * slope).astype(BF16)
    for send, block in zip(sends, slices):
        send[:cells, :] = value
        send[cells:, :] = block[...]


def slices_kernel(count_y, quarter, column, *refs):
    sends, slices = refs[:-1], refs[-1]
    cells, wide = column.shape
    span = 4 * quarter
    half = 2 * quarter
    lane = lax.broadcasted_iota(jnp.int32, (half, 128), 1)
    for pair in range(wide // 128):
        for g in range(cells // span):
            top = column[g * span : g * span + half, pair * 128 : (pair + 1) * 128].astype(F32)
            end = column[g * span + half : (g + 1) * span, pair * 128 : (pair + 1) * 128].astype(F32)
            rows = slice(g * half, (g + 1) * half)
            slices[2 * pair, rows, :] = jnp.where(lane < 64, top, pltpu.roll(end, 64, 1)).astype(BF16)
            slices[2 * pair + 1, rows, :] = jnp.where(lane < 64, pltpu.roll(top, 64, 1), end).astype(BF16)
    p = plane_index(count_y)
    lines = slices.shape[1]
    for i, send in enumerate(sends):
        send[:lines, :] = slices[p ^ (2 * i)]
        send[lines:, :] = slices[p ^ (2 * i + 1)]


def coarse_grad_kernel(count_y, count_z, quarter, *refs):
    grads, (bottle, shift, w_bottle) = refs[: -count_z - 6], refs[-count_z - 6 : -count_z - 3]
    sends, (window, gathered, blocks) = refs[-count_z - 3 : -3], refs[-3:]
    count_p = len(grads)
    cells, outs = bottle.shape
    rows = count_p * quarter
    depth = cells // quarter
    own_cells = cells // count_z
    inputs = w_bottle.shape[1]
    p = plane_index(count_y)
    for i, part in enumerate(grads):
        gathered[p ^ (-i % count_p)] = part[:cells, :]
    mine = pl.multiple_of(p * quarter, quarter)
    picks = jnp.concatenate([shift[pl.ds((8 - bc) * rows + mine, quarter), :] for bc in range(9)], axis=0)
    window[:quarter, :] = jnp.zeros((quarter, 9 * outs), BF16)
    window[(depth + 1) * quarter :, :] = jnp.zeros((quarter, 9 * outs), BF16)
    for z in range(depth):
        plane = jnp.concatenate([gathered[q, z * quarter : (z + 1) * quarter, :] for q in range(count_p)], axis=0)
        moved = matmul(picks, plane).astype(BF16)
        for bc in range(9):
            window[(z + 1) * quarter : (z + 2) * quarter, bc * outs : (bc + 1) * outs] = moved[
                bc * quarter : (bc + 1) * quarter, :
            ]
    total = None
    for a in range(3):
        weight = jnp.concatenate([w_bottle[9 * a + bc] for bc in range(9)], axis=1)
        term = matmul_nt(window[(2 - a) * quarter : (2 - a + depth) * quarter, :], weight)
        total = term if total is None else total + term
    total = total.astype(BF16)
    for q in range(count_z):
        blocks[q, :, :inputs] = total[q * own_cells : (q + 1) * own_cells, :]
        blocks[q, :, inputs:] = bottle[q * own_cells : (q + 1) * own_cells, :]
    hand_out(blocks, sends, lax.axis_index("gz"))


def wide_kernel(count_y, quarter, *refs):
    parts, (wide, grads) = refs[:-2], refs[-2:]
    count_p, cells, outs = grads.shape
    rows = count_p * quarter
    depth = cells // quarter
    take_in([part.at[:cells, :] for part in parts], grads, plane_index(count_y))
    planes = [
        jnp.concatenate([grads[q, z * quarter : (z + 1) * quarter, :] for q in range(count_p)], axis=0)
        for z in range(depth)
    ]
    zeros = jnp.zeros((rows, outs), BF16)
    for j in range(depth // 2):
        for slot in range(5):
            z = j // 2 * 4 + j % 2 + slot - 1
            wide[j * rows : (j + 1) * rows, slot * outs : (slot + 1) * outs] = planes[z] if 0 <= z < depth else zeros


def coarse_transpose_kernel(count_y, shift, *refs):
    parts, (turned, slices) = refs[:-2], refs[-2:]
    count_p, lines, _ = slices.shape
    rows = shift.shape[1]
    quarter = rows // count_p
    p = plane_index(count_y)
    for d, part in enumerate(parts):
        start = (2 + d % 2) * lines
        slices[p ^ d] = part[start : start + lines, :]
    for j in range(lines // quarter):
        plane = jnp.concatenate([slices[q, j * quarter : (j + 1) * quarter, :] for q in range(count_p)], axis=0)
        plane = plane.astype(F32).T.astype(BF16)
        for bc in range(9):
            turned[bc * 128 : (bc + 1) * 128, j * rows : (j + 1) * rows] = matmul(
                plane, shift[(8 - bc) * rows : (9 - bc) * rows, :]
            ).astype(BF16)


def grad_bottle_kernel(turned, wide, out):
    _, channels, outs = out.shape
    full = matmul(turned[...], wide[...])
    for bc in range(9):
        top = full[bc * 128 : bc * 128 + channels, :]
        end = full[bc * 128 + channels : (bc + 1) * 128, :]
        for a in range(3):
            out[9 * a + bc] = top[:, (2 - a) * outs : (3 - a) * outs] + end[:, (4 - a) * outs : (5 - a) * outs]


def half_grad(turned, shifted, parity, chip, out, blocks):
    chips, rows, channels = blocks.shape
    group = rows // 27
    full = matmul(turned[parity], shifted[...])
    for bc in range(9):
        for a in range(3):
            t = 9 * a + bc
            for q in range(chips):
                start = (bc * chips + q) * group
                blocks[q, t * group : (t + 1) * group, :] = full[
                    start : start + group, a * channels : (a + 1) * channels
                ].astype(BF16)
    for i in range(chips):
        out[i] = blocks[chip ^ i]


def hidden_grad_kernel(count_y, count_z, *refs):
    parts, (slope, ordered, w_down, turned) = refs[:count_z], refs[count_z : count_z + 4]
    shifted, bottle, give, bottles, blocks = refs[count_z + 4 :]
    size_z, own, channels = ordered.shape
    quarter = own // 4
    inputs = w_down.shape[2]
    pz = lax.axis_index("gz")
    grad = total_of([part.at[:, :inputs] for part in parts]).astype(BF16)
    for i, part in enumerate(parts):
        bottles[pz ^ (-i % count_z)] = part[:, inputs:]
    bottle[...] = jnp.concatenate([bottles[q] for q in range(count_z)], axis=1)
    shifted[...] = jnp.zeros_like(shifted)
    for s in range(8):
        a, bc = s // 4, s % 4
        spread_grad = matmul_nt(grad, w_down[s])
        for kz in range(size_z // 2):
            z = 2 * kz + a
            part = slice(bc * quarter, (bc + 1) * quarter)
            line = slice(kz * quarter, (kz + 1) * quarter)
            value = ((spread_grad[line, :] + ordered[z, part, :].astype(F32)) * slope[z, part, :]).astype(BF16)
            for t in range(3):
                start = (z + t) * own + bc * quarter
                shifted[start : start + quarter, t * channels : (t + 1) * channels] = value
    p = plane_index(count_y)
    half_grad(turned, shifted, 1 - p % 2, p // 2, give, blocks)


def keep_kernel(count_y, shifted, turned, keep, blocks):
    p = plane_index(count_y)
    half_grad(turned, shifted, p % 2, p // 2, keep, blocks)


def output_kernel(bottle, hidden, w_up, order_t, output, rows_out):
    size_z, own, channels = hidden.shape
    quarter = own // 4
    for s in range(8):
        a, bc = s // 4, s % 4
        lifted = matmul(bottle[...], w_up[s])
        for kz in range(size_z // 2):
            z = 2 * kz + a
            part = slice(bc * quarter, (bc + 1) * quarter)
            line = slice(kz * quarter, (kz + 1) * quarter)
            rows_out[z, part, :] = (lifted[line, :] + hidden[z, part, :].astype(F32)).astype(BF16)
    for z in range(size_z):
        plane = matmul(order_t[...], rows_out[z])
        output[z] = plane.reshape(output.shape[1:]).astype(BF16)


def pair_sum_kernel(keep, got, *sends):
    for i, send in enumerate(sends):
        send[...] = (keep[i].astype(F32) + got[i].astype(F32)).astype(BF16)


def sum_kernel(*refs):
    out = refs[-1]
    out[...] = total_of(refs[:-1]).reshape(out.shape).astype(out.dtype)


def shape_of(shape, dtype=BF16):
    return jax.ShapeDtypeStruct(shape, dtype)


def gathered_body(counts, volume, cotangent, w_conv, w_down, w_bottle, w_up):
    count_x, count_y, count_z = counts
    count_p = count_x * count_y
    size_z, size_x, size_y, channels = volume.shape
    wide = w_down.shape[2]
    group = w_bottle.shape[2]
    half_x, half_y = size_x // 2, size_y // 2
    own = size_x * size_y
    quarter = half_x * half_y
    own_cells = size_z // 2 * quarter
    cells = count_z * own_cells
    depth = count_z * size_z // 2
    rows = count_p * quarter
    planes = size_z + 2
    share_c = channels // count_p
    share_w = wide // count_p
    plane_axes = ("gx", "gy")

    order, taps = fine_maps(size_x, size_y)
    pair_taps = np.zeros((2, 2 * own, 9, 2, own), np.float32)
    for i in range(2):
        pair_taps[i, :, :, i, :] = taps.transpose(2, 0, 1)
    shift = coarse_maps(count_x, count_y, half_x, half_y)
    order_m = jnp.asarray(order, BF16)
    order_t = jnp.asarray(order.T, BF16)
    taps_m = jnp.asarray(taps.reshape(9 * own, 2 * own), BF16)
    taps_t = jnp.asarray(pair_taps.reshape(4 * own, 18 * own), BF16)
    shift_m = jnp.asarray(shift.reshape(9 * rows, rows), BF16)

    send_maps, rim_maps = column_maps(half_x, half_y, depth)
    send_m = jnp.asarray(send_maps, BF16)
    rim_m = jnp.asarray(rim_maps.reshape(count_x, 36 * quarter, 8 * quarter), BF16)

    w_conv_t = jnp.transpose(w_conv, (1, 0, 2))
    w_bottle_t = jnp.transpose(w_bottle, (1, 0, 2))
    send_a, send_b = local_call(ends_kernel, "ends", [shape_of((size_x, size_y, channels))] * 2)(volume)
    z_pairs = line_pairs(count_z)
    z_b = lax.ppermute(send_b, "gz", z_pairs[1])
    z_a = lax.ppermute(send_a, "gz", z_pairs[0])
    *backs, ordered = local_call(
        lambda *refs: back_kernel(count_z, *refs),
        "back",
        [shape_of((own_cells, group))] * count_z + [shape_of((size_z, own, channels))],
        [pltpu.VMEM((count_z, own_cells, group), BF16)],
    )(cotangent, w_up, order_m)
    sends = local_call(
        faces_kernel,
        "faces",
        [shape_of((16 * size_y, channels))] + [shape_of((planes * size_x, channels))] * 2 + [shape_of((16, channels))],
        [pltpu.VMEM((16 * own, channels), F32)],
    )(volume, z_a, z_b)
    x_send, send_a, send_b, corner_b = sends
    x_rim, across, corner = swap_rims(x_send, send_b, corner_b, counts)
    relayed = relay_rims(x_rim, across, corner, send_a, counts)
    hidden, slope, rim, *sends = local_call(
        lambda *refs: hidden_kernel(count_z, *refs),
        "hidden",
        [
            shape_of((size_z, own, channels)),
            shape_of((size_z, own, channels), F32),
            shape_of((planes, 2 * own, channels)),
        ]
        + [shape_of((own_cells, wide + group))] * count_z,
        [
            pltpu.VMEM((planes * 2 * own, channels), F32),
            pltpu.VMEM((planes, own, 9 * channels), BF16),
        ],
        flops=2_000_000_000,
    )(volume, z_a, z_b, x_rim, relayed, taps_m, w_conv_t, w_down, *backs)
    parts = trade(sends, "gz", count_z)
    column, back, *sends = local_call(
        lambda *refs: column_kernel(count_z, *refs),
        "column",
        [shape_of((cells, wide)), shape_of((cells, group)), shape_of((depth * half_y, wide))]
        + [shape_of((depth * half_x, wide))] * 2
        + [shape_of((depth, wide))],
    )(parts[0], *parts[:0:-1], send_m)
    x_send, send_a, send_b, corner_b = sends
    x_rim, across, corner = swap_rims(x_send, send_b, corner_b, counts)
    relayed = relay_rims(x_rim, across, corner, send_a, counts)
    slices = local_call(
        lambda *refs: slices_kernel(count_y, quarter, *refs),
        "slices",
        [shape_of((cells, 128))] * (count_p // 2),
        [pltpu.VMEM((count_p, cells // 2, 128), BF16)],
    )(column)
    column, *slices = lax.optimization_barrier((column, *slices))
    bottle, *sends = local_call(
        lambda *refs: bottle_kernel(quarter, *refs),
        "bottle",
        [shape_of((cells, group))] + [shape_of((2 * cells, group))] * (count_p // 2),
        [
            pltpu.VMEM((depth // 4, 16, wide), F32),
            pltpu.VMEM(((depth + 2) * quarter, 9 * wide), BF16),
        ],
        flops=2_000_000_000,
    )(column, back, x_rim, relayed, rim_m, w_bottle_t, *slices)
    grads = [None] * count_p
    grads[0] = sends[0]
    for d in (6, 4, 2):
        grads[d] = swap(sends[d // 2], plane_axes, count_p, d)
    for d in (0, 2, 4, 6):
        grads[d + 1] = swap(grads[d], plane_axes, count_p, 1)
    sends = local_call(
        lambda *refs: coarse_grad_kernel(count_y, count_z, quarter, *refs),
        "coarse_grad",
        [shape_of((own_cells, wide + group))] * count_z,
        [
            pltpu.VMEM(((depth + 2) * quarter, 9 * group), BF16),
            pltpu.VMEM((count_p, cells, group), BF16),
            pltpu.VMEM((count_z, own_cells, wide + group), BF16),
        ],
    )(grads[0], *grads[:0:-1], bottle, shift_m, w_bottle_t)
    parts = trade(sends, "gz", count_z)
    rim, late, _ = lax.optimization_barrier((rim, grads[0], sends[1]))
    turned = local_call(
        lambda *refs: rim_transpose_kernel(count_p, *refs),
        "rim_transpose",
        shape_of((2, 9 * channels // 2, planes * own)),
    )(rim, taps_t)
    coarse_turned = local_call(
        lambda *refs: coarse_transpose_kernel(count_y, *refs),
        "coarse_transpose",
        shape_of((18 * share_w, depth // 2 * rows)),
        [pltpu.VMEM((count_p, cells // 2, 128), BF16)],
    )(shift_m, late, *grads[1:])
    turned, coarse_turned = lax.optimization_barrier((turned, coarse_turned))
    shifted, bottle, give = local_call(
        lambda *refs: hidden_grad_kernel(count_y, count_z, *refs),
        "hidden_grad",
        [
            shape_of((planes * own, 3 * channels)),
            shape_of((own_cells, wide)),
            shape_of((count_p // 2, 27 * share_c, channels)),
        ],
        [
            pltpu.VMEM((count_z, own_cells, group), BF16),
            pltpu.VMEM((count_p // 2, 27 * share_c, channels), BF16),
        ],
    )(parts[0], *parts[:0:-1], slope, ordered, w_down, turned)
    got = swap(give, plane_axes, count_p, 1)
    keep = local_call(
        lambda *refs: keep_kernel(count_y, *refs),
        "keep",
        shape_of((count_p // 2, 27 * share_c, channels)),
        [pltpu.VMEM((count_p // 2, 27 * share_c, channels), BF16)],
    )(shifted, turned)
    output = local_call(
        output_kernel,
        "output",
        shape_of(volume.shape),
        [pltpu.VMEM((size_z, own, channels), BF16)],
    )(bottle, hidden, w_up, order_t)
    sends = local_call(
        pair_sum_kernel,
        "pair_sum",
        [shape_of((27 * share_c, channels))] * (count_p // 2),
    )(keep, got)
    parts = [sends[0]] + [swap(sends[d // 2], plane_axes, count_p, d) for d in (6, 4, 2)]
    part = local_call(sum_kernel, "plane_sum", shape_of((27 * share_c, channels)))(*parts)
    part, output = lax.optimization_barrier((part, output))
    got = swap(part, "gz", count_z, 1)
    wide_grads = local_call(
        lambda *refs: wide_kernel(count_y, quarter, *refs),
        "wide",
        shape_of((depth // 2 * rows, 5 * group)),
        [pltpu.VMEM((count_p, cells, group), BF16)],
    )(*grads)
    got, wide_grads = lax.optimization_barrier((got, wide_grads))
    part = local_call(sum_kernel, "depth_sum", shape_of((27 * share_c, channels)))(part, got)
    got = swap(part, "gz", count_z, 2)
    grad_bottle = local_call(
        grad_bottle_kernel,
        "grad_bottle",
        shape_of((27, share_w, group), F32),
        flops=4_000_000_000,
    )(coarse_turned, wide_grads)
    grad_conv = local_call(
        sum_kernel,
        "grad_conv",
        shape_of((27, share_c, channels), F32),
    )(part, got)
    return (output, jnp.transpose(grad_conv, (1, 0, 2)), jnp.transpose(grad_bottle, (1, 0, 2)))


def with_halo(cells, sides, width):
    for axis, dim in sides:
        count = lax.axis_size(axis)
        ends = count - 1
        head = lax.slice_in_dim(cells, 0, width, axis=dim)
        tail = lax.slice_in_dim(cells, cells.shape[dim] - width, cells.shape[dim], axis=dim)
        cells = jnp.concatenate(
            [
                lax.ppermute(tail, axis, [(i, (i + 1) % count) for i in range(ends)]),
                cells,
                lax.ppermute(head, axis, [((i + 1) % count, i) for i in range(ends)]),
            ],
            axis=dim,
        )
    return cells


def silu_slope(values):
    sig = jax.nn.sigmoid(values)
    return sig * (1.0 + values * (1.0 - sig))


def conv_forward(padded, weight, extent):
    size_z, size_x, size_y = extent
    count_cells = size_z * size_x * size_y
    summed = jnp.zeros((count_cells, weight.shape[2]), jnp.float32)
    for tap_index in range(27):
        shift_z, shift_x, shift_y = (tap_index // 9, tap_index // 3 % 3, tap_index % 3)
        window = padded[
            shift_z : shift_z + size_z, shift_x : shift_x + size_x, shift_y : shift_y + size_y, :
        ]
        window = window.reshape(count_cells, padded.shape[3])
        summed = summed + jnp.dot(
            window, weight[:, tap_index, :], preferred_element_type=jnp.float32
        )
    return summed.reshape(size_z, size_x, size_y, weight.shape[2])


def conv_weight_grad(padded, gradient, extent):
    size_z, size_x, size_y = extent
    count_cells = size_z * size_x * size_y
    flat_gradient = gradient.reshape(count_cells, gradient.shape[3])
    pieces = []
    for tap_index in range(27):
        shift_z, shift_x, shift_y = (tap_index // 9, tap_index // 3 % 3, tap_index % 3)
        window = padded[
            shift_z : shift_z + size_z, shift_x : shift_x + size_x, shift_y : shift_y + size_y, :
        ]
        window = window.reshape(count_cells, padded.shape[3])
        pieces.append(
            lax.dot_general(
                window, flat_gradient, (((0,), (0,)), ((), ())), preferred_element_type=jnp.float32
            )
        )
    return jnp.stack(pieces, axis=1)


def conv_input_grad(padded, weight, extent):
    size_z, size_x, size_y = extent
    count_cells = size_z * size_x * size_y
    summed = jnp.zeros((count_cells, weight.shape[0]), jnp.float32)
    for tap_index in range(27):
        shift_z, shift_x, shift_y = (2 - tap_index // 9, 2 - tap_index // 3 % 3, 2 - tap_index % 3)
        window = padded[
            shift_z : shift_z + size_z, shift_x : shift_x + size_x, shift_y : shift_y + size_y, :
        ]
        window = window.reshape(count_cells, padded.shape[3])
        summed = summed + lax.dot_general(
            window,
            weight[:, tap_index, :],
            (((1,), (1,)), ((), ())),
            preferred_element_type=jnp.float32,
        )
    return summed.reshape(size_z, size_x, size_y, weight.shape[0])


def pool_features(fine, kernel):
    size_z, size_x, size_y, channels = fine.shape
    blocks = fine.reshape(size_z // 2, 2, size_x // 2, 2, size_y // 2, 2, channels)
    kernel_cube = kernel.reshape(2, 2, 2, kernel.shape[1], kernel.shape[2])
    return jnp.einsum(
        "zaxbycf,abcfg->zxyg", blocks, kernel_cube, preferred_element_type=jnp.float32
    )


def pool_adjoint(coarse_in, kernel):
    size_z, size_x, size_y, wide_channels = coarse_in.shape
    kernel_cube = kernel.reshape(2, 2, 2, kernel.shape[1], kernel.shape[2])
    result = jnp.einsum(
        "zxyg,abcfg->zaxbycf", coarse_in, kernel_cube, preferred_element_type=jnp.float32
    )
    return result.reshape(2 * size_z, 2 * size_x, 2 * size_y, kernel.shape[1])


def lift_features(coarse_in, kernel):
    size_z, size_x, size_y, wide_channels = coarse_in.shape
    kernel_cube = kernel.reshape(2, 2, 2, kernel.shape[1], kernel.shape[2])
    result = jnp.einsum(
        "zxyg,abcgf->zaxbycf", coarse_in, kernel_cube, preferred_element_type=jnp.float32
    )
    return result.reshape(2 * size_z, 2 * size_x, 2 * size_y, kernel.shape[2])


def lift_adjoint(fine, kernel):
    size_z, size_x, size_y, channels = fine.shape
    blocks = fine.reshape(size_z // 2, 2, size_x // 2, 2, size_y // 2, 2, channels)
    kernel_cube = kernel.reshape(2, 2, 2, kernel.shape[1], kernel.shape[2])
    return jnp.einsum(
        "zaxbycf,abcgf->zxyg", blocks, kernel_cube, preferred_element_type=jnp.float32
    )


def column_body(volume, cotangent, w_conv, w_down, w_bottle, w_up):
    size_z, size_x, size_y, channels = volume.shape
    group_channels = w_bottle.shape[2]
    half_x = size_x // 2
    half_y = size_y // 2
    padded = with_halo(volume, (("gx", 1), ("gy", 2), ("gz", 0)), 1)
    pre_hidden = conv_forward(padded, w_conv, (size_z, size_x, size_y))
    hidden = jax.nn.silu(pre_hidden).astype(jnp.bfloat16)
    hidden_slope = silu_slope(pre_hidden)
    coarse = pool_features(hidden, w_down).astype(jnp.bfloat16)
    stacked = lax.all_gather(coarse, "gz", axis=0, tiled=True)
    rimmed = with_halo(stacked, (("gx", 1), ("gy", 2)), 1)
    column_z = rimmed.shape[0]
    coarse_pad = jnp.pad(rimmed, ((1, 1), (0, 0), (0, 0), (0, 0)))
    pre_bottle = conv_forward(coarse_pad, w_bottle, (column_z, half_x, half_y))
    bottle = jax.nn.silu(pre_bottle).astype(jnp.bfloat16)
    bottle_slope = silu_slope(pre_bottle)
    own_start = lax.axis_index("gz") * group_channels
    own_up = lax.dynamic_slice_in_dim(w_up, own_start, group_channels, 1)
    lifted = lax.psum_scatter(
        lift_features(bottle, own_up).astype(jnp.bfloat16), "gz", scatter_dimension=0, tiled=True
    ).astype(jnp.float32)
    output = (lifted + hidden.astype(jnp.float32)).astype(jnp.bfloat16)
    back_bottle = lift_adjoint(cotangent, w_up).astype(jnp.bfloat16)
    split_grad = lax.all_to_all(back_bottle, "gz", split_axis=3, concat_axis=0, tiled=True)
    bottle_grad = (split_grad.astype(jnp.float32) * bottle_slope).astype(jnp.bfloat16)
    grad_bottle = lax.psum_scatter(
        conv_weight_grad(coarse_pad, bottle_grad, (column_z, half_x, half_y)),
        ("gx", "gy"),
        scatter_dimension=0,
        tiled=True,
    )
    grad_rimmed = with_halo(bottle_grad, (("gx", 1), ("gy", 2)), 1)
    grad_pad = jnp.pad(grad_rimmed, ((1, 1), (0, 0), (0, 0), (0, 0)))
    coarse_grad = lax.psum_scatter(
        conv_input_grad(
            grad_pad, w_bottle, (lax.axis_size("gz") * (size_z // 2), half_x, half_y)
        ).astype(jnp.bfloat16),
        "gz",
        scatter_dimension=0,
        tiled=True,
    )
    hidden_grad = (
        (pool_adjoint(coarse_grad, w_down) + cotangent.astype(jnp.float32)) * hidden_slope
    ).astype(jnp.bfloat16)
    full_term = conv_weight_grad(padded, hidden_grad, (size_z, size_x, size_y))
    depth_summed = lax.psum(full_term.astype(jnp.bfloat16), "gz").astype(jnp.float32)
    grad_conv = lax.psum_scatter(depth_summed, ("gx", "gy"), scatter_dimension=0, tiled=True)
    return (output, grad_conv, grad_bottle)


def fits_one_plane(counts, brick, wide):
    count_p = counts[0] * counts[1]
    size_z, size_x, size_y, channels = brick
    return (
        counts == (2, 4, 4)
        and count_p * (size_x // 2) * (size_y // 2) == 128
        and wide // count_p == 64
        and (size_z, size_x, size_y, channels) == (8, 8, 8, 128)
    )


def solution(mesh):
    in_specs = (
        P("gz", "gx", "gy", None),
        P("gz", "gx", "gy", None),
        P(),
        P(),
        P(None, None, "gz"),
        P(),
    )
    out_specs = (
        P("gz", "gx", "gy", None),
        P(("gx", "gy"), None, None),
        P(("gx", "gy"), None, "gz"),
    )
    counts = (mesh.shape["gx"], mesh.shape["gy"], mesh.shape["gz"])

    def body(volume, cotangent, w_conv, w_down, w_bottle, w_up):
        if fits_one_plane(counts, volume.shape, w_down.shape[2]):
            return gathered_body(counts, volume, cotangent, w_conv, w_down, w_bottle, w_up)
        return column_body(volume, cotangent, w_conv, w_down, w_bottle, w_up)

    return jax.shard_map(body, mesh=mesh, in_specs=in_specs, out_specs=out_specs, check_vma=False)
```

```python
import numpy as np
import jax
import jax.numpy as jnp
from jax import lax
from jax.experimental import pallas as pl
from jax.experimental.pallas import tpu as pltpu
from jax.sharding import PartitionSpec as P

BF16 = jnp.bfloat16
F32 = jnp.float32
VMEM_LIMIT = 24 * 1024 * 1024


def local_call(kernel, name, out_shapes, scratch=(), flops=300_000_000):
    whole = pl.BlockSpec(memory_space=pltpu.VMEM)

    def call(*operands):
        return pl.pallas_call(
            kernel,
            name=name,
            out_shape=out_shapes,
            in_specs=[whole] * len(operands),
            out_specs=jax.tree.map(lambda _: whole, out_shapes),
            scratch_shapes=list(scratch),
            compiler_params=pltpu.CompilerParams(vmem_limit_bytes=VMEM_LIMIT),
            cost_estimate=pl.CostEstimate(flops=flops, bytes_accessed=flops // 1000, transcendentals=0),
        )(*operands)

    return call


def matmul(left, right):
    return jnp.dot(left, right, preferred_element_type=F32)


def matmul_nt(left, right):
    return lax.dot_general(left, right, (((1,), (1,)), ((), ())), preferred_element_type=F32)


def sub_order(size_x, size_y):
    half_x, half_y = size_x // 2, size_y // 2
    return {
        (2 * kx + b, 2 * ky + c): ((2 * b + c) * half_x + kx) * half_y + ky
        for b in range(2)
        for c in range(2)
        for kx in range(half_x)
        for ky in range(half_y)
    }


def fine_maps(size_x, size_y):
    own = size_x * size_y
    rows = sub_order(size_x, size_y)
    order = np.zeros((own, own), np.float32)
    taps = np.zeros((9, own, 2 * own), np.float32)
    for (x, y), row in rows.items():
        order[row, x * size_y + y] = 1
        for b in range(3):
            for c in range(3):
                sx, sy = x + b - 1, y + c - 1
                if sx < 0:
                    part = 0 if 0 <= sy < size_y else (4 if sy < 0 else 5)
                    source = own + 8 * part + sy % size_y
                elif sx >= size_x:
                    part = 1 if 0 <= sy < size_y else (6 if sy < 0 else 7)
                    source = own + 8 * part + sy % size_y
                elif sy < 0:
                    source = own + 16 + sx
                elif sy >= size_y:
                    source = own + 24 + sx
                else:
                    source = sx * size_y + sy
                taps[3 * b + c, row, source] = 1
    return order, taps


def coarse_maps(count_x, count_y, half_x, half_y):
    wide_x, wide_y = count_x * half_x, count_y * half_y

    def row_of(x, y):
        brick = (x // half_x) * count_y + y // half_y
        return (brick * half_x + x % half_x) * half_y + y % half_y

    shift = np.zeros((9, wide_x * wide_y, wide_x * wide_y), np.float32)
    for x in range(wide_x):
        for y in range(wide_y):
            for b in range(3):
                for c in range(3):
                    sx, sy = x + b - 1, y + c - 1
                    if 0 <= sx < wide_x and 0 <= sy < wide_y:
                        shift[3 * b + c, row_of(x, y), row_of(sx, sy)] = 1
    return shift


def column_maps(half_x, half_y, depth):
    quarter = half_x * half_y
    rows = depth * quarter
    send = np.zeros((2, depth * (half_y + 2 * half_x + 2), rows), np.float32)
    rim = np.zeros((2, 9, 4, quarter, 8 * quarter), np.float32)
    for px in range(2):
        edge = 0 if px else half_x - 1
        for z in range(depth):
            base = z * quarter
            for ky in range(half_y):
                send[px, z * half_y + ky, base + edge * half_y + ky] = 1
            for side, ky in enumerate((0, half_y - 1)):
                row = depth * (half_y + side * half_x) + z * half_x
                for kx in range(half_x):
                    send[px, row + kx, base + kx * half_y + ky] = 1
                send[px, depth * (half_y + 2 * half_x + side) + z, base + edge * half_y + ky] = 1
    for px in range(2):
        for b in range(3):
            for c in range(3):
                for kx in range(half_x):
                    for ky in range(half_y):
                        sx, sy = kx + b - 1, ky + c - 1
                        beyond = sx < 0 if px else sx >= half_x
                        if (sx < 0 or sx >= half_x) and not beyond:
                            continue
                        for z in range(4):
                            if beyond and 0 <= sy < half_y:
                                source = 4 * quarter + z * half_y + sy
                            elif beyond:
                                source = 7 * quarter + 4 * (sy >= half_y) + z
                            elif sy < 0:
                                source = 5 * quarter + z * half_x + sx
                            elif sy >= half_y:
                                source = 6 * quarter + z * half_x + sx
                            else:
                                source = z * quarter + sx * half_y + sy
                            rim[px, 3 * b + c, z, kx * half_y + ky, source] = 1
    return send, rim


def swap(block, axes, count, distance):
    return lax.ppermute(block, axes, [(i, i ^ distance) for i in range(count)])


def trade(blocks, axes, count):
    got = {d: swap(blocks[d], axes, count, d) for d in reversed(range(1, count))}
    return [blocks[0]] + [got[d] for d in range(1, count)]


def line_pairs(length):
    first = [(i, i ^ 1) for i in range(length)]
    second = [(i, i + 1 if i % 2 else i - 1) for i in range(1, length - 1)]
    return first, second


def swap_rims(x_send, send_b, corner_b, counts):
    count_x, count_y, _ = counts
    axes, count = ("gx", "gy"), count_x * count_y
    corner = swap(corner_b, axes, count, count_y + 2)
    x_rim = swap(x_send, axes, count, count_y)
    across = swap(send_b, axes, count, 2)
    return x_rim, across, corner


def line_sides(axis, pair_a, pair_b):
    even = lax.axis_index(axis) % 2 == 0
    return jnp.where(even, pair_b, pair_a), jnp.where(even, pair_a, pair_b)


def relay_rims_kernel(corner, across, x_rim, send_a, send, side):
    face, lines = across.shape[0], corner.shape[0]
    pitch = x_rim.shape[0] // lines
    even = lax.axis_index("gy") % 2 == 0
    for part in range(0, x_rim.shape[1], 128):
        columns = slice(part, part + 128)
        side[...] = x_rim[:, columns].astype(F32)
        ends = [side[pl.ds(y, lines, stride=pitch), :] for y in (pitch - 1, 0)]
        send[face + lines : face + 2 * lines, columns] = jnp.where(even, ends[0], ends[1]).astype(BF16)
    send[face + 2 * lines :, :] = send_a[...]
    send[:face, :] = across[...]
    send[face : face + lines, :] = corner[...]


def pass_kernel(block, out):
    out[...] = block[...]


def relay_rims(x_rim, across, corner, send_a, counts):
    rows = 2 * (across.shape[0] + corner.shape[0])
    corner = local_call(pass_kernel, "corner", shape_of(corner.shape), flops=5_000_000_000)(corner)
    send = local_call(
        relay_rims_kernel,
        "relay_rims",
        shape_of((rows, across.shape[1])),
        [pltpu.VMEM((x_rim.shape[0], 128), F32)],
    )(corner, across, x_rim, send_a)
    return swap(send, ("gx", "gy"), counts[0] * counts[1], 1)


def y_rims(relayed, lines):
    py = lax.axis_index("gy")
    face = relayed.shape[0] // 2 - lines
    inner = (py > 0) & (py < lax.axis_size("gy") - 1)
    face_b = jnp.where(inner, relayed[:face, :].astype(F32), 0.0)
    corner_b = jnp.where(inner, relayed[face : face + lines, :].astype(F32), 0.0)
    corner_a = relayed[face + lines : face + 2 * lines, :].astype(F32)
    face_a = relayed[face + 2 * lines :, :].astype(F32)
    return *line_sides("gy", face_a, face_b), *line_sides("gy", corner_a, corner_b)


def plane_index(count_y):
    return lax.axis_index("gx") * count_y + lax.axis_index("gy")


def plane_rows(ref, z):
    _, size_x, size_y, channels = ref.shape
    return ref[z].astype(F32).reshape(size_x * size_y, channels)


def hand_out(blocks, outs, me):
    for d, out in enumerate(outs):
        out[...] = blocks[me ^ d]


def take_in(parts, blocks, me):
    for d, part in enumerate(parts):
        blocks[me ^ d] = part[...]


def total_of(parts):
    terms = [part[...].astype(F32) for part in parts]
    while len(terms) > 1:
        terms = [terms[i] + terms[i + 1] for i in range(0, len(terms), 2)]
    return terms[0]


def back_kernel(count_z, cotangent, w_up, order, *refs):
    sends, (ordered, blocks) = refs[:count_z], refs[count_z:]
    size_z, size_x, size_y, channels = cotangent.shape
    own = size_x * size_y
    quarter = own // 4
    for z in range(size_z):
        ordered[z] = matmul(order[...], plane_rows(cotangent, z).astype(BF16)).astype(BF16)
    back = None
    for s in range(8):
        a, bc = s // 4, s % 4
        cells = jnp.concatenate(
            [ordered[2 * kz + a, bc * quarter : (bc + 1) * quarter, :] for kz in range(size_z // 2)], axis=0
        )
        term = matmul_nt(cells, w_up[s])
        back = term if back is None else back + term
    back = back.astype(BF16)
    group = back.shape[1] // count_z
    for q in range(count_z):
        blocks[q] = back[:, q * group : (q + 1) * group]
    hand_out(blocks, sends, lax.axis_index("gz"))


def deepen(volume, z_a, z_b, deep, pitch):
    size_z, size_x, size_y, channels = volume.shape
    own = size_x * size_y
    below, above = line_sides("gz", z_a[...], z_b[...])
    deep[:own, :] = below.astype(F32).reshape(own, channels)
    for z in range(size_z):
        deep[(z + 1) * pitch : (z + 1) * pitch + own, :] = plane_rows(volume, z)
    deep[(size_z + 1) * pitch : (size_z + 1) * pitch + own, :] = above.astype(F32).reshape(own, channels)


def ends_kernel(volume, send_a, send_b):
    below, above = volume[0], volume[volume.shape[0] - 1]
    send_b[...], send_a[...] = line_sides("gz", above, below)


def faces_kernel(volume, z_a, z_b, x_send, send_a, send_b, corner_b, deep):
    size_z, size_x, size_y, channels = volume.shape
    own = size_x * size_y
    planes = x_send.shape[0] // size_y
    deepen(volume, z_a, z_b, deep, own)
    start = (size_z + 2) * own
    deep[start:, :] = jnp.zeros((deep.shape[0] - start, channels), F32)
    first = lax.axis_index("gx") == 0
    far = (size_x - 1) * size_y

    def x_face(start):
        return jnp.concatenate([deep[z * own + start : z * own + start + size_y, :] for z in range(planes)], axis=0)

    x_send[...] = jnp.where(first, x_face(far), x_face(0)).astype(BF16)
    faces, corners = [], []
    for y in (0, size_y - 1):
        faces.append(deep[pl.ds(y, send_a.shape[0], stride=size_y), :].astype(BF16))
        ends = [deep[pl.ds(start + y, planes, stride=own), :] for start in (far, 0)]
        corners.append(jnp.where(first, ends[0], ends[1]).astype(BF16))
    send_b[...], send_a[...] = line_sides("gy", faces[1], faces[0])
    corner_b[...], _ = line_sides("gy", corners[1], corners[0])


def hidden_kernel(count_z, volume, z_a, z_b, x_rim, relayed, taps, w_conv, w_down, *refs):
    backs, (hidden, slope, rim), sends, (rim32, cells) = (
        refs[:count_z],
        refs[count_z : count_z + 3],
        refs[count_z + 3 : -2],
        refs[-2:],
    )
    size_z, size_x, size_y, channels = volume.shape
    own = size_x * size_y
    quarter = own // 4
    planes = size_z + 2
    pitch = 2 * own
    first = lax.axis_index("gx") == 0
    deepen(volume, z_a, z_b, rim32, pitch)
    y_low, y_high, xy_low, xy_high = y_rims(relayed, x_rim.shape[0] // size_y)
    x_side = x_rim[...].astype(F32)
    x_low, x_high = jnp.where(first, 0.0, x_side), jnp.where(first, x_side, 0.0)
    faces = (x_low, x_high, y_low, y_high)
    for z in range(planes):
        for part, block in enumerate(faces):
            start = z * pitch + own + 8 * part
            rim32[start : start + 8, :] = block[8 * z : 8 * (z + 1), :]
        rim32[z * pitch + own + 32 : (z + 1) * pitch, :] = jnp.zeros((own - 32, channels), F32)
    corners = ((xy_low, 7, True), (xy_high, 0, True), (xy_low, 7, False), (xy_high, 0, False))
    for part, (block, row, low) in enumerate(corners):
        start = own + 32 + 8 * part + row
        value = jnp.where(first == low, 0.0, block)
        rim32[pl.ds(start, 8, stride=pitch), :] = value[:8, :]
        for z in range(8, planes):
            rim32[z * pitch + start : z * pitch + start + 1, :] = value[z : z + 1, :]
    for z in range(0, planes, 2):
        pair = [rim32[(z + i) * pitch : (z + i + 1) * pitch, :].astype(BF16) for i in range(2)]
        moved = matmul(taps[...], jnp.concatenate(pair, axis=1)).astype(BF16)
        for i in range(2):
            rim[z + i] = pair[i]
            for bc in range(9):
                cells[z + i, :, bc * channels : (bc + 1) * channels] = moved[
                    bc * own : (bc + 1) * own, i * channels : (i + 1) * channels
                ]
    weights = [w_conv[9 * a : 9 * (a + 1)].reshape(9 * channels, channels) for a in range(3)]
    window = cells[: size_z + 1].reshape((size_z + 1) * own, 9 * channels)
    both = matmul(window, jnp.concatenate(weights[:2], axis=1))
    window = cells[2:].reshape(size_z * own, 9 * channels)
    pre = both[:-own, :channels] + both[own:, channels:] + matmul(window, weights[2])
    sig = jax.nn.sigmoid(pre)
    slope[...] = (sig * (1.0 + pre * (1.0 - sig))).reshape(size_z, own, channels)
    hidden[...] = (pre * sig).astype(BF16).reshape(size_z, own, channels)
    parts = []
    for s in range(8):
        a, bc = s // 4, s % 4
        parts.append(
            jnp.concatenate(
                [hidden[2 * kz + a, bc * quarter : (bc + 1) * quarter, :] for kz in range(size_z // 2)], axis=0
            )
        )
    coarse = matmul(jnp.concatenate(parts, axis=1), w_down[...].reshape(8 * channels, w_down.shape[2]))
    coarse = coarse.astype(BF16)
    wide = coarse.shape[1]
    for send, back in zip(sends, backs):
        send[:, :wide] = coarse
        send[:, wide:] = back[...]


def rim_transpose_kernel(count_p, rim, taps_t, turned):
    planes, rows, channels = rim.shape
    share = channels // count_p
    for pair in range(planes // 2):
        sides = [rim[2 * pair + i].astype(F32).T for i in range(2)]
        moved = matmul(jnp.concatenate(sides, axis=1).astype(BF16), taps_t[...]).astype(BF16)
        for bc in range(9):
            for p in range(count_p):
                start = (bc * count_p // 2 + p // 2) * share
                turned[p % 2, start : start + share, pair * rows : (pair + 1) * rows] = moved[
                    p * share : (p + 1) * share, bc * rows : (bc + 1) * rows
                ]


def column_kernel(count_z, *refs):
    parts, picks, (column, back, x_send, send_a, send_b, corner_b) = refs[:count_z], refs[count_z], refs[count_z + 1 :]
    own_cells = parts[0].shape[0]
    wide = column.shape[1]
    pz = lax.axis_index("gz")
    for i, part in enumerate(parts):
        rows = pl.ds(pl.multiple_of((pz ^ (-i % count_z)) * own_cells, own_cells), own_cells)
        column[rows, :] = part[:, :wide]
        back[rows, :] = part[:, wide:]
    rims = matmul(picks[lax.axis_index("gx")], column[...]).astype(BF16)
    cuts, start = [], 0
    for size in (x_send.shape[0], *[send_a.shape[0]] * 2, *[corner_b.shape[0]] * 2):
        cuts.append(rims[start : start + size, :])
        start += size
    x_send[...] = cuts[0]
    send_b[...], send_a[...] = line_sides("gy", cuts[2], cuts[1])
    corner_b[...], _ = line_sides("gy", cuts[4], cuts[3])


def bottle_kernel(quarter, column, back, x_rim, relayed, shift, w_bottle, *refs):
    count = len(refs) // 2 - 1
    slices, bottle, sends, (corners, window) = refs[:count], refs[count], refs[count + 1 : -2], refs[-2:]
    cells, wide = column.shape
    outs = w_bottle.shape[2]
    side = x_rim.shape[0]
    depth = cells // quarter
    span = 4 * quarter
    picks = shift[lax.axis_index("gx")]
    window[:quarter, :] = jnp.zeros((quarter, 9 * wide), BF16)
    window[(depth + 1) * quarter :, :] = jnp.zeros((quarter, 9 * wide), BF16)
    edge = side // (depth // 4)
    y_low, y_high, xy_low, xy_high = y_rims(relayed, depth)
    y_low, y_high = y_low.astype(BF16), y_high.astype(BF16)
    for g in range(depth // 4):
        corners[g, :4, :] = xy_low[4 * g : 4 * g + 4, :]
        corners[g, 4:8, :] = xy_high[4 * g : 4 * g + 4, :]
        corners[g, 8:, :] = jnp.zeros((8, wide), F32)
        faces = [block[g * edge : (g + 1) * edge, :] for block in (x_rim, y_low, y_high)]
        rows = [column[g * span : (g + 1) * span, :], *faces, corners[g].astype(BF16)]
        moved = matmul(picks, jnp.concatenate(rows, axis=0)).astype(BF16)
        for bc in range(9):
            window[quarter + g * span : quarter + (g + 1) * span, bc * wide : (bc + 1) * wide] = moved[
                bc * span : (bc + 1) * span, :
            ]
    both = pre = None
    for bc in range(9):
        part = slice(bc * wide, (bc + 1) * wide)
        weight = jnp.concatenate([w_bottle[bc], w_bottle[9 + bc]], axis=1)
        term = matmul(window[: cells + quarter, part], weight)
        both = term if both is None else both + term
        term = matmul(window[2 * quarter :, part], w_bottle[18 + bc])
        pre = term if pre is None else pre + term
    pre = pre + both[:cells, :outs] + both[quarter:, outs:]
    sig = jax.nn.sigmoid(pre)
    bottle[...] = (pre * sig).astype(BF16)
    slope = sig * (1.0 + pre * (1.0 - sig))
    value = (back[...].astype(F32) * slope).astype(BF16)
    for send, block in zip(sends, slices):
        send[:cells, :] = value
        send[cells:, :] = block[...]


def slices_kernel(count_y, quarter, column, *refs):
    sends, slices = refs[:-1], refs[-1]
    cells, wide = column.shape
    span = 4 * quarter
    half = 2 * quarter
    lane = lax.broadcasted_iota(jnp.int32, (half, 128), 1)
    for pair in range(wide // 128):
        for g in range(cells // span):
            top = column[g * span : g * span + half, pair * 128 : (pair + 1) * 128].astype(F32)
            end = column[g * span + half : (g + 1) * span, pair * 128 : (pair + 1) * 128].astype(F32)
            rows = slice(g * half, (g + 1) * half)
            slices[2 * pair, rows, :] = jnp.where(lane < 64, top, pltpu.roll(end, 64, 1)).astype(BF16)
            slices[2 * pair + 1, rows, :] = jnp.where(lane < 64, pltpu.roll(top, 64, 1), end).astype(BF16)
    p = plane_index(count_y)
    lines = slices.shape[1]
    for i, send in enumerate(sends):
        send[:lines, :] = slices[p ^ (2 * i)]
        send[lines:, :] = slices[p ^ (2 * i + 1)]


def coarse_grad_kernel(count_y, count_z, quarter, *refs):
    grads, (bottle, shift, w_bottle) = refs[: -count_z - 6], refs[-count_z - 6 : -count_z - 3]
    sends, (window, gathered, blocks) = refs[-count_z - 3 : -3], refs[-3:]
    count_p = len(grads)
    cells, outs = bottle.shape
    rows = count_p * quarter
    depth = cells // quarter
    own_cells = cells // count_z
    inputs = w_bottle.shape[1]
    p = plane_index(count_y)
    for i, part in enumerate(grads):
        gathered[p ^ (-i % count_p)] = part[:cells, :]
    mine = pl.multiple_of(p * quarter, quarter)
    picks = jnp.concatenate([shift[pl.ds((8 - bc) * rows + mine, quarter), :] for bc in range(9)], axis=0)
    window[:quarter, :] = jnp.zeros((quarter, 9 * outs), BF16)
    window[(depth + 1) * quarter :, :] = jnp.zeros((quarter, 9 * outs), BF16)
    for z in range(depth):
        plane = jnp.concatenate([gathered[q, z * quarter : (z + 1) * quarter, :] for q in range(count_p)], axis=0)
        moved = matmul(picks, plane).astype(BF16)
        for bc in range(9):
            window[(z + 1) * quarter : (z + 2) * quarter, bc * outs : (bc + 1) * outs] = moved[
                bc * quarter : (bc + 1) * quarter, :
            ]
    total = None
    for a in range(3):
        weight = jnp.concatenate([w_bottle[9 * a + bc] for bc in range(9)], axis=1)
        term = matmul_nt(window[(2 - a) * quarter : (2 - a + depth) * quarter, :], weight)
        total = term if total is None else total + term
    total = total.astype(BF16)
    for q in range(count_z):
        blocks[q, :, :inputs] = total[q * own_cells : (q + 1) * own_cells, :]
        blocks[q, :, inputs:] = bottle[q * own_cells : (q + 1) * own_cells, :]
    hand_out(blocks, sends, lax.axis_index("gz"))


def wide_kernel(count_y, quarter, *refs):
    parts, (wide, grads) = refs[:-2], refs[-2:]
    count_p, cells, outs = grads.shape
    rows = count_p * quarter
    depth = cells // quarter
    take_in([part.at[:cells, :] for part in parts], grads, plane_index(count_y))
    planes = [
        jnp.concatenate([grads[q, z * quarter : (z + 1) * quarter, :] for q in range(count_p)], axis=0)
        for z in range(depth)
    ]
    zeros = jnp.zeros((rows, outs), BF16)
    for j in range(depth // 2):
        for slot in range(5):
            z = j // 2 * 4 + j % 2 + slot - 1
            wide[j * rows : (j + 1) * rows, slot * outs : (slot + 1) * outs] = planes[z] if 0 <= z < depth else zeros


def coarse_transpose_kernel(count_y, shift, *refs):
    parts, (turned, slices) = refs[:-2], refs[-2:]
    count_p, lines, _ = slices.shape
    rows = shift.shape[1]
    quarter = rows // count_p
    p = plane_index(count_y)
    for d, part in enumerate(parts):
        start = (2 + d % 2) * lines
        slices[p ^ d] = part[start : start + lines, :]
    for j in range(lines // quarter):
        plane = jnp.concatenate([slices[q, j * quarter : (j + 1) * quarter, :] for q in range(count_p)], axis=0)
        plane = plane.astype(F32).T.astype(BF16)
        for bc in range(9):
            turned[bc * 128 : (bc + 1) * 128, j * rows : (j + 1) * rows] = matmul(
                plane, shift[(8 - bc) * rows : (9 - bc) * rows, :]
            ).astype(BF16)


def grad_bottle_kernel(turned, wide, out):
    _, channels, outs = out.shape
    full = matmul(turned[...], wide[...])
    for bc in range(9):
        top = full[bc * 128 : bc * 128 + channels, :]
        end = full[bc * 128 + channels : (bc + 1) * 128, :]
        for a in range(3):
            out[9 * a + bc] = top[:, (2 - a) * outs : (3 - a) * outs] + end[:, (4 - a) * outs : (5 - a) * outs]


def half_grad(turned, shifted, parity, chip, out, blocks):
    chips, rows, channels = blocks.shape
    group = rows // 27
    full = matmul(turned[parity], shifted[...])
    for bc in range(9):
        for a in range(3):
            t = 9 * a + bc
            for q in range(chips):
                start = (bc * chips + q) * group
                blocks[q, t * group : (t + 1) * group, :] = full[
                    start : start + group, a * channels : (a + 1) * channels
                ].astype(BF16)
    for i in range(chips):
        out[i] = blocks[chip ^ i]


def hidden_grad_kernel(count_y, count_z, *refs):
    parts, (slope, ordered, w_down, turned) = refs[:count_z], refs[count_z : count_z + 4]
    shifted, bottle, give, bottles, blocks = refs[count_z + 4 :]
    size_z, own, channels = ordered.shape
    quarter = own // 4
    inputs = w_down.shape[2]
    pz = lax.axis_index("gz")
    grad = total_of([part.at[:, :inputs] for part in parts]).astype(BF16)
    for i, part in enumerate(parts):
        bottles[pz ^ (-i % count_z)] = part[:, inputs:]
    bottle[...] = jnp.concatenate([bottles[q] for q in range(count_z)], axis=1)
    shifted[...] = jnp.zeros_like(shifted)
    for s in range(8):
        a, bc = s // 4, s % 4
        spread_grad = matmul_nt(grad, w_down[s])
        for kz in range(size_z // 2):
            z = 2 * kz + a
            part = slice(bc * quarter, (bc + 1) * quarter)
            line = slice(kz * quarter, (kz + 1) * quarter)
            value = ((spread_grad[line, :] + ordered[z, part, :].astype(F32)) * slope[z, part, :]).astype(BF16)
            for t in range(3):
                start = (z + t) * own + bc * quarter
                shifted[start : start + quarter, t * channels : (t + 1) * channels] = value
    p = plane_index(count_y)
    half_grad(turned, shifted, 1 - p % 2, p // 2, give, blocks)


def keep_kernel(count_y, shifted, turned, keep, blocks):
    p = plane_index(count_y)
    half_grad(turned, shifted, p % 2, p // 2, keep, blocks)


def output_kernel(bottle, hidden, w_up, order_t, output, rows_out):
    size_z, own, channels = hidden.shape
    quarter = own // 4
    for s in range(8):
        a, bc = s // 4, s % 4
        lifted = matmul(bottle[...], w_up[s])
        for kz in range(size_z // 2):
            z = 2 * kz + a
            part = slice(bc * quarter, (bc + 1) * quarter)
            line = slice(kz * quarter, (kz + 1) * quarter)
            rows_out[z, part, :] = (lifted[line, :] + hidden[z, part, :].astype(F32)).astype(BF16)
    for z in range(size_z):
        plane = matmul(order_t[...], rows_out[z])
        output[z] = plane.reshape(output.shape[1:]).astype(BF16)


def pair_sum_kernel(keep, got, *sends):
    for i, send in enumerate(sends):
        send[...] = (keep[i].astype(F32) + got[i].astype(F32)).astype(BF16)


def sum_kernel(*refs):
    out = refs[-1]
    out[...] = total_of(refs[:-1]).reshape(out.shape).astype(out.dtype)


def shape_of(shape, dtype=BF16):
    return jax.ShapeDtypeStruct(shape, dtype)


def gathered_body(counts, volume, cotangent, w_conv, w_down, w_bottle, w_up):
    count_x, count_y, count_z = counts
    count_p = count_x * count_y
    size_z, size_x, size_y, channels = volume.shape
    wide = w_down.shape[2]
    group = w_bottle.shape[2]
    half_x, half_y = size_x // 2, size_y // 2
    own = size_x * size_y
    quarter = half_x * half_y
    own_cells = size_z // 2 * quarter
    cells = count_z * own_cells
    depth = count_z * size_z // 2
    rows = count_p * quarter
    planes = size_z + 2
    share_c = channels // count_p
    share_w = wide // count_p
    plane_axes = ("gx", "gy")

    order, taps = fine_maps(size_x, size_y)
    pair_taps = np.zeros((2, 2 * own, 9, 2, own), np.float32)
    for i in range(2):
        pair_taps[i, :, :, i, :] = taps.transpose(2, 0, 1)
    shift = coarse_maps(count_x, count_y, half_x, half_y)
    order_m = jnp.asarray(order, BF16)
    order_t = jnp.asarray(order.T, BF16)
    taps_m = jnp.asarray(taps.reshape(9 * own, 2 * own), BF16)
    taps_t = jnp.asarray(pair_taps.reshape(4 * own, 18 * own), BF16)
    shift_m = jnp.asarray(shift.reshape(9 * rows, rows), BF16)

    send_maps, rim_maps = column_maps(half_x, half_y, depth)
    send_m = jnp.asarray(send_maps, BF16)
    rim_m = jnp.asarray(rim_maps.reshape(count_x, 36 * quarter, 8 * quarter), BF16)

    w_conv_t = jnp.transpose(w_conv, (1, 0, 2))
    w_bottle_t = jnp.transpose(w_bottle, (1, 0, 2))
    send_a, send_b = local_call(ends_kernel, "ends", [shape_of((size_x, size_y, channels))] * 2)(volume)
    z_pairs = line_pairs(count_z)
    z_b = lax.ppermute(send_b, "gz", z_pairs[1])
    z_a = lax.ppermute(send_a, "gz", z_pairs[0])
    *backs, ordered = local_call(
        lambda *refs: back_kernel(count_z, *refs),
        "back",
        [shape_of((own_cells, group))] * count_z + [shape_of((size_z, own, channels))],
        [pltpu.VMEM((count_z, own_cells, group), BF16)],
    )(cotangent, w_up, order_m)
    sends = local_call(
        faces_kernel,
        "faces",
        [shape_of((16 * size_y, channels))] + [shape_of((planes * size_x, channels))] * 2 + [shape_of((16, channels))],
        [pltpu.VMEM((16 * own, channels), F32)],
    )(volume, z_a, z_b)
    x_send, send_a, send_b, corner_b = sends
    x_rim, across, corner = swap_rims(x_send, send_b, corner_b, counts)
    relayed = relay_rims(x_rim, across, corner, send_a, counts)
    hidden, slope, rim, *sends = local_call(
        lambda *refs: hidden_kernel(count_z, *refs),
        "hidden",
        [
            shape_of((size_z, own, channels)),
            shape_of((size_z, own, channels), F32),
            shape_of((planes, 2 * own, channels)),
        ]
        + [shape_of((own_cells, wide + group))] * count_z,
        [
            pltpu.VMEM((planes * 2 * own, channels), F32),
            pltpu.VMEM((planes, own, 9 * channels), BF16),
        ],
        flops=2_000_000_000,
    )(volume, z_a, z_b, x_rim, relayed, taps_m, w_conv_t, w_down, *backs)
    parts = trade(sends, "gz", count_z)
    column, back, *sends = local_call(
        lambda *refs: column_kernel(count_z, *refs),
        "column",
        [shape_of((cells, wide)), shape_of((cells, group)), shape_of((depth * half_y, wide))]
        + [shape_of((depth * half_x, wide))] * 2
        + [shape_of((depth, wide))],
    )(parts[0], *parts[:0:-1], send_m)
    x_send, send_a, send_b, corner_b = sends
    x_rim, across, corner = swap_rims(x_send, send_b, corner_b, counts)
    relayed = relay_rims(x_rim, across, corner, send_a, counts)
    slices = local_call(
        lambda *refs: slices_kernel(count_y, quarter, *refs),
        "slices",
        [shape_of((cells, 128))] * (count_p // 2),
        [pltpu.VMEM((count_p, cells // 2, 128), BF16)],
    )(column)
    column, *slices = lax.optimization_barrier((column, *slices))
    bottle, *sends = local_call(
        lambda *refs: bottle_kernel(quarter, *refs),
        "bottle",
        [shape_of((cells, group))] + [shape_of((2 * cells, group))] * (count_p // 2),
        [
            pltpu.VMEM((depth // 4, 16, wide), F32),
            pltpu.VMEM(((depth + 2) * quarter, 9 * wide), BF16),
        ],
        flops=2_000_000_000,
    )(column, back, x_rim, relayed, rim_m, w_bottle_t, *slices)
    grads = [None] * count_p
    grads[0] = sends[0]
    for d in (6, 4, 2):
        grads[d] = swap(sends[d // 2], plane_axes, count_p, d)
    for d in (0, 2, 4, 6):
        grads[d + 1] = swap(grads[d], plane_axes, count_p, 1)
    sends = local_call(
        lambda *refs: coarse_grad_kernel(count_y, count_z, quarter, *refs),
        "coarse_grad",
        [shape_of((own_cells, wide + group))] * count_z,
        [
            pltpu.VMEM(((depth + 2) * quarter, 9 * group), BF16),
            pltpu.VMEM((count_p, cells, group), BF16),
            pltpu.VMEM((count_z, own_cells, wide + group), BF16),
        ],
    )(grads[0], *grads[:0:-1], bottle, shift_m, w_bottle_t)
    parts = trade(sends, "gz", count_z)
    rim, late, _ = lax.optimization_barrier((rim, grads[0], sends[1]))
    turned = local_call(
        lambda *refs: rim_transpose_kernel(count_p, *refs),
        "rim_transpose",
        shape_of((2, 9 * channels // 2, planes * own)),
    )(rim, taps_t)
    coarse_turned = local_call(
        lambda *refs: coarse_transpose_kernel(count_y, *refs),
        "coarse_transpose",
        shape_of((18 * share_w, depth // 2 * rows)),
        [pltpu.VMEM((count_p, cells // 2, 128), BF16)],
    )(shift_m, late, *grads[1:])
    turned, coarse_turned = lax.optimization_barrier((turned, coarse_turned))
    shifted, bottle, give = local_call(
        lambda *refs: hidden_grad_kernel(count_y, count_z, *refs),
        "hidden_grad",
        [
            shape_of((planes * own, 3 * channels)),
            shape_of((own_cells, wide)),
            shape_of((count_p // 2, 27 * share_c, channels)),
        ],
        [
            pltpu.VMEM((count_z, own_cells, group), BF16),
            pltpu.VMEM((count_p // 2, 27 * share_c, channels), BF16),
        ],
    )(parts[0], *parts[:0:-1], slope, ordered, w_down, turned)
    got = swap(give, plane_axes, count_p, 1)
    keep = local_call(
        lambda *refs: keep_kernel(count_y, *refs),
        "keep",
        shape_of((count_p // 2, 27 * share_c, channels)),
        [pltpu.VMEM((count_p // 2, 27 * share_c, channels), BF16)],
    )(shifted, turned)
    output = local_call(
        output_kernel,
        "output",
        shape_of(volume.shape),
        [pltpu.VMEM((size_z, own, channels), BF16)],
    )(bottle, hidden, w_up, order_t)
    sends = local_call(
        pair_sum_kernel,
        "pair_sum",
        [shape_of((27 * share_c, channels))] * (count_p // 2),
    )(keep, got)
    parts = [sends[0]] + [swap(sends[d // 2], plane_axes, count_p, d) for d in (6, 4, 2)]
    part = local_call(sum_kernel, "plane_sum", shape_of((27 * share_c, channels)))(*parts)
    part, output = lax.optimization_barrier((part, output))
    got = swap(part, "gz", count_z, 1)
    wide_grads = local_call(
        lambda *refs: wide_kernel(count_y, quarter, *refs),
        "wide",
        shape_of((depth // 2 * rows, 5 * group)),
        [pltpu.VMEM((count_p, cells, group), BF16)],
    )(*grads)
    got, wide_grads = lax.optimization_barrier((got, wide_grads))
    part = local_call(sum_kernel, "depth_sum", shape_of((27 * share_c, channels)))(part, got)
    got = swap(part, "gz", count_z, 2)
    grad_bottle = local_call(
        grad_bottle_kernel,
        "grad_bottle",
        shape_of((27, share_w, group), F32),
        flops=4_000_000_000,
    )(coarse_turned, wide_grads)
    grad_conv = local_call(
        sum_kernel,
        "grad_conv",
        shape_of((27, share_c, channels), F32),
    )(part, got)
    return (output, jnp.transpose(grad_conv, (1, 0, 2)), jnp.transpose(grad_bottle, (1, 0, 2)))


def with_halo(cells, sides, width):
    for axis, dim in sides:
        count = lax.axis_size(axis)
        ends = count - 1
        head = lax.slice_in_dim(cells, 0, width, axis=dim)
        tail = lax.slice_in_dim(cells, cells.shape[dim] - width, cells.shape[dim], axis=dim)
        cells = jnp.concatenate(
            [
                lax.ppermute(tail, axis, [(i, (i + 1) % count) for i in range(ends)]),
                cells,
                lax.ppermute(head, axis, [((i + 1) % count, i) for i in range(ends)]),
            ],
            axis=dim,
        )
    return cells


def silu_slope(values):
    sig = jax.nn.sigmoid(values)
    return sig * (1.0 + values * (1.0 - sig))


def conv_forward(padded, weight, extent):
    size_z, size_x, size_y = extent
    count_cells = size_z * size_x * size_y
    summed = jnp.zeros((count_cells, weight.shape[2]), jnp.float32)
    for tap_index in range(27):
        shift_z, shift_x, shift_y = (tap_index // 9, tap_index // 3 % 3, tap_index % 3)
        window = padded[
            shift_z : shift_z + size_z, shift_x : shift_x + size_x, shift_y : shift_y + size_y, :
        ]
        window = window.reshape(count_cells, padded.shape[3])
        summed = summed + jnp.dot(
            window, weight[:, tap_index, :], preferred_element_type=jnp.float32
        )
    return summed.reshape(size_z, size_x, size_y, weight.shape[2])


def conv_weight_grad(padded, gradient, extent):
    size_z, size_x, size_y = extent
    count_cells = size_z * size_x * size_y
    flat_gradient = gradient.reshape(count_cells, gradient.shape[3])
    pieces = []
    for tap_index in range(27):
        shift_z, shift_x, shift_y = (tap_index // 9, tap_index // 3 % 3, tap_index % 3)
        window = padded[
            shift_z : shift_z + size_z, shift_x : shift_x + size_x, shift_y : shift_y + size_y, :
        ]
        window = window.reshape(count_cells, padded.shape[3])
        pieces.append(
            lax.dot_general(
                window, flat_gradient, (((0,), (0,)), ((), ())), preferred_element_type=jnp.float32
            )
        )
    return jnp.stack(pieces, axis=1)


def conv_input_grad(padded, weight, extent):
    size_z, size_x, size_y = extent
    count_cells = size_z * size_x * size_y
    summed = jnp.zeros((count_cells, weight.shape[0]), jnp.float32)
    for tap_index in range(27):
        shift_z, shift_x, shift_y = (2 - tap_index // 9, 2 - tap_index // 3 % 3, 2 - tap_index % 3)
        window = padded[
            shift_z : shift_z + size_z, shift_x : shift_x + size_x, shift_y : shift_y + size_y, :
        ]
        window = window.reshape(count_cells, padded.shape[3])
        summed = summed + lax.dot_general(
            window,
            weight[:, tap_index, :],
            (((1,), (1,)), ((), ())),
            preferred_element_type=jnp.float32,
        )
    return summed.reshape(size_z, size_x, size_y, weight.shape[0])


def pool_features(fine, kernel):
    size_z, size_x, size_y, channels = fine.shape
    blocks = fine.reshape(size_z // 2, 2, size_x // 2, 2, size_y // 2, 2, channels)
    kernel_cube = kernel.reshape(2, 2, 2, kernel.shape[1], kernel.shape[2])
    return jnp.einsum(
        "zaxbycf,abcfg->zxyg", blocks, kernel_cube, preferred_element_type=jnp.float32
    )


def pool_adjoint(coarse_in, kernel):
    size_z, size_x, size_y, wide_channels = coarse_in.shape
    kernel_cube = kernel.reshape(2, 2, 2, kernel.shape[1], kernel.shape[2])
    result = jnp.einsum(
        "zxyg,abcfg->zaxbycf", coarse_in, kernel_cube, preferred_element_type=jnp.float32
    )
    return result.reshape(2 * size_z, 2 * size_x, 2 * size_y, kernel.shape[1])


def lift_features(coarse_in, kernel):
    size_z, size_x, size_y, wide_channels = coarse_in.shape
    kernel_cube = kernel.reshape(2, 2, 2, kernel.shape[1], kernel.shape[2])
    result = jnp.einsum(
        "zxyg,abcgf->zaxbycf", coarse_in, kernel_cube, preferred_element_type=jnp.float32
    )
    return result.reshape(2 * size_z, 2 * size_x, 2 * size_y, kernel.shape[2])


def lift_adjoint(fine, kernel):
    size_z, size_x, size_y, channels = fine.shape
    blocks = fine.reshape(size_z // 2, 2, size_x // 2, 2, size_y // 2, 2, channels)
    kernel_cube = kernel.reshape(2, 2, 2, kernel.shape[1], kernel.shape[2])
    return jnp.einsum(
        "zaxbycf,abcgf->zxyg", blocks, kernel_cube, preferred_element_type=jnp.float32
    )


def column_body(volume, cotangent, w_conv, w_down, w_bottle, w_up):
    size_z, size_x, size_y, channels = volume.shape
    group_channels = w_bottle.shape[2]
    half_x = size_x // 2
    half_y = size_y // 2
    padded = with_halo(volume, (("gx", 1), ("gy", 2), ("gz", 0)), 1)
    pre_hidden = conv_forward(padded, w_conv, (size_z, size_x, size_y))
    hidden = jax.nn.silu(pre_hidden).astype(jnp.bfloat16)
    hidden_slope = silu_slope(pre_hidden)
    coarse = pool_features(hidden, w_down).astype(jnp.bfloat16)
    stacked = lax.all_gather(coarse, "gz", axis=0, tiled=True)
    rimmed = with_halo(stacked, (("gx", 1), ("gy", 2)), 1)
    column_z = rimmed.shape[0]
    coarse_pad = jnp.pad(rimmed, ((1, 1), (0, 0), (0, 0), (0, 0)))
    pre_bottle = conv_forward(coarse_pad, w_bottle, (column_z, half_x, half_y))
    bottle = jax.nn.silu(pre_bottle).astype(jnp.bfloat16)
    bottle_slope = silu_slope(pre_bottle)
    own_start = lax.axis_index("gz") * group_channels
    own_up = lax.dynamic_slice_in_dim(w_up, own_start, group_channels, 1)
    lifted = lax.psum_scatter(
        lift_features(bottle, own_up).astype(jnp.bfloat16), "gz", scatter_dimension=0, tiled=True
    ).astype(jnp.float32)
    output = (lifted + hidden.astype(jnp.float32)).astype(jnp.bfloat16)
    back_bottle = lift_adjoint(cotangent, w_up).astype(jnp.bfloat16)
    split_grad = lax.all_to_all(back_bottle, "gz", split_axis=3, concat_axis=0, tiled=True)
    bottle_grad = (split_grad.astype(jnp.float32) * bottle_slope).astype(jnp.bfloat16)
    grad_bottle = lax.psum_scatter(
        conv_weight_grad(coarse_pad, bottle_grad, (column_z, half_x, half_y)),
        ("gx", "gy"),
        scatter_dimension=0,
        tiled=True,
    )
    grad_rimmed = with_halo(bottle_grad, (("gx", 1), ("gy", 2)), 1)
    grad_pad = jnp.pad(grad_rimmed, ((1, 1), (0, 0), (0, 0), (0, 0)))
    coarse_grad = lax.psum_scatter(
        conv_input_grad(
            grad_pad, w_bottle, (lax.axis_size("gz") * (size_z // 2), half_x, half_y)
        ).astype(jnp.bfloat16),
        "gz",
        scatter_dimension=0,
        tiled=True,
    )
    hidden_grad = (
        (pool_adjoint(coarse_grad, w_down) + cotangent.astype(jnp.float32)) * hidden_slope
    ).astype(jnp.bfloat16)
    full_term = conv_weight_grad(padded, hidden_grad, (size_z, size_x, size_y))
    depth_summed = lax.psum(full_term.astype(jnp.bfloat16), "gz").astype(jnp.float32)
    grad_conv = lax.psum_scatter(depth_summed, ("gx", "gy"), scatter_dimension=0, tiled=True)
    return (output, grad_conv, grad_bottle)


def fits_one_plane(counts, brick, wide):
    count_p = counts[0] * counts[1]
    size_z, size_x, size_y, channels = brick
    return (
        counts == (2, 4, 4)
        and count_p * (size_x // 2) * (size_y // 2) == 128
        and wide // count_p == 64
        and (size_z, size_x, size_y, channels) == (8, 8, 8, 128)
    )


def solution(mesh):
    in_specs = (
        P("gz", "gx", "gy", None),
        P("gz", "gx", "gy", None),
        P(),
        P(),
        P(None, None, "gz"),
        P(),
    )
    out_specs = (
        P("gz", "gx", "gy", None),
        P(("gx", "gy"), None, None),
        P(("gx", "gy"), None, "gz"),
    )
    counts = (mesh.shape["gx"], mesh.shape["gy"], mesh.shape["gz"])

    def body(volume, cotangent, w_conv, w_down, w_bottle, w_up):
        if fits_one_plane(counts, volume.shape, w_down.shape[2]):
            return gathered_body(counts, volume, cotangent, w_conv, w_down, w_bottle, w_up)
        return column_body(volume, cotangent, w_conv, w_down, w_bottle, w_up)

    return jax.shard_map(body, mesh=mesh, in_specs=in_specs, out_specs=out_specs, check_vma=False)
```

```python
import numpy as np
import jax
import jax.numpy as jnp
from jax import lax
from jax.experimental import pallas as pl
from jax.experimental.pallas import tpu as pltpu
from jax.sharding import PartitionSpec as P

BF16 = jnp.bfloat16
F32 = jnp.float32
VMEM_LIMIT = 24 * 1024 * 1024


def local_call(kernel, name, out_shapes, scratch=(), flops=300_000_000):
    whole = pl.BlockSpec(memory_space=pltpu.VMEM)

    def call(*operands):
        return pl.pallas_call(
            kernel,
            name=name,
            out_shape=out_shapes,
            in_specs=[whole] * len(operands),
            out_specs=jax.tree.map(lambda _: whole, out_shapes),
            scratch_shapes=list(scratch),
            compiler_params=pltpu.CompilerParams(vmem_limit_bytes=VMEM_LIMIT),
            cost_estimate=pl.CostEstimate(flops=flops, bytes_accessed=flops // 1000, transcendentals=0),
        )(*operands)

    return call


def matmul(left, right):
    return jnp.dot(left, right, preferred_element_type=F32)


def matmul_nt(left, right):
    return lax.dot_general(left, right, (((1,), (1,)), ((), ())), preferred_element_type=F32)


def sub_order(size_x, size_y):
    half_x, half_y = size_x // 2, size_y // 2
    return {
        (2 * kx + b, 2 * ky + c): ((2 * b + c) * half_x + kx) * half_y + ky
        for b in range(2)
        for c in range(2)
        for kx in range(half_x)
        for ky in range(half_y)
    }


def fine_maps(size_x, size_y):
    own = size_x * size_y
    rows = sub_order(size_x, size_y)
    order = np.zeros((own, own), np.float32)
    taps = np.zeros((9, own, 2 * own), np.float32)
    for (x, y), row in rows.items():
        order[row, x * size_y + y] = 1
        for b in range(3):
            for c in range(3):
                sx, sy = x + b - 1, y + c - 1
                if sx < 0:
                    part = 0 if 0 <= sy < size_y else (4 if sy < 0 else 5)
                    source = own + 8 * part + sy % size_y
                elif sx >= size_x:
                    part = 1 if 0 <= sy < size_y else (6 if sy < 0 else 7)
                    source = own + 8 * part + sy % size_y
                elif sy < 0:
                    source = own + 16 + sx
                elif sy >= size_y:
                    source = own + 24 + sx
                else:
                    source = sx * size_y + sy
                taps[3 * b + c, row, source] = 1
    return order, taps


def coarse_maps(count_x, count_y, half_x, half_y):
    wide_x, wide_y = count_x * half_x, count_y * half_y

    def row_of(x, y):
        brick = (x // half_x) * count_y + y // half_y
        return (brick * half_x + x % half_x) * half_y + y % half_y

    shift = np.zeros((9, wide_x * wide_y, wide_x * wide_y), np.float32)
    for x in range(wide_x):
        for y in range(wide_y):
            for b in range(3):
                for c in range(3):
                    sx, sy = x + b - 1, y + c - 1
                    if 0 <= sx < wide_x and 0 <= sy < wide_y:
                        shift[3 * b + c, row_of(x, y), row_of(sx, sy)] = 1
    return shift


def column_maps(half_x, half_y, depth):
    quarter = half_x * half_y
    rows = depth * quarter
    send = np.zeros((2, depth * (half_y + 2 * half_x + 2), rows), np.float32)
    rim = np.zeros((2, 9, 4, quarter, 8 * quarter), np.float32)
    for px in range(2):
        edge = 0 if px else half_x - 1
        for z in range(depth):
            base = z * quarter
            for ky in range(half_y):
                send[px, z * half_y + ky, base + edge * half_y + ky] = 1
            for side, ky in enumerate((0, half_y - 1)):
                row = depth * (half_y + side * half_x) + z * half_x
                for kx in range(half_x):
                    send[px, row + kx, base + kx * half_y + ky] = 1
                send[px, depth * (half_y + 2 * half_x + side) + z, base + edge * half_y + ky] = 1
    for px in range(2):
        for b in range(3):
            for c in range(3):
                for kx in range(half_x):
                    for ky in range(half_y):
                        sx, sy = kx + b - 1, ky + c - 1
                        beyond = sx < 0 if px else sx >= half_x
                        if (sx < 0 or sx >= half_x) and not beyond:
                            continue
                        for z in range(4):
                            if beyond and 0 <= sy < half_y:
                                source = 4 * quarter + z * half_y + sy
                            elif beyond:
                                source = 7 * quarter + 4 * (sy >= half_y) + z
                            elif sy < 0:
                                source = 5 * quarter + z * half_x + sx
                            elif sy >= half_y:
                                source = 6 * quarter + z * half_x + sx
                            else:
                                source = z * quarter + sx * half_y + sy
                            rim[px, 3 * b + c, z, kx * half_y + ky, source] = 1
    return send, rim


def swap(block, axes, count, distance):
    return lax.ppermute(block, axes, [(i, i ^ distance) for i in range(count)])


def trade(blocks, axes, count):
    got = {d: swap(blocks[d], axes, count, d) for d in reversed(range(1, count))}
    return [blocks[0]] + [got[d] for d in range(1, count)]


def line_pairs(length):
    first = [(i, i ^ 1) for i in range(length)]
    second = [(i, i + 1 if i % 2 else i - 1) for i in range(1, length - 1)]
    return first, second


def swap_rims(x_send, send_b, corner_b, counts):
    count_x, count_y, _ = counts
    axes, count = ("gx", "gy"), count_x * count_y
    corner = swap(corner_b, axes, count, count_y + 2)
    x_rim = swap(x_send, axes, count, count_y)
    across = swap(send_b, axes, count, 2)
    return x_rim, across, corner


def line_sides(axis, pair_a, pair_b):
    even = lax.axis_index(axis) % 2 == 0
    return jnp.where(even, pair_b, pair_a), jnp.where(even, pair_a, pair_b)


def relay_rims_kernel(corner, across, x_rim, send_a, send, side):
    face, lines = across.shape[0], corner.shape[0]
    pitch = x_rim.shape[0] // lines
    even = lax.axis_index("gy") % 2 == 0
    for part in range(0, x_rim.shape[1], 128):
        columns = slice(part, part + 128)
        side[...] = x_rim[:, columns].astype(F32)
        ends = [side[pl.ds(y, lines, stride=pitch), :] for y in (pitch - 1, 0)]
        send[face + lines : face + 2 * lines, columns] = jnp.where(even, ends[0], ends[1]).astype(BF16)
    send[face + 2 * lines :, :] = send_a[...]
    send[:face, :] = across[...]
    send[face : face + lines, :] = corner[...]


def pass_kernel(block, out):
    out[...] = block[...]


def relay_rims(x_rim, across, corner, send_a, counts):
    rows = 2 * (across.shape[0] + corner.shape[0])
    corner = local_call(pass_kernel, "corner", shape_of(corner.shape), flops=5_000_000_000)(corner)
    send = local_call(
        relay_rims_kernel,
        "relay_rims",
        shape_of((rows, across.shape[1])),
        [pltpu.VMEM((x_rim.shape[0], 128), F32)],
    )(corner, across, x_rim, send_a)
    return swap(send, ("gx", "gy"), counts[0] * counts[1], 1)


def y_rims(relayed, lines):
    py = lax.axis_index("gy")
    face = relayed.shape[0] // 2 - lines
    inner = (py > 0) & (py < lax.axis_size("gy") - 1)
    face_b = jnp.where(inner, relayed[:face, :].astype(F32), 0.0)
    corner_b = jnp.where(inner, relayed[face : face + lines, :].astype(F32), 0.0)
    corner_a = relayed[face + lines : face + 2 * lines, :].astype(F32)
    face_a = relayed[face + 2 * lines :, :].astype(F32)
    return *line_sides("gy", face_a, face_b), *line_sides("gy", corner_a, corner_b)


def plane_index(count_y):
    return lax.axis_index("gx") * count_y + lax.axis_index("gy")


def plane_rows(ref, z):
    _, size_x, size_y, channels = ref.shape
    return ref[z].astype(F32).reshape(size_x * size_y, channels)


def hand_out(blocks, outs, me):
    for d, out in enumerate(outs):
        out[...] = blocks[me ^ d]


def take_in(parts, blocks, me):
    for d, part in enumerate(parts):
        blocks[me ^ d] = part[...]


def total_of(parts):
    terms = [part[...].astype(F32) for part in parts]
    while len(terms) > 1:
        terms = [terms[i] + terms[i + 1] for i in range(0, len(terms), 2)]
    return terms[0]


def back_kernel(count_z, cotangent, w_up, order, *refs):
    sends, (ordered, blocks) = refs[:count_z], refs[count_z:]
    size_z, size_x, size_y, channels = cotangent.shape
    own = size_x * size_y
    quarter = own // 4
    for z in range(size_z):
        ordered[z] = matmul(order[...], plane_rows(cotangent, z).astype(BF16)).astype(BF16)
    back = None
    for s in range(8):
        a, bc = s // 4, s % 4
        cells = jnp.concatenate(
            [ordered[2 * kz + a, bc * quarter : (bc + 1) * quarter, :] for kz in range(size_z // 2)], axis=0
        )
        term = matmul_nt(cells, w_up[s])
        back = term if back is None else back + term
    back = back.astype(BF16)
    group = back.shape[1] // count_z
    for q in range(count_z):
        blocks[q] = back[:, q * group : (q + 1) * group]
    hand_out(blocks, sends, lax.axis_index("gz"))


def deepen(volume, z_a, z_b, deep, pitch):
    size_z, size_x, size_y, channels = volume.shape
    own = size_x * size_y
    below, above = line_sides("gz", z_a[...], z_b[...])
    deep[:own, :] = below.astype(F32).reshape(own, channels)
    for z in range(size_z):
        deep[(z + 1) * pitch : (z + 1) * pitch + own, :] = plane_rows(volume, z)
    deep[(size_z + 1) * pitch : (size_z + 1) * pitch + own, :] = above.astype(F32).reshape(own, channels)


def ends_kernel(volume, send_a, send_b):
    below, above = volume[0], volume[volume.shape[0] - 1]
    send_b[...], send_a[...] = line_sides("gz", above, below)


def faces_kernel(volume, z_a, z_b, x_send, send_a, send_b, corner_b, deep):
    size_z, size_x, size_y, channels = volume.shape
    own = size_x * size_y
    planes = x_send.shape[0] // size_y
    deepen(volume, z_a, z_b, deep, own)
    start = (size_z + 2) * own
    deep[start:, :] = jnp.zeros((deep.shape[0] - start, channels), F32)
    first = lax.axis_index("gx") == 0
    far = (size_x - 1) * size_y

    def x_face(start):
        return jnp.concatenate([deep[z * own + start : z * own + start + size_y, :] for z in range(planes)], axis=0)

    x_send[...] = jnp.where(first, x_face(far), x_face(0)).astype(BF16)
    faces, corners = [], []
    for y in (0, size_y - 1):
        faces.append(deep[pl.ds(y, send_a.shape[0], stride=size_y), :].astype(BF16))
        ends = [deep[pl.ds(start + y, planes, stride=own), :] for start in (far, 0)]
        corners.append(jnp.where(first, ends[0], ends[1]).astype(BF16))
    send_b[...], send_a[...] = line_sides("gy", faces[1], faces[0])
    corner_b[...], _ = line_sides("gy", corners[1], corners[0])


def hidden_kernel(count_z, volume, z_a, z_b, x_rim, relayed, taps, w_conv, w_down, *refs):
    backs, (hidden, slope, rim), sends, (rim32, cells) = (
        refs[:count_z],
        refs[count_z : count_z + 3],
        refs[count_z + 3 : -2],
        refs[-2:],
    )
    size_z, size_x, size_y, channels = volume.shape
    own = size_x * size_y
    quarter = own // 4
    planes = size_z + 2
    pitch = 2 * own
    first = lax.axis_index("gx") == 0
    deepen(volume, z_a, z_b, rim32, pitch)
    y_low, y_high, xy_low, xy_high = y_rims(relayed, x_rim.shape[0] // size_y)
    x_side = x_rim[...].astype(F32)
    x_low, x_high = jnp.where(first, 0.0, x_side), jnp.where(first, x_side, 0.0)
    faces = (x_low, x_high, y_low, y_high)
    for z in range(planes):
        for part, block in enumerate(faces):
            start = z * pitch + own + 8 * part
            rim32[start : start + 8, :] = block[8 * z : 8 * (z + 1), :]
        rim32[z * pitch + own + 32 : (z + 1) * pitch, :] = jnp.zeros((own - 32, channels), F32)
    corners = ((xy_low, 7, True), (xy_high, 0, True), (xy_low, 7, False), (xy_high, 0, False))
    for part, (block, row, low) in enumerate(corners):
        start = own + 32 + 8 * part + row
        value = jnp.where(first == low, 0.0, block)
        rim32[pl.ds(start, 8, stride=pitch), :] = value[:8, :]
        for z in range(8, planes):
            rim32[z * pitch + start : z * pitch + start + 1, :] = value[z : z + 1, :]
    for z in range(0, planes, 2):
        pair = [rim32[(z + i) * pitch : (z + i + 1) * pitch, :].astype(BF16) for i in range(2)]
        moved = matmul(taps[...], jnp.concatenate(pair, axis=1)).astype(BF16)
        for i in range(2):
            rim[z + i] = pair[i]
            for bc in range(9):
                cells[z + i, :, bc * channels : (bc + 1) * channels] = moved[
                    bc * own : (bc + 1) * own, i * channels : (i + 1) * channels
                ]
    weights = [w_conv[9 * a : 9 * (a + 1)].reshape(9 * channels, channels) for a in range(3)]
    window = cells[: size_z + 1].reshape((size_z + 1) * own, 9 * channels)
    both = matmul(window, jnp.concatenate(weights[:2], axis=1))
    window = cells[2:].reshape(size_z * own, 9 * channels)
    pre = both[:-own, :channels] + both[own:, channels:] + matmul(window, weights[2])
    sig = jax.nn.sigmoid(pre)
    slope[...] = (sig * (1.0 + pre * (1.0 - sig))).reshape(size_z, own, channels)
    hidden[...] = (pre * sig).astype(BF16).reshape(size_z, own, channels)
    parts = []
    for s in range(8):
        a, bc = s // 4, s % 4
        parts.append(
            jnp.concatenate(
                [hidden[2 * kz + a, bc * quarter : (bc + 1) * quarter, :] for kz in range(size_z // 2)], axis=0
            )
        )
    coarse = matmul(jnp.concatenate(parts, axis=1), w_down[...].reshape(8 * channels, w_down.shape[2]))
    coarse = coarse.astype(BF16)
    wide = coarse.shape[1]
    for send, back in zip(sends, backs):
        send[:, :wide] = coarse
        send[:, wide:] = back[...]


def rim_transpose_kernel(count_p, rim, taps_t, turned):
    planes, rows, channels = rim.shape
    share = channels // count_p
    for pair in range(planes // 2):
        sides = [rim[2 * pair + i].astype(F32).T for i in range(2)]
        moved = matmul(jnp.concatenate(sides, axis=1).astype(BF16), taps_t[...]).astype(BF16)
        for bc in range(9):
            for p in range(count_p):
                start = (bc * count_p // 2 + p // 2) * share
                turned[p % 2, start : start + share, pair * rows : (pair + 1) * rows] = moved[
                    p * share : (p + 1) * share, bc * rows : (bc + 1) * rows
                ]


def column_kernel(count_z, *refs):
    parts, picks, (column, back, x_send, send_a, send_b, corner_b) = refs[:count_z], refs[count_z], refs[count_z + 1 :]
    own_cells = parts[0].shape[0]
    wide = column.shape[1]
    pz = lax.axis_index("gz")
    for i, part in enumerate(parts):
        rows = pl.ds(pl.multiple_of((pz ^ (-i % count_z)) * own_cells, own_cells), own_cells)
        column[rows, :] = part[:, :wide]
        back[rows, :] = part[:, wide:]
    rims = matmul(picks[lax.axis_index("gx")], column[...]).astype(BF16)
    cuts, start = [], 0
    for size in (x_send.shape[0], *[send_a.shape[0]] * 2, *[corner_b.shape[0]] * 2):
        cuts.append(rims[start : start + size, :])
        start += size
    x_send[...] = cuts[0]
    send_b[...], send_a[...] = line_sides("gy", cuts[2], cuts[1])
    corner_b[...], _ = line_sides("gy", cuts[4], cuts[3])


def bottle_kernel(quarter, column, back, x_rim, relayed, shift, w_bottle, *refs):
    count = len(refs) // 2 - 1
    slices, bottle, sends, (corners, window) = refs[:count], refs[count], refs[count + 1 : -2], refs[-2:]
    cells, wide = column.shape
    outs = w_bottle.shape[2]
    side = x_rim.shape[0]
    depth = cells // quarter
    span = 4 * quarter
    picks = shift[lax.axis_index("gx")]
    window[:quarter, :] = jnp.zeros((quarter, 9 * wide), BF16)
    window[(depth + 1) * quarter :, :] = jnp.zeros((quarter, 9 * wide), BF16)
    edge = side // (depth // 4)
    y_low, y_high, xy_low, xy_high = y_rims(relayed, depth)
    y_low, y_high = y_low.astype(BF16), y_high.astype(BF16)
    for g in range(depth // 4):
        corners[g, :4, :] = xy_low[4 * g : 4 * g + 4, :]
        corners[g, 4:8, :] = xy_high[4 * g : 4 * g + 4, :]
        corners[g, 8:, :] = jnp.zeros((8, wide), F32)
        faces = [block[g * edge : (g + 1) * edge, :] for block in (x_rim, y_low, y_high)]
        rows = [column[g * span : (g + 1) * span, :], *faces, corners[g].astype(BF16)]
        moved = matmul(picks, jnp.concatenate(rows, axis=0)).astype(BF16)
        for bc in range(9):
            window[quarter + g * span : quarter + (g + 1) * span, bc * wide : (bc + 1) * wide] = moved[
                bc * span : (bc + 1) * span, :
            ]
    pre = matmul(window[2 * quarter :, :], w_bottle[18:].reshape(9 * wide, outs))
    both = None
    for bc in range(9):
        part = slice(bc * wide, (bc + 1) * wide)
        weight = jnp.concatenate([w_bottle[bc], w_bottle[9 + bc]], axis=1)
        term = matmul(window[: cells + quarter, part], weight)
        both = term if both is None else both + term
    pre = pre + both[:cells, :outs] + both[quarter:, outs:]
    sig = jax.nn.sigmoid(pre)
    bottle[...] = (pre * sig).astype(BF16)
    slope = sig * (1.0 + pre * (1.0 - sig))
    value = (back[...].astype(F32) * slope).astype(BF16)
    for send, block in zip(sends, slices):
        send[:cells, :] = value
        send[cells:, :] = block[...]


def slices_kernel(count_y, quarter, column, *refs):
    sends, slices = refs[:-1], refs[-1]
    cells, wide = column.shape
    span = 4 * quarter
    half = 2 * quarter
    lane = lax.broadcasted_iota(jnp.int32, (half, 128), 1)
    for pair in range(wide // 128):
        for g in range(cells // span):
            top = column[g * span : g * span + half, pair * 128 : (pair + 1) * 128].astype(F32)
            end = column[g * span + half : (g + 1) * span, pair * 128 : (pair + 1) * 128].astype(F32)
            rows = slice(g * half, (g + 1) * half)
            slices[2 * pair, rows, :] = jnp.where(lane < 64, top, pltpu.roll(end, 64, 1)).astype(BF16)
            slices[2 * pair + 1, rows, :] = jnp.where(lane < 64, pltpu.roll(top, 64, 1), end).astype(BF16)
    p = plane_index(count_y)
    lines = slices.shape[1]
    for i, send in enumerate(sends):
        send[:lines, :] = slices[p ^ (2 * i)]
        send[lines:, :] = slices[p ^ (2 * i + 1)]


def coarse_grad_kernel(count_y, count_z, quarter, *refs):
    grads, (bottle, shift, w_bottle) = refs[: -count_z - 6], refs[-count_z - 6 : -count_z - 3]
    sends, (window, gathered, blocks) = refs[-count_z - 3 : -3], refs[-3:]
    count_p = len(grads)
    cells, outs = bottle.shape
    rows = count_p * quarter
    depth = cells // quarter
    own_cells = cells // count_z
    inputs = w_bottle.shape[1]
    p = plane_index(count_y)
    for i, part in enumerate(grads):
        gathered[p ^ (-i % count_p)] = part[:cells, :]
    mine = pl.multiple_of(p * quarter, quarter)
    picks = jnp.concatenate([shift[pl.ds((8 - bc) * rows + mine, quarter), :] for bc in range(9)], axis=0)
    window[:quarter, :] = jnp.zeros((quarter, 9 * outs), BF16)
    window[(depth + 1) * quarter :, :] = jnp.zeros((quarter, 9 * outs), BF16)
    for z in range(depth):
        plane = jnp.concatenate([gathered[q, z * quarter : (z + 1) * quarter, :] for q in range(count_p)], axis=0)
        moved = matmul(picks, plane).astype(BF16)
        for bc in range(9):
            window[(z + 1) * quarter : (z + 2) * quarter, bc * outs : (bc + 1) * outs] = moved[
                bc * quarter : (bc + 1) * quarter, :
            ]
    total = None
    for a in range(3):
        weight = jnp.concatenate([w_bottle[9 * a + bc] for bc in range(9)], axis=1)
        term = matmul_nt(window[(2 - a) * quarter : (2 - a + depth) * quarter, :], weight)
        total = term if total is None else total + term
    total = total.astype(BF16)
    for q in range(count_z):
        blocks[q, :, :inputs] = total[q * own_cells : (q + 1) * own_cells, :]
        blocks[q, :, inputs:] = bottle[q * own_cells : (q + 1) * own_cells, :]
    hand_out(blocks, sends, lax.axis_index("gz"))


def wide_kernel(count_y, quarter, *refs):
    parts, (wide, grads) = refs[:-2], refs[-2:]
    count_p, cells, outs = grads.shape
    rows = count_p * quarter
    depth = cells // quarter
    take_in([part.at[:cells, :] for part in parts], grads, plane_index(count_y))
    planes = [
        jnp.concatenate([grads[q, z * quarter : (z + 1) * quarter, :] for q in range(count_p)], axis=0)
        for z in range(depth)
    ]
    zeros = jnp.zeros((rows, outs), BF16)
    for j in range(depth // 2):
        for slot in range(5):
            z = j // 2 * 4 + j % 2 + slot - 1
            wide[j * rows : (j + 1) * rows, slot * outs : (slot + 1) * outs] = planes[z] if 0 <= z < depth else zeros


def coarse_transpose_kernel(count_y, shift, *refs):
    parts, (turned, slices) = refs[:-2], refs[-2:]
    count_p, lines, _ = slices.shape
    rows = shift.shape[1]
    quarter = rows // count_p
    p = plane_index(count_y)
    for d, part in enumerate(parts):
        start = (2 + d % 2) * lines
        slices[p ^ d] = part[start : start + lines, :]
    for j in range(lines // quarter):
        plane = jnp.concatenate([slices[q, j * quarter : (j + 1) * quarter, :] for q in range(count_p)], axis=0)
        plane = plane.astype(F32).T.astype(BF16)
        for bc in range(9):
            turned[bc * 128 : (bc + 1) * 128, j * rows : (j + 1) * rows] = matmul(
                plane, shift[(8 - bc) * rows : (9 - bc) * rows, :]
            ).astype(BF16)


def grad_bottle_kernel(turned, wide, out):
    _, channels, outs = out.shape
    full = matmul(turned[...], wide[...])
    for bc in range(9):
        top = full[bc * 128 : bc * 128 + channels, :]
        end = full[bc * 128 + channels : (bc + 1) * 128, :]
        for a in range(3):
            out[9 * a + bc] = top[:, (2 - a) * outs : (3 - a) * outs] + end[:, (4 - a) * outs : (5 - a) * outs]


def half_grad(turned, shifted, parity, chip, out, blocks):
    chips, rows, channels = blocks.shape
    group = rows // 27
    full = matmul(turned[parity], shifted[...])
    for bc in range(9):
        for a in range(3):
            t = 9 * a + bc
            for q in range(chips):
                start = (bc * chips + q) * group
                blocks[q, t * group : (t + 1) * group, :] = full[
                    start : start + group, a * channels : (a + 1) * channels
                ].astype(BF16)
    for i in range(chips):
        out[i] = blocks[chip ^ i]


def hidden_grad_kernel(count_y, count_z, *refs):
    parts, (slope, ordered, w_down, turned) = refs[:count_z], refs[count_z : count_z + 4]
    shifted, bottle, give, bottles, blocks = refs[count_z + 4 :]
    size_z, own, channels = ordered.shape
    quarter = own // 4
    inputs = w_down.shape[2]
    pz = lax.axis_index("gz")
    grad = total_of([part.at[:, :inputs] for part in parts]).astype(BF16)
    for i, part in enumerate(parts):
        bottles[pz ^ (-i % count_z)] = part[:, inputs:]
    bottle[...] = jnp.concatenate([bottles[q] for q in range(count_z)], axis=1)
    shifted[...] = jnp.zeros_like(shifted)
    for s in range(8):
        a, bc = s // 4, s % 4
        spread_grad = matmul_nt(grad, w_down[s])
        for kz in range(size_z // 2):
            z = 2 * kz + a
            part = slice(bc * quarter, (bc + 1) * quarter)
            line = slice(kz * quarter, (kz + 1) * quarter)
            value = ((spread_grad[line, :] + ordered[z, part, :].astype(F32)) * slope[z, part, :]).astype(BF16)
            for t in range(3):
                start = (z + t) * own + bc * quarter
                shifted[start : start + quarter, t * channels : (t + 1) * channels] = value
    p = plane_index(count_y)
    half_grad(turned, shifted, 1 - p % 2, p // 2, give, blocks)


def keep_kernel(count_y, shifted, turned, keep, blocks):
    p = plane_index(count_y)
    half_grad(turned, shifted, p % 2, p // 2, keep, blocks)


def output_kernel(bottle, hidden, w_up, order_t, output, rows_out):
    size_z, own, channels = hidden.shape
    quarter = own // 4
    for s in range(8):
        a, bc = s // 4, s % 4
        lifted = matmul(bottle[...], w_up[s])
        for kz in range(size_z // 2):
            z = 2 * kz + a
            part = slice(bc * quarter, (bc + 1) * quarter)
            line = slice(kz * quarter, (kz + 1) * quarter)
            rows_out[z, part, :] = (lifted[line, :] + hidden[z, part, :].astype(F32)).astype(BF16)
    for z in range(size_z):
        plane = matmul(order_t[...], rows_out[z])
        output[z] = plane.reshape(output.shape[1:]).astype(BF16)


def pair_sum_kernel(keep, got, *sends):
    for i, send in enumerate(sends):
        send[...] = (keep[i].astype(F32) + got[i].astype(F32)).astype(BF16)


def sum_kernel(*refs):
    out = refs[-1]
    out[...] = total_of(refs[:-1]).reshape(out.shape).astype(out.dtype)


def shape_of(shape, dtype=BF16):
    return jax.ShapeDtypeStruct(shape, dtype)


def gathered_body(counts, volume, cotangent, w_conv, w_down, w_bottle, w_up):
    count_x, count_y, count_z = counts
    count_p = count_x * count_y
    size_z, size_x, size_y, channels = volume.shape
    wide = w_down.shape[2]
    group = w_bottle.shape[2]
    half_x, half_y = size_x // 2, size_y // 2
    own = size_x * size_y
    quarter = half_x * half_y
    own_cells = size_z // 2 * quarter
    cells = count_z * own_cells
    depth = count_z * size_z // 2
    rows = count_p * quarter
    planes = size_z + 2
    share_c = channels // count_p
    share_w = wide // count_p
    plane_axes = ("gx", "gy")

    order, taps = fine_maps(size_x, size_y)
    pair_taps = np.zeros((2, 2 * own, 9, 2, own), np.float32)
    for i in range(2):
        pair_taps[i, :, :, i, :] = taps.transpose(2, 0, 1)
    shift = coarse_maps(count_x, count_y, half_x, half_y)
    order_m = jnp.asarray(order, BF16)
    order_t = jnp.asarray(order.T, BF16)
    taps_m = jnp.asarray(taps.reshape(9 * own, 2 * own), BF16)
    taps_t = jnp.asarray(pair_taps.reshape(4 * own, 18 * own), BF16)
    shift_m = jnp.asarray(shift.reshape(9 * rows, rows), BF16)

    send_maps, rim_maps = column_maps(half_x, half_y, depth)
    send_m = jnp.asarray(send_maps, BF16)
    rim_m = jnp.asarray(rim_maps.reshape(count_x, 36 * quarter, 8 * quarter), BF16)

    w_conv_t = jnp.transpose(w_conv, (1, 0, 2))
    w_bottle_t = jnp.transpose(w_bottle, (1, 0, 2))
    send_a, send_b = local_call(ends_kernel, "ends", [shape_of((size_x, size_y, channels))] * 2)(volume)
    z_pairs = line_pairs(count_z)
    z_b = lax.ppermute(send_b, "gz", z_pairs[1])
    z_a = lax.ppermute(send_a, "gz", z_pairs[0])
    *backs, ordered = local_call(
        lambda *refs: back_kernel(count_z, *refs),
        "back",
        [shape_of((own_cells, group))] * count_z + [shape_of((size_z, own, channels))],
        [pltpu.VMEM((count_z, own_cells, group), BF16)],
    )(cotangent, w_up, order_m)
    sends = local_call(
        faces_kernel,
        "faces",
        [shape_of((16 * size_y, channels))] + [shape_of((planes * size_x, channels))] * 2 + [shape_of((16, channels))],
        [pltpu.VMEM((16 * own, channels), F32)],
    )(volume, z_a, z_b)
    x_send, send_a, send_b, corner_b = sends
    x_rim, across, corner = swap_rims(x_send, send_b, corner_b, counts)
    relayed = relay_rims(x_rim, across, corner, send_a, counts)
    hidden, slope, rim, *sends = local_call(
        lambda *refs: hidden_kernel(count_z, *refs),
        "hidden",
        [
            shape_of((size_z, own, channels)),
            shape_of((size_z, own, channels), F32),
            shape_of((planes, 2 * own, channels)),
        ]
        + [shape_of((own_cells, wide + group))] * count_z,
        [
            pltpu.VMEM((planes * 2 * own, channels), F32),
            pltpu.VMEM((planes, own, 9 * channels), BF16),
        ],
        flops=2_000_000_000,
    )(volume, z_a, z_b, x_rim, relayed, taps_m, w_conv_t, w_down, *backs)
    parts = trade(sends, "gz", count_z)
    column, back, *sends = local_call(
        lambda *refs: column_kernel(count_z, *refs),
        "column",
        [shape_of((cells, wide)), shape_of((cells, group)), shape_of((depth * half_y, wide))]
        + [shape_of((depth * half_x, wide))] * 2
        + [shape_of((depth, wide))],
    )(parts[0], *parts[:0:-1], send_m)
    x_send, send_a, send_b, corner_b = sends
    x_rim, across, corner = swap_rims(x_send, send_b, corner_b, counts)
    relayed = relay_rims(x_rim, across, corner, send_a, counts)
    slices = local_call(
        lambda *refs: slices_kernel(count_y, quarter, *refs),
        "slices",
        [shape_of((cells, 128))] * (count_p // 2),
        [pltpu.VMEM((count_p, cells // 2, 128), BF16)],
    )(column)
    column, *slices = lax.optimization_barrier((column, *slices))
    bottle, *sends = local_call(
        lambda *refs: bottle_kernel(quarter, *refs),
        "bottle",
        [shape_of((cells, group))] + [shape_of((2 * cells, group))] * (count_p // 2),
        [
            pltpu.VMEM((depth // 4, 16, wide), F32),
            pltpu.VMEM(((depth + 2) * quarter, 9 * wide), BF16),
        ],
        flops=2_000_000_000,
    )(column, back, x_rim, relayed, rim_m, w_bottle_t, *slices)
    grads = [None] * count_p
    grads[0] = sends[0]
    for d in (6, 4, 2):
        grads[d] = swap(sends[d // 2], plane_axes, count_p, d)
    for d in (0, 2, 4, 6):
        grads[d + 1] = swap(grads[d], plane_axes, count_p, 1)
    sends = local_call(
        lambda *refs: coarse_grad_kernel(count_y, count_z, quarter, *refs),
        "coarse_grad",
        [shape_of((own_cells, wide + group))] * count_z,
        [
            pltpu.VMEM(((depth + 2) * quarter, 9 * group), BF16),
            pltpu.VMEM((count_p, cells, group), BF16),
            pltpu.VMEM((count_z, own_cells, wide + group), BF16),
        ],
    )(grads[0], *grads[:0:-1], bottle, shift_m, w_bottle_t)
    parts = trade(sends, "gz", count_z)
    rim, late, _ = lax.optimization_barrier((rim, grads[0], sends[1]))
    turned = local_call(
        lambda *refs: rim_transpose_kernel(count_p, *refs),
        "rim_transpose",
        shape_of((2, 9 * channels // 2, planes * own)),
    )(rim, taps_t)
    coarse_turned = local_call(
        lambda *refs: coarse_transpose_kernel(count_y, *refs),
        "coarse_transpose",
        shape_of((18 * share_w, depth // 2 * rows)),
        [pltpu.VMEM((count_p, cells // 2, 128), BF16)],
    )(shift_m, late, *grads[1:])
    turned, coarse_turned = lax.optimization_barrier((turned, coarse_turned))
    shifted, bottle, give = local_call(
        lambda *refs: hidden_grad_kernel(count_y, count_z, *refs),
        "hidden_grad",
        [
            shape_of((planes * own, 3 * channels)),
            shape_of((own_cells, wide)),
            shape_of((count_p // 2, 27 * share_c, channels)),
        ],
        [
            pltpu.VMEM((count_z, own_cells, group), BF16),
            pltpu.VMEM((count_p // 2, 27 * share_c, channels), BF16),
        ],
    )(parts[0], *parts[:0:-1], slope, ordered, w_down, turned)
    got = swap(give, plane_axes, count_p, 1)
    keep = local_call(
        lambda *refs: keep_kernel(count_y, *refs),
        "keep",
        shape_of((count_p // 2, 27 * share_c, channels)),
        [pltpu.VMEM((count_p // 2, 27 * share_c, channels), BF16)],
    )(shifted, turned)
    output = local_call(
        output_kernel,
        "output",
        shape_of(volume.shape),
        [pltpu.VMEM((size_z, own, channels), BF16)],
    )(bottle, hidden, w_up, order_t)
    sends = local_call(
        pair_sum_kernel,
        "pair_sum",
        [shape_of((27 * share_c, channels))] * (count_p // 2),
    )(keep, got)
    parts = [sends[0]] + [swap(sends[d // 2], plane_axes, count_p, d) for d in (6, 4, 2)]
    part = local_call(sum_kernel, "plane_sum", shape_of((27 * share_c, channels)))(*parts)
    part, output = lax.optimization_barrier((part, output))
    got = swap(part, "gz", count_z, 1)
    wide_grads = local_call(
        lambda *refs: wide_kernel(count_y, quarter, *refs),
        "wide",
        shape_of((depth // 2 * rows, 5 * group)),
        [pltpu.VMEM((count_p, cells, group), BF16)],
    )(*grads)
    got, wide_grads = lax.optimization_barrier((got, wide_grads))
    part = local_call(sum_kernel, "depth_sum", shape_of((27 * share_c, channels)))(part, got)
    got = swap(part, "gz", count_z, 2)
    grad_bottle = local_call(
        grad_bottle_kernel,
        "grad_bottle",
        shape_of((27, share_w, group), F32),
        flops=4_000_000_000,
    )(coarse_turned, wide_grads)
    grad_conv = local_call(
        sum_kernel,
        "grad_conv",
        shape_of((27, share_c, channels), F32),
    )(part, got)
    return (output, jnp.transpose(grad_conv, (1, 0, 2)), jnp.transpose(grad_bottle, (1, 0, 2)))


def with_halo(cells, sides, width):
    for axis, dim in sides:
        count = lax.axis_size(axis)
        ends = count - 1
        head = lax.slice_in_dim(cells, 0, width, axis=dim)
        tail = lax.slice_in_dim(cells, cells.shape[dim] - width, cells.shape[dim], axis=dim)
        cells = jnp.concatenate(
            [
                lax.ppermute(tail, axis, [(i, (i + 1) % count) for i in range(ends)]),
                cells,
                lax.ppermute(head, axis, [((i + 1) % count, i) for i in range(ends)]),
            ],
            axis=dim,
        )
    return cells


def silu_slope(values):
    sig = jax.nn.sigmoid(values)
    return sig * (1.0 + values * (1.0 - sig))


def conv_forward(padded, weight, extent):
    size_z, size_x, size_y = extent
    count_cells = size_z * size_x * size_y
    summed = jnp.zeros((count_cells, weight.shape[2]), jnp.float32)
    for tap_index in range(27):
        shift_z, shift_x, shift_y = (tap_index // 9, tap_index // 3 % 3, tap_index % 3)
        window = padded[
            shift_z : shift_z + size_z, shift_x : shift_x + size_x, shift_y : shift_y + size_y, :
        ]
        window = window.reshape(count_cells, padded.shape[3])
        summed = summed + jnp.dot(
            window, weight[:, tap_index, :], preferred_element_type=jnp.float32
        )
    return summed.reshape(size_z, size_x, size_y, weight.shape[2])


def conv_weight_grad(padded, gradient, extent):
    size_z, size_x, size_y = extent
    count_cells = size_z * size_x * size_y
    flat_gradient = gradient.reshape(count_cells, gradient.shape[3])
    pieces = []
    for tap_index in range(27):
        shift_z, shift_x, shift_y = (tap_index // 9, tap_index // 3 % 3, tap_index % 3)
        window = padded[
            shift_z : shift_z + size_z, shift_x : shift_x + size_x, shift_y : shift_y + size_y, :
        ]
        window = window.reshape(count_cells, padded.shape[3])
        pieces.append(
            lax.dot_general(
                window, flat_gradient, (((0,), (0,)), ((), ())), preferred_element_type=jnp.float32
            )
        )
    return jnp.stack(pieces, axis=1)


def conv_input_grad(padded, weight, extent):
    size_z, size_x, size_y = extent
    count_cells = size_z * size_x * size_y
    summed = jnp.zeros((count_cells, weight.shape[0]), jnp.float32)
    for tap_index in range(27):
        shift_z, shift_x, shift_y = (2 - tap_index // 9, 2 - tap_index // 3 % 3, 2 - tap_index % 3)
        window = padded[
            shift_z : shift_z + size_z, shift_x : shift_x + size_x, shift_y : shift_y + size_y, :
        ]
        window = window.reshape(count_cells, padded.shape[3])
        summed = summed + lax.dot_general(
            window,
            weight[:, tap_index, :],
            (((1,), (1,)), ((), ())),
            preferred_element_type=jnp.float32,
        )
    return summed.reshape(size_z, size_x, size_y, weight.shape[0])


def pool_features(fine, kernel):
    size_z, size_x, size_y, channels = fine.shape
    blocks = fine.reshape(size_z // 2, 2, size_x // 2, 2, size_y // 2, 2, channels)
    kernel_cube = kernel.reshape(2, 2, 2, kernel.shape[1], kernel.shape[2])
    return jnp.einsum(
        "zaxbycf,abcfg->zxyg", blocks, kernel_cube, preferred_element_type=jnp.float32
    )


def pool_adjoint(coarse_in, kernel):
    size_z, size_x, size_y, wide_channels = coarse_in.shape
    kernel_cube = kernel.reshape(2, 2, 2, kernel.shape[1], kernel.shape[2])
    result = jnp.einsum(
        "zxyg,abcfg->zaxbycf", coarse_in, kernel_cube, preferred_element_type=jnp.float32
    )
    return result.reshape(2 * size_z, 2 * size_x, 2 * size_y, kernel.shape[1])


def lift_features(coarse_in, kernel):
    size_z, size_x, size_y, wide_channels = coarse_in.shape
    kernel_cube = kernel.reshape(2, 2, 2, kernel.shape[1], kernel.shape[2])
    result = jnp.einsum(
        "zxyg,abcgf->zaxbycf", coarse_in, kernel_cube, preferred_element_type=jnp.float32
    )
    return result.reshape(2 * size_z, 2 * size_x, 2 * size_y, kernel.shape[2])


def lift_adjoint(fine, kernel):
    size_z, size_x, size_y, channels = fine.shape
    blocks = fine.reshape(size_z // 2, 2, size_x // 2, 2, size_y // 2, 2, channels)
    kernel_cube = kernel.reshape(2, 2, 2, kernel.shape[1], kernel.shape[2])
    return jnp.einsum(
        "zaxbycf,abcgf->zxyg", blocks, kernel_cube, preferred_element_type=jnp.float32
    )


def column_body(volume, cotangent, w_conv, w_down, w_bottle, w_up):
    size_z, size_x, size_y, channels = volume.shape
    group_channels = w_bottle.shape[2]
    half_x = size_x // 2
    half_y = size_y // 2
    padded = with_halo(volume, (("gx", 1), ("gy", 2), ("gz", 0)), 1)
    pre_hidden = conv_forward(padded, w_conv, (size_z, size_x, size_y))
    hidden = jax.nn.silu(pre_hidden).astype(jnp.bfloat16)
    hidden_slope = silu_slope(pre_hidden)
    coarse = pool_features(hidden, w_down).astype(jnp.bfloat16)
    stacked = lax.all_gather(coarse, "gz", axis=0, tiled=True)
    rimmed = with_halo(stacked, (("gx", 1), ("gy", 2)), 1)
    column_z = rimmed.shape[0]
    coarse_pad = jnp.pad(rimmed, ((1, 1), (0, 0), (0, 0), (0, 0)))
    pre_bottle = conv_forward(coarse_pad, w_bottle, (column_z, half_x, half_y))
    bottle = jax.nn.silu(pre_bottle).astype(jnp.bfloat16)
    bottle_slope = silu_slope(pre_bottle)
    own_start = lax.axis_index("gz") * group_channels
    own_up = lax.dynamic_slice_in_dim(w_up, own_start, group_channels, 1)
    lifted = lax.psum_scatter(
        lift_features(bottle, own_up).astype(jnp.bfloat16), "gz", scatter_dimension=0, tiled=True
    ).astype(jnp.float32)
    output = (lifted + hidden.astype(jnp.float32)).astype(jnp.bfloat16)
    back_bottle = lift_adjoint(cotangent, w_up).astype(jnp.bfloat16)
    split_grad = lax.all_to_all(back_bottle, "gz", split_axis=3, concat_axis=0, tiled=True)
    bottle_grad = (split_grad.astype(jnp.float32) * bottle_slope).astype(jnp.bfloat16)
    grad_bottle = lax.psum_scatter(
        conv_weight_grad(coarse_pad, bottle_grad, (column_z, half_x, half_y)),
        ("gx", "gy"),
        scatter_dimension=0,
        tiled=True,
    )
    grad_rimmed = with_halo(bottle_grad, (("gx", 1), ("gy", 2)), 1)
    grad_pad = jnp.pad(grad_rimmed, ((1, 1), (0, 0), (0, 0), (0, 0)))
    coarse_grad = lax.psum_scatter(
        conv_input_grad(
            grad_pad, w_bottle, (lax.axis_size("gz") * (size_z // 2), half_x, half_y)
        ).astype(jnp.bfloat16),
        "gz",
        scatter_dimension=0,
        tiled=True,
    )
    hidden_grad = (
        (pool_adjoint(coarse_grad, w_down) + cotangent.astype(jnp.float32)) * hidden_slope
    ).astype(jnp.bfloat16)
    full_term = conv_weight_grad(padded, hidden_grad, (size_z, size_x, size_y))
    depth_summed = lax.psum(full_term.astype(jnp.bfloat16), "gz").astype(jnp.float32)
    grad_conv = lax.psum_scatter(depth_summed, ("gx", "gy"), scatter_dimension=0, tiled=True)
    return (output, grad_conv, grad_bottle)


def fits_one_plane(counts, brick, wide):
    count_p = counts[0] * counts[1]
    size_z, size_x, size_y, channels = brick
    return (
        counts == (2, 4, 4)
        and count_p * (size_x // 2) * (size_y // 2) == 128
        and wide // count_p == 64
        and (size_z, size_x, size_y, channels) == (8, 8, 8, 128)
    )


def solution(mesh):
    in_specs = (
        P("gz", "gx", "gy", None),
        P("gz", "gx", "gy", None),
        P(),
        P(),
        P(None, None, "gz"),
        P(),
    )
    out_specs = (
        P("gz", "gx", "gy", None),
        P(("gx", "gy"), None, None),
        P(("gx", "gy"), None, "gz"),
    )
    counts = (mesh.shape["gx"], mesh.shape["gy"], mesh.shape["gz"])

    def body(volume, cotangent, w_conv, w_down, w_bottle, w_up):
        if fits_one_plane(counts, volume.shape, w_down.shape[2]):
            return gathered_body(counts, volume, cotangent, w_conv, w_down, w_bottle, w_up)
        return column_body(volume, cotangent, w_conv, w_down, w_bottle, w_up)

    return jax.shard_map(body, mesh=mesh, in_specs=in_specs, out_specs=out_specs, check_vma=False)
```
